32 devices in a mesh: parts: 2 (over y), mem: 4 (over z), tp: 2 (over x), rep: 2 (over core).
Axes of the slice: x: 2, y: 2, z: 4, core: 2. Of those that a mesh axis runs over, the one named last changes fastest.
Arguments:
- hidden: bfloat16 [4096, 4608], P(('parts', 'mem', 'rep'), 'tp'), parts along dimension 0, may hold values from -40 to 40
- row_ids: int32 [4096, 16], P(('parts', 'mem', 'rep'), 'tp'), parts along dimension 0, may hold values from 0 to 4095, as said below
- row_place: int32 [8192], P('parts'), parts along dimension 0, may hold values from 0 to 4095, as said below
- table_codes: bfloat16 [32, 4096, 80], P(('parts', 'tp'), 'mem'), parts along dimension 0, may hold values from -4 to 4
- table_scales: bfloat16 [32, 4096, 5], P(('parts', 'tp'), 'mem'), parts along dimension 0, may hold values from 0.25 to 4
- key_weight: bfloat16 [1280, 4608], P(None, ('tp', 'rep')), may hold values from -0.36336105 to 0.36336105
- value_weight: bfloat16 [1280, 4608], P(None, ('tp', 'rep')), may hold values from -0.36336105 to 0.36336105
- conv_weight: float32 [4, 4608], P(None, 'tp'), may hold values from -2.5 to 2.5
Outputs:
- output: bfloat16 [4096, 4608], P(('parts', 'mem', 'rep'), 'tp'), parts along dimension 0
The draws below stay inside these ranges and needn't reach their ends.
There are 2 independent parts, one for each index of `parts`. The reference program is written for one: setup_inputs(seed, part) draws one part's arguments, and reference() takes and returns one part's arrays. A program takes and returns all parts, laid end to end along the dimension named above; an argument that names none is the same for every part. Nothing has to cross between parts.
Inputs may be any that keep to these rules, and one draw needn't show every extreme that they name: row_place is a permutation; row r of table g is stored at position row_place[r], on mem index row_place[r] // 1024. `row_ids`: within the 256 tokens of one index of mem+rep and the 8 heads of one index of tp, at most 1280 of the 2048 requested rows are stored on one index of mem; for each index of rep and of tp, some index of mem receives exactly 1280 from every such block.
All inputs are finite; a program needn't handle non-finite values.
Results may differ from the reference program's by a relative error of at most 0.0039.
Values may be sent and summed in bfloat16 or wider, within the bound.
No kernel may reach another device: no remote copies, remote signals or barrier semaphores. Data moves between devices by JAX's collectives and lax.ppermute only.
A program may use at most 128 MiB of HBM per device.

```python
import math
import jax
import jax.numpy as jnp
from jax import lax

D = 4608
MHEADS = 16
HW = 80
KERNEL = 4
DILATION = 3
TOK_DEV = 256
ROWS_DEV = 1024
HPT = 8
E = 1280
NBLK = 5
ROWS = 4096
TOKENS = 2048
LENGTH = 512
REQ = 2048
CAP = 1280
N_MEM = 4
N_REP = 2


def column_factor(width):
    return 10.0 ** (jnp.arange(width, dtype=jnp.float32) / width - 0.5)


def shared_place(key):
    return jax.random.permutation(jax.random.fold_in(key, 5), ROWS).astype(jnp.int32)


def draw_row_place(key, part):
    return shared_place(key)


def draw_hidden(key, part):
    key = jax.random.fold_in(key, 11)
    row_key, value_key = jax.random.split(key)
    row_scale = jnp.exp(jax.random.uniform(row_key, (TOKENS, 1), jnp.float32, math.log(0.3), math.log(3.0)))
    values = jax.random.truncated_normal(value_key, -4.0, 4.0, (TOKENS, D), jnp.float32)
    return (values * row_scale * column_factor(D)[None, :]).astype(jnp.bfloat16)


def draw_key_weight(key, part):
    key = jax.random.fold_in(key, 21)
    values = jax.random.truncated_normal(key, -4.0, 4.0, (E, D), jnp.float32)
    return (values * column_factor(D)[None, :] / math.sqrt(E)).astype(jnp.bfloat16)


def draw_value_weight(key, part):
    key = jax.random.fold_in(key, 23)
    values = jax.random.truncated_normal(key, -4.0, 4.0, (E, D), jnp.float32)
    return (values * column_factor(D)[None, :] / math.sqrt(E)).astype(jnp.bfloat16)


def draw_row_ids(key, part):
    placement = shared_place(key)
    inverse = jnp.argsort(placement, stable=True).astype(jnp.int32)
    key = jax.random.fold_in(key, 31)
    sub_keys = jax.random.split(key, 5)
    blocks = TOKENS // TOK_DEV
    tp_groups = MHEADS // HPT
    forced = jax.random.randint(sub_keys[0], (N_REP, tp_groups), 0, N_MEM).astype(jnp.int32)
    forced_owner = forced[jnp.arange(blocks, dtype=jnp.int32) % N_REP]
    owner_bias = jax.random.randint(sub_keys[1], (blocks, tp_groups, N_MEM, 1), 0, 8).astype(jnp.int32)
    owner_noise = jax.random.randint(sub_keys[2], (blocks, tp_groups, N_MEM, CAP), 0, 4096).astype(jnp.int32)
    owner_grid = jnp.arange(N_MEM, dtype=jnp.int32)[None, None, :, None]
    slot_score = jnp.where(owner_grid == forced_owner[:, :, None, None], 8192, owner_bias * 512 + owner_noise)
    slot_score = slot_score.reshape(blocks, tp_groups, N_MEM * CAP) * (N_MEM * CAP) + jnp.arange(N_MEM * CAP, dtype=jnp.int32)
    chosen = lax.top_k(slot_score, REQ)[1].astype(jnp.int32) // CAP
    order_keys = jax.random.randint(sub_keys[3], (blocks, tp_groups, REQ), 0, 1024).astype(jnp.int32) * REQ + jnp.arange(REQ, dtype=jnp.int32)
    shuffle = jnp.argsort(order_keys, axis=-1, stable=True)
    owners = jnp.take_along_axis(chosen, shuffle, axis=-1)
    within = jax.random.randint(sub_keys[4], (blocks, tp_groups, REQ), 0, ROWS_DEV).astype(jnp.int32)
    row_values = inverse[owners * ROWS_DEV + within]
    row_values = row_values.reshape(blocks, tp_groups, TOK_DEV, HPT).transpose(0, 2, 1, 3).reshape(TOKENS, MHEADS)
    return row_values.astype(jnp.int32)


def levels(key, shape, cuts, least, top_value):
    def one(axis_at, shards_of):
        draws = jax.random.uniform(jax.random.fold_in(jax.random.fold_in(key, 6), axis_at), (shards_of,), jnp.float32, least / len(cuts), top_value / len(cuts))
        return jnp.repeat(jnp.exp(draws), shape[axis_at] // shards_of).reshape((-1,) + (1,) * (len(shape) - axis_at - 1))

    level = one(*cuts[0])
    for cut in cuts[1:]:
        level = level * one(*cut)
    return level


def centred(own_key, dims, scale, limit, cuts=(), held_as=jnp.bfloat16):
    factor_of = levels(own_key, dims, cuts, -0.22, 0.18) if cuts else 1.0
    array = jax.random.normal(own_key, dims, jnp.float32) * scale * factor_of
    return jnp.minimum(jnp.maximum(array, -limit), limit).astype(held_as)


def setup_inputs(seed: int = 0, part: int = 0) -> dict:
    arg_keys = jax.random.split(jax.random.key(seed), 9)
    part_keys = jax.random.split(jax.random.fold_in(arg_keys[8], part), 9)
    hidden = draw_hidden(jax.random.fold_in(jax.random.fold_in(arg_keys[8], part), 71), part)
    row_ids = draw_row_ids(jax.random.fold_in(jax.random.fold_in(arg_keys[8], part), 71), part)
    row_place = draw_row_place(jax.random.fold_in(jax.random.fold_in(arg_keys[8], part), 71), part)
    table_codes = centred(part_keys[3], (MHEADS, ROWS, HW), 1.0, 4.0, ((0, 2), (1, 4)))
    table_scales = jnp.clip(jnp.exp(math.log(4.0) - 2.7725887 * jax.random.uniform(part_keys[4], (MHEADS, ROWS, NBLK), jnp.float32) ** levels(part_keys[4], (MHEADS, ROWS, NBLK), ((0, 2), (1, 4)), -0.2, 0.2)), 0.25, 4.0).astype(jnp.bfloat16)
    key_weight = draw_key_weight(jax.random.fold_in(arg_keys[8], 71), part)
    value_weight = draw_value_weight(jax.random.fold_in(arg_keys[8], 71), part)
    conv_weight = centred(arg_keys[7], (KERNEL, D), 0.5, 2.5, ((1, 2),), jnp.float32)
    return dict(hidden=hidden, row_ids=row_ids, row_place=row_place, table_codes=table_codes, table_scales=table_scales, key_weight=key_weight, value_weight=value_weight, conv_weight=conv_weight)


EPSILON = 1e-06

def hadamard_block():
    entry_index = jnp.arange(16, dtype=jnp.int32)
    parity = jnp.zeros((16, 16), jnp.int32)
    for shift_bit in range(4):
        parity = parity + (entry_index[:, None] >> shift_bit & 1) * (entry_index[None, :] >> shift_bit & 1)
    return (1.0 - 2.0 * (parity % 2)).astype(jnp.float32) * 0.25

def reference(hidden, row_ids, row_place, table_codes, table_scales, key_weight, value_weight, conv_weight):
    tokens = hidden.shape[0]
    stored = row_place[row_ids]
    head_index = jnp.arange(MHEADS, dtype=jnp.int32)[None, :]
    fetched = table_codes[head_index, stored].astype(jnp.float32)
    factors = table_scales[head_index, stored].astype(jnp.float32)
    scaled = fetched.reshape(tokens, MHEADS, HW // 16, 16) * factors[..., None]
    rotated = jnp.einsum('tgbi,ij->tgbj', scaled, hadamard_block(), precision=lax.Precision.HIGHEST)
    memory = rotated.reshape(tokens, MHEADS * HW).astype(jnp.bfloat16)
    key_field = jnp.dot(memory, key_weight, preferred_element_type=jnp.float32)
    value_field = jnp.dot(memory, value_weight, preferred_element_type=jnp.float32)
    states = hidden.astype(jnp.float32)
    inverse_states = lax.rsqrt(lax.optimization_barrier(jnp.mean(states * states, axis=1)) + EPSILON)
    inverse_keys = lax.rsqrt(lax.optimization_barrier(jnp.mean(key_field * key_field, axis=1)) + EPSILON)
    gate_score = lax.optimization_barrier(jnp.sum(states * key_field, axis=1)) * inverse_states * inverse_keys / math.sqrt(D)
    gate_open = jax.nn.sigmoid(gate_score)
    gated_value = gate_open[:, None] * value_field
    normed = gated_value * lax.rsqrt(lax.optimization_barrier(jnp.mean(gated_value * gated_value, axis=1)) + EPSILON)[:, None]
    position = jnp.arange(tokens, dtype=jnp.int32) % LENGTH
    conv_sum = jnp.zeros((tokens, D), jnp.float32)
    for tap_index in range(KERNEL):
        lag_rows = DILATION * tap_index
        shifted = jnp.concatenate([jnp.zeros((lag_rows, D), jnp.float32), normed[:tokens - lag_rows]], 0)
        conv_sum = conv_sum + conv_weight[tap_index][None, :] * jnp.where((position >= lag_rows)[:, None], shifted, 0.0)
    return (states + jax.nn.silu(conv_sum) + gated_value).astype(jnp.bfloat16)
```

```python
import functools

import jax
import jax.numpy as jnp
from jax import lax
from jax.experimental import pallas as pl
from jax.experimental.pallas import tpu as pltpu
from jax.sharding import PartitionSpec as P

D = 4608
KERNEL = 4
DILATION = 3
SEQS = 4
EPSILON = 1e-06
RIM = 16
LANES = 128

F32 = jnp.float32
BF16 = jnp.bfloat16
I32 = jnp.int32


def iota(shape, axis):
    return lax.broadcasted_iota(I32, shape, axis)


def dot(a, b):
    return jnp.dot(a, b, preferred_element_type=F32)


def dot_nt(a, b, precision=None):
    return lax.dot_general(
        a, b, (((1,), (1,)), ((), ())), precision=precision, preferred_element_type=F32
    )


def unit(n, dtype):
    return (iota((n, n), 0) == iota((n, n), 1)).astype(F32).astype(dtype)


def to_bf16(x):
    return x.astype(F32).astype(BF16)


def flipped(ids):
    eye = unit(ids.shape[1], BF16)
    return (dot_nt(eye, to_bf16(ids >> 8)) * 256.0 + dot_nt(eye, to_bf16(ids & 255))).astype(I32)


def place_kernel(ids_ref, place_ref, out_ref):
    ids = ids_ref[...]
    place = place_ref[...]
    heads = ids.shape[1]
    rows = place.shape[0]
    eye = unit(LANES, BF16)
    table = jnp.concatenate(
        [dot_nt(eye, to_bf16(place >> 8)), dot_nt(eye, to_bf16(place & 255))], axis=0
    ).astype(BF16)
    turned = flipped(ids)
    for head in range(heads):
        row = turned[head : head + 1, :]
        hot = to_bf16(iota((rows, row.shape[1]), 0) == (row >> 7))
        both = dot(table, hot)
        value = both[:LANES] * 256.0 + both[LANES:]
        chosen = jnp.where(iota(value.shape, 0) == (row & 127), value, 0.0)
        out_ref[head : head + 1, :] = jnp.sum(chosen, axis=0, keepdims=True).astype(I32)


def decode_kernel(codes_ref, scales_ref, out_ref):
    width = codes_ref.shape[-1]
    blocks = scales_ref.shape[-1]
    wide = out_ref.shape[-1]
    offset = (pl.program_id(0) * width) % LANES
    spread = to_bf16((iota((blocks, width), 1) >> 4) == iota((blocks, width), 0))
    scaled = codes_ref[0].astype(F32) * dot(scales_ref[0], spread)
    upper = scaled.astype(BF16)
    lower = (scaled - upper.astype(F32)).astype(BF16)
    entry = iota((width, wide), 0)
    column = iota((width, wide), 1) - offset
    parity = entry & column & 15
    parity = parity ^ (parity >> 2)
    parity = (parity ^ (parity >> 1)) & 1
    same = (entry >> 4) == (column >> 4)
    rotation = jnp.where(same, 0.25 - 0.5 * parity.astype(F32), 0.0).astype(BF16)
    out_ref[0] = (dot(upper, rotation) + dot(lower, rotation)).astype(BF16)


def pick_kernel(width, base_ref, ids_ref, table_ref, out_ref, total):
    heads, tokens = ids_ref.shape[1:]
    rows = table_ref.shape[1]
    wide = table_ref.shape[2]
    local = flipped(ids_ref[0]) - base_ref[0]
    total[...] = jnp.zeros_like(total)
    for head in range(heads):
        hot = to_bf16(iota((tokens, rows), 1) == local[:, head : head + 1])
        start = head * width // LANES * LANES
        total[:, start : start + wide] += dot(hot, table_ref[head])
    out_ref[...] = total[:, : out_ref.shape[1]].astype(BF16)


def project_kernel(count, where_ref, *refs):
    halos = refs[:count]
    pieces = refs[count : 2 * count]
    hidden_halo, hidden = refs[2 * count : 2 * count + 2]
    weights = refs[2 * count + 2 : 2 * count + 6]
    value_ref, stats_ref = refs[2 * count + 6 : 2 * count + 8]
    held, memory, sems = refs[2 * count + 8 :]
    half = value_ref.shape[-1]
    depth = memory.shape[-1]
    rep = where_ref[0]
    tp = where_ref[1]
    copies = []
    for far in range(2):
        slot = rep if far == 0 else 1 - rep
        for which in range(2):
            copy = pltpu.make_async_copy(
                weights[2 * far + which], held.at[slot, which], sems.at[2 * far + which]
            )
            copy.start()
            copies.append(copy)
    for s in range(count):
        memory[s, :RIM] = halos[s][...]
        memory[s, RIM:] = pieces[s][...]
    for copy in copies:
        copy.wait()
    sums = [0.0] * 4
    for j in range(2):
        fields = []
        for which in range(2):
            field = None
            for s in range(count):
                at = pl.multiple_of(lax.rem(tp + count - s, count) * depth, depth)
                part = dot(memory[s], held[j, which, pl.ds(at, depth), :])
                field = part if field is None else field + part
            fields.append(field)
        keys, values = fields
        span = slice(j * half, (j + 1) * half)
        states = jnp.concatenate([hidden_halo[:, span], hidden[:, span]], axis=0).astype(F32)
        terms = (states * states, keys * keys, states * keys, values * values)
        sums = [a + jnp.sum(t, axis=1, keepdims=True) for a, t in zip(sums, terms)]
        value_ref[j] = values
    rows = memory.shape[1]
    lane = iota((rows, 8), 1)
    packed = jnp.zeros((rows, 8), F32)
    for k in range(4):
        packed = jnp.where(lane == k, sums[k], packed)
    stats_ref[...] = dot_nt(unit(8, F32), packed, lax.Precision.HIGHEST)


def finish_kernel(count, keep_ref, *refs):
    stats = refs[:count]
    value_ref, hidden_ref, taps_ref, out_ref, columns, normed = refs[count:]
    rows = normed.shape[0]
    tokens = out_ref.shape[0]

    @pl.when(pl.program_id(0) == 0)
    def _():
        total = stats[0][...]
        for other in stats[1:]:
            total = total + other[...]
        inverse_states = lax.rsqrt(total[0:1] / D + EPSILON)
        inverse_keys = lax.rsqrt(total[1:2] / D + EPSILON)
        gate = jax.nn.sigmoid(total[2:3] * inverse_states * inverse_keys / D**0.5)
        factor = gate * lax.rsqrt(gate * gate * total[3:4] / D + EPSILON)
        factor = jnp.where((iota(factor.shape, 1) < RIM) & (keep_ref[0] == 0), 0.0, factor)
        line = iota(total.shape, 0)
        both = jnp.where(line == 0, gate, jnp.where(line == 1, factor, 0.0))
        columns[...] = dot_nt(unit(rows, F32), both, lax.Precision.HIGHEST)

    values = value_ref[...]
    normed[...] = values * columns[:, 1:2]
    conv = None
    for tap in range(KERNEL):
        lag = DILATION * tap
        term = taps_ref[tap : tap + 1, :] * normed[RIM - lag : RIM - lag + tokens, :]
        conv = term if conv is None else conv + term
    gated = values[RIM:] * columns[RIM:, 0:1]
    out_ref[...] = (hidden_ref[...].astype(F32) + jax.nn.silu(conv) + gated).astype(BF16)


def whole(array):
    return pl.BlockSpec(array.shape, lambda *_: (0,) * array.ndim)


def shards(
    hidden, row_ids, row_place, table_codes, table_scales, key_weight, value_weight, conv_weight
):
    mems = lax.axis_size("mem")
    tps = lax.axis_size("tp")
    reps = lax.axis_size("rep")
    blocks = mems * reps
    tokens, heads = row_ids.shape
    rows, width = table_codes.shape[1:]
    depth = heads * width
    entries, half = key_weight.shape
    seq_length = tokens * blocks // SEQS
    assert reps == 2 and seq_length % tokens == 0 and row_place.shape[0] % LANES == 0
    block = lax.axis_index(("mem", "rep"))
    smem = pl.BlockSpec(memory_space=pltpu.SMEM)
    anywhere = pl.BlockSpec(memory_space=pl.ANY)

    def shift(x, axis, by, wrap):
        size = lax.axis_size(axis)
        pairs = [
            (i, (i + by) % size) for i in range(size) if wrap or 0 <= i + by < size
        ]
        return lax.ppermute(x, axis, pairs)

    stored = pl.pallas_call(
        place_kernel,
        out_shape=jax.ShapeDtypeStruct((heads, tokens), I32),
        name="place_rows",
    )(row_ids, row_place.reshape(-1, LANES))
    asked = lax.all_gather(stored, "mem", axis=0)

    other_key = shift(key_weight, "rep", 1, True)
    other_value = shift(value_weight, "rep", 1, True)
    hidden_halo = shift(hidden[tokens - RIM :], ("mem", "rep"), 1, False)

    wide = 2 * LANES
    decoded = pl.pallas_call(
        decode_kernel,
        grid=(heads,),
        in_specs=[
            pl.BlockSpec((1, rows, width), lambda h: (h, 0, 0)),
            pl.BlockSpec((1, rows, table_scales.shape[2]), lambda h: (h, 0, 0)),
        ],
        out_specs=pl.BlockSpec((1, rows, wide), lambda h: (h, 0, 0)),
        out_shape=jax.ShapeDtypeStruct((heads, rows, wide), BF16),
        name="decode_tables",
    )(table_codes, table_scales)

    base = (lax.axis_index("mem") * rows).astype(I32).reshape(1)
    total_width = ((heads - 1) * width // LANES) * LANES + wide
    total_width = max(total_width, depth)
    partial = pl.pallas_call(
        functools.partial(pick_kernel, width),
        grid=(mems,),
        in_specs=[
            smem,
            pl.BlockSpec((1, heads, tokens), lambda m: (m, 0, 0)),
            whole(decoded),
        ],
        out_specs=pl.BlockSpec((tokens, depth), lambda m: (m, 0)),
        out_shape=jax.ShapeDtypeStruct((mems * tokens, depth), BF16),
        scratch_shapes=[pltpu.VMEM((tokens, total_width), F32)],
        compiler_params=pltpu.CompilerParams(vmem_limit_bytes=40 << 20),
        name="pick_rows",
    )(base, asked, decoded)
    memory = lax.psum_scatter(partial, "mem", scatter_dimension=0, tiled=True)

    halo = shift(memory[tokens - RIM :], ("mem", "rep"), 1, False)
    pieces = [memory] + [shift(memory, "tp", s, True) for s in range(1, tps)]
    halos = [halo] + [shift(halo, "tp", s, True) for s in range(1, tps)]

    where = jnp.stack([lax.axis_index("rep"), lax.axis_index("tp")]).astype(I32)
    extended = tokens + RIM
    operands = (*halos, *pieces, hidden_halo, hidden)
    values, stats = pl.pallas_call(
        functools.partial(project_kernel, tps),
        in_specs=[smem] + [pl.BlockSpec(memory_space=pltpu.VMEM)] * len(operands) + [anywhere] * 4,
        out_shape=(
            jax.ShapeDtypeStruct((2, extended, half), F32),
            jax.ShapeDtypeStruct((8, extended), F32),
        ),
        scratch_shapes=[
            pltpu.VMEM((2, 2, entries, half), BF16),
            pltpu.VMEM((tps, extended, depth), BF16),
            pltpu.SemaphoreType.DMA((4,)),
        ],
        compiler_params=pltpu.CompilerParams(vmem_limit_bytes=56 << 20),
        name="project",
    )(where, *operands, key_weight, value_weight, other_key, other_value)

    all_stats = [stats] + [shift(stats, "tp", s, True) for s in range(1, tps)]
    keep = (block * tokens % seq_length != 0).astype(I32).reshape(1)
    aligned = half % LANES == 0
    if aligned:
        step = next(c for c in (384, 256, 128) if half % c == 0)
        split = lambda x: x
        spec = lambda r: pl.BlockSpec((r, step), lambda i: (0, i))
        out_shape = jax.ShapeDtypeStruct((tokens, 2 * half), BF16)
    else:
        step = half
        split = lambda x: jnp.stack([x[:, :half], x[:, half:]])
        spec = lambda r: pl.BlockSpec((None, r, step), lambda i: (i, 0, 0))
        out_shape = jax.ShapeDtypeStruct((2, tokens, half), BF16)
    per = half // step
    out = pl.pallas_call(
        functools.partial(finish_kernel, tps),
        grid=(2 * per,),
        in_specs=[smem]
        + [whole(stats)] * tps
        + [
            pl.BlockSpec((None, extended, step), lambda i: (i // per, 0, i % per)),
            spec(tokens),
            spec(KERNEL),
        ],
        out_specs=spec(tokens),
        out_shape=out_shape,
        scratch_shapes=[pltpu.VMEM((extended, 8), F32), pltpu.VMEM((extended, step), F32)],
        compiler_params=pltpu.CompilerParams(vmem_limit_bytes=40 << 20),
        name="finish",
    )(keep, *all_stats, values, split(hidden), split(conv_weight))
    return out if aligned else jnp.concatenate([out[0], out[1]], axis=1)


def solution(mesh):
    in_specs = (
        P(("parts", "mem", "rep"), "tp"),
        P(("parts", "mem", "rep"), "tp"),
        P("parts"),
        P(("parts", "tp"), "mem", None),
        P(("parts", "tp"), "mem", None),
        P(None, ("tp", "rep")),
        P(None, ("tp", "rep")),
        P(None, "tp"),
    )
    out_specs = P(("parts", "mem", "rep"), "tp")
    return jax.shard_map(shards, mesh=mesh, in_specs=in_specs, out_specs=out_specs, check_vma=False)
```

```python
import functools

import jax
import jax.numpy as jnp
from jax import lax
from jax.experimental import pallas as pl
from jax.experimental.pallas import tpu as pltpu
from jax.sharding import PartitionSpec as P

D = 4608
KERNEL = 4
DILATION = 3
SEQS = 4
EPSILON = 1e-06
RIM = 16
LANES = 128

F32 = jnp.float32
BF16 = jnp.bfloat16
I32 = jnp.int32


def iota(shape, axis):
    return lax.broadcasted_iota(I32, shape, axis)


def dot(a, b):
    return jnp.dot(a, b, preferred_element_type=F32)


def dot_nt(a, b, precision=None):
    return lax.dot_general(
        a, b, (((1,), (1,)), ((), ())), precision=precision, preferred_element_type=F32
    )


def unit(n, dtype):
    return (iota((n, n), 0) == iota((n, n), 1)).astype(F32).astype(dtype)


def to_bf16(x):
    return x.astype(F32).astype(BF16)


def place_kernel(ids_ref, place_ref, out_ref):
    place = place_ref[...]
    rows = place.shape[0]
    heads, tokens = ids_ref.shape
    eye = unit(LANES, BF16)
    table = jnp.concatenate(
        [dot_nt(eye, to_bf16(place >> 8)), dot_nt(eye, to_bf16(place & 255))], axis=0
    ).astype(BF16)
    for head in range(heads):
        row = ids_ref[head : head + 1, :]
        hot = to_bf16(iota((rows, tokens), 0) == (row >> 7))
        both = dot(table, hot)
        value = both[:LANES] * 256.0 + both[LANES:]
        chosen = jnp.where(iota(value.shape, 0) == (row & 127), value, 0.0)
        out_ref[head : head + 1, :] = jnp.sum(chosen, axis=0, keepdims=True).astype(I32)


def decode_kernel(codes_ref, scales_ref, out_ref):
    heads, width, rows = codes_ref.shape
    blocks = scales_ref.shape[0]
    entry = iota((width, 2 * width), 0)
    column = iota((width, 2 * width), 1)
    column = jnp.where(column < width, column, column - width)
    parity = entry & column & 15
    parity = parity ^ (parity >> 2)
    parity = (parity ^ (parity >> 1)) & 1
    same = (entry >> 4) == (column >> 4)
    rotation = jnp.where(same, 0.25 - 0.5 * parity.astype(F32), 0.0).astype(BF16)
    for head in range(heads):
        factors = jnp.concatenate(
            [
                jnp.broadcast_to(scales_ref[b, head : head + 1, :].astype(F32), (16, rows))
                for b in range(blocks)
            ],
            axis=0,
        )
        scaled = codes_ref[head].astype(F32) * factors
        upper = scaled.astype(BF16)
        lower = (scaled - upper.astype(F32)).astype(BF16)
        out_ref[head] = dot(rotation, jnp.concatenate([upper, lower], axis=0)).astype(BF16)


def pick_kernel(count, scalars_ref, *refs):
    pieces = refs[:count]
    table_ref, out_ref, stack = refs[count:]
    heads, width, rows = table_ref.shape
    tokens = out_ref.shape[0]
    step = pl.program_id(0)
    if count > 1:

        @pl.when(step == 0)
        def _():
            for k in range(count):
                stack[k] = pieces[k][...]

        ids = stack[scalars_ref[1 + step]]
    else:
        ids = pieces[0][step]
    local = ids - scalars_ref[0]
    found = []
    for head in range(heads):
        hot = to_bf16(iota((rows, tokens), 0) == local[head : head + 1, :])
        found.append(dot(table_ref[head], hot))
    out_ref[...] = jnp.concatenate(found, axis=0).T.astype(BF16)


def project_kernel(count, where_ref, *refs):
    halos = refs[:count]
    pieces = refs[count : 2 * count]
    hidden_halo, hidden = refs[2 * count : 2 * count + 2]
    weights = refs[2 * count + 2 : 2 * count + 6]
    value_ref, stats_ref = refs[2 * count + 6 : 2 * count + 8]
    memory, states = refs[2 * count + 8 :]
    half = value_ref.shape[-1]
    depth = memory.shape[-1]
    rep = where_ref[0]
    tp = where_ref[1]
    for s in range(count):
        memory[s, :RIM] = halos[s][...]
        memory[s, RIM:] = pieces[s][...]
    for slot in range(2):
        states[slot, :RIM] = hidden_halo[:, slot * half : (slot + 1) * half]
        states[slot, RIM:] = hidden[:, slot * half : (slot + 1) * half]
    sums = [0.0] * 4
    for far in range(2):
        slot = rep if far == 0 else 1 - rep
        fields = []
        for which in range(2):
            field = None
            for s in range(count):
                at = pl.multiple_of(lax.rem(tp + count - s, count) * depth, depth)
                part = dot(memory[s], weights[2 * far + which][pl.ds(at, depth), :])
                field = part if field is None else field + part
            fields.append(field)
        keys, values = fields
        here = states[slot].astype(F32)
        terms = (here * here, keys * keys, here * keys, values * values)
        sums = [a + jnp.sum(t, axis=1, keepdims=True) for a, t in zip(sums, terms)]
        value_ref[slot] = values
    rows = memory.shape[1]
    lane = iota((rows, 8), 1)
    packed = jnp.zeros((rows, 8), F32)
    for k in range(4):
        packed = jnp.where(lane == k, sums[k], packed)
    stats_ref[...] = dot_nt(unit(8, F32), packed, lax.Precision.HIGHEST)


def finish_kernel(count, keep_ref, *refs):
    stats = refs[:count]
    value_ref, hidden_ref, taps_ref, out_ref, columns, normed = refs[count:]
    rows = normed.shape[0]
    tokens = out_ref.shape[0]

    @pl.when(pl.program_id(0) == 0)
    def _():
        total = stats[0][...]
        for other in stats[1:]:
            total = total + other[...]
        inverse_states = lax.rsqrt(total[0:1] / D + EPSILON)
        inverse_keys = lax.rsqrt(total[1:2] / D + EPSILON)
        gate = jax.nn.sigmoid(total[2:3] * inverse_states * inverse_keys / D**0.5)
        factor = gate * lax.rsqrt(gate * gate * total[3:4] / D + EPSILON)
        factor = jnp.where((iota(factor.shape, 1) < RIM) & (keep_ref[0] == 0), 0.0, factor)
        line = iota(total.shape, 0)
        both = jnp.where(line == 0, gate, jnp.where(line == 1, factor, 0.0))
        columns[...] = dot_nt(unit(rows, F32), both, lax.Precision.HIGHEST)

    values = value_ref[...]
    normed[...] = values * columns[:, 1:2]
    conv = None
    for tap in range(KERNEL):
        lag = DILATION * tap
        term = taps_ref[tap : tap + 1, :] * normed[RIM - lag : RIM - lag + tokens, :]
        conv = term if conv is None else conv + term
    gated = values[RIM:] * columns[RIM:, 0:1]
    out_ref[...] = (hidden_ref[...].astype(F32) + jax.nn.silu(conv) + gated).astype(BF16)


def whole(array):
    return pl.BlockSpec(array.shape, lambda *_: (0,) * array.ndim)


def shards(
    hidden, row_ids, row_place, table_codes, table_scales, key_weight, value_weight, conv_weight
):
    mems = lax.axis_size("mem")
    tps = lax.axis_size("tp")
    reps = lax.axis_size("rep")
    blocks = mems * reps
    tokens, heads = row_ids.shape
    rows, width = table_codes.shape[1:]
    depth = heads * width
    half = key_weight.shape[1]
    seq_length = tokens * blocks // SEQS
    assert reps == 2 and seq_length % tokens == 0 and row_place.shape[0] % LANES == 0
    block = lax.axis_index(("mem", "rep"))
    smem = pl.BlockSpec(memory_space=pltpu.SMEM)

    def shift(x, axis, by, wrap):
        size = lax.axis_size(axis)
        pairs = [
            (i, (i + by) % size) for i in range(size) if wrap or 0 <= i + by < size
        ]
        return lax.ppermute(x, axis, pairs)

    stored = pl.pallas_call(
        place_kernel,
        out_shape=jax.ShapeDtypeStruct((heads, tokens), I32),
        name="place_rows",
    )(row_ids.T, row_place.reshape(-1, LANES))
    here = lax.axis_index("mem")
    if mems <= 4:
        asked = [stored] + [
            lax.ppermute(stored, "mem", [(i, i ^ x) for i in range(mems)]) for x in range(1, mems)
        ]
        order = [here ^ m for m in range(mems)]
    else:
        asked = [lax.all_gather(stored, "mem", axis=0)]
        order = list(range(mems))
    hidden_halo = shift(hidden[tokens - RIM :], ("mem", "rep"), 1, False)
    asked, hidden_halo = lax.optimization_barrier((asked, hidden_halo))
    other_key = shift(key_weight, "rep", 1, True)
    other_value = shift(value_weight, "rep", 1, True)

    decoded = pl.pallas_call(
        decode_kernel,
        out_shape=jax.ShapeDtypeStruct((heads, width, rows), BF16),
        compiler_params=pltpu.CompilerParams(vmem_limit_bytes=16 << 20),
        name="decode_tables",
    )(table_codes.transpose(0, 2, 1), table_scales.transpose(2, 0, 1))

    scalars = jnp.stack([here * rows] + order).astype(I32)
    partial = pl.pallas_call(
        functools.partial(pick_kernel, len(asked)),
        grid=(mems,),
        in_specs=[smem] + [whole(a) for a in asked] + [whole(decoded)],
        out_specs=pl.BlockSpec((tokens, depth), lambda m: (m, 0)),
        out_shape=jax.ShapeDtypeStruct((mems * tokens, depth), BF16),
        scratch_shapes=[pltpu.VMEM((len(asked), heads, tokens), I32)],
        compiler_params=pltpu.CompilerParams(vmem_limit_bytes=16 << 20),
        name="pick_rows",
    )(scalars, *asked, decoded)
    memory = lax.psum_scatter(partial, "mem", scatter_dimension=0, tiled=True)

    halo = shift(memory[tokens - RIM :], ("mem", "rep"), 1, False)
    pieces = [memory] + [shift(memory, "tp", s, True) for s in range(1, tps)]
    halos = [halo] + [shift(halo, "tp", s, True) for s in range(1, tps)]

    where = jnp.stack([lax.axis_index("rep"), lax.axis_index("tp")]).astype(I32)
    extended = tokens + RIM
    operands = (*halos, *pieces, hidden_halo, hidden)
    weights = (key_weight, value_weight, other_key, other_value)
    weights = [pltpu.with_memory_space_constraint(w, pltpu.VMEM) for w in weights]
    values, stats = pl.pallas_call(
        functools.partial(project_kernel, tps),
        in_specs=[smem] + [pl.BlockSpec(memory_space=pltpu.VMEM)] * (len(operands) + 4),
        out_shape=(
            jax.ShapeDtypeStruct((2, extended, half), F32),
            jax.ShapeDtypeStruct((8, extended), F32),
        ),
        scratch_shapes=[
            pltpu.VMEM((tps, extended, depth), BF16),
            pltpu.VMEM((2, extended, half), BF16),
        ],
        compiler_params=pltpu.CompilerParams(vmem_limit_bytes=24 << 20),
        name="project",
    )(where, *operands, *weights)

    all_stats = [stats] + [shift(stats, "tp", s, True) for s in range(1, tps)]
    keep = (block * tokens % seq_length != 0).astype(I32).reshape(1)
    aligned = half % LANES == 0
    if aligned:
        step = next(c for c in (384, 256, 128) if half % c == 0)
        split = lambda x: x
        spec = lambda r: pl.BlockSpec((r, step), lambda i: (0, i))
        out_shape = jax.ShapeDtypeStruct((tokens, 2 * half), BF16)
    else:
        step = half
        split = lambda x: jnp.stack([x[:, :half], x[:, half:]])
        spec = lambda r: pl.BlockSpec((None, r, step), lambda i: (i, 0, 0))
        out_shape = jax.ShapeDtypeStruct((2, tokens, half), BF16)
    per = half // step
    out = pl.pallas_call(
        functools.partial(finish_kernel, tps),
        grid=(2 * per,),
        in_specs=[smem]
        + [whole(stats)] * tps
        + [
            pl.BlockSpec((None, extended, step), lambda i: (i // per, 0, i % per)),
            spec(tokens),
            spec(KERNEL),
        ],
        out_specs=spec(tokens),
        out_shape=out_shape,
        scratch_shapes=[pltpu.VMEM((extended, 8), F32), pltpu.VMEM((extended, step), F32)],
        compiler_params=pltpu.CompilerParams(vmem_limit_bytes=16 << 20),
        name="finish",
    )(keep, *all_stats, values, split(hidden), split(conv_weight))
    return out if aligned else jnp.concatenate([out[0], out[1]], axis=1)


def solution(mesh):
    in_specs = (
        P(("parts", "mem", "rep"), "tp"),
        P(("parts", "mem", "rep"), "tp"),
        P("parts"),
        P(("parts", "tp"), "mem", None),
        P(("parts", "tp"), "mem", None),
        P(None, ("tp", "rep")),
        P(None, ("tp", "rep")),
        P(None, "tp"),
    )
    out_specs = P(("parts", "mem", "rep"), "tp")
    return jax.shard_map(shards, mesh=mesh, in_specs=in_specs, out_specs=out_specs, check_vma=False)
```

```python
import functools

import jax
import jax.numpy as jnp
from jax import lax
from jax.experimental import pallas as pl
from jax.experimental.pallas import tpu as pltpu
from jax.sharding import PartitionSpec as P

D = 4608
KERNEL = 4
DILATION = 3
SEQS = 4
EPSILON = 1e-06
RIM = 16
LANES = 128

F32 = jnp.float32
BF16 = jnp.bfloat16
I32 = jnp.int32


def iota(shape, axis):
    return lax.broadcasted_iota(I32, shape, axis)


def dot(a, b):
    return jnp.dot(a, b, preferred_element_type=F32)


def dot_nt(a, b, precision=None):
    return lax.dot_general(
        a, b, (((1,), (1,)), ((), ())), precision=precision, preferred_element_type=F32
    )


def unit(n, dtype):
    return (iota((n, n), 0) == iota((n, n), 1)).astype(F32).astype(dtype)


def to_bf16(x):
    return x.astype(F32).astype(BF16)


def place_kernel(ids_ref, place_ref, out_ref):
    place = place_ref[...]
    rows = place.shape[0]
    heads, tokens = ids_ref.shape
    eye = unit(LANES, BF16)
    table = jnp.concatenate(
        [dot_nt(eye, to_bf16(place >> 8)), dot_nt(eye, to_bf16(place & 255))], axis=0
    ).astype(BF16)
    for head in range(heads):
        row = ids_ref[head : head + 1, :]
        hot = to_bf16(iota((rows, tokens), 0) == (row >> 7))
        both = dot(table, hot)
        value = both[:LANES] * 256.0 + both[LANES:]
        chosen = jnp.where(iota(value.shape, 0) == (row & 127), value, 0.0)
        out_ref[head : head + 1, :] = jnp.sum(chosen, axis=0, keepdims=True).astype(I32)


def decode_kernel(codes_ref, scales_ref, out_ref):
    heads, width, rows = codes_ref.shape
    blocks = scales_ref.shape[0]
    entry = iota((width, 2 * width), 0)
    column = iota((width, 2 * width), 1)
    column = jnp.where(column < width, column, column - width)
    parity = entry & column & 15
    parity = parity ^ (parity >> 2)
    parity = (parity ^ (parity >> 1)) & 1
    same = (entry >> 4) == (column >> 4)
    rotation = jnp.where(same, 0.25 - 0.5 * parity.astype(F32), 0.0).astype(BF16)
    for head in range(heads):
        factors = jnp.concatenate(
            [
                jnp.broadcast_to(scales_ref[b, head : head + 1, :].astype(F32), (16, rows))
                for b in range(blocks)
            ],
            axis=0,
        )
        scaled = codes_ref[head].astype(F32) * factors
        upper = scaled.astype(BF16)
        lower = (scaled - upper.astype(F32)).astype(BF16)
        out_ref[head] = dot(rotation, jnp.concatenate([upper, lower], axis=0)).astype(BF16)


def picked(local, table_ref, head):
    rows = table_ref.shape[2]
    hot = to_bf16(iota((rows, local.shape[1]), 0) == local[head : head + 1, :])
    return dot(table_ref[head], hot).astype(BF16)


def pick_all_kernel(base_ref, ids_ref, table_ref, out_ref):
    heads, width, _ = table_ref.shape
    local = ids_ref[...] - base_ref[0]
    for head in range(heads):
        out_ref[head * width : (head + 1) * width, :] = picked(local, table_ref, head)


def pick_kernel(count, targets, scalars_ref, *refs):
    pieces = refs[:count]
    table_ref = refs[count]
    outs = refs[count + 1 : -1]
    stack = refs[-1]
    heads, width, _ = table_ref.shape
    for k in range(count):
        stack[k] = pieces[k][...]
    for n, target in enumerate(targets):
        local = stack[scalars_ref[1 + target]] - scalars_ref[0]
        for head in range(heads):
            stream, at = divmod(head, heads // 2)
            outs[2 * n + stream][at * width : (at + 1) * width, :] = picked(
                local, table_ref, head
            )


def merge_kernel(middle_ref, inner_ref, outer_ref, *refs):
    received = refs[:-2]
    out_ref, rim_ref = refs[-2:]
    total = jnp.where(middle_ref[0] == 1, inner_ref[...].astype(F32), outer_ref[...].astype(F32))
    for other in received:
        total = total + other[...].astype(F32)
    total = total.astype(BF16)
    out_ref[...] = total
    rim_ref[...] = total[:, total.shape[1] - LANES :]


def project_kernel(count, stream, where_ref, *refs):
    rims = refs[:count]
    pieces = refs[count : 2 * count]
    refs = refs[2 * count :]
    weights = refs[:4]
    if stream == 0:
        key_ref, value_ref, held, sems = refs[4:]
    else:
        begun_keys, begun_values, hidden_halo, hidden, value_ref, stats_ref = refs[4:10]
        held, sems, states = refs[10:]
    half = value_ref.shape[-1]
    depth, tokens = pieces[0].shape
    rep = where_ref[0]
    tp = where_ref[1]
    copies = []
    for far in range(2):
        for which in range(2):
            for s in range(count):
                owner = lax.rem(tp + count - s, count)
                at = pl.multiple_of((2 * owner + stream) * depth, depth)
                copy = pltpu.make_async_copy(
                    weights[2 * far + which].at[pl.ds(at, depth), :],
                    held.at[far, which, pl.ds(s * depth, depth), :],
                    sems.at[(2 * far + which) * count + s],
                )
                copy.start()
                copies.append(copy)
    body = jnp.concatenate([p[...].astype(F32) for p in pieces], axis=0).T.astype(BF16)
    rim = jnp.concatenate([r[...].astype(F32) for r in rims], axis=0).T.astype(BF16)
    memory = jnp.concatenate([rim[LANES - RIM :], body], axis=0)
    if stream == 1:
        for slot in range(2):
            states[slot, :RIM] = hidden_halo[:, slot * half : (slot + 1) * half]
            states[slot, RIM:] = hidden[:, slot * half : (slot + 1) * half]
    sums = [0.0] * 4
    for far in range(2):
        slot = rep if far == 0 else 1 - rep
        fields = []
        for which in range(2):
            for s in range(count):
                copies[(2 * far + which) * count + s].wait()
            fields.append(dot(memory, held[far, which]))
        keys, values = fields
        if stream == 0:
            key_ref[slot] = keys
            value_ref[slot] = values
        else:
            keys = keys + begun_keys[slot]
            values = values + begun_values[slot]
            here = states[slot].astype(F32)
            terms = (here * here, keys * keys, here * keys, values * values)
            sums = [a + jnp.sum(t, axis=1, keepdims=True) for a, t in zip(sums, terms)]
            value_ref[slot] = values
    if stream == 1:
        rows = memory.shape[0]
        lane = iota((rows, 8), 1)
        packed = jnp.zeros((rows, 8), F32)
        for k in range(4):
            packed = jnp.where(lane == k, sums[k], packed)
        stats_ref[...] = dot_nt(unit(8, F32), packed, lax.Precision.HIGHEST)


def finish_kernel(count, keep_ref, *refs):
    stats = refs[:count]
    value_ref, hidden_ref, taps_ref, out_ref, columns, normed = refs[count:]
    rows = normed.shape[0]
    tokens = out_ref.shape[0]

    @pl.when(pl.program_id(0) == 0)
    def _():
        total = stats[0][...]
        for other in stats[1:]:
            total = total + other[...]
        inverse_states = lax.rsqrt(total[0:1] / D + EPSILON)
        inverse_keys = lax.rsqrt(total[1:2] / D + EPSILON)
        gate = jax.nn.sigmoid(total[2:3] * inverse_states * inverse_keys / D**0.5)
        factor = gate * lax.rsqrt(gate * gate * total[3:4] / D + EPSILON)
        factor = jnp.where((iota(factor.shape, 1) < RIM) & (keep_ref[0] == 0), 0.0, factor)
        line = iota(total.shape, 0)
        both = jnp.where(line == 0, gate, jnp.where(line == 1, factor, 0.0))
        columns[...] = dot_nt(unit(rows, F32), both, lax.Precision.HIGHEST)

    values = value_ref[...]
    normed[...] = values * columns[:, 1:2]
    conv = None
    for tap in range(KERNEL):
        lag = DILATION * tap
        term = taps_ref[tap : tap + 1, :] * normed[RIM - lag : RIM - lag + tokens, :]
        conv = term if conv is None else conv + term
    gated = values[RIM:] * columns[RIM:, 0:1]
    out_ref[...] = (hidden_ref[...].astype(F32) + jax.nn.silu(conv) + gated).astype(BF16)


def whole(array):
    return pl.BlockSpec(array.shape, lambda *_: (0,) * array.ndim)


def in_vmem(array):
    return pltpu.with_memory_space_constraint(array, pltpu.VMEM)


def scattered_sum(stored, decoded, here):
    mems = lax.axis_size("mem")
    heads, width, rows = decoded.shape
    tokens = stored.shape[1]
    asked = lax.all_gather(stored, "mem", axis=0)
    partial = pl.pallas_call(
        pick_all_kernel,
        grid=(mems,),
        in_specs=[
            pl.BlockSpec(memory_space=pltpu.SMEM),
            pl.BlockSpec((None, heads, tokens), lambda m: (m, 0, 0)),
            whole(decoded),
        ],
        out_specs=pl.BlockSpec((None, heads * width, tokens), lambda m: (m, 0, 0)),
        out_shape=jax.ShapeDtypeStruct((mems, heads * width, tokens), BF16),
        compiler_params=pltpu.CompilerParams(vmem_limit_bytes=16 << 20),
        name="pick_all",
    )((here * rows).astype(I32).reshape(1), asked, decoded)
    total = lax.psum_scatter(partial, "mem", scatter_dimension=0, tiled=False)
    memory = jnp.split(total, 2, axis=0)
    return memory, [m[:, tokens - LANES :] for m in memory]


def line_sum(stored, decoded, here):
    heads, width, rows = decoded.shape
    tokens = stored.shape[1]
    asked = [stored] + [
        lax.ppermute(stored, "mem", [(i, i ^ x) for i in range(4)]) for x in range(1, 4)
    ]
    right = here >= 2
    order = [here ^ jnp.where(right, j, 3 - j) for j in range(4)]
    scalars = jnp.stack([here * rows] + order).astype(I32)
    block = jax.ShapeDtypeStruct((heads * width // 2, tokens), BF16)

    def pick(*targets):
        return pl.pallas_call(
            functools.partial(pick_kernel, 4, targets),
            in_specs=[pl.BlockSpec(memory_space=pltpu.SMEM)]
            + [pl.BlockSpec(memory_space=pltpu.VMEM)] * 5,
            out_shape=(block,) * (2 * len(targets)),
            scratch_shapes=[pltpu.VMEM((4, heads, tokens), I32)],
            compiler_params=pltpu.CompilerParams(vmem_limit_bytes=16 << 20),
            name="pick_rows",
        )(scalars, *asked, decoded)

    def after(x, *others):
        return lax.optimization_barrier((x, *others))[0]

    inward = lambda x: lax.ppermute(x, "mem", [(0, 1), (3, 2)])
    across = lambda x: lax.ppermute(x, "mem", [(1, 2), (2, 1)])
    outward = lambda x: lax.ppermute(x, "mem", [(1, 0), (2, 3)])

    farthest = pick(0)
    first = [inward(x) for x in farthest]
    second_own = pick(1)
    rest = pick(2, 3)
    inner, outer = rest[:2], rest[2:]
    middle = ((here == 1) | (here == 2)).astype(I32).reshape(1)
    memory, rims = [], []
    for n in range(2):
        crossed = across(farthest[n] + first[n])
        second = inward(after(second_own[n], first[n]))
        crossed_near = across(second_own[n] + second)
        third = inward(after(inner[n], second))
        last = outward(outer[n] + crossed)
        total, rim = pl.pallas_call(
            merge_kernel,
            in_specs=[pl.BlockSpec(memory_space=pltpu.SMEM)]
            + [pl.BlockSpec(memory_space=pltpu.VMEM)] * 5,
            out_shape=(block, jax.ShapeDtypeStruct((block.shape[0], LANES), BF16)),
            name="merge",
        )(middle, inner[n], outer[n], third, crossed_near, last)
        memory.append(total)
        rims.append(rim)
    return memory, rims


def shards(
    hidden, row_ids, row_place, table_codes, table_scales, key_weight, value_weight, conv_weight
):
    mems = lax.axis_size("mem")
    tps = lax.axis_size("tp")
    reps = lax.axis_size("rep")
    blocks = mems * reps
    tokens, heads = row_ids.shape
    rows, width = table_codes.shape[1:]
    depth = heads * width
    half = key_weight.shape[1]
    seq_length = tokens * blocks // SEQS
    assert reps == 2 and seq_length % tokens == 0 and row_place.shape[0] % LANES == 0
    block = lax.axis_index(("mem", "rep"))
    smem = pl.BlockSpec(memory_space=pltpu.SMEM)

    stored = pl.pallas_call(
        place_kernel,
        out_shape=jax.ShapeDtypeStruct((heads, tokens), I32),
        name="place_rows",
    )(row_ids.T, row_place.reshape(-1, LANES))
    decoded = pl.pallas_call(
        decode_kernel,
        out_shape=jax.ShapeDtypeStruct((heads, width, rows), BF16),
        compiler_params=pltpu.CompilerParams(vmem_limit_bytes=16 << 20),
        name="decode_tables",
    )(table_codes.transpose(0, 2, 1), table_scales.transpose(2, 0, 1))
    here = lax.axis_index("mem")
    if mems == 4:
        memory, rims = line_sum(stored, decoded, here)
    else:
        memory, rims = scattered_sum(stored, decoded, here)

    _, tail = lax.optimization_barrier((stored, hidden[tokens - RIM :]))
    needed = [(i, i + 1) for i in range(blocks - 1) if (i + 1) * tokens % seq_length]
    hidden_halo = lax.ppermute(tail, ("mem", "rep"), needed)
    other_key = lax.ppermute(key_weight, "rep", [(0, 1), (1, 0)])
    other_value = lax.ppermute(value_weight, "rep", [(0, 1), (1, 0)])
    weights = (key_weight, value_weight, other_key, other_value)

    where = jnp.stack([lax.axis_index("rep"), lax.axis_index("tp")]).astype(I32)
    extended = tokens + RIM
    part = depth // 2
    field = jax.ShapeDtypeStruct((2, extended, half), F32)
    held = pltpu.VMEM((2, 2, tps * part, half), BF16)
    sems = pltpu.SemaphoreType.DMA((4 * tps,))
    anywhere = pl.BlockSpec(memory_space=pl.ANY)
    resident = pl.BlockSpec(memory_space=pltpu.VMEM)
    limit = pltpu.CompilerParams(vmem_limit_bytes=16 << 20)
    inputs = []
    for stream in range(2):
        inner = [memory[stream]] + [
            lax.ppermute(memory[stream], "tp", [(i, (i + s) % tps) for i in range(tps)])
            for s in range(1, tps)
        ]
        rim = [
            lax.ppermute(
                rims[stream],
                ("mem", "tp", "rep"),
                [
                    ((a // reps * tps + i) * reps + a % reps, (b // reps * tps + (i + s) % tps) * reps + b % reps)
                    for a, b in needed
                    for i in range(tps)
                ],
            )
            for s in range(tps)
        ]
        inputs.append((where, *rim, *inner, *weights))
    begun = pl.pallas_call(
        functools.partial(project_kernel, tps, 0),
        in_specs=[smem] + [resident] * (2 * tps) + [anywhere] * 4,
        out_shape=(field, field),
        scratch_shapes=[held, sems],
        compiler_params=limit,
        name="project_first",
    )(*inputs[0])
    values, stats = pl.pallas_call(
        functools.partial(project_kernel, tps, 1),
        in_specs=[smem] + [resident] * (2 * tps) + [anywhere] * 4 + [resident] * 4,
        out_shape=(field, jax.ShapeDtypeStruct((8, extended), F32)),
        scratch_shapes=[held, sems, pltpu.VMEM((2, extended, half), BF16)],
        compiler_params=limit,
        name="project_second",
    )(*inputs[1], *[in_vmem(b) for b in begun], hidden_halo, hidden)

    all_stats = [stats] + [
        lax.ppermute(stats, "tp", [(i, (i + s) % tps) for i in range(tps)]) for s in range(1, tps)
    ]
    keep = (block * tokens % seq_length != 0).astype(I32).reshape(1)
    aligned = half % LANES == 0
    if aligned:
        step = next(c for c in (384, 256, 128) if half % c == 0)
        split = lambda x: x
        spec = lambda r: pl.BlockSpec((r, step), lambda i: (0, i))
        out_shape = jax.ShapeDtypeStruct((tokens, 2 * half), BF16)
    else:
        step = half
        split = lambda x: jnp.stack([x[:, :half], x[:, half:]])
        spec = lambda r: pl.BlockSpec((None, r, step), lambda i: (i, 0, 0))
        out_shape = jax.ShapeDtypeStruct((2, tokens, half), BF16)
    per = half // step
    out = pl.pallas_call(
        functools.partial(finish_kernel, tps),
        grid=(2 * per,),
        in_specs=[smem]
        + [whole(stats)] * tps
        + [
            pl.BlockSpec((None, extended, step), lambda i: (i // per, 0, i % per)),
            spec(tokens),
            spec(KERNEL),
        ],
        out_specs=spec(tokens),
        out_shape=out_shape,
        scratch_shapes=[pltpu.VMEM((extended, 8), F32), pltpu.VMEM((extended, step), F32)],
        compiler_params=pltpu.CompilerParams(vmem_limit_bytes=16 << 20),
        name="finish",
    )(keep, *all_stats, in_vmem(values), split(hidden), split(conv_weight))
    return out if aligned else jnp.concatenate([out[0], out[1]], axis=1)


def solution(mesh):
    in_specs = (
        P(("parts", "mem", "rep"), "tp"),
        P(("parts", "mem", "rep"), "tp"),
        P("parts"),
        P(("parts", "tp"), "mem", None),
        P(("parts", "tp"), "mem", None),
        P(None, ("tp", "rep")),
        P(None, ("tp", "rep")),
        P(None, "tp"),
    )
    out_specs = P(("parts", "mem", "rep"), "tp")
    return jax.shard_map(shards, mesh=mesh, in_specs=in_specs, out_specs=out_specs, check_vma=False)
```

```python
import functools

import jax
import jax.numpy as jnp
from jax import lax
from jax.experimental import pallas as pl
from jax.experimental.pallas import tpu as pltpu
from jax.sharding import PartitionSpec as P

D = 4608
KERNEL = 4
DILATION = 3
SEQS = 4
EPSILON = 1e-06
RIM = 16
LANES = 128

F32 = jnp.float32
BF16 = jnp.bfloat16
I32 = jnp.int32


def iota(shape, axis):
    return lax.broadcasted_iota(I32, shape, axis)


def dot(a, b):
    return jnp.dot(a, b, preferred_element_type=F32)


def dot_nt(a, b, precision=None):
    return lax.dot_general(
        a, b, (((1,), (1,)), ((), ())), precision=precision, preferred_element_type=F32
    )


def unit(n, dtype):
    return (iota((n, n), 0) == iota((n, n), 1)).astype(F32).astype(dtype)


def to_bf16(x):
    return x.astype(F32).astype(BF16)


def place_kernel(ids_ref, place_ref, out_ref):
    place = place_ref[...]
    rows = place.shape[0]
    heads, tokens = ids_ref.shape
    eye = unit(LANES, BF16)
    table = jnp.concatenate(
        [dot_nt(eye, to_bf16(place >> 8)), dot_nt(eye, to_bf16(place & 255))], axis=0
    ).astype(BF16)
    for head in range(heads):
        row = ids_ref[head : head + 1, :]
        hot = to_bf16(iota((rows, tokens), 0) == (row >> 7))
        both = dot(table, hot)
        value = both[:LANES] * 256.0 + both[LANES:]
        chosen = jnp.where(iota(value.shape, 0) == (row & 127), value, 0.0)
        out_ref[head : head + 1, :] = jnp.sum(chosen, axis=0, keepdims=True).astype(I32)


def decode_kernel(codes_ref, scales_ref, out_ref):
    heads, width, rows = codes_ref.shape
    blocks = scales_ref.shape[0]
    entry = iota((width, 2 * width), 0)
    column = iota((width, 2 * width), 1)
    column = jnp.where(column < width, column, column - width)
    parity = entry & column & 15
    parity = parity ^ (parity >> 2)
    parity = (parity ^ (parity >> 1)) & 1
    same = (entry >> 4) == (column >> 4)
    rotation = jnp.where(same, 0.25 - 0.5 * parity.astype(F32), 0.0).astype(BF16)
    for head in range(heads):
        factors = jnp.concatenate(
            [
                jnp.broadcast_to(scales_ref[b, head : head + 1, :].astype(F32), (16, rows))
                for b in range(blocks)
            ],
            axis=0,
        )
        scaled = codes_ref[head].astype(F32) * factors
        upper = scaled.astype(BF16)
        lower = (scaled - upper.astype(F32)).astype(BF16)
        out_ref[head] = dot(rotation, jnp.concatenate([upper, lower], axis=0)).astype(BF16)


def picked(local, table_ref, head):
    rows = table_ref.shape[2]
    hot = to_bf16(iota((rows, local.shape[1]), 0) == local[head : head + 1, :])
    return dot(table_ref[head], hot).astype(BF16)


def pick_all_kernel(base_ref, ids_ref, table_ref, out_ref):
    heads, width, _ = table_ref.shape
    local = ids_ref[...] - base_ref[0]
    for head in range(heads):
        out_ref[head * width : (head + 1) * width, :] = picked(local, table_ref, head)


def pick_kernel(count, targets, scalars_ref, *refs):
    pieces = refs[:count]
    table_ref = refs[count]
    outs = refs[count + 1 : -1]
    stack = refs[-1]
    heads, width, _ = table_ref.shape
    for k in range(count):
        stack[k] = pieces[k][...]
    for n, target in enumerate(targets):
        local = stack[scalars_ref[1 + target]] - scalars_ref[0]
        for head in range(heads):
            outs[n][head * width : (head + 1) * width, :] = picked(local, table_ref, head)


def merge_kernel(middle_ref, inner_ref, outer_ref, *refs):
    received = refs[:-2]
    out_ref, rim_ref = refs[-2:]
    total = jnp.where(middle_ref[0] == 1, inner_ref[...].astype(F32), outer_ref[...].astype(F32))
    for other in received:
        total = total + other[...].astype(F32)
    total = total.astype(BF16)
    out_ref[...] = total
    rim_ref[...] = total[:, total.shape[1] - LANES :]


def project_kernel(shifts, count, where_ref, *refs):
    pieces = len(shifts)
    first = 0 in shifts
    rims = refs[:pieces]
    bodies = refs[pieces : 2 * pieces]
    refs = refs[2 * pieces :]
    weights = refs[:4]
    if first:
        key_ref, value_ref, held, sems = refs[4:]
    else:
        begun_keys, begun_values, hidden_halo, hidden, value_ref, stats_ref = refs[4:10]
        held, sems, states, done, done_sems = refs[10:]
    half = held.shape[-1]
    depth, tokens = bodies[0].shape
    rep = where_ref[0]
    tp = where_ref[1]
    copies = []
    for far in range(2):
        for which in range(2):
            for n, s in enumerate(shifts):
                at = pl.multiple_of(lax.rem(tp + count - s, count) * depth, depth)
                copy = pltpu.make_async_copy(
                    weights[2 * far + which].at[pl.ds(at, depth), :],
                    held.at[far, which, pl.ds(n * depth, depth), :],
                    sems.at[(2 * far + which) * pieces + n],
                )
                copy.start()
                copies.append(copy)
    body = jnp.concatenate([b[...].astype(F32) for b in bodies], axis=0).T.astype(BF16)
    rim = jnp.concatenate([r[...].astype(F32) for r in rims], axis=0).T.astype(BF16)
    memory = jnp.concatenate([rim[LANES - RIM :], body], axis=0)
    if not first:
        for slot in range(2):
            states[slot, :RIM] = hidden_halo[:, slot * half : (slot + 1) * half]
            states[slot, RIM:] = hidden[:, slot * half : (slot + 1) * half]
    sums = [0.0] * 4
    out_copies = []
    for far in range(2):
        slot = rep if far == 0 else 1 - rep
        fields = []
        for which in range(2):
            for n in range(pieces):
                copies[(2 * far + which) * pieces + n].wait()
            fields.append(dot(memory, held[far, which]))
        keys, values = fields
        if first:
            key_ref[slot] = keys
            value_ref[slot] = values
        else:
            keys = keys + begun_keys[slot]
            values = values + begun_values[slot]
            done[far] = values
            copy = pltpu.make_async_copy(done.at[far], value_ref.at[slot], done_sems.at[far])
            copy.start()
            out_copies.append(copy)
            here = states[slot].astype(F32)
            terms = (here * here, keys * keys, here * keys, values * values)
            sums = [a + jnp.sum(t, axis=1, keepdims=True) for a, t in zip(sums, terms)]
    if not first:
        rows = memory.shape[0]
        lane = iota((rows, 8), 1)
        packed = jnp.zeros((rows, 8), F32)
        for k in range(4):
            packed = jnp.where(lane == k, sums[k], packed)
        stats_ref[...] = dot_nt(unit(8, F32), packed, lax.Precision.HIGHEST)
        for copy in out_copies:
            copy.wait()


def finish_kernel(count, keep_ref, *refs):
    stats = refs[:count]
    value_ref, hidden_ref, taps_ref, out_ref, gates, factors, normed = refs[count:]
    rows = normed.shape[0]
    tokens, step = out_ref.shape

    @pl.when(pl.program_id(0) == 0)
    def _():
        total = stats[0][...]
        for other in stats[1:]:
            total = total + other[...]
        inverse_states = lax.rsqrt(total[0:1] / D + EPSILON)
        inverse_keys = lax.rsqrt(total[1:2] / D + EPSILON)
        gate = jax.nn.sigmoid(total[2:3] * inverse_states * inverse_keys / D**0.5)
        factor = gate * lax.rsqrt(gate * gate * total[3:4] / D + EPSILON)
        factor = jnp.where((iota(factor.shape, 1) < RIM) & (keep_ref[0] == 0), 0.0, factor)
        line = iota(total.shape, 0)
        both = jnp.where(line == 0, gate, jnp.where(line == 1, factor, 0.0))
        columns = dot_nt(unit(rows, F32), both, lax.Precision.HIGHEST)
        gates[...] = jnp.broadcast_to(columns[RIM:, 0:1], gates.shape)
        factors[...] = jnp.broadcast_to(columns[:, 1:2], factors.shape)

    for start in range(0, step, LANES):
        size = min(LANES, step - start)
        span = slice(start, start + size)
        values = value_ref[:, span]
        normed[:, span] = values * factors[:, :size]
        conv = None
        for tap in range(KERNEL):
            lag = DILATION * tap
            term = taps_ref[tap : tap + 1, span] * normed[RIM - lag : RIM - lag + tokens, span]
            conv = term if conv is None else conv + term
        gated = values[RIM:] * gates[:, :size]
        out_ref[:, span] = (
            hidden_ref[:, span].astype(F32) + jax.nn.silu(conv) + gated
        ).astype(BF16)


def whole(array):
    return pl.BlockSpec(array.shape, lambda *_: (0,) * array.ndim)


def in_hbm(array):
    return pltpu.with_memory_space_constraint(array, pltpu.HBM)


def limit(mib):
    return pltpu.CompilerParams(vmem_limit_bytes=mib << 20)


def scattered_sum(stored, decoded, here):
    mems = lax.axis_size("mem")
    heads, width, rows = decoded.shape
    tokens = stored.shape[1]
    asked = lax.all_gather(stored, "mem", axis=0)
    partial = pl.pallas_call(
        pick_all_kernel,
        grid=(mems,),
        in_specs=[
            pl.BlockSpec(memory_space=pltpu.SMEM),
            pl.BlockSpec((None, heads, tokens), lambda m: (m, 0, 0)),
            whole(decoded),
        ],
        out_specs=pl.BlockSpec((None, heads * width, tokens), lambda m: (m, 0, 0)),
        out_shape=jax.ShapeDtypeStruct((mems, heads * width, tokens), BF16),
        compiler_params=limit(16),
        name="pick_all",
    )((here * rows).astype(I32).reshape(1), asked, decoded)
    total = lax.psum_scatter(partial, "mem", scatter_dimension=0, tiled=False)
    return total, total[:, tokens - LANES :]


def line_sum(stored, decoded, here):
    heads, width, rows = decoded.shape
    tokens = stored.shape[1]
    asked = [stored] + [
        lax.ppermute(stored, "mem", [(i, i ^ x) for i in range(4)]) for x in range(1, 4)
    ]
    right = here >= 2
    order = [here ^ jnp.where(right, j, 3 - j) for j in range(4)]
    scalars = jnp.stack([here * rows] + order).astype(I32)
    block = jax.ShapeDtypeStruct((heads * width, tokens), BF16)

    def pick(*targets):
        return pl.pallas_call(
            functools.partial(pick_kernel, 4, targets),
            in_specs=[pl.BlockSpec(memory_space=pltpu.SMEM)]
            + [pl.BlockSpec(memory_space=pltpu.VMEM)] * 5,
            out_shape=(block,) * len(targets),
            scratch_shapes=[pltpu.VMEM((4, heads, tokens), I32)],
            compiler_params=limit(8),
            name="pick_rows",
        )(scalars, *asked, decoded)

    def after(x, *others):
        return lax.optimization_barrier((x, *others))[0]

    def inward(x):
        return lax.ppermute(x, "mem", [(0, 1), (3, 2)])

    def across(x):
        return lax.ppermute(x, "mem", [(1, 2), (2, 1)])

    def outward(x):
        return lax.ppermute(x, "mem", [(1, 0), (2, 3)])

    (farthest,) = pick(0)
    first = inward(farthest)
    far_own, inner, outer = pick(1, 2, 3)
    far_own, crossing = lax.optimization_barrier((far_own, farthest + first))
    second = inward(far_own)
    crossed = across(crossing)
    inner, near, leaving = lax.optimization_barrier((inner, far_own + second, outer + crossed))
    third = inward(inner)
    crossed_near = across(near)
    last = outward(leaving)
    middle = ((here == 1) | (here == 2)).astype(I32).reshape(1)
    return pl.pallas_call(
        merge_kernel,
        in_specs=[pl.BlockSpec(memory_space=pltpu.SMEM)]
        + [pl.BlockSpec(memory_space=pltpu.VMEM)] * 5,
        out_shape=(block, jax.ShapeDtypeStruct((block.shape[0], LANES), BF16)),
        compiler_params=limit(4),
        name="merge",
    )(middle, inner, outer, third, crossed_near, last)


def shards(
    hidden, row_ids, row_place, table_codes, table_scales, key_weight, value_weight, conv_weight
):
    mems = lax.axis_size("mem")
    tps = lax.axis_size("tp")
    reps = lax.axis_size("rep")
    blocks = mems * reps
    tokens, heads = row_ids.shape
    rows, width = table_codes.shape[1:]
    depth = heads * width
    half = key_weight.shape[1]
    seq_length = tokens * blocks // SEQS
    assert reps == 2 and seq_length % tokens == 0 and row_place.shape[0] % LANES == 0
    block = lax.axis_index(("mem", "rep"))
    smem = pl.BlockSpec(memory_space=pltpu.SMEM)

    stored = pl.pallas_call(
        place_kernel,
        out_shape=jax.ShapeDtypeStruct((heads, tokens), I32),
        compiler_params=limit(4),
        name="place_rows",
    )(row_ids.T, row_place.reshape(-1, LANES))
    decoded = pl.pallas_call(
        decode_kernel,
        out_shape=jax.ShapeDtypeStruct((heads, width, rows), BF16),
        compiler_params=limit(16),
        name="decode_tables",
    )(table_codes.transpose(0, 2, 1), table_scales.transpose(2, 0, 1))
    here = lax.axis_index("mem")
    if mems == 4:
        memory, rim = line_sum(stored, decoded, here)
    else:
        memory, rim = scattered_sum(stored, decoded, here)

    _, tail = lax.optimization_barrier((stored, hidden[tokens - RIM :]))
    needed = [(i, i + 1) for i in range(blocks - 1) if (i + 1) * tokens % seq_length]
    hidden_halo = lax.ppermute(tail, ("mem", "rep"), needed)
    other_key = lax.ppermute(key_weight, "rep", [(0, 1), (1, 0)])
    other_value = lax.ppermute(value_weight, "rep", [(0, 1), (1, 0)])
    weights = [in_hbm(w) for w in (key_weight, value_weight, other_key, other_value)]

    where = jnp.stack([lax.axis_index("rep"), lax.axis_index("tp")]).astype(I32)
    extended = tokens + RIM
    bodies = [memory] + [
        lax.ppermute(memory, "tp", [(i, (i + s) % tps) for i in range(tps)])
        for s in range(1, tps)
    ]
    rims = [
        lax.ppermute(
            rim,
            ("mem", "tp", "rep"),
            [
                (
                    (a // reps * tps + i) * reps + a % reps,
                    (b // reps * tps + (i + s) % tps) * reps + b % reps,
                )
                for a, b in needed
                for i in range(tps)
            ],
        )
        for s in range(tps)
    ]
    field = jax.ShapeDtypeStruct((2, extended, half), F32)
    anywhere = pl.BlockSpec(memory_space=pl.ANY)
    resident = pl.BlockSpec(memory_space=pltpu.VMEM)
    begun = pl.pallas_call(
        functools.partial(project_kernel, (0,), tps),
        in_specs=[smem] + [resident] * 2 + [anywhere] * 4,
        out_shape=(field, field),
        scratch_shapes=[pltpu.VMEM((2, 2, depth, half), BF16), pltpu.SemaphoreType.DMA((4,))],
        compiler_params=limit(16),
        name="project_own",
    )(where, rims[0], memory, *weights)
    others = tps - 1
    values, stats = pl.pallas_call(
        functools.partial(project_kernel, tuple(range(1, tps)), tps),
        in_specs=[smem] + [resident] * (2 * others) + [anywhere] * 4 + [resident] * 4,
        out_specs=(pl.BlockSpec(memory_space=pltpu.HBM), resident),
        out_shape=(pltpu.HBM(field.shape, F32), jax.ShapeDtypeStruct((8, extended), F32)),
        scratch_shapes=[
            pltpu.VMEM((2, 2, others * depth, half), BF16),
            pltpu.SemaphoreType.DMA((4 * others,)),
            pltpu.VMEM((2, extended, half), BF16),
            pltpu.VMEM((2, extended, half), F32),
            pltpu.SemaphoreType.DMA((2,)),
        ],
        compiler_params=limit(20),
        name="project_others",
    )(where, *rims[1:], *bodies[1:], *weights, *begun, hidden_halo, hidden)

    all_stats = [stats] + [
        lax.ppermute(stats, "tp", [(i, (i + s) % tps) for i in range(tps)]) for s in range(1, tps)
    ]
    keep = (block * tokens % seq_length != 0).astype(I32).reshape(1)
    aligned = half % LANES == 0
    if aligned:
        step = next(c for c in (384, 256, 128) if half % c == 0)
        split = lambda x: x
        spec = lambda r: pl.BlockSpec((r, step), lambda i: (0, i))
        out_shape = jax.ShapeDtypeStruct((tokens, 2 * half), BF16)
    else:
        step = half
        split = lambda x: jnp.stack([x[:, :half], x[:, half:]])
        spec = lambda r: pl.BlockSpec((None, r, step), lambda i: (i, 0, 0))
        out_shape = jax.ShapeDtypeStruct((2, tokens, half), BF16)
    per = half // step
    out = pl.pallas_call(
        functools.partial(finish_kernel, tps),
        grid=(2 * per,),
        in_specs=[smem]
        + [whole(stats)] * tps
        + [
            pl.BlockSpec((None, extended, step), lambda i: (i // per, 0, i % per)),
            spec(tokens),
            spec(KERNEL),
        ],
        out_specs=spec(tokens),
        out_shape=out_shape,
        scratch_shapes=[
            pltpu.VMEM((tokens, LANES), F32),
            pltpu.VMEM((extended, LANES), F32),
            pltpu.VMEM((extended, step), F32),
        ],
        compiler_params=limit(16),
        name="finish",
    )(keep, *all_stats, in_hbm(values), split(hidden), split(conv_weight))
    return out if aligned else jnp.concatenate([out[0], out[1]], axis=1)


def solution(mesh):
    in_specs = (
        P(("parts", "mem", "rep"), "tp"),
        P(("parts", "mem", "rep"), "tp"),
        P("parts"),
        P(("parts", "tp"), "mem", None),
        P(("parts", "tp"), "mem", None),
        P(None, ("tp", "rep")),
        P(None, ("tp", "rep")),
        P(None, "tp"),
    )
    out_specs = P(("parts", "mem", "rep"), "tp")
    return jax.shard_map(shards, mesh=mesh, in_specs=in_specs, out_specs=out_specs, check_vma=False)
```

```python
import functools

import jax
import jax.numpy as jnp
from jax import lax
from jax.experimental import pallas as pl
from jax.experimental.pallas import tpu as pltpu
from jax.sharding import PartitionSpec as P

D = 4608
KERNEL = 4
DILATION = 3
SEQS = 4
EPSILON = 1e-06
RIM = 16
LANES = 128

F32 = jnp.float32
BF16 = jnp.bfloat16
I32 = jnp.int32


def iota(shape, axis):
    return lax.broadcasted_iota(I32, shape, axis)


def dot(a, b):
    return jnp.dot(a, b, preferred_element_type=F32)


def dot_nt(a, b, precision=None):
    return lax.dot_general(
        a, b, (((1,), (1,)), ((), ())), precision=precision, preferred_element_type=F32
    )


def unit(n, dtype):
    return (iota((n, n), 0) == iota((n, n), 1)).astype(F32).astype(dtype)


def to_bf16(x):
    return x.astype(F32).astype(BF16)


def place_kernel(ids_hbm, place_hbm, out_ref, ids_ref, place_ref, sems):
    copies = [
        pltpu.make_async_copy(place_hbm, place_ref, sems.at[0]),
        pltpu.make_async_copy(ids_hbm, ids_ref, sems.at[1]),
    ]
    for copy in copies:
        copy.start()
    copies[0].wait()
    place = place_ref[...]
    rows = place.shape[0]
    heads, tokens = ids_ref.shape
    eye = unit(LANES, BF16)
    table = jnp.concatenate(
        [dot_nt(eye, to_bf16(place >> 8)), dot_nt(eye, to_bf16(place & 255))], axis=0
    ).astype(BF16)
    copies[1].wait()
    for head in range(heads):
        row = ids_ref[head : head + 1, :]
        hot = to_bf16(iota((rows, tokens), 0) == (row >> 7))
        both = dot(table, hot)
        value = both[:LANES] * 256.0 + both[LANES:]
        chosen = jnp.where(iota(value.shape, 0) == (row & 127), value, 0.0)
        out_ref[head : head + 1, :] = jnp.sum(chosen, axis=0, keepdims=True).astype(I32)


def decode_kernel(codes_hbm, scales_hbm, out_ref, codes_ref, scales_ref, sems):
    heads, width, rows = codes_ref.shape
    blocks = scales_ref.shape[0]
    scales_copy = pltpu.make_async_copy(scales_hbm, scales_ref, sems.at[heads])
    scales_copy.start()
    copies = []
    for head in range(heads):
        copies.append(
            pltpu.make_async_copy(codes_hbm.at[head], codes_ref.at[head], sems.at[head])
        )
        copies[-1].start()
    entry = iota((width, 2 * width), 0)
    column = iota((width, 2 * width), 1)
    column = jnp.where(column < width, column, column - width)
    parity = entry & column & 15
    parity = parity ^ (parity >> 2)
    parity = (parity ^ (parity >> 1)) & 1
    same = (entry >> 4) == (column >> 4)
    rotation = jnp.where(same, 0.25 - 0.5 * parity.astype(F32), 0.0).astype(BF16)
    scales_copy.wait()
    for head in range(heads):
        copies[head].wait()
        factors = jnp.concatenate(
            [
                jnp.broadcast_to(scales_ref[b, head : head + 1, :].astype(F32), (16, rows))
                for b in range(blocks)
            ],
            axis=0,
        )
        scaled = codes_ref[head].astype(F32) * factors
        upper = scaled.astype(BF16)
        lower = (scaled - upper.astype(F32)).astype(BF16)
        out_ref[head] = dot(rotation, jnp.concatenate([upper, lower], axis=0)).astype(BF16)


def picked(local, table_ref, head):
    rows = table_ref.shape[2]
    hot = to_bf16(iota((rows, local.shape[1]), 0) == local[head : head + 1, :])
    return dot(table_ref[head], hot).astype(BF16)


def pick_all_kernel(base_ref, ids_ref, table_ref, out_ref):
    heads, width, _ = table_ref.shape
    local = ids_ref[...] - base_ref[0]
    for head in range(heads):
        out_ref[head * width : (head + 1) * width, :] = picked(local, table_ref, head)


def pick_kernel(count, targets, scalars_ref, *refs):
    pieces = refs[:count]
    table_ref = refs[count]
    outs = refs[count + 1 : -1]
    stack = refs[-1]
    heads, width, _ = table_ref.shape
    for k in range(count):
        stack[k] = pieces[k][...]
    for n, target in enumerate(targets):
        local = stack[scalars_ref[1 + target]] - scalars_ref[0]
        for head in range(heads):
            outs[n][head * width : (head + 1) * width, :] = picked(local, table_ref, head)


def merge_kernel(middle_ref, inner_ref, outer_ref, *refs):
    received = refs[:-2]
    out_ref, rim_ref = refs[-2:]
    total = jnp.where(middle_ref[0] == 1, inner_ref[...].astype(F32), outer_ref[...].astype(F32))
    for other in received:
        total = total + other[...].astype(F32)
    total = total.astype(BF16)
    out_ref[...] = total
    rim_ref[...] = total[:, total.shape[1] - LANES :]


def load_kernel(*refs):
    sources, targets, sems = refs[:2], refs[2:4], refs[4]
    rows = sources[0].shape[0]
    pieces = sems.shape[0] // 2
    step = rows // pieces
    copies = []
    for n in range(pieces):
        for which in range(2):
            span = pl.ds(n * step, step)
            copy = pltpu.make_async_copy(
                sources[which].at[span, :], targets[which].at[span, :], sems.at[2 * n + which]
            )
            copy.start()
            copies.append(copy)
    for copy in copies:
        copy.wait()


def project_kernel(shifts, count, where_ref, *refs):
    pieces = len(shifts)
    first = 0 in shifts
    rims = refs[:pieces]
    bodies = refs[pieces : 2 * pieces]
    refs = refs[2 * pieces :]
    weights = refs[:4]
    if first:
        key_ref, value_ref = refs[4:]
    else:
        begun_keys, begun_values, hidden_halo, hidden, value_ref, stats_ref, states = refs[4:]
    half = value_ref.shape[-1]
    depth, tokens = bodies[0].shape
    rep = where_ref[0]
    tp = where_ref[1]
    body = jnp.concatenate([b[...].astype(F32) for b in bodies], axis=0).T.astype(BF16)
    rim = jnp.concatenate([r[...].astype(F32) for r in rims], axis=0).T.astype(BF16)
    memory = jnp.concatenate([rim[LANES - RIM :], body], axis=0)
    if not first:
        for slot in range(2):
            states[slot, :RIM] = hidden_halo[:, slot * half : (slot + 1) * half]
            states[slot, RIM:] = hidden[:, slot * half : (slot + 1) * half]
    sums = [0.0] * 4
    for far in range(2):
        slot = rep if far == 0 else 1 - rep
        fields = []
        for which in range(2):
            field = None
            for n, s in enumerate(shifts):
                at = pl.multiple_of(lax.rem(tp + count - s, count) * depth, depth)
                part = dot(
                    memory[:, n * depth : (n + 1) * depth],
                    weights[2 * far + which][pl.ds(at, depth), :],
                )
                field = part if field is None else field + part
            fields.append(field)
        keys, values = fields
        if first:
            key_ref[slot] = keys
            value_ref[slot] = values
        else:
            keys = keys + begun_keys[slot]
            values = values + begun_values[slot]
            value_ref[slot] = values
            here = states[slot].astype(F32)
            terms = (here * here, keys * keys, here * keys, values * values)
            sums = [a + jnp.sum(t, axis=1, keepdims=True) for a, t in zip(sums, terms)]
    if not first:
        rows = memory.shape[0]
        lane = iota((rows, 8), 1)
        packed = jnp.zeros((rows, 8), F32)
        for k in range(4):
            packed = jnp.where(lane == k, sums[k], packed)
        stats_ref[...] = dot_nt(unit(8, F32), packed, lax.Precision.HIGHEST)


def finish_kernel(count, step, keep_ref, *refs):
    stats = refs[:count]
    value_ref, hidden_ref, taps_ref, out_hbm, gates, factors, normed, out_ref, sems = refs[count:]
    rows, half = normed.shape
    tokens, width = out_ref.shape
    total = stats[0][...]
    for other in stats[1:]:
        total = total + other[...]
    inverse_states = lax.rsqrt(total[0:1] / D + EPSILON)
    inverse_keys = lax.rsqrt(total[1:2] / D + EPSILON)
    gate = jax.nn.sigmoid(total[2:3] * inverse_states * inverse_keys / D**0.5)
    factor = gate * lax.rsqrt(gate * gate * total[3:4] / D + EPSILON)
    factor = jnp.where((iota(factor.shape, 1) < RIM) & (keep_ref[0] == 0), 0.0, factor)
    line = iota(total.shape, 0)
    both = jnp.where(line == 0, gate, jnp.where(line == 1, factor, 0.0))
    columns = dot_nt(unit(rows, F32), both, lax.Precision.HIGHEST)
    gates[...] = jnp.broadcast_to(columns[RIM:, 0:1], gates.shape)
    factors[...] = jnp.broadcast_to(columns[:, 1:2], factors.shape)
    copies = []
    for slot in range(2):
        for start in range(0, half, LANES):
            size = min(LANES, half - start)
            span = slice(start, start + size)
            there = slice(slot * half + start, slot * half + start + size)
            values = value_ref[slot, :, span]
            normed[:, span] = values * factors[:, :size]
            conv = None
            for tap in range(KERNEL):
                lag = DILATION * tap
                term = taps_ref[tap : tap + 1, there] * normed[RIM - lag : RIM - lag + tokens, span]
                conv = term if conv is None else conv + term
            gated = values[RIM:] * gates[:, :size]
            out_ref[:, there] = (
                hidden_ref[:, there].astype(F32) + jax.nn.silu(conv) + gated
            ).astype(BF16)
            if there.stop % step == 0:
                ready = pl.ds(there.stop - step, step)
                copy = pltpu.make_async_copy(
                    out_ref.at[:, ready], out_hbm.at[:, ready], sems.at[len(copies)]
                )
                copy.start()
                copies.append(copy)
    for copy in copies:
        copy.wait()


def whole(array):
    return pl.BlockSpec(array.shape, lambda *_: (0,) * array.ndim)


def in_hbm(array):
    return pltpu.with_memory_space_constraint(array, pltpu.HBM)


def in_vmem(array):
    return pltpu.with_memory_space_constraint(array, pltpu.VMEM)


def after(array, *others):
    return lax.optimization_barrier((array, *others))[0]


def load(pair):
    target = pltpu.VMEM(pair[0].shape, pair[0].dtype)
    return pl.pallas_call(
        load_kernel,
        in_specs=[pl.BlockSpec(memory_space=pl.ANY)] * 2,
        out_specs=(pl.BlockSpec(memory_space=pltpu.VMEM),) * 2,
        out_shape=(target, target),
        scratch_shapes=[pltpu.SemaphoreType.DMA((8,))],
        compiler_params=limit(4),
        name="load_weights",
    )(*pair)


def limit(mib):
    return pltpu.CompilerParams(vmem_limit_bytes=mib << 20)


def scattered_sum(stored, decoded, here, early, late):
    mems = lax.axis_size("mem")
    heads, width, rows = decoded.shape
    tokens = stored.shape[1]
    asked = lax.all_gather(stored, "mem", axis=0)
    partial = pl.pallas_call(
        pick_all_kernel,
        grid=(mems,),
        in_specs=[
            pl.BlockSpec(memory_space=pltpu.SMEM),
            pl.BlockSpec((None, heads, tokens), lambda m: (m, 0, 0)),
            whole(decoded),
        ],
        out_specs=pl.BlockSpec((None, heads * width, tokens), lambda m: (m, 0, 0)),
        out_shape=jax.ShapeDtypeStruct((mems, heads * width, tokens), BF16),
        compiler_params=limit(16),
        name="pick_all",
    )((here * rows).astype(I32).reshape(1), asked, decoded)
    total = lax.psum_scatter(partial, "mem", scatter_dimension=0, tiled=False)
    return total, total[:, tokens - LANES :], early(partial), late(total)


def line_sum(stored, decoded, here, early, late):
    heads, width, rows = decoded.shape
    tokens = stored.shape[1]
    asked = [stored] + [
        lax.ppermute(stored, "mem", [(i, i ^ x) for i in range(4)]) for x in range(1, 4)
    ]
    right = here >= 2
    order = [here ^ jnp.where(right, j, 3 - j) for j in range(4)]
    scalars = jnp.stack([here * rows] + order).astype(I32)
    block = jax.ShapeDtypeStruct((heads * width, tokens), BF16)

    def pick(*targets):
        return pl.pallas_call(
            functools.partial(pick_kernel, 4, targets),
            in_specs=[pl.BlockSpec(memory_space=pltpu.SMEM)]
            + [pl.BlockSpec(memory_space=pltpu.VMEM)] * 5,
            out_shape=(block,) * len(targets),
            scratch_shapes=[pltpu.VMEM((4, heads, tokens), I32)],
            compiler_params=limit(8),
            name="pick_rows",
        )(scalars, *asked, decoded)

    def inward(x):
        return lax.ppermute(x, "mem", [(0, 1), (3, 2)])

    def across(x):
        return lax.ppermute(x, "mem", [(1, 2), (2, 1)])

    def outward(x):
        return lax.ppermute(x, "mem", [(1, 0), (2, 3)])

    (farthest,) = pick(0)
    first = inward(farthest)
    begun = early(farthest)
    far_own, inner, outer = pick(1, 2, 3)
    far_own, begun = lax.optimization_barrier((far_own, begun))
    second = inward(far_own)
    crossed = across(farthest + first)
    ended = late(first)
    inner, ended = lax.optimization_barrier((inner, ended))
    third = inward(inner)
    crossed_near = across(far_own + after(second, *ended))
    last = outward(outer + crossed)
    middle = ((here == 1) | (here == 2)).astype(I32).reshape(1)
    memory, rim = pl.pallas_call(
        merge_kernel,
        in_specs=[pl.BlockSpec(memory_space=pltpu.SMEM)]
        + [pl.BlockSpec(memory_space=pltpu.VMEM)] * 5,
        out_shape=(block, jax.ShapeDtypeStruct((block.shape[0], LANES), BF16)),
        compiler_params=limit(4),
        name="merge",
    )(middle, inner, outer, third, crossed_near, last)
    return memory, rim, begun, ended


def shards(
    hidden, row_ids, row_place, table_codes, table_scales, key_weight, value_weight, conv_weight
):
    mems = lax.axis_size("mem")
    tps = lax.axis_size("tp")
    reps = lax.axis_size("rep")
    blocks = mems * reps
    tokens, heads = row_ids.shape
    rows, width = table_codes.shape[1:]
    depth = heads * width
    half = key_weight.shape[1]
    seq_length = tokens * blocks // SEQS
    assert reps == 2 and seq_length % tokens == 0 and row_place.shape[0] % LANES == 0
    block = lax.axis_index(("mem", "rep"))
    smem = pl.BlockSpec(memory_space=pltpu.SMEM)

    anywhere = pl.BlockSpec(memory_space=pl.ANY)
    resident = pl.BlockSpec(memory_space=pltpu.VMEM)
    places = row_place.reshape(-1, LANES)
    stored = pl.pallas_call(
        place_kernel,
        in_specs=[anywhere] * 2,
        out_shape=jax.ShapeDtypeStruct((heads, tokens), I32),
        scratch_shapes=[
            pltpu.VMEM((heads, tokens), I32),
            pltpu.VMEM(places.shape, I32),
            pltpu.SemaphoreType.DMA((2,)),
        ],
        compiler_params=limit(4),
        name="place_rows",
    )(in_hbm(row_ids.T), in_hbm(places))
    codes = table_codes.transpose(0, 2, 1)
    scales = table_scales.transpose(2, 0, 1)
    decoded = pl.pallas_call(
        decode_kernel,
        in_specs=[anywhere] * 2,
        out_shape=jax.ShapeDtypeStruct(codes.shape, BF16),
        scratch_shapes=[
            pltpu.VMEM(codes.shape, BF16),
            pltpu.VMEM(scales.shape, BF16),
            pltpu.SemaphoreType.DMA((heads + 1,)),
        ],
        compiler_params=limit(12),
        name="decode_tables",
    )(in_hbm(codes), in_hbm(scales))
    here = lax.axis_index("mem")
    other_key = lax.ppermute(key_weight, "rep", [(0, 1), (1, 0)])
    other_value = lax.ppermute(value_weight, "rep", [(0, 1), (1, 0)])
    needed = [(i, i + 1) for i in range(blocks - 1) if (i + 1) * tokens % seq_length]

    def early(token):
        tail = after(hidden[tokens - RIM :], token)
        halo = lax.ppermute(tail, ("mem", "rep"), needed)
        return halo, load([in_hbm(after(w, token)) for w in (key_weight, value_weight)])

    def late(token):
        return load([after(w, token) for w in (other_key, other_value)])

    summed = line_sum if mems == 4 else scattered_sum
    memory, rim, (hidden_halo, own_weights), other_weights = summed(
        stored, decoded, here, early, late
    )
    weights = [in_vmem(w) for w in (*own_weights, *other_weights)]

    where = jnp.stack([lax.axis_index("rep"), lax.axis_index("tp")]).astype(I32)
    extended = tokens + RIM
    bodies = [memory] + [
        lax.ppermute(memory, "tp", [(i, (i + s) % tps) for i in range(tps)])
        for s in range(1, tps)
    ]

    def next_rim(rim, s):
        pairs = [
            (
                (a // reps * tps + i) * reps + a % reps,
                (b // reps * tps + (i + s) % tps) * reps + b % reps,
            )
            for a, b in needed
            for i in range(tps)
        ]
        return lax.ppermute(rim, ("mem", "tp", "rep"), pairs)

    field = pltpu.VMEM((2, extended, half), F32)
    begun = pl.pallas_call(
        functools.partial(project_kernel, (0,), tps),
        in_specs=[smem] + [resident] * 6,
        out_specs=(resident,) * 2,
        out_shape=(field, field),
        compiler_params=limit(12),
        name="project_own",
    )(where, next_rim(rim, 0), memory, *weights)
    rim = after(rim, *begun)
    others = tps - 1
    values, stats = pl.pallas_call(
        functools.partial(project_kernel, tuple(range(1, tps)), tps),
        in_specs=[smem] + [resident] * (2 * others + 8),
        out_specs=(resident,) * 2,
        out_shape=(field, jax.ShapeDtypeStruct((8, extended), F32)),
        scratch_shapes=[pltpu.VMEM((2, extended, half), BF16)],
        compiler_params=limit(14),
        name="project_others",
    )(
        where,
        *[next_rim(rim, s) for s in range(1, tps)],
        *bodies[1:],
        *weights,
        *[in_vmem(b) for b in begun],
        hidden_halo,
        hidden,
    )

    all_stats = [stats] + [
        lax.ppermute(stats, "tp", [(i, (i + s) % tps) for i in range(tps)]) for s in range(1, tps)
    ]
    keep = (block * tokens % seq_length != 0).astype(I32).reshape(1)
    step = 2 * half
    if half % LANES == 0:
        step = next(c for c in (384, 256, 128) if half % c == 0)
    return pl.pallas_call(
        functools.partial(finish_kernel, tps, step),
        in_specs=[smem] + [resident] * (tps + 3),
        out_specs=anywhere,
        out_shape=jax.ShapeDtypeStruct((tokens, 2 * half), BF16),
        scratch_shapes=[
            pltpu.VMEM((tokens, LANES), F32),
            pltpu.VMEM((extended, LANES), F32),
            pltpu.VMEM((extended, half), F32),
            pltpu.VMEM((tokens, 2 * half), BF16),
            pltpu.SemaphoreType.DMA((2 * half // step,)),
        ],
        compiler_params=limit(12),
        name="finish",
    )(keep, *all_stats, in_vmem(values), hidden, conv_weight)


def solution(mesh):
    in_specs = (
        P(("parts", "mem", "rep"), "tp"),
        P(("parts", "mem", "rep"), "tp"),
        P("parts"),
        P(("parts", "tp"), "mem", None),
        P(("parts", "tp"), "mem", None),
        P(None, ("tp", "rep")),
        P(None, ("tp", "rep")),
        P(None, "tp"),
    )
    out_specs = P(("parts", "mem", "rep"), "tp")
    return jax.shard_map(shards, mesh=mesh, in_specs=in_specs, out_specs=out_specs, check_vma=False)
```

```python
import functools

import jax
import jax.numpy as jnp
from jax import lax
from jax.experimental import pallas as pl
from jax.experimental.pallas import tpu as pltpu
from jax.sharding import PartitionSpec as P

D = 4608
KERNEL = 4
DILATION = 3
SEQS = 4
EPSILON = 1e-06
RIM = 16
LANES = 128

F32 = jnp.float32
BF16 = jnp.bfloat16
I32 = jnp.int32


def iota(shape, axis):
    return lax.broadcasted_iota(I32, shape, axis)


def dot(a, b):
    return jnp.dot(a, b, preferred_element_type=F32)


def dot_nt(a, b, precision=None):
    return lax.dot_general(
        a, b, (((1,), (1,)), ((), ())), precision=precision, preferred_element_type=F32
    )


def unit(n, dtype):
    return (iota((n, n), 0) == iota((n, n), 1)).astype(F32).astype(dtype)


def to_bf16(x):
    return x.astype(F32).astype(BF16)


def place_kernel(ids_hbm, place_hbm, out_ref, ids_ref, place_ref, sems):
    copies = [
        pltpu.make_async_copy(place_hbm, place_ref, sems.at[0]),
        pltpu.make_async_copy(ids_hbm, ids_ref, sems.at[1]),
    ]
    for copy in copies:
        copy.start()
    copies[0].wait()
    place = place_ref[...]
    rows = place.shape[0]
    heads, tokens = ids_ref.shape
    eye = unit(LANES, BF16)
    table = jnp.concatenate(
        [dot_nt(eye, to_bf16(place >> 8)), dot_nt(eye, to_bf16(place & 255))], axis=0
    ).astype(BF16)
    copies[1].wait()
    for head in range(heads):
        row = ids_ref[head : head + 1, :]
        hot = to_bf16(iota((rows, tokens), 0) == (row >> 7))
        both = dot(table, hot)
        value = both[:LANES] * 256.0 + both[LANES:]
        chosen = jnp.where(iota(value.shape, 0) == (row & 127), value, 0.0)
        out_ref[head : head + 1, :] = jnp.sum(chosen, axis=0, keepdims=True).astype(I32)


def decode_kernel(codes_hbm, scales_hbm, out_ref, codes_ref, scales_ref, sems):
    heads, width, rows = codes_ref.shape
    blocks = scales_ref.shape[0]
    scales_copy = pltpu.make_async_copy(scales_hbm, scales_ref, sems.at[heads])
    scales_copy.start()
    copies = []
    for head in range(heads):
        copies.append(
            pltpu.make_async_copy(codes_hbm.at[head], codes_ref.at[head], sems.at[head])
        )
        copies[-1].start()
    entry = iota((width, 2 * width), 0)
    column = iota((width, 2 * width), 1)
    column = jnp.where(column < width, column, column - width)
    parity = entry & column & 15
    parity = parity ^ (parity >> 2)
    parity = (parity ^ (parity >> 1)) & 1
    same = (entry >> 4) == (column >> 4)
    rotation = jnp.where(same, 0.25 - 0.5 * parity.astype(F32), 0.0).astype(BF16)
    scales_copy.wait()
    for head in range(heads):
        copies[head].wait()
        factors = jnp.concatenate(
            [
                jnp.broadcast_to(scales_ref[b, head : head + 1, :].astype(F32), (16, rows))
                for b in range(blocks)
            ],
            axis=0,
        )
        scaled = codes_ref[head].astype(F32) * factors
        upper = scaled.astype(BF16)
        lower = (scaled - upper.astype(F32)).astype(BF16)
        out_ref[head] = dot(rotation, jnp.concatenate([upper, lower], axis=0)).astype(BF16)


def picked(local, table_ref, head):
    rows = table_ref.shape[2]
    hot = to_bf16(iota((rows, local.shape[1]), 0) == local[head : head + 1, :])
    return dot(table_ref[head], hot).astype(BF16)


def pick_all_kernel(base_ref, ids_ref, table_ref, out_ref):
    heads, width, _ = table_ref.shape
    local = ids_ref[...] - base_ref[0]
    for head in range(heads):
        out_ref[head * width : (head + 1) * width, :] = picked(local, table_ref, head)


def pick_kernel(count, targets, scalars_ref, *refs):
    pieces = refs[:count]
    table_ref = refs[count]
    outs = refs[count + 1 : -1]
    stack = refs[-1]
    heads, width, _ = table_ref.shape
    for k in range(count):
        stack[k] = pieces[k][...]
    for n, target in enumerate(targets):
        local = stack[scalars_ref[1 + target]] - scalars_ref[0]
        for head in range(heads):
            outs[n][head * width : (head + 1) * width, :] = picked(local, table_ref, head)


def merge_kernel(middle_ref, inner_ref, outer_ref, *refs):
    received = refs[:-1]
    total = jnp.where(middle_ref[0] == 1, inner_ref[...].astype(F32), outer_ref[...].astype(F32))
    for other in received:
        total = total + other[...].astype(F32)
    refs[-1][...] = total.astype(BF16)


def project_kernel(shifts, count, where_ref, *refs):
    pieces = len(shifts)
    first = 0 in shifts
    rims = refs[:pieces]
    bodies = refs[pieces : 2 * pieces]
    refs = refs[2 * pieces :]
    depth, tokens = bodies[0].shape
    rep = where_ref[0]
    tp = where_ref[1]
    if first:
        weights = refs[:4]
        key_ref, value_ref, rest, held, sems, rest_sems = refs[4:]
        half = held.shape[-1]

        def bring(target, far, which, n, s, sem):
            owner = lax.rem(tp + count - s, count)
            rows = pl.ds(pl.multiple_of(owner * depth, depth), depth)
            copy = pltpu.make_async_copy(
                weights[2 * far + which].at[rows, :],
                target.at[far, which, pl.ds(n * depth, depth), :],
                sem,
            )
            copy.start()
            return copy

        copies = [
            bring(held, far, which, 0, 0, sems.at[2 * far + which])
            for far in range(2)
            for which in range(2)
        ]
    else:
        rest, begun_keys, begun_values, hidden_halo, hidden = refs[:5]
        value_hbm, stats_ref, states, done, done_sems = refs[5:]
        held = rest
        half = held.shape[-1]
        for slot in range(2):
            states[slot, :RIM] = hidden_halo[:, slot * half : (slot + 1) * half]
            states[slot, RIM:] = hidden[:, slot * half : (slot + 1) * half]
    body = jnp.concatenate([b[...].astype(F32) for b in bodies], axis=0).T.astype(BF16)
    rim = jnp.concatenate([r[...].astype(F32) for r in rims], axis=0).T.astype(BF16)
    memory = jnp.concatenate([rim[LANES - RIM :], body], axis=0)
    sums = [0.0] * 4
    later = []
    for far in range(2):
        slot = rep if far == 0 else 1 - rep
        fields = [None, None]
        for which in (1, 0):
            if first:
                copies[2 * far + which].wait()
            fields[which] = dot(memory, held[far, which])
            if not first and which == 1:
                done[far] = fields[1] + begun_values[slot]
                copy = pltpu.make_async_copy(done.at[far], value_hbm.at[slot], done_sems.at[far])
                copy.start()
                later.append(copy)
        if first:
            value_ref[slot] = fields[1]
            key_ref[slot] = fields[0]
            for which in range(2):
                for n in range(count - 1):
                    sem = rest_sems.at[(2 * far + which) * (count - 1) + n]
                    later.append(bring(rest, far, which, n, n + 1, sem))
        else:
            keys = fields[0] + begun_keys[slot]
            values = done[far]
            here = states[slot].astype(F32)
            terms = (here * here, keys * keys, here * keys, values * values)
            sums = [a + jnp.sum(t, axis=1, keepdims=True) for a, t in zip(sums, terms)]
    if not first:
        rows = memory.shape[0]
        lane = iota((rows, 8), 1)
        packed = jnp.zeros((rows, 8), F32)
        for k in range(4):
            packed = jnp.where(lane == k, sums[k], packed)
        stats_ref[...] = dot_nt(unit(8, F32), packed, lax.Precision.HIGHEST)
    for copy in later:
        copy.wait()


def finish_kernel(count, step, keep_ref, *refs):
    stats = refs[:count]
    value_hbm, hidden_ref, taps_ref, out_hbm = refs[count : count + 4]
    gates, factors, value_ref, normed, out_ref, in_sems, sems = refs[count + 4 :]
    rows, half = normed.shape
    tokens, width = out_ref.shape
    arrivals = {}
    chunk = min(step, half)
    for slot in range(2):
        for start in range(0, half, chunk):
            span = pl.ds(start, chunk)
            copy = pltpu.make_async_copy(
                value_hbm.at[slot, :, span], value_ref.at[slot, :, span], in_sems.at[len(arrivals)]
            )
            copy.start()
            arrivals[slot, start] = copy
    total = stats[0][...]
    for other in stats[1:]:
        total = total + other[...]
    inverse_states = lax.rsqrt(total[0:1] / D + EPSILON)
    inverse_keys = lax.rsqrt(total[1:2] / D + EPSILON)
    gate = jax.nn.sigmoid(total[2:3] * inverse_states * inverse_keys / D**0.5)
    factor = gate * lax.rsqrt(gate * gate * total[3:4] / D + EPSILON)
    factor = jnp.where((iota(factor.shape, 1) < RIM) & (keep_ref[0] == 0), 0.0, factor)
    line = iota(total.shape, 0)
    both = jnp.where(line == 0, gate, jnp.where(line == 1, factor, 0.0))
    columns = dot_nt(unit(rows, F32), both, lax.Precision.HIGHEST)
    gates[...] = jnp.broadcast_to(columns[RIM:, 0:1], gates.shape)
    factors[...] = jnp.broadcast_to(columns[:, 1:2], factors.shape)
    copies = []
    for slot in range(2):
        for start in range(0, half, LANES):
            size = min(LANES, half - start)
            span = slice(start, start + size)
            there = slice(slot * half + start, slot * half + start + size)
            if start % chunk == 0:
                arrivals[slot, start].wait()
            values = value_ref[slot, :, span]
            normed[:, span] = values * factors[:, :size]
            conv = None
            for tap in range(KERNEL):
                lag = DILATION * tap
                term = taps_ref[tap : tap + 1, there] * normed[RIM - lag : RIM - lag + tokens, span]
                conv = term if conv is None else conv + term
            gated = values[RIM:] * gates[:, :size]
            out_ref[:, there] = (
                hidden_ref[:, there].astype(F32) + jax.nn.silu(conv) + gated
            ).astype(BF16)
            if there.stop % step == 0:
                ready = pl.ds(there.stop - step, step)
                copy = pltpu.make_async_copy(
                    out_ref.at[:, ready], out_hbm.at[:, ready], sems.at[len(copies)]
                )
                copy.start()
                copies.append(copy)
    for copy in copies:
        copy.wait()


def whole(array):
    return pl.BlockSpec(array.shape, lambda *_: (0,) * array.ndim)


def in_hbm(array):
    return pltpu.with_memory_space_constraint(array, pltpu.HBM)


def after(array, *others):
    return lax.optimization_barrier((array, *others))[0]


def limit(mib):
    return pltpu.CompilerParams(vmem_limit_bytes=mib << 20)


def scattered_sum(stored, decoded, here, meanwhile):
    mems = lax.axis_size("mem")
    heads, width, rows = decoded.shape
    tokens = stored.shape[1]
    asked = lax.all_gather(stored, "mem", axis=0)
    partial = pl.pallas_call(
        pick_all_kernel,
        grid=(mems,),
        in_specs=[
            pl.BlockSpec(memory_space=pltpu.SMEM),
            pl.BlockSpec((None, heads, tokens), lambda m: (m, 0, 0)),
            whole(decoded),
        ],
        out_specs=pl.BlockSpec((None, heads * width, tokens), lambda m: (m, 0, 0)),
        out_shape=jax.ShapeDtypeStruct((mems, heads * width, tokens), BF16),
        compiler_params=limit(16),
        name="pick_all",
    )((here * rows).astype(I32).reshape(1), asked, decoded)
    total = lax.psum_scatter(partial, "mem", scatter_dimension=0, tiled=False)
    return total, meanwhile(partial)


def line_sum(stored, decoded, here, meanwhile):
    heads, width, rows = decoded.shape
    tokens = stored.shape[1]
    asked = [stored] + [
        lax.ppermute(stored, "mem", [(i, i ^ x) for i in range(4)]) for x in range(1, 4)
    ]
    right = here >= 2
    order = [here ^ jnp.where(right, j, 3 - j) for j in range(4)]
    scalars = jnp.stack([here * rows] + order).astype(I32)
    block = jax.ShapeDtypeStruct((heads * width, tokens), BF16)

    def pick(*targets):
        return pl.pallas_call(
            functools.partial(pick_kernel, 4, targets),
            in_specs=[pl.BlockSpec(memory_space=pltpu.SMEM)]
            + [pl.BlockSpec(memory_space=pltpu.VMEM)] * 5,
            out_shape=(block,) * len(targets),
            scratch_shapes=[pltpu.VMEM((4, heads, tokens), I32)],
            compiler_params=limit(8),
            name="pick_rows",
        )(scalars, *asked, decoded)

    def send(x, *pairs):
        return lax.ppermute(x, "mem", pairs)

    middle = ((here == 1) | (here == 2)).astype(I32)
    (farthest,) = pick(0)
    inward = send(farthest, (0, 1), (3, 2))
    other = meanwhile(farthest)
    (far,) = pick(1)
    across = send(far, (1, 2), (2, 1))
    inner, outer = pick(2, 3)
    beside = send(jnp.where(middle == 1, outer, inner), (0, 1), (1, 0), (2, 3), (3, 2))
    onward, other = lax.optimization_barrier((farthest + inward, other))
    onward = send(onward, (1, 3), (2, 0))
    past = send(after(far, inward), (0, 2), (3, 1))
    memory = pl.pallas_call(
        merge_kernel,
        in_specs=[pl.BlockSpec(memory_space=pltpu.SMEM)]
        + [pl.BlockSpec(memory_space=pltpu.VMEM)] * 6,
        out_shape=block,
        compiler_params=limit(4),
        name="merge",
    )(middle.reshape(1), inner, outer, across, beside, onward, past)
    return memory, other


def shards(
    hidden, row_ids, row_place, table_codes, table_scales, key_weight, value_weight, conv_weight
):
    mems = lax.axis_size("mem")
    tps = lax.axis_size("tp")
    reps = lax.axis_size("rep")
    blocks = mems * reps
    tokens, heads = row_ids.shape
    rows, width = table_codes.shape[1:]
    depth = heads * width
    half = key_weight.shape[1]
    seq_length = tokens * blocks // SEQS
    assert reps == 2 and seq_length % tokens == 0 and row_place.shape[0] % LANES == 0
    block = lax.axis_index(("mem", "rep"))
    smem = pl.BlockSpec(memory_space=pltpu.SMEM)

    anywhere = pl.BlockSpec(memory_space=pl.ANY)
    resident = pl.BlockSpec(memory_space=pltpu.VMEM)
    places = row_place.reshape(-1, LANES)
    stored = pl.pallas_call(
        place_kernel,
        in_specs=[anywhere] * 2,
        out_shape=jax.ShapeDtypeStruct((heads, tokens), I32),
        scratch_shapes=[
            pltpu.VMEM((heads, tokens), I32),
            pltpu.VMEM(places.shape, I32),
            pltpu.SemaphoreType.DMA((2,)),
        ],
        compiler_params=limit(4),
        name="place_rows",
    )(in_hbm(row_ids.T), in_hbm(places))
    codes = table_codes.transpose(0, 2, 1)
    scales = table_scales.transpose(2, 0, 1)
    decoded = pl.pallas_call(
        decode_kernel,
        in_specs=[anywhere] * 2,
        out_shape=jax.ShapeDtypeStruct(codes.shape, BF16),
        scratch_shapes=[
            pltpu.VMEM(codes.shape, BF16),
            pltpu.VMEM(scales.shape, BF16),
            pltpu.SemaphoreType.DMA((heads + 1,)),
        ],
        compiler_params=limit(12),
        name="decode_tables",
    )(in_hbm(codes), in_hbm(scales))
    here = lax.axis_index("mem")
    other_key = lax.ppermute(key_weight, "rep", [(0, 1), (1, 0)])
    other_value = lax.ppermute(value_weight, "rep", [(0, 1), (1, 0)])
    needed = [(i, i + 1) for i in range(blocks - 1) if (i + 1) * tokens % seq_length]

    def meanwhile(token):
        tail = after(hidden[tokens - RIM :], token)
        return lax.ppermute(tail, ("mem", "rep"), needed)

    summed = line_sum if mems == 4 else scattered_sum
    memory, hidden_halo = summed(stored, decoded, here, meanwhile)
    weights = [in_hbm(w) for w in (key_weight, value_weight, other_key, other_value)]

    where = jnp.stack([lax.axis_index("rep"), lax.axis_index("tp")]).astype(I32)
    extended = tokens + RIM
    bodies = [memory] + [
        lax.ppermute(memory, "tp", [(i, (i + s) % tps) for i in range(tps)])
        for s in range(1, tps)
    ]

    def next_rim(rim, s):
        pairs = [
            (
                (a // reps * tps + i) * reps + a % reps,
                (b // reps * tps + (i + s) % tps) * reps + b % reps,
            )
            for a, b in needed
            for i in range(tps)
        ]
        return lax.ppermute(rim, ("mem", "tp", "rep"), pairs)

    rim = memory[:, tokens - LANES :]
    others = tps - 1
    field = jax.ShapeDtypeStruct((2, extended, half), F32)
    *begun, rest = pl.pallas_call(
        functools.partial(project_kernel, (0,), tps),
        in_specs=[smem] + [resident] * 2 + [anywhere] * 4,
        out_specs=(resident,) * 3,
        out_shape=(field, field, pltpu.VMEM((2, 2, others * depth, half), BF16)),
        scratch_shapes=[
            pltpu.VMEM((2, 2, depth, half), BF16),
            pltpu.SemaphoreType.DMA((4,)),
            pltpu.SemaphoreType.DMA((4 * others,)),
        ],
        compiler_params=limit(12),
        name="project_own",
    )(where, next_rim(rim, 0), memory, *weights)
    rim = after(rim, *begun)
    values, stats = pl.pallas_call(
        functools.partial(project_kernel, tuple(range(1, tps)), tps),
        in_specs=[smem] + [resident] * (2 * others + 5),
        out_specs=(pl.BlockSpec(memory_space=pltpu.HBM), resident),
        out_shape=(pltpu.HBM(field.shape, F32), jax.ShapeDtypeStruct((8, extended), F32)),
        scratch_shapes=[
            pltpu.VMEM((2, extended, half), BF16),
            pltpu.VMEM((2, extended, half), F32),
            pltpu.SemaphoreType.DMA((2,)),
        ],
        compiler_params=limit(14),
        name="project_others",
    )(
        where,
        *[next_rim(rim, s) for s in range(1, tps)],
        *bodies[1:],
        rest,
        *begun,
        hidden_halo,
        hidden,
    )

    all_stats = [stats] + [
        lax.ppermute(stats, "tp", [(i, (i + s) % tps) for i in range(tps)]) for s in range(1, tps)
    ]
    keep = (block * tokens % seq_length != 0).astype(I32).reshape(1)
    step = 2 * half
    if half % LANES == 0:
        step = next(c for c in (384, 256, 128) if half % c == 0)
    return pl.pallas_call(
        functools.partial(finish_kernel, tps, step),
        in_specs=[smem] + [resident] * tps + [anywhere] + [resident] * 2,
        out_specs=anywhere,
        out_shape=jax.ShapeDtypeStruct((tokens, 2 * half), BF16),
        scratch_shapes=[
            pltpu.VMEM((tokens, LANES), F32),
            pltpu.VMEM((extended, LANES), F32),
            pltpu.VMEM((2, extended, half), F32),
            pltpu.VMEM((extended, half), F32),
            pltpu.VMEM((tokens, 2 * half), BF16),
            pltpu.SemaphoreType.DMA((2 * half // min(step, half),)),
            pltpu.SemaphoreType.DMA((2 * half // step,)),
        ],
        compiler_params=limit(12),
        name="finish",
    )(keep, *all_stats, in_hbm(values), hidden, conv_weight)


def solution(mesh):
    in_specs = (
        P(("parts", "mem", "rep"), "tp"),
        P(("parts", "mem", "rep"), "tp"),
        P("parts"),
        P(("parts", "tp"), "mem", None),
        P(("parts", "tp"), "mem", None),
        P(None, ("tp", "rep")),
        P(None, ("tp", "rep")),
        P(None, "tp"),
    )
    out_specs = P(("parts", "mem", "rep"), "tp")
    return jax.shard_map(shards, mesh=mesh, in_specs=in_specs, out_specs=out_specs, check_vma=False)
```

```python
import functools

import jax
import jax.numpy as jnp
from jax import lax
from jax.experimental import pallas as pl
from jax.experimental.pallas import tpu as pltpu
from jax.sharding import PartitionSpec as P

D = 4608
KERNEL = 4
DILATION = 3
SEQS = 4
EPSILON = 1e-06
RIM = 16
LANES = 128

F32 = jnp.float32
BF16 = jnp.bfloat16
I32 = jnp.int32


def iota(shape, axis):
    return lax.broadcasted_iota(I32, shape, axis)


def dot(a, b):
    return jnp.dot(a, b, preferred_element_type=F32)


def dot_nt(a, b, precision=None):
    return lax.dot_general(
        a, b, (((1,), (1,)), ((), ())), precision=precision, preferred_element_type=F32
    )


def unit(n, dtype):
    return (iota((n, n), 0) == iota((n, n), 1)).astype(F32).astype(dtype)


def to_bf16(x):
    return x.astype(F32).astype(BF16)


def place_kernel(ids_hbm, place_hbm, out_ref, ids_ref, place_ref, sems):
    copies = [
        pltpu.make_async_copy(place_hbm, place_ref, sems.at[0]),
        pltpu.make_async_copy(ids_hbm, ids_ref, sems.at[1]),
    ]
    for copy in copies:
        copy.start()
    copies[0].wait()
    place = place_ref[...]
    rows = place.shape[0]
    heads, tokens = ids_ref.shape
    eye = unit(LANES, BF16)
    table = jnp.concatenate(
        [dot_nt(eye, to_bf16(place >> 8)), dot_nt(eye, to_bf16(place & 255))], axis=0
    ).astype(BF16)
    copies[1].wait()
    for head in range(heads):
        row = ids_ref[head : head + 1, :]
        hot = to_bf16(iota((rows, tokens), 0) == (row >> 7))
        both = dot(table, hot)
        value = both[:LANES] * 256.0 + both[LANES:]
        chosen = jnp.where(iota(value.shape, 0) == (row & 127), value, 0.0)
        out_ref[head : head + 1, :] = jnp.sum(chosen, axis=0, keepdims=True).astype(I32)


def decode_kernel(codes_hbm, scales_hbm, out_ref, codes_ref, scales_ref, sems):
    heads, width, rows = codes_ref.shape
    blocks = scales_ref.shape[0]
    scales_copy = pltpu.make_async_copy(scales_hbm, scales_ref, sems.at[heads])
    scales_copy.start()
    copies = []
    for head in range(heads):
        copies.append(
            pltpu.make_async_copy(codes_hbm.at[head], codes_ref.at[head], sems.at[head])
        )
        copies[-1].start()
    entry = iota((width, 2 * width), 0)
    column = iota((width, 2 * width), 1)
    column = jnp.where(column < width, column, column - width)
    parity = entry & column & 15
    parity = parity ^ (parity >> 2)
    parity = (parity ^ (parity >> 1)) & 1
    same = (entry >> 4) == (column >> 4)
    rotation = jnp.where(same, 0.25 - 0.5 * parity.astype(F32), 0.0).astype(BF16)
    scales_copy.wait()
    for head in range(heads):
        copies[head].wait()
        factors = jnp.concatenate(
            [
                jnp.broadcast_to(scales_ref[b, head : head + 1, :].astype(F32), (16, rows))
                for b in range(blocks)
            ],
            axis=0,
        )
        scaled = codes_ref[head].astype(F32) * factors
        upper = scaled.astype(BF16)
        lower = (scaled - upper.astype(F32)).astype(BF16)
        out_ref[head] = dot(rotation, jnp.concatenate([upper, lower], axis=0)).astype(BF16)


def picked(local, table_ref, head):
    rows = table_ref.shape[2]
    hot = to_bf16(iota((rows, local.shape[1]), 0) == local[head : head + 1, :])
    return dot(table_ref[head], hot).astype(BF16)


def pick_all_kernel(base_ref, ids_ref, table_ref, out_ref):
    heads, width, _ = table_ref.shape
    local = ids_ref[...] - base_ref[0]
    for head in range(heads):
        out_ref[head * width : (head + 1) * width, :] = picked(local, table_ref, head)


def pick_kernel(count, targets, scalars_ref, *refs):
    pieces = refs[:count]
    table_ref = refs[count]
    outs = refs[count + 1 : -1]
    stack = refs[-1]
    heads, width, _ = table_ref.shape
    for k in range(count):
        stack[k] = pieces[k][...]
    for n, target in enumerate(targets):
        local = stack[scalars_ref[1 + target]] - scalars_ref[0]
        for head in range(heads):
            outs[n][head * width : (head + 1) * width, :] = picked(local, table_ref, head)


def merge_kernel(middle_ref, inner_ref, outer_ref, *refs):
    received = refs[:-1]
    total = jnp.where(middle_ref[0] == 1, inner_ref[...].astype(F32), outer_ref[...].astype(F32))
    for other in received:
        total = total + other[...].astype(F32)
    refs[-1][...] = total.astype(BF16)


def project_kernel(shifts, count, where_ref, *refs):
    pieces = len(shifts)
    first = 0 in shifts
    rims = refs[:pieces]
    bodies = refs[pieces : 2 * pieces]
    refs = refs[2 * pieces :]
    depth, tokens = bodies[0].shape
    rep = where_ref[0]
    tp = where_ref[1]
    if first:
        weights = refs[:4]
        key_ref, value_ref, rest, held, sems, rest_sems = refs[4:]
        half = held.shape[-1]

        def bring(target, far, which, n, s, sem):
            owner = lax.rem(tp + count - s, count)
            rows = pl.ds(pl.multiple_of(owner * depth, depth), depth)
            copy = pltpu.make_async_copy(
                weights[2 * far + which].at[rows, :],
                target.at[far, which, pl.ds(n * depth, depth), :],
                sem,
            )
            copy.start()
            return copy

        copies = [
            bring(held, far, which, 0, 0, sems.at[2 * far + which])
            for far in range(2)
            for which in (1, 0)
        ]
        later = [
            bring(rest, far, which, n, n + 1, rest_sems.at[(2 * far + which) * (count - 1) + n])
            for far in range(2)
            for which in (1, 0)
            for n in range(count - 1)
        ]
    else:
        later = []
        rest, begun_keys, begun_values, hidden_halo, hidden = refs[:5]
        value_hbm, stats_ref, states, done, done_sems = refs[5:]
        held = rest
        half = held.shape[-1]
        for slot in range(2):
            states[slot, :RIM] = hidden_halo[:, slot * half : (slot + 1) * half]
            states[slot, RIM:] = hidden[:, slot * half : (slot + 1) * half]
    body = jnp.concatenate([b[...].astype(F32) for b in bodies], axis=0).T.astype(BF16)
    rim = jnp.concatenate([r[...].astype(F32) for r in rims], axis=0).T.astype(BF16)
    memory = jnp.concatenate([rim[LANES - RIM :], body], axis=0)
    sums = [0.0] * 4
    for far in range(2):
        slot = rep if far == 0 else 1 - rep
        fields = [None, None]
        for which in (1, 0):
            if first:
                copies[2 * far + 1 - which].wait()
            fields[which] = dot(memory, held[far, which])
            if not first and which == 1:
                done[far] = fields[1] + begun_values[slot]
                copy = pltpu.make_async_copy(done.at[far], value_hbm.at[slot], done_sems.at[far])
                copy.start()
                later.append(copy)
        if first:
            value_ref[slot] = fields[1]
            key_ref[slot] = fields[0]
        else:
            keys = fields[0] + begun_keys[slot]
            values = done[far]
            here = states[slot].astype(F32)
            terms = (here * here, keys * keys, here * keys, values * values)
            sums = [a + jnp.sum(t, axis=1, keepdims=True) for a, t in zip(sums, terms)]
    if not first:
        rows = memory.shape[0]
        lane = iota((rows, 8), 1)
        packed = jnp.zeros((rows, 8), F32)
        for k in range(4):
            packed = jnp.where(lane == k, sums[k], packed)
        stats_ref[...] = dot_nt(unit(8, F32), packed, lax.Precision.HIGHEST)
    for copy in later:
        copy.wait()


def finish_kernel(count, step, keep_ref, *refs):
    stats = refs[:count]
    value_hbm, hidden_ref, taps_ref, out_hbm = refs[count : count + 4]
    gates, factors, value_ref, normed, out_ref, in_sems, sems = refs[count + 4 :]
    rows, half = normed.shape
    tokens, width = out_ref.shape
    arrivals = {}
    chunk = min(step, half)
    for slot in range(2):
        for start in range(0, half, chunk):
            span = pl.ds(start, chunk)
            copy = pltpu.make_async_copy(
                value_hbm.at[slot, :, span], value_ref.at[slot, :, span], in_sems.at[len(arrivals)]
            )
            copy.start()
            arrivals[slot, start] = copy
    total = stats[0][...]
    for other in stats[1:]:
        total = total + other[...]
    inverse_states = lax.rsqrt(total[0:1] / D + EPSILON)
    inverse_keys = lax.rsqrt(total[1:2] / D + EPSILON)
    gate = jax.nn.sigmoid(total[2:3] * inverse_states * inverse_keys / D**0.5)
    factor = gate * lax.rsqrt(gate * gate * total[3:4] / D + EPSILON)
    factor = jnp.where((iota(factor.shape, 1) < RIM) & (keep_ref[0] == 0), 0.0, factor)
    line = iota(total.shape, 0)
    both = jnp.where(line == 0, gate, jnp.where(line == 1, factor, 0.0))
    columns = dot_nt(unit(rows, F32), both, lax.Precision.HIGHEST)
    gates[...] = jnp.broadcast_to(columns[RIM:, 0:1], gates.shape)
    factors[...] = jnp.broadcast_to(columns[:, 1:2], factors.shape)
    copies = []
    for slot in range(2):
        for start in range(0, half, LANES):
            size = min(LANES, half - start)
            span = slice(start, start + size)
            there = slice(slot * half + start, slot * half + start + size)
            if start % chunk == 0:
                arrivals[slot, start].wait()
            values = value_ref[slot, :, span]
            normed[:, span] = values * factors[:, :size]
            conv = None
            for tap in range(KERNEL):
                lag = DILATION * tap
                term = taps_ref[tap : tap + 1, there] * normed[RIM - lag : RIM - lag + tokens, span]
                conv = term if conv is None else conv + term
            gated = values[RIM:] * gates[:, :size]
            out_ref[:, there] = (
                hidden_ref[:, there].astype(F32) + jax.nn.silu(conv) + gated
            ).astype(BF16)
            if there.stop % step == 0:
                ready = pl.ds(there.stop - step, step)
                copy = pltpu.make_async_copy(
                    out_ref.at[:, ready], out_hbm.at[:, ready], sems.at[len(copies)]
                )
                copy.start()
                copies.append(copy)
    for copy in copies:
        copy.wait()


def whole(array):
    return pl.BlockSpec(array.shape, lambda *_: (0,) * array.ndim)


def in_hbm(array):
    return pltpu.with_memory_space_constraint(array, pltpu.HBM)


def after(array, *others):
    return lax.optimization_barrier((array, *others))[0]


def limit(mib):
    return pltpu.CompilerParams(vmem_limit_bytes=mib << 20)


def scattered_sum(stored, decoded, here, meanwhile, settled):
    mems = lax.axis_size("mem")
    heads, width, rows = decoded.shape
    tokens = stored.shape[1]
    asked = lax.all_gather(stored, "mem", axis=0)
    partial = pl.pallas_call(
        pick_all_kernel,
        grid=(mems,),
        in_specs=[
            pl.BlockSpec(memory_space=pltpu.SMEM),
            pl.BlockSpec((None, heads, tokens), lambda m: (m, 0, 0)),
            whole(decoded),
        ],
        out_specs=pl.BlockSpec((None, heads * width, tokens), lambda m: (m, 0, 0)),
        out_shape=jax.ShapeDtypeStruct((mems, heads * width, tokens), BF16),
        compiler_params=limit(16),
        name="pick_all",
    )((here * rows).astype(I32).reshape(1), asked, decoded)
    total = lax.psum_scatter(partial, "mem", scatter_dimension=0, tiled=False)
    return total, meanwhile(partial), settled


def line_sum(stored, decoded, here, meanwhile, settled):
    heads, width, rows = decoded.shape
    tokens = stored.shape[1]
    asked = [stored] + [
        lax.ppermute(stored, "mem", [(i, i ^ x) for i in range(4)]) for x in range(1, 4)
    ]
    asked, settled = lax.optimization_barrier((asked, settled))
    right = here >= 2
    order = [here ^ jnp.where(right, j, 3 - j) for j in range(4)]
    scalars = jnp.stack([here * rows] + order).astype(I32)
    block = jax.ShapeDtypeStruct((heads * width, tokens), BF16)

    def pick(*targets):
        return pl.pallas_call(
            functools.partial(pick_kernel, 4, targets),
            in_specs=[pl.BlockSpec(memory_space=pltpu.SMEM)]
            + [pl.BlockSpec(memory_space=pltpu.VMEM)] * 5,
            out_shape=(block,) * len(targets),
            scratch_shapes=[pltpu.VMEM((4, heads, tokens), I32)],
            compiler_params=limit(8),
            name="pick_rows",
        )(scalars, *asked, decoded)

    def send(x, *pairs):
        return lax.ppermute(x, "mem", pairs)

    middle = ((here == 1) | (here == 2)).astype(I32)
    (farthest,) = pick(0)
    inward = send(farthest, (0, 1), (3, 2))
    (far,) = pick(1)
    across = send(far, (1, 2), (2, 1))
    inner, outer = pick(2, 3)
    beside = send(jnp.where(middle == 1, outer, inner), (0, 1), (1, 0), (2, 3), (3, 2))
    past = send(far, (0, 2), (3, 1))
    onward = farthest + inward
    other = meanwhile(onward)
    onward = send(onward, (1, 3), (2, 0))
    memory = pl.pallas_call(
        merge_kernel,
        in_specs=[pl.BlockSpec(memory_space=pltpu.SMEM)]
        + [pl.BlockSpec(memory_space=pltpu.VMEM)] * 6,
        out_shape=block,
        compiler_params=limit(4),
        name="merge",
    )(middle.reshape(1), inner, outer, across, beside, onward, past)
    return memory, other, settled


def shards(
    hidden, row_ids, row_place, table_codes, table_scales, key_weight, value_weight, conv_weight
):
    mems = lax.axis_size("mem")
    tps = lax.axis_size("tp")
    reps = lax.axis_size("rep")
    blocks = mems * reps
    tokens, heads = row_ids.shape
    rows, width = table_codes.shape[1:]
    depth = heads * width
    half = key_weight.shape[1]
    seq_length = tokens * blocks // SEQS
    assert reps == 2 and seq_length % tokens == 0 and row_place.shape[0] % LANES == 0
    block = lax.axis_index(("mem", "rep"))
    smem = pl.BlockSpec(memory_space=pltpu.SMEM)

    anywhere = pl.BlockSpec(memory_space=pl.ANY)
    resident = pl.BlockSpec(memory_space=pltpu.VMEM)
    places = row_place.reshape(-1, LANES)
    stored = pl.pallas_call(
        place_kernel,
        in_specs=[anywhere] * 2,
        out_shape=jax.ShapeDtypeStruct((heads, tokens), I32),
        scratch_shapes=[
            pltpu.VMEM((heads, tokens), I32),
            pltpu.VMEM(places.shape, I32),
            pltpu.SemaphoreType.DMA((2,)),
        ],
        compiler_params=limit(4),
        name="place_rows",
    )(in_hbm(row_ids.T), in_hbm(places))
    codes = table_codes.transpose(0, 2, 1)
    scales = table_scales.transpose(2, 0, 1)
    decoded = pl.pallas_call(
        decode_kernel,
        in_specs=[anywhere] * 2,
        out_shape=jax.ShapeDtypeStruct(codes.shape, BF16),
        scratch_shapes=[
            pltpu.VMEM(codes.shape, BF16),
            pltpu.VMEM(scales.shape, BF16),
            pltpu.SemaphoreType.DMA((heads + 1,)),
        ],
        compiler_params=limit(12),
        name="decode_tables",
    )(in_hbm(codes), in_hbm(scales))
    here = lax.axis_index("mem")
    other_key = lax.ppermute(key_weight, "rep", [(0, 1), (1, 0)])
    other_value = lax.ppermute(value_weight, "rep", [(0, 1), (1, 0)])
    needed = [(i, i + 1) for i in range(blocks - 1) if (i + 1) * tokens % seq_length]

    def meanwhile(token):
        tail = after(hidden[tokens - RIM :], token)
        return lax.ppermute(tail, ("mem", "rep"), needed)

    summed = line_sum if mems == 4 else scattered_sum
    memory, hidden_halo, others = summed(
        stored, decoded, here, meanwhile, (other_key, other_value)
    )
    weights = [in_hbm(w) for w in (key_weight, value_weight, *others)]

    where = jnp.stack([lax.axis_index("rep"), lax.axis_index("tp")]).astype(I32)
    extended = tokens + RIM
    bodies = [memory] + [
        lax.ppermute(memory, "tp", [(i, (i + s) % tps) for i in range(tps)])
        for s in range(1, tps)
    ]

    def next_rim(rim, s):
        pairs = [
            (
                (a // reps * tps + i) * reps + a % reps,
                (b // reps * tps + (i + s) % tps) * reps + b % reps,
            )
            for a, b in needed
            for i in range(tps)
        ]
        return lax.ppermute(rim, ("mem", "tp", "rep"), pairs)

    rim = memory[:, tokens - LANES :]
    rims = [next_rim(rim, s) for s in range(tps)]
    others = tps - 1
    field = jax.ShapeDtypeStruct((2, extended, half), F32)
    *begun, rest = pl.pallas_call(
        functools.partial(project_kernel, (0,), tps),
        in_specs=[smem] + [resident] * 2 + [anywhere] * 4,
        out_specs=(resident,) * 3,
        out_shape=(field, field, pltpu.VMEM((2, 2, others * depth, half), BF16)),
        scratch_shapes=[
            pltpu.VMEM((2, 2, depth, half), BF16),
            pltpu.SemaphoreType.DMA((4,)),
            pltpu.SemaphoreType.DMA((4 * others,)),
        ],
        compiler_params=limit(12),
        name="project_own",
    )(where, rims[0], memory, *weights)
    values, stats = pl.pallas_call(
        functools.partial(project_kernel, tuple(range(1, tps)), tps),
        in_specs=[smem] + [resident] * (2 * others + 5),
        out_specs=(pl.BlockSpec(memory_space=pltpu.HBM), resident),
        out_shape=(pltpu.HBM(field.shape, F32), jax.ShapeDtypeStruct((8, extended), F32)),
        scratch_shapes=[
            pltpu.VMEM((2, extended, half), BF16),
            pltpu.VMEM((2, extended, half), F32),
            pltpu.SemaphoreType.DMA((2,)),
        ],
        compiler_params=limit(14),
        name="project_others",
    )(
        where,
        *rims[1:],
        *bodies[1:],
        rest,
        *begun,
        hidden_halo,
        hidden,
    )

    all_stats = [stats] + [
        lax.ppermute(stats, "tp", [(i, (i + s) % tps) for i in range(tps)]) for s in range(1, tps)
    ]
    keep = (block * tokens % seq_length != 0).astype(I32).reshape(1)
    step = 2 * half
    if half % LANES == 0:
        step = next(c for c in (384, 256, 128) if half % c == 0)
    return pl.pallas_call(
        functools.partial(finish_kernel, tps, step),
        in_specs=[smem] + [resident] * tps + [anywhere] + [resident] * 2,
        out_specs=anywhere,
        out_shape=jax.ShapeDtypeStruct((tokens, 2 * half), BF16),
        scratch_shapes=[
            pltpu.VMEM((tokens, LANES), F32),
            pltpu.VMEM((extended, LANES), F32),
            pltpu.VMEM((2, extended, half), F32),
            pltpu.VMEM((extended, half), F32),
            pltpu.VMEM((tokens, 2 * half), BF16),
            pltpu.SemaphoreType.DMA((2 * half // min(step, half),)),
            pltpu.SemaphoreType.DMA((2 * half // step,)),
        ],
        compiler_params=limit(12),
        name="finish",
    )(keep, *all_stats, in_hbm(values), hidden, conv_weight)


def solution(mesh):
    in_specs = (
        P(("parts", "mem", "rep"), "tp"),
        P(("parts", "mem", "rep"), "tp"),
        P("parts"),
        P(("parts", "tp"), "mem", None),
        P(("parts", "tp"), "mem", None),
        P(None, ("tp", "rep")),
        P(None, ("tp", "rep")),
        P(None, "tp"),
    )
    out_specs = P(("parts", "mem", "rep"), "tp")
    return jax.shard_map(shards, mesh=mesh, in_specs=in_specs, out_specs=out_specs, check_vma=False)
```

```python
import functools

import jax
import jax.numpy as jnp
from jax import lax
from jax.experimental import pallas as pl
from jax.experimental.pallas import tpu as pltpu
from jax.sharding import PartitionSpec as P

D = 4608
KERNEL = 4
DILATION = 3
SEQS = 4
EPSILON = 1e-06
RIM = 16
LANES = 128

F32 = jnp.float32
BF16 = jnp.bfloat16
I32 = jnp.int32


def iota(shape, axis):
    return lax.broadcasted_iota(I32, shape, axis)


def dot(a, b):
    return jnp.dot(a, b, preferred_element_type=F32)


def dot_nt(a, b, precision=None):
    return lax.dot_general(
        a, b, (((1,), (1,)), ((), ())), precision=precision, preferred_element_type=F32
    )


def unit(n, dtype):
    return (iota((n, n), 0) == iota((n, n), 1)).astype(F32).astype(dtype)


def to_bf16(x):
    return x.astype(F32).astype(BF16)


def place_kernel(ids_hbm, place_hbm, out_ref, ids_ref, place_ref, sems):
    copies = [
        pltpu.make_async_copy(place_hbm, place_ref, sems.at[0]),
        pltpu.make_async_copy(ids_hbm, ids_ref, sems.at[1]),
    ]
    for copy in copies:
        copy.start()
    copies[0].wait()
    place = place_ref[...]
    rows = place.shape[0]
    heads, tokens = ids_ref.shape
    eye = unit(LANES, BF16)
    table = jnp.concatenate(
        [dot_nt(eye, to_bf16(place >> 8)), dot_nt(eye, to_bf16(place & 255))], axis=0
    ).astype(BF16)
    copies[1].wait()
    for head in range(heads):
        row = ids_ref[head : head + 1, :]
        hot = to_bf16(iota((rows, tokens), 0) == (row >> 7))
        both = dot(table, hot)
        value = both[:LANES] * 256.0 + both[LANES:]
        chosen = jnp.where(iota(value.shape, 0) == (row & 127), value, 0.0)
        out_ref[head : head + 1, :] = jnp.sum(chosen, axis=0, keepdims=True).astype(I32)


def decode_kernel(codes_hbm, scales_hbm, out_ref, codes_ref, scales_ref, sems):
    heads, width, rows = codes_ref.shape
    blocks = scales_ref.shape[0]
    scales_copy = pltpu.make_async_copy(scales_hbm, scales_ref, sems.at[heads])
    scales_copy.start()
    copies = []
    for head in range(heads):
        copies.append(
            pltpu.make_async_copy(codes_hbm.at[head], codes_ref.at[head], sems.at[head])
        )
        copies[-1].start()
    entry = iota((width, 2 * width), 0)
    column = iota((width, 2 * width), 1)
    column = jnp.where(column < width, column, column - width)
    parity = entry & column & 15
    parity = parity ^ (parity >> 2)
    parity = (parity ^ (parity >> 1)) & 1
    same = (entry >> 4) == (column >> 4)
    rotation = jnp.where(same, 0.25 - 0.5 * parity.astype(F32), 0.0).astype(BF16)
    scales_copy.wait()
    for head in range(heads):
        copies[head].wait()
        factors = jnp.concatenate(
            [
                jnp.broadcast_to(scales_ref[b, head : head + 1, :].astype(F32), (16, rows))
                for b in range(blocks)
            ],
            axis=0,
        )
        scaled = codes_ref[head].astype(F32) * factors
        upper = scaled.astype(BF16)
        lower = (scaled - upper.astype(F32)).astype(BF16)
        out_ref[head] = dot(rotation, jnp.concatenate([upper, lower], axis=0)).astype(BF16)


def picked(local, table_ref, head):
    rows = table_ref.shape[2]
    hot = to_bf16(iota((rows, local.shape[1]), 0) == local[head : head + 1, :])
    return dot(table_ref[head], hot).astype(BF16)


def pick_kernel(base_ref, ids_ref, table_ref, out_ref):
    heads, width, _ = table_ref.shape
    local = ids_ref[...] - base_ref[0]
    for head in range(heads):
        out_ref[head * width : (head + 1) * width, :] = picked(local, table_ref, head)


def merge_kernel(*refs):
    total = refs[0][...].astype(F32)
    for other in refs[1:-1]:
        total = total + other[...].astype(F32)
    refs[-1][...] = total.astype(BF16)


def project_kernel(shifts, count, where_ref, *refs):
    pieces = len(shifts)
    first = 0 in shifts
    rims = refs[:pieces]
    bodies = refs[pieces : 2 * pieces]
    refs = refs[2 * pieces :]
    depth, tokens = bodies[0].shape
    rep = where_ref[0]
    tp = where_ref[1]
    if first:
        weights = refs[:4]
        key_ref, value_ref, rest, held, sems, rest_sems = refs[4:]
        half = held.shape[-1]

        def bring(target, far, which, n, s, sem):
            owner = lax.rem(tp + count - s, count)
            rows = pl.ds(pl.multiple_of(owner * depth, depth), depth)
            copy = pltpu.make_async_copy(
                weights[2 * far + which].at[rows, :],
                target.at[far, which, pl.ds(n * depth, depth), :],
                sem,
            )
            copy.start()
            return copy

        copies = [
            bring(held, far, which, 0, 0, sems.at[2 * far + which])
            for far in range(2)
            for which in (1, 0)
        ]
        later = [
            bring(rest, far, which, n, n + 1, rest_sems.at[(2 * far + which) * (count - 1) + n])
            for far in range(2)
            for which in (1, 0)
            for n in range(count - 1)
        ]
    else:
        later = []
        rest, begun_keys, begun_values, hidden_halo, hidden = refs[:5]
        value_hbm, stats_ref, states, done, done_sems = refs[5:]
        held = rest
        half = held.shape[-1]
        for slot in range(2):
            states[slot, :RIM] = hidden_halo[:, slot * half : (slot + 1) * half]
            states[slot, RIM:] = hidden[:, slot * half : (slot + 1) * half]
    body = jnp.concatenate([b[...].astype(F32) for b in bodies], axis=0).T.astype(BF16)
    rim = jnp.concatenate([r[...].astype(F32) for r in rims], axis=0).T.astype(BF16)
    memory = jnp.concatenate([rim[LANES - RIM :], body], axis=0)
    sums = [0.0] * 4
    for far in range(2):
        slot = rep if far == 0 else 1 - rep
        fields = [None, None]
        for which in (1, 0):
            if first:
                copies[2 * far + 1 - which].wait()
            fields[which] = dot(memory, held[far, which])
            if not first and which == 1:
                done[far] = fields[1] + begun_values[slot]
                copy = pltpu.make_async_copy(done.at[far], value_hbm.at[slot], done_sems.at[far])
                copy.start()
                later.append(copy)
        if first:
            value_ref[slot] = fields[1]
            key_ref[slot] = fields[0]
        else:
            keys = fields[0] + begun_keys[slot]
            values = done[far]
            here = states[slot].astype(F32)
            terms = (here * here, keys * keys, here * keys, values * values)
            sums = [a + jnp.sum(t, axis=1, keepdims=True) for a, t in zip(sums, terms)]
    if not first:
        rows = memory.shape[0]
        lane = iota((rows, 8), 1)
        packed = jnp.zeros((rows, 8), F32)
        for k in range(4):
            packed = jnp.where(lane == k, sums[k], packed)
        stats_ref[...] = dot_nt(unit(8, F32), packed, lax.Precision.HIGHEST)
    for copy in later:
        copy.wait()


def finish_kernel(count, step, keep_ref, *refs):
    stats = refs[:count]
    value_hbm, hidden_ref, taps_ref, out_hbm = refs[count : count + 4]
    gates, factors, value_ref, normed, out_ref, in_sems, sems = refs[count + 4 :]
    rows, half = normed.shape
    tokens, width = out_ref.shape
    arrivals = {}
    chunk = min(step, half)
    for slot in range(2):
        for start in range(0, half, chunk):
            span = pl.ds(start, chunk)
            copy = pltpu.make_async_copy(
                value_hbm.at[slot, :, span], value_ref.at[slot, :, span], in_sems.at[len(arrivals)]
            )
            copy.start()
            arrivals[slot, start] = copy
    total = stats[0][...]
    for other in stats[1:]:
        total = total + other[...]
    inverse_states = lax.rsqrt(total[0:1] / D + EPSILON)
    inverse_keys = lax.rsqrt(total[1:2] / D + EPSILON)
    gate = jax.nn.sigmoid(total[2:3] * inverse_states * inverse_keys / D**0.5)
    factor = gate * lax.rsqrt(gate * gate * total[3:4] / D + EPSILON)
    factor = jnp.where((iota(factor.shape, 1) < RIM) & (keep_ref[0] == 0), 0.0, factor)
    line = iota(total.shape, 0)
    both = jnp.where(line == 0, gate, jnp.where(line == 1, factor, 0.0))
    columns = dot_nt(unit(rows, F32), both, lax.Precision.HIGHEST)
    gates[...] = jnp.broadcast_to(columns[RIM:, 0:1], gates.shape)
    factors[...] = jnp.broadcast_to(columns[:, 1:2], factors.shape)
    copies = []
    for slot in range(2):
        for start in range(0, half, LANES):
            size = min(LANES, half - start)
            span = slice(start, start + size)
            there = slice(slot * half + start, slot * half + start + size)
            if start % chunk == 0:
                arrivals[slot, start].wait()
            values = value_ref[slot, :, span]
            normed[:, span] = values * factors[:, :size]
            conv = None
            for tap in range(KERNEL):
                lag = DILATION * tap
                term = taps_ref[tap : tap + 1, there] * normed[RIM - lag : RIM - lag + tokens, span]
                conv = term if conv is None else conv + term
            gated = values[RIM:] * gates[:, :size]
            out_ref[:, there] = (
                hidden_ref[:, there].astype(F32) + jax.nn.silu(conv) + gated
            ).astype(BF16)
            if there.stop % step == 0:
                ready = pl.ds(there.stop - step, step)
                copy = pltpu.make_async_copy(
                    out_ref.at[:, ready], out_hbm.at[:, ready], sems.at[len(copies)]
                )
                copy.start()
                copies.append(copy)
    for copy in copies:
        copy.wait()


def whole(array):
    return pl.BlockSpec(array.shape, lambda *_: (0,) * array.ndim)


def in_hbm(array):
    return pltpu.with_memory_space_constraint(array, pltpu.HBM)


def after(array, *others):
    return lax.optimization_barrier((array, *others))[0]


def limit(mib):
    return pltpu.CompilerParams(vmem_limit_bytes=mib << 20)


def scattered_sum(stored, decoded, here, meanwhile, settled):
    mems = lax.axis_size("mem")
    heads, width, rows = decoded.shape
    tokens = stored.shape[1]
    asked = lax.all_gather(stored, "mem", axis=0)
    partial = pl.pallas_call(
        pick_kernel,
        grid=(mems,),
        in_specs=[
            pl.BlockSpec(memory_space=pltpu.SMEM),
            pl.BlockSpec((None, heads, tokens), lambda m: (m, 0, 0)),
            whole(decoded),
        ],
        out_specs=pl.BlockSpec((None, heads * width, tokens), lambda m: (m, 0, 0)),
        out_shape=jax.ShapeDtypeStruct((mems, heads * width, tokens), BF16),
        compiler_params=limit(16),
        name="pick_all",
    )((here * rows).astype(I32).reshape(1), asked, decoded)
    total = lax.psum_scatter(partial, "mem", scatter_dimension=0, tiled=False)
    return total, meanwhile(partial), settled


def line_sum(stored, decoded, here, meanwhile, settled):
    heads, width, rows = decoded.shape
    tokens = stored.shape[1]
    base = (here * rows).astype(I32).reshape(1)
    block = jax.ShapeDtypeStruct((heads * width, tokens), BF16)

    def ask(ids, x):
        return lax.ppermute(ids, "mem", [(i, i ^ x) for i in range(4)])

    def pick(ids):
        return pl.pallas_call(
            pick_kernel,
            in_specs=[pl.BlockSpec(memory_space=pltpu.SMEM)]
            + [pl.BlockSpec(memory_space=pltpu.VMEM)] * 2,
            out_shape=block,
            compiler_params=limit(8),
            name="pick_rows",
        )(base, ids, decoded)

    def send(x, *pairs):
        return lax.ppermute(x, "mem", pairs)

    rows_3 = pick(ask(stored, 3))
    inward = send(rows_3, (0, 1), (3, 2))
    across = send(rows_3, (1, 2), (2, 1))
    own = pick(after(stored, rows_3))
    stored, settled = lax.optimization_barrier((after(stored, own), settled))
    asked = ask(stored, 2), ask(stored, 1)
    rows_2 = pick(asked[0])
    past = send(rows_2, (0, 2), (3, 1))
    rows_1 = pick(asked[1])
    onward = after(rows_2, rows_1, across) + inward
    other = meanwhile(onward)
    onward = send(onward, (1, 3), (2, 0))
    beside = send(after(rows_1, inward), (0, 1), (1, 0), (2, 3), (3, 2))
    own, other = lax.optimization_barrier((own + past, other))
    memory = pl.pallas_call(
        merge_kernel,
        in_specs=[pl.BlockSpec(memory_space=pltpu.VMEM)] * 4,
        out_shape=block,
        compiler_params=limit(4),
        name="merge",
    )(own, across, beside, onward)
    return memory, other, settled


def shards(
    hidden, row_ids, row_place, table_codes, table_scales, key_weight, value_weight, conv_weight
):
    mems = lax.axis_size("mem")
    tps = lax.axis_size("tp")
    reps = lax.axis_size("rep")
    blocks = mems * reps
    tokens, heads = row_ids.shape
    rows, width = table_codes.shape[1:]
    depth = heads * width
    half = key_weight.shape[1]
    seq_length = tokens * blocks // SEQS
    assert reps == 2 and seq_length % tokens == 0 and row_place.shape[0] % LANES == 0
    block = lax.axis_index(("mem", "rep"))
    smem = pl.BlockSpec(memory_space=pltpu.SMEM)

    anywhere = pl.BlockSpec(memory_space=pl.ANY)
    resident = pl.BlockSpec(memory_space=pltpu.VMEM)
    places = row_place.reshape(-1, LANES)
    stored = pl.pallas_call(
        place_kernel,
        in_specs=[anywhere] * 2,
        out_shape=jax.ShapeDtypeStruct((heads, tokens), I32),
        scratch_shapes=[
            pltpu.VMEM((heads, tokens), I32),
            pltpu.VMEM(places.shape, I32),
            pltpu.SemaphoreType.DMA((2,)),
        ],
        compiler_params=limit(4),
        name="place_rows",
    )(in_hbm(row_ids.T), in_hbm(places))
    codes = table_codes.transpose(0, 2, 1)
    scales = table_scales.transpose(2, 0, 1)
    decoded = pl.pallas_call(
        decode_kernel,
        in_specs=[anywhere] * 2,
        out_shape=jax.ShapeDtypeStruct(codes.shape, BF16),
        scratch_shapes=[
            pltpu.VMEM(codes.shape, BF16),
            pltpu.VMEM(scales.shape, BF16),
            pltpu.SemaphoreType.DMA((heads + 1,)),
        ],
        compiler_params=limit(12),
        name="decode_tables",
    )(in_hbm(codes), in_hbm(scales))
    here = lax.axis_index("mem")
    other_key = lax.ppermute(key_weight, "rep", [(0, 1), (1, 0)])
    other_value = lax.ppermute(value_weight, "rep", [(0, 1), (1, 0)])
    needed = [(i, i + 1) for i in range(blocks - 1) if (i + 1) * tokens % seq_length]

    def meanwhile(token):
        tail = after(hidden[tokens - RIM :], token)
        return lax.ppermute(tail, ("mem", "rep"), needed)

    summed = line_sum if mems == 4 else scattered_sum
    memory, hidden_halo, others = summed(
        stored, decoded, here, meanwhile, (other_key, other_value)
    )
    weights = [in_hbm(w) for w in (key_weight, value_weight, *others)]

    where = jnp.stack([lax.axis_index("rep"), lax.axis_index("tp")]).astype(I32)
    extended = tokens + RIM
    bodies = [memory] + [
        lax.ppermute(memory, "tp", [(i, (i + s) % tps) for i in range(tps)])
        for s in range(1, tps)
    ]

    def next_rim(rim, s):
        pairs = [
            (
                (a // reps * tps + i) * reps + a % reps,
                (b // reps * tps + (i + s) % tps) * reps + b % reps,
            )
            for a, b in needed
            for i in range(tps)
        ]
        return lax.ppermute(rim, ("mem", "tp", "rep"), pairs)

    rim = memory[:, tokens - LANES :]
    rims = [next_rim(rim, s) for s in range(tps)]
    others = tps - 1
    field = jax.ShapeDtypeStruct((2, extended, half), F32)
    *begun, rest = pl.pallas_call(
        functools.partial(project_kernel, (0,), tps),
        in_specs=[smem] + [resident] * 2 + [anywhere] * 4,
        out_specs=(resident,) * 3,
        out_shape=(field, field, pltpu.VMEM((2, 2, others * depth, half), BF16)),
        scratch_shapes=[
            pltpu.VMEM((2, 2, depth, half), BF16),
            pltpu.SemaphoreType.DMA((4,)),
            pltpu.SemaphoreType.DMA((4 * others,)),
        ],
        compiler_params=limit(12),
        name="project_own",
    )(where, rims[0], memory, *weights)
    values, stats = pl.pallas_call(
        functools.partial(project_kernel, tuple(range(1, tps)), tps),
        in_specs=[smem] + [resident] * (2 * others + 5),
        out_specs=(pl.BlockSpec(memory_space=pltpu.HBM), resident),
        out_shape=(pltpu.HBM(field.shape, F32), jax.ShapeDtypeStruct((8, extended), F32)),
        scratch_shapes=[
            pltpu.VMEM((2, extended, half), BF16),
            pltpu.VMEM((2, extended, half), F32),
            pltpu.SemaphoreType.DMA((2,)),
        ],
        compiler_params=limit(14),
        name="project_others",
    )(
        where,
        *rims[1:],
        *bodies[1:],
        rest,
        *begun,
        hidden_halo,
        hidden,
    )

    all_stats = [stats] + [
        lax.ppermute(stats, "tp", [(i, (i + s) % tps) for i in range(tps)]) for s in range(1, tps)
    ]
    keep = (block * tokens % seq_length != 0).astype(I32).reshape(1)
    step = 2 * half
    if half % LANES == 0:
        step = next(c for c in (384, 256, 128) if half % c == 0)
    return pl.pallas_call(
        functools.partial(finish_kernel, tps, step),
        in_specs=[smem] + [resident] * tps + [anywhere] + [resident] * 2,
        out_specs=anywhere,
        out_shape=jax.ShapeDtypeStruct((tokens, 2 * half), BF16),
        scratch_shapes=[
            pltpu.VMEM((tokens, LANES), F32),
            pltpu.VMEM((extended, LANES), F32),
            pltpu.VMEM((2, extended, half), F32),
            pltpu.VMEM((extended, half), F32),
            pltpu.VMEM((tokens, 2 * half), BF16),
            pltpu.SemaphoreType.DMA((2 * half // min(step, half),)),
            pltpu.SemaphoreType.DMA((2 * half // step,)),
        ],
        compiler_params=limit(12),
        name="finish",
    )(keep, *all_stats, in_hbm(values), hidden, conv_weight)


def solution(mesh):
    in_specs = (
        P(("parts", "mem", "rep"), "tp"),
        P(("parts", "mem", "rep"), "tp"),
        P("parts"),
        P(("parts", "tp"), "mem", None),
        P(("parts", "tp"), "mem", None),
        P(None, ("tp", "rep")),
        P(None, ("tp", "rep")),
        P(None, "tp"),
    )
    out_specs = P(("parts", "mem", "rep"), "tp")
    return jax.shard_map(shards, mesh=mesh, in_specs=in_specs, out_specs=out_specs, check_vma=False)
```

```python
import functools

import jax
import jax.numpy as jnp
from jax import lax
from jax.experimental import pallas as pl
from jax.experimental.pallas import tpu as pltpu
from jax.sharding import PartitionSpec as P

D = 4608
KERNEL = 4
DILATION = 3
SEQS = 4
EPSILON = 1e-06
RIM = 16
LANES = 128

F32 = jnp.float32
BF16 = jnp.bfloat16
I32 = jnp.int32


def iota(shape, axis):
    return lax.broadcasted_iota(I32, shape, axis)


def dot(a, b):
    return jnp.dot(a, b, preferred_element_type=F32)


def dot_nt(a, b, precision=None):
    return lax.dot_general(
        a, b, (((1,), (1,)), ((), ())), precision=precision, preferred_element_type=F32
    )


def unit(n, dtype):
    return (iota((n, n), 0) == iota((n, n), 1)).astype(F32).astype(dtype)


def to_bf16(x):
    return x.astype(F32).astype(BF16)


def place_kernel(ids_hbm, place_hbm, out_ref, ids_ref, place_ref, sems):
    copies = [
        pltpu.make_async_copy(place_hbm, place_ref, sems.at[0]),
        pltpu.make_async_copy(ids_hbm, ids_ref, sems.at[1]),
    ]
    for copy in copies:
        copy.start()
    copies[0].wait()
    place = place_ref[...]
    rows = place.shape[0]
    heads, tokens = ids_ref.shape
    eye = unit(LANES, BF16)
    table = jnp.concatenate(
        [dot_nt(eye, to_bf16(place >> 8)), dot_nt(eye, to_bf16(place & 255))], axis=0
    ).astype(BF16)
    copies[1].wait()
    for head in range(heads):
        row = ids_ref[head : head + 1, :]
        hot = to_bf16(iota((rows, tokens), 0) == (row >> 7))
        both = dot(table, hot)
        value = both[:LANES] * 256.0 + both[LANES:]
        chosen = jnp.where(iota(value.shape, 0) == (row & 127), value, 0.0)
        out_ref[head : head + 1, :] = jnp.sum(chosen, axis=0, keepdims=True).astype(I32)


def decode_kernel(codes_hbm, scales_hbm, out_ref, codes_ref, scales_ref, sems):
    heads, width, rows = codes_ref.shape
    blocks = scales_ref.shape[0]
    scales_copy = pltpu.make_async_copy(scales_hbm, scales_ref, sems.at[heads])
    scales_copy.start()
    copies = []
    for head in range(heads):
        copies.append(
            pltpu.make_async_copy(codes_hbm.at[head], codes_ref.at[head], sems.at[head])
        )
        copies[-1].start()
    entry = iota((width, 2 * width), 0)
    column = iota((width, 2 * width), 1)
    column = jnp.where(column < width, column, column - width)
    parity = entry & column & 15
    parity = parity ^ (parity >> 2)
    parity = (parity ^ (parity >> 1)) & 1
    same = (entry >> 4) == (column >> 4)
    rotation = jnp.where(same, 0.25 - 0.5 * parity.astype(F32), 0.0).astype(BF16)
    scales_copy.wait()
    for head in range(heads):
        copies[head].wait()
        factors = jnp.concatenate(
            [
                jnp.broadcast_to(scales_ref[b, head : head + 1, :].astype(F32), (16, rows))
                for b in range(blocks)
            ],
            axis=0,
        )
        scaled = codes_ref[head].astype(F32) * factors
        upper = scaled.astype(BF16)
        lower = (scaled - upper.astype(F32)).astype(BF16)
        out_ref[head] = dot(rotation, jnp.concatenate([upper, lower], axis=0)).astype(BF16)


def picked(local, table_ref, head):
    rows = table_ref.shape[2]
    hot = to_bf16(iota((rows, local.shape[1]), 0) == local[head : head + 1, :])
    return dot(table_ref[head], hot).astype(BF16)


def pick_kernel(base_ref, ids_ref, table_ref, out_ref):
    heads, width, _ = table_ref.shape
    local = ids_ref[...] - base_ref[0]
    for head in range(heads):
        out_ref[head * width : (head + 1) * width, :] = picked(local, table_ref, head)


def merge_kernel(*refs):
    total = refs[0][...].astype(F32)
    for other in refs[1:-1]:
        total = total + other[...].astype(F32)
    refs[-1][...] = total.astype(BF16)


def project_kernel(shifts, count, where_ref, *refs):
    pieces = len(shifts)
    first = 0 in shifts
    rims = refs[:pieces]
    bodies = refs[pieces : 2 * pieces]
    refs = refs[2 * pieces :]
    depth, tokens = bodies[0].shape
    rep = where_ref[0]
    tp = where_ref[1]
    if first:
        weights = refs[:4]
        key_ref, value_ref, rest, held, sems, rest_sems = refs[4:]
        half = held.shape[-1]

        def bring(target, far, which, n, s, sem):
            owner = lax.rem(tp + count - s, count)
            rows = pl.ds(pl.multiple_of(owner * depth, depth), depth)
            copy = pltpu.make_async_copy(
                weights[2 * far + which].at[rows, :],
                target.at[far, which, pl.ds(n * depth, depth), :],
                sem,
            )
            copy.start()
            return copy

        copies = [
            bring(held, far, which, 0, 0, sems.at[2 * far + which])
            for far in range(2)
            for which in (1, 0)
        ]
        later = [
            bring(rest, far, which, n, n + 1, rest_sems.at[(2 * far + which) * (count - 1) + n])
            for far in range(2)
            for which in (1, 0)
            for n in range(count - 1)
        ]
    else:
        later = []
        rest, begun_keys, begun_values, hidden_halo, hidden = refs[:5]
        value_hbm, stats_ref, states, done, done_sems = refs[5:]
        held = rest
        half = held.shape[-1]
        for slot in range(2):
            states[slot, :RIM] = hidden_halo[:, slot * half : (slot + 1) * half]
            states[slot, RIM:] = hidden[:, slot * half : (slot + 1) * half]
    body = jnp.concatenate([b[...].astype(F32) for b in bodies], axis=0).T.astype(BF16)
    rim = jnp.concatenate([r[...].astype(F32) for r in rims], axis=0).T.astype(BF16)
    memory = jnp.concatenate([rim[LANES - RIM :], body], axis=0)
    sums = [0.0] * 4
    for far in range(2):
        slot = rep if far == 0 else 1 - rep
        fields = [None, None]
        for which in (1, 0):
            if first:
                copies[2 * far + 1 - which].wait()
            fields[which] = dot(memory, held[far, which])
            if not first and which == 1:
                done[far] = fields[1] + begun_values[slot]
                copy = pltpu.make_async_copy(done.at[far], value_hbm.at[slot], done_sems.at[far])
                copy.start()
                later.append(copy)
        if first:
            value_ref[slot] = fields[1]
            key_ref[slot] = fields[0]
        else:
            keys = fields[0] + begun_keys[slot]
            values = done[far]
            here = states[slot].astype(F32)
            terms = (here * here, keys * keys, here * keys, values * values)
            sums = [a + jnp.sum(t, axis=1, keepdims=True) for a, t in zip(sums, terms)]
    if not first:
        rows = memory.shape[0]
        lane = iota((rows, 8), 1)
        packed = jnp.zeros((rows, 8), F32)
        for k in range(4):
            packed = jnp.where(lane == k, sums[k], packed)
        stats_ref[...] = dot_nt(unit(8, F32), packed, lax.Precision.HIGHEST)
    for copy in later:
        copy.wait()


def finish_kernel(count, step, keep_ref, *refs):
    stats = refs[:count]
    value_hbm, hidden_ref, taps_ref, out_hbm = refs[count : count + 4]
    gates, factors, value_ref, normed, out_ref, in_sems, sems = refs[count + 4 :]
    rows, half = normed.shape
    tokens, width = out_ref.shape
    arrivals = {}
    chunk = min(step, half)
    for slot in range(2):
        for start in range(0, half, chunk):
            span = pl.ds(start, chunk)
            copy = pltpu.make_async_copy(
                value_hbm.at[slot, :, span], value_ref.at[slot, :, span], in_sems.at[len(arrivals)]
            )
            copy.start()
            arrivals[slot, start] = copy
    total = stats[0][...]
    for other in stats[1:]:
        total = total + other[...]
    inverse_states = lax.rsqrt(total[0:1] / D + EPSILON)
    inverse_keys = lax.rsqrt(total[1:2] / D + EPSILON)
    gate = jax.nn.sigmoid(total[2:3] * inverse_states * inverse_keys / D**0.5)
    factor = gate * lax.rsqrt(gate * gate * total[3:4] / D + EPSILON)
    factor = jnp.where((iota(factor.shape, 1) < RIM) & (keep_ref[0] == 0), 0.0, factor)
    line = iota(total.shape, 0)
    both = jnp.where(line == 0, gate, jnp.where(line == 1, factor, 0.0))
    columns = dot_nt(unit(rows, F32), both, lax.Precision.HIGHEST)
    gates[...] = jnp.broadcast_to(columns[RIM:, 0:1], gates.shape)
    factors[...] = jnp.broadcast_to(columns[:, 1:2], factors.shape)
    copies = []
    for slot in range(2):
        for start in range(0, half, LANES):
            size = min(LANES, half - start)
            span = slice(start, start + size)
            there = slice(slot * half + start, slot * half + start + size)
            if start % chunk == 0:
                arrivals[slot, start].wait()
            values = value_ref[slot, :, span]
            normed[:, span] = values * factors[:, :size]
            conv = None
            for tap in range(KERNEL):
                lag = DILATION * tap
                term = taps_ref[tap : tap + 1, there] * normed[RIM - lag : RIM - lag + tokens, span]
                conv = term if conv is None else conv + term
            gated = values[RIM:] * gates[:, :size]
            out_ref[:, there] = (
                hidden_ref[:, there].astype(F32) + jax.nn.silu(conv) + gated
            ).astype(BF16)
            if there.stop % step == 0:
                ready = pl.ds(there.stop - step, step)
                copy = pltpu.make_async_copy(
                    out_ref.at[:, ready], out_hbm.at[:, ready], sems.at[len(copies)]
                )
                copy.start()
                copies.append(copy)
    for copy in copies:
        copy.wait()


def whole(array):
    return pl.BlockSpec(array.shape, lambda *_: (0,) * array.ndim)


def in_hbm(array):
    return pltpu.with_memory_space_constraint(array, pltpu.HBM)


def after(array, *others):
    return lax.optimization_barrier((array, *others))[0]


def limit(mib):
    return pltpu.CompilerParams(vmem_limit_bytes=mib << 20)


def scattered_sum(stored, decoded, here, meanwhile, settled):
    mems = lax.axis_size("mem")
    heads, width, rows = decoded.shape
    tokens = stored.shape[1]
    asked = lax.all_gather(stored, "mem", axis=0)
    partial = pl.pallas_call(
        pick_kernel,
        grid=(mems,),
        in_specs=[
            pl.BlockSpec(memory_space=pltpu.SMEM),
            pl.BlockSpec((None, heads, tokens), lambda m: (m, 0, 0)),
            whole(decoded),
        ],
        out_specs=pl.BlockSpec((None, heads * width, tokens), lambda m: (m, 0, 0)),
        out_shape=jax.ShapeDtypeStruct((mems, heads * width, tokens), BF16),
        compiler_params=limit(16),
        name="pick_all",
    )((here * rows).astype(I32).reshape(1), asked, decoded)
    total = lax.psum_scatter(partial, "mem", scatter_dimension=0, tiled=False)
    return total, meanwhile(partial), settled


def line_sum(stored, decoded, here, meanwhile, settled):
    heads, width, rows = decoded.shape
    tokens = stored.shape[1]
    base = (here * rows).astype(I32).reshape(1)
    block = jax.ShapeDtypeStruct((heads * width, tokens), BF16)

    def ask(ids, x):
        return lax.ppermute(ids, "mem", [(i, i ^ x) for i in range(4)])

    def crossing(x, pairs):
        return lax.ppermute(x, ("mem", "rep"), [(2 * a + b, 2 * c + d) for a, b, c, d in pairs])

    def pick(ids):
        return pl.pallas_call(
            pick_kernel,
            in_specs=[pl.BlockSpec(memory_space=pltpu.SMEM)]
            + [pl.BlockSpec(memory_space=pltpu.VMEM)] * 2,
            out_shape=block,
            compiler_params=limit(8),
            name="pick_rows",
        )(base, ids, decoded)

    def send(x, *pairs):
        return lax.ppermute(x, "mem", pairs)

    first = ask(stored, 3)
    second = crossing(
        stored,
        [(m, r, m ^ 2, r ^ int(m in (1, 2))) for m in range(4) for r in range(2)],
    )
    first, second = lax.optimization_barrier((first, second))
    rows_3 = pick(first)
    inward = send(rows_3, (0, 1), (3, 2))
    across = send(rows_3, (1, 2), (2, 1))
    rows_2 = pick(after(second, rows_3))
    past = crossing(rows_2, [(m, r, m ^ 2, r ^ 1) for m in (0, 3) for r in range(2)])
    stored, settled = lax.optimization_barrier((after(stored, rows_2), settled))
    rows_1 = pick(ask(stored, 1))
    own = pick(stored)
    onward = after(rows_2, own, across) + inward
    other = meanwhile(onward)
    onward = send(onward, (1, 3), (2, 0))
    beside = send(rows_1, (0, 1), (1, 0), (2, 3), (3, 2))
    own, other = lax.optimization_barrier((own + past, other))
    memory = pl.pallas_call(
        merge_kernel,
        in_specs=[pl.BlockSpec(memory_space=pltpu.VMEM)] * 4,
        out_shape=block,
        compiler_params=limit(4),
        name="merge",
    )(own, across, beside, onward)
    return memory, other, settled


def shards(
    hidden, row_ids, row_place, table_codes, table_scales, key_weight, value_weight, conv_weight
):
    mems = lax.axis_size("mem")
    tps = lax.axis_size("tp")
    reps = lax.axis_size("rep")
    blocks = mems * reps
    tokens, heads = row_ids.shape
    rows, width = table_codes.shape[1:]
    depth = heads * width
    half = key_weight.shape[1]
    seq_length = tokens * blocks // SEQS
    assert reps == 2 and seq_length % tokens == 0 and row_place.shape[0] % LANES == 0
    block = lax.axis_index(("mem", "rep"))
    smem = pl.BlockSpec(memory_space=pltpu.SMEM)

    anywhere = pl.BlockSpec(memory_space=pl.ANY)
    resident = pl.BlockSpec(memory_space=pltpu.VMEM)
    places = row_place.reshape(-1, LANES)
    stored = pl.pallas_call(
        place_kernel,
        in_specs=[anywhere] * 2,
        out_shape=jax.ShapeDtypeStruct((heads, tokens), I32),
        scratch_shapes=[
            pltpu.VMEM((heads, tokens), I32),
            pltpu.VMEM(places.shape, I32),
            pltpu.SemaphoreType.DMA((2,)),
        ],
        compiler_params=limit(4),
        name="place_rows",
    )(in_hbm(row_ids.T), in_hbm(places))
    codes = table_codes.transpose(0, 2, 1)
    scales = table_scales.transpose(2, 0, 1)
    decoded = pl.pallas_call(
        decode_kernel,
        in_specs=[anywhere] * 2,
        out_shape=jax.ShapeDtypeStruct(codes.shape, BF16),
        scratch_shapes=[
            pltpu.VMEM(codes.shape, BF16),
            pltpu.VMEM(scales.shape, BF16),
            pltpu.SemaphoreType.DMA((heads + 1,)),
        ],
        compiler_params=limit(12),
        name="decode_tables",
    )(in_hbm(after(codes, stored)), in_hbm(scales))
    here = lax.axis_index("mem")
    other_key = lax.ppermute(key_weight, "rep", [(0, 1), (1, 0)])
    other_value = lax.ppermute(value_weight, "rep", [(0, 1), (1, 0)])
    needed = [(i, i + 1) for i in range(blocks - 1) if (i + 1) * tokens % seq_length]

    def meanwhile(token):
        tail = after(hidden[tokens - RIM :], token)
        return lax.ppermute(tail, ("mem", "rep"), needed)

    summed = line_sum if mems == 4 else scattered_sum
    memory, hidden_halo, others = summed(
        stored, decoded, here, meanwhile, (other_key, other_value)
    )
    weights = [in_hbm(w) for w in (key_weight, value_weight, *others)]

    where = jnp.stack([lax.axis_index("rep"), lax.axis_index("tp")]).astype(I32)
    extended = tokens + RIM
    bodies = [memory] + [
        lax.ppermute(memory, "tp", [(i, (i + s) % tps) for i in range(tps)])
        for s in range(1, tps)
    ]

    def next_rim(rim, s):
        pairs = [
            (
                (a // reps * tps + i) * reps + a % reps,
                (b // reps * tps + (i + s) % tps) * reps + b % reps,
            )
            for a, b in needed
            for i in range(tps)
        ]
        return lax.ppermute(rim, ("mem", "tp", "rep"), pairs)

    rim = memory[:, tokens - LANES :]
    rims = [next_rim(rim, s) for s in range(tps)]
    others = tps - 1
    field = jax.ShapeDtypeStruct((2, extended, half), F32)
    *begun, rest = pl.pallas_call(
        functools.partial(project_kernel, (0,), tps),
        in_specs=[smem] + [resident] * 2 + [anywhere] * 4,
        out_specs=(resident,) * 3,
        out_shape=(field, field, pltpu.VMEM((2, 2, others * depth, half), BF16)),
        scratch_shapes=[
            pltpu.VMEM((2, 2, depth, half), BF16),
            pltpu.SemaphoreType.DMA((4,)),
            pltpu.SemaphoreType.DMA((4 * others,)),
        ],
        compiler_params=limit(12),
        name="project_own",
    )(where, rims[0], memory, *weights)
    values, stats = pl.pallas_call(
        functools.partial(project_kernel, tuple(range(1, tps)), tps),
        in_specs=[smem] + [resident] * (2 * others + 5),
        out_specs=(pl.BlockSpec(memory_space=pltpu.HBM), resident),
        out_shape=(pltpu.HBM(field.shape, F32), jax.ShapeDtypeStruct((8, extended), F32)),
        scratch_shapes=[
            pltpu.VMEM((2, extended, half), BF16),
            pltpu.VMEM((2, extended, half), F32),
            pltpu.SemaphoreType.DMA((2,)),
        ],
        compiler_params=limit(14),
        name="project_others",
    )(
        where,
        *rims[1:],
        *bodies[1:],
        rest,
        *begun,
        hidden_halo,
        hidden,
    )

    all_stats = [stats] + [
        lax.ppermute(stats, "tp", [(i, (i + s) % tps) for i in range(tps)]) for s in range(1, tps)
    ]
    keep = (block * tokens % seq_length != 0).astype(I32).reshape(1)
    step = 2 * half
    if half % LANES == 0:
        step = next(c for c in (384, 256, 128) if half % c == 0)
    return pl.pallas_call(
        functools.partial(finish_kernel, tps, step),
        in_specs=[smem] + [resident] * tps + [anywhere] + [resident] * 2,
        out_specs=anywhere,
        out_shape=jax.ShapeDtypeStruct((tokens, 2 * half), BF16),
        scratch_shapes=[
            pltpu.VMEM((tokens, LANES), F32),
            pltpu.VMEM((extended, LANES), F32),
            pltpu.VMEM((2, extended, half), F32),
            pltpu.VMEM((extended, half), F32),
            pltpu.VMEM((tokens, 2 * half), BF16),
            pltpu.SemaphoreType.DMA((2 * half // min(step, half),)),
            pltpu.SemaphoreType.DMA((2 * half // step,)),
        ],
        compiler_params=limit(12),
        name="finish",
    )(keep, *all_stats, in_hbm(values), hidden, conv_weight)


def solution(mesh):
    in_specs = (
        P(("parts", "mem", "rep"), "tp"),
        P(("parts", "mem", "rep"), "tp"),
        P("parts"),
        P(("parts", "tp"), "mem", None),
        P(("parts", "tp"), "mem", None),
        P(None, ("tp", "rep")),
        P(None, ("tp", "rep")),
        P(None, "tp"),
    )
    out_specs = P(("parts", "mem", "rep"), "tp")
    return jax.shard_map(shards, mesh=mesh, in_specs=in_specs, out_specs=out_specs, check_vma=False)
```

```python
import functools

import jax
import jax.numpy as jnp
from jax import lax
from jax.experimental import pallas as pl
from jax.experimental.pallas import tpu as pltpu
from jax.sharding import PartitionSpec as P

D = 4608
KERNEL = 4
DILATION = 3
SEQS = 4
EPSILON = 1e-06
RIM = 16
LANES = 128

F32 = jnp.float32
BF16 = jnp.bfloat16
I32 = jnp.int32


def iota(shape, axis):
    return lax.broadcasted_iota(I32, shape, axis)


def dot(a, b):
    return jnp.dot(a, b, preferred_element_type=F32)


def dot_nt(a, b, precision=None):
    return lax.dot_general(
        a, b, (((1,), (1,)), ((), ())), precision=precision, preferred_element_type=F32
    )


def unit(n, dtype):
    return (iota((n, n), 0) == iota((n, n), 1)).astype(F32).astype(dtype)


def to_bf16(x):
    return x.astype(F32).astype(BF16)


def place_kernel(ids_hbm, place_hbm, out_ref, ids_ref, place_ref, sems):
    copies = [
        pltpu.make_async_copy(place_hbm, place_ref, sems.at[0]),
        pltpu.make_async_copy(ids_hbm, ids_ref, sems.at[1]),
    ]
    for copy in copies:
        copy.start()
    copies[0].wait()
    place = place_ref[...]
    rows = place.shape[0]
    heads, tokens = ids_ref.shape
    eye = unit(LANES, BF16)
    table = jnp.concatenate(
        [dot_nt(eye, to_bf16(place >> 8)), dot_nt(eye, to_bf16(place & 255))], axis=0
    ).astype(BF16)
    copies[1].wait()
    for head in range(heads):
        row = ids_ref[head : head + 1, :]
        hot = to_bf16(iota((rows, tokens), 0) == (row >> 7))
        both = dot(table, hot)
        value = both[:LANES] * 256.0 + both[LANES:]
        chosen = jnp.where(iota(value.shape, 0) == (row & 127), value, 0.0)
        out_ref[head : head + 1, :] = jnp.sum(chosen, axis=0, keepdims=True).astype(I32)


def decode_kernel(codes_hbm, scales_hbm, out_ref, codes_ref, scales_ref, sems):
    heads, width, rows = codes_ref.shape
    blocks = scales_ref.shape[0]
    scales_copy = pltpu.make_async_copy(scales_hbm, scales_ref, sems.at[heads])
    scales_copy.start()
    copies = []
    for head in range(heads):
        copies.append(
            pltpu.make_async_copy(codes_hbm.at[head], codes_ref.at[head], sems.at[head])
        )
        copies[-1].start()
    entry = iota((width, 2 * width), 0)
    column = iota((width, 2 * width), 1)
    column = jnp.where(column < width, column, column - width)
    parity = entry & column & 15
    parity = parity ^ (parity >> 2)
    parity = (parity ^ (parity >> 1)) & 1
    same = (entry >> 4) == (column >> 4)
    rotation = jnp.where(same, 0.25 - 0.5 * parity.astype(F32), 0.0).astype(BF16)
    scales_copy.wait()
    for head in range(heads):
        copies[head].wait()
        factors = jnp.concatenate(
            [
                jnp.broadcast_to(scales_ref[b, head : head + 1, :].astype(F32), (16, rows))
                for b in range(blocks)
            ],
            axis=0,
        )
        scaled = codes_ref[head].astype(F32) * factors
        upper = scaled.astype(BF16)
        lower = (scaled - upper.astype(F32)).astype(BF16)
        out_ref[head] = dot(rotation, jnp.concatenate([upper, lower], axis=0)).astype(BF16)


def picked(local, table_ref, head):
    rows = table_ref.shape[2]
    hot = to_bf16(iota((rows, local.shape[1]), 0) == local[head : head + 1, :])
    return dot(table_ref[head], hot).astype(BF16)


def pick_kernel(base_ref, ids_ref, table_ref, out_ref):
    heads, width, _ = table_ref.shape
    local = ids_ref[...] - base_ref[0]
    for head in range(heads):
        out_ref[head * width : (head + 1) * width, :] = picked(local, table_ref, head)


def merge_kernel(*refs):
    total = refs[0][...].astype(F32)
    for other in refs[1:-1]:
        total = total + other[...].astype(F32)
    refs[-1][...] = total.astype(BF16)


def project_kernel(shifts, count, where_ref, *refs):
    pieces = len(shifts)
    first = 0 in shifts
    rims = refs[:pieces]
    bodies = refs[pieces : 2 * pieces]
    refs = refs[2 * pieces :]
    depth, tokens = bodies[0].shape
    rep = where_ref[0]
    tp = where_ref[1]
    if first:
        weights = refs[:4]
        key_ref, value_ref, rest, held, sems, rest_sems = refs[4:]
        half = held.shape[-1]

        def bring(target, far, which, n, s, sem):
            owner = lax.rem(tp + count - s, count)
            rows = pl.ds(pl.multiple_of(owner * depth, depth), depth)
            copy = pltpu.make_async_copy(
                weights[2 * far + which].at[rows, :],
                target.at[far, which, pl.ds(n * depth, depth), :],
                sem,
            )
            copy.start()
            return copy

        copies = [
            bring(held, far, which, 0, 0, sems.at[2 * far + which])
            for far in range(2)
            for which in (1, 0)
        ]
        later = [
            bring(rest, far, which, n, n + 1, rest_sems.at[(2 * far + which) * (count - 1) + n])
            for far in range(2)
            for which in (1, 0)
            for n in range(count - 1)
        ]
    else:
        later = []
        rest, begun_keys, begun_values, hidden_halo, hidden = refs[:5]
        value_hbm, stats_ref, states, done, done_sems = refs[5:]
        held = rest
        half = held.shape[-1]
        for slot in range(2):
            states[slot, :RIM] = hidden_halo[:, slot * half : (slot + 1) * half]
            states[slot, RIM:] = hidden[:, slot * half : (slot + 1) * half]
    body = jnp.concatenate([b[...].astype(F32) for b in bodies], axis=0).T.astype(BF16)
    rim = jnp.concatenate([r[...].astype(F32) for r in rims], axis=0).T.astype(BF16)
    memory = jnp.concatenate([rim[LANES - RIM :], body], axis=0)
    sums = [0.0] * 4
    for far in range(2):
        slot = rep if far == 0 else 1 - rep
        fields = [None, None]
        for which in (1, 0):
            if first:
                copies[2 * far + 1 - which].wait()
            fields[which] = dot(memory, held[far, which])
            if not first and which == 1:
                done[far] = fields[1] + begun_values[slot]
                copy = pltpu.make_async_copy(done.at[far], value_hbm.at[slot], done_sems.at[far])
                copy.start()
                later.append(copy)
        if first:
            value_ref[slot] = fields[1]
            key_ref[slot] = fields[0]
        else:
            keys = fields[0] + begun_keys[slot]
            values = done[far]
            here = states[slot].astype(F32)
            terms = (here * here, keys * keys, here * keys, values * values)
            sums = [a + jnp.sum(t, axis=1, keepdims=True) for a, t in zip(sums, terms)]
    if not first:
        rows = memory.shape[0]
        lane = iota((rows, 8), 1)
        packed = jnp.zeros((rows, 8), F32)
        for k in range(4):
            packed = jnp.where(lane == k, sums[k], packed)
        stats_ref[...] = dot_nt(unit(8, F32), packed, lax.Precision.HIGHEST)
    for copy in later:
        copy.wait()


def finish_kernel(count, step, keep_ref, *refs):
    stats = refs[:count]
    value_hbm, hidden_ref, taps_ref, out_hbm = refs[count : count + 4]
    gates, factors, value_ref, normed, out_ref, in_sems, sems = refs[count + 4 :]
    rows, half = normed.shape
    tokens, width = out_ref.shape
    arrivals = {}
    chunk = min(step, half)
    for slot in range(2):
        for start in range(0, half, chunk):
            span = pl.ds(start, chunk)
            copy = pltpu.make_async_copy(
                value_hbm.at[slot, :, span], value_ref.at[slot, :, span], in_sems.at[len(arrivals)]
            )
            copy.start()
            arrivals[slot, start] = copy
    total = stats[0][...]
    for other in stats[1:]:
        total = total + other[...]
    inverse_states = lax.rsqrt(total[0:1] / D + EPSILON)
    inverse_keys = lax.rsqrt(total[1:2] / D + EPSILON)
    gate = jax.nn.sigmoid(total[2:3] * inverse_states * inverse_keys / D**0.5)
    factor = gate * lax.rsqrt(gate * gate * total[3:4] / D + EPSILON)
    factor = jnp.where((iota(factor.shape, 1) < RIM) & (keep_ref[0] == 0), 0.0, factor)
    line = iota(total.shape, 0)
    both = jnp.where(line == 0, gate, jnp.where(line == 1, factor, 0.0))
    columns = dot_nt(unit(rows, F32), both, lax.Precision.HIGHEST)
    gates[...] = jnp.broadcast_to(columns[RIM:, 0:1], gates.shape)
    factors[...] = jnp.broadcast_to(columns[:, 1:2], factors.shape)
    copies = []
    for slot in range(2):
        for start in range(0, half, LANES):
            size = min(LANES, half - start)
            span = slice(start, start + size)
            there = slice(slot * half + start, slot * half + start + size)
            if start % chunk == 0:
                arrivals[slot, start].wait()
            values = value_ref[slot, :, span]
            normed[:, span] = values * factors[:, :size]
            conv = None
            for tap in range(KERNEL):
                lag = DILATION * tap
                term = taps_ref[tap : tap + 1, there] * normed[RIM - lag : RIM - lag + tokens, span]
                conv = term if conv is None else conv + term
            gated = values[RIM:] * gates[:, :size]
            out_ref[:, there] = (
                hidden_ref[:, there].astype(F32) + jax.nn.silu(conv) + gated
            ).astype(BF16)
            if there.stop % step == 0:
                ready = pl.ds(there.stop - step, step)
                copy = pltpu.make_async_copy(
                    out_ref.at[:, ready], out_hbm.at[:, ready], sems.at[len(copies)]
                )
                copy.start()
                copies.append(copy)
    for copy in copies:
        copy.wait()


def whole(array):
    return pl.BlockSpec(array.shape, lambda *_: (0,) * array.ndim)


def in_hbm(array):
    return pltpu.with_memory_space_constraint(array, pltpu.HBM)


def after(array, *others):
    return lax.optimization_barrier((array, *others))[0]


def limit(mib):
    return pltpu.CompilerParams(vmem_limit_bytes=mib << 20)


def scattered_sum(stored, decoded, here, meanwhile, settled):
    mems = lax.axis_size("mem")
    heads, width, rows = decoded.shape
    tokens = stored.shape[1]
    asked = lax.all_gather(stored, "mem", axis=0)
    partial = pl.pallas_call(
        pick_kernel,
        grid=(mems,),
        in_specs=[
            pl.BlockSpec(memory_space=pltpu.SMEM),
            pl.BlockSpec((None, heads, tokens), lambda m: (m, 0, 0)),
            whole(decoded),
        ],
        out_specs=pl.BlockSpec((None, heads * width, tokens), lambda m: (m, 0, 0)),
        out_shape=jax.ShapeDtypeStruct((mems, heads * width, tokens), BF16),
        compiler_params=limit(16),
        name="pick_all",
    )((here * rows).astype(I32).reshape(1), asked, decoded)
    total = lax.psum_scatter(partial, "mem", scatter_dimension=0, tiled=False)
    return total, meanwhile(partial), settled


def line_sum(stored, decoded, here, meanwhile, settled):
    heads, width, rows = decoded.shape
    tokens = stored.shape[1]
    base = (here * rows).astype(I32).reshape(1)
    block = jax.ShapeDtypeStruct((heads * width, tokens), BF16)

    def ask(ids, x):
        return lax.ppermute(ids, "mem", [(i, i ^ x) for i in range(4)])

    def crossing(x, pairs):
        return lax.ppermute(x, ("mem", "rep"), [(2 * a + b, 2 * c + d) for a, b, c, d in pairs])

    def pick(ids):
        return pl.pallas_call(
            pick_kernel,
            in_specs=[pl.BlockSpec(memory_space=pltpu.SMEM)]
            + [pl.BlockSpec(memory_space=pltpu.VMEM)] * 2,
            out_shape=block,
            compiler_params=limit(8),
            name="pick_rows",
        )(base, ids, decoded)

    def send(x, *pairs):
        return lax.ppermute(x, "mem", pairs)

    first = ask(stored, 3)
    second = crossing(
        stored,
        [(m, r, m ^ 2, r ^ int(m in (1, 2))) for m in range(4) for r in range(2)],
    )
    first, second = lax.optimization_barrier((first, second))
    rows_3 = pick(first)
    inward = send(rows_3, (0, 1), (3, 2))
    across = send(rows_3, (1, 2), (2, 1))
    rows_2 = pick(after(second, rows_3))
    stored, settled = lax.optimization_barrier((after(stored, rows_2), settled))
    rows_1 = pick(ask(stored, 1))
    own = pick(stored)
    onward = after(rows_2, rows_1, own) + inward
    onward = after(onward, across)
    rows_1, rows_2 = after(rows_1, onward), after(rows_2, onward)
    other = meanwhile(onward)
    onward = send(onward, (1, 3), (2, 0))
    beside = send(rows_1, (0, 1), (1, 0), (2, 3), (3, 2))
    past = crossing(rows_2, [(m, r, m ^ 2, r ^ 1) for m in (0, 3) for r in range(2)])
    own, other = lax.optimization_barrier((own + onward, other))
    memory = pl.pallas_call(
        merge_kernel,
        in_specs=[pl.BlockSpec(memory_space=pltpu.VMEM)] * 4,
        out_shape=block,
        compiler_params=limit(4),
        name="merge",
    )(own, across, beside, past)
    return memory, other, settled


def shards(
    hidden, row_ids, row_place, table_codes, table_scales, key_weight, value_weight, conv_weight
):
    mems = lax.axis_size("mem")
    tps = lax.axis_size("tp")
    reps = lax.axis_size("rep")
    blocks = mems * reps
    tokens, heads = row_ids.shape
    rows, width = table_codes.shape[1:]
    depth = heads * width
    half = key_weight.shape[1]
    seq_length = tokens * blocks // SEQS
    assert reps == 2 and seq_length % tokens == 0 and row_place.shape[0] % LANES == 0
    block = lax.axis_index(("mem", "rep"))
    smem = pl.BlockSpec(memory_space=pltpu.SMEM)

    anywhere = pl.BlockSpec(memory_space=pl.ANY)
    resident = pl.BlockSpec(memory_space=pltpu.VMEM)
    places = row_place.reshape(-1, LANES)
    stored = pl.pallas_call(
        place_kernel,
        in_specs=[anywhere] * 2,
        out_shape=jax.ShapeDtypeStruct((heads, tokens), I32),
        scratch_shapes=[
            pltpu.VMEM((heads, tokens), I32),
            pltpu.VMEM(places.shape, I32),
            pltpu.SemaphoreType.DMA((2,)),
        ],
        compiler_params=limit(4),
        name="place_rows",
    )(in_hbm(row_ids.T), in_hbm(places))
    codes = table_codes.transpose(0, 2, 1)
    scales = table_scales.transpose(2, 0, 1)
    decoded = pl.pallas_call(
        decode_kernel,
        in_specs=[anywhere] * 2,
        out_shape=jax.ShapeDtypeStruct(codes.shape, BF16),
        scratch_shapes=[
            pltpu.VMEM(codes.shape, BF16),
            pltpu.VMEM(scales.shape, BF16),
            pltpu.SemaphoreType.DMA((heads + 1,)),
        ],
        compiler_params=limit(12),
        name="decode_tables",
    )(in_hbm(after(codes, stored)), in_hbm(scales))
    here = lax.axis_index("mem")
    other_key = lax.ppermute(key_weight, "rep", [(0, 1), (1, 0)])
    other_value = lax.ppermute(value_weight, "rep", [(0, 1), (1, 0)])
    needed = [(i, i + 1) for i in range(blocks - 1) if (i + 1) * tokens % seq_length]

    def meanwhile(token):
        tail = after(hidden[tokens - RIM :], token)
        return lax.ppermute(tail, ("mem", "rep"), needed)

    summed = line_sum if mems == 4 else scattered_sum
    memory, hidden_halo, others = summed(
        stored, decoded, here, meanwhile, (other_key, other_value)
    )
    weights = [in_hbm(w) for w in (key_weight, value_weight, *others)]

    where = jnp.stack([lax.axis_index("rep"), lax.axis_index("tp")]).astype(I32)
    extended = tokens + RIM
    bodies = [memory] + [
        lax.ppermute(memory, "tp", [(i, (i + s) % tps) for i in range(tps)])
        for s in range(1, tps)
    ]

    def next_rim(rim, s):
        pairs = [
            (
                (a // reps * tps + i) * reps + a % reps,
                (b // reps * tps + (i + s) % tps) * reps + b % reps,
            )
            for a, b in needed
            for i in range(tps)
        ]
        return lax.ppermute(rim, ("mem", "tp", "rep"), pairs)

    rim = memory[:, tokens - LANES :]
    rims = [next_rim(rim, s) for s in range(tps)]
    others = tps - 1
    field = jax.ShapeDtypeStruct((2, extended, half), F32)
    *begun, rest = pl.pallas_call(
        functools.partial(project_kernel, (0,), tps),
        in_specs=[smem] + [resident] * 2 + [anywhere] * 4,
        out_specs=(resident,) * 3,
        out_shape=(field, field, pltpu.VMEM((2, 2, others * depth, half), BF16)),
        scratch_shapes=[
            pltpu.VMEM((2, 2, depth, half), BF16),
            pltpu.SemaphoreType.DMA((4,)),
            pltpu.SemaphoreType.DMA((4 * others,)),
        ],
        compiler_params=limit(12),
        name="project_own",
    )(where, rims[0], memory, *weights)
    values, stats = pl.pallas_call(
        functools.partial(project_kernel, tuple(range(1, tps)), tps),
        in_specs=[smem] + [resident] * (2 * others + 5),
        out_specs=(pl.BlockSpec(memory_space=pltpu.HBM), resident),
        out_shape=(pltpu.HBM(field.shape, F32), jax.ShapeDtypeStruct((8, extended), F32)),
        scratch_shapes=[
            pltpu.VMEM((2, extended, half), BF16),
            pltpu.VMEM((2, extended, half), F32),
            pltpu.SemaphoreType.DMA((2,)),
        ],
        compiler_params=limit(14),
        name="project_others",
    )(
        where,
        *rims[1:],
        *bodies[1:],
        rest,
        *begun,
        hidden_halo,
        hidden,
    )

    all_stats = [stats] + [
        lax.ppermute(stats, "tp", [(i, (i + s) % tps) for i in range(tps)]) for s in range(1, tps)
    ]
    keep = (block * tokens % seq_length != 0).astype(I32).reshape(1)
    step = 2 * half
    if half % LANES == 0:
        step = next(c for c in (384, 256, 128) if half % c == 0)
    return pl.pallas_call(
        functools.partial(finish_kernel, tps, step),
        in_specs=[smem] + [resident] * tps + [anywhere] + [resident] * 2,
        out_specs=anywhere,
        out_shape=jax.ShapeDtypeStruct((tokens, 2 * half), BF16),
        scratch_shapes=[
            pltpu.VMEM((tokens, LANES), F32),
            pltpu.VMEM((extended, LANES), F32),
            pltpu.VMEM((2, extended, half), F32),
            pltpu.VMEM((extended, half), F32),
            pltpu.VMEM((tokens, 2 * half), BF16),
            pltpu.SemaphoreType.DMA((2 * half // min(step, half),)),
            pltpu.SemaphoreType.DMA((2 * half // step,)),
        ],
        compiler_params=limit(12),
        name="finish",
    )(keep, *all_stats, in_hbm(values), hidden, conv_weight)


def solution(mesh):
    in_specs = (
        P(("parts", "mem", "rep"), "tp"),
        P(("parts", "mem", "rep"), "tp"),
        P("parts"),
        P(("parts", "tp"), "mem", None),
        P(("parts", "tp"), "mem", None),
        P(None, ("tp", "rep")),
        P(None, ("tp", "rep")),
        P(None, "tp"),
    )
    out_specs = P(("parts", "mem", "rep"), "tp")
    return jax.shard_map(shards, mesh=mesh, in_specs=in_specs, out_specs=out_specs, check_vma=False)
```

```python
import functools

import jax
import jax.numpy as jnp
from jax import lax
from jax.experimental import pallas as pl
from jax.experimental.pallas import tpu as pltpu
from jax.sharding import PartitionSpec as P

D = 4608
KERNEL = 4
DILATION = 3
SEQS = 4
EPSILON = 1e-06
RIM = 16
LANES = 128

F32 = jnp.float32
BF16 = jnp.bfloat16
I32 = jnp.int32


def iota(shape, axis):
    return lax.broadcasted_iota(I32, shape, axis)


def dot(a, b):
    return jnp.dot(a, b, preferred_element_type=F32)


def dot_nt(a, b, precision=None):
    return lax.dot_general(
        a, b, (((1,), (1,)), ((), ())), precision=precision, preferred_element_type=F32
    )


def unit(n, dtype):
    return (iota((n, n), 0) == iota((n, n), 1)).astype(F32).astype(dtype)


def to_bf16(x):
    return x.astype(F32).astype(BF16)


def place_kernel(ids_hbm, place_hbm, out_ref, ids_ref, place_ref, sems):
    copies = [
        pltpu.make_async_copy(place_hbm, place_ref, sems.at[0]),
        pltpu.make_async_copy(ids_hbm, ids_ref, sems.at[1]),
    ]
    for copy in copies:
        copy.start()
    copies[0].wait()
    place = place_ref[...]
    rows = place.shape[0]
    heads, tokens = ids_ref.shape
    eye = unit(LANES, BF16)
    table = jnp.concatenate(
        [dot_nt(eye, to_bf16(place >> 8)), dot_nt(eye, to_bf16(place & 255))], axis=0
    ).astype(BF16)
    copies[1].wait()
    for head in range(heads):
        row = ids_ref[head : head + 1, :]
        hot = to_bf16(iota((rows, tokens), 0) == (row >> 7))
        both = dot(table, hot)
        value = both[:LANES] * 256.0 + both[LANES:]
        chosen = jnp.where(iota(value.shape, 0) == (row & 127), value, 0.0)
        out_ref[head : head + 1, :] = jnp.sum(chosen, axis=0, keepdims=True).astype(I32)


def rotation_twice(width):
    entry = iota((width, 2 * width), 0)
    column = iota((width, 2 * width), 1)
    column = jnp.where(column < width, column, column - width)
    parity = entry & column & 15
    parity = parity ^ (parity >> 2)
    parity = (parity ^ (parity >> 1)) & 1
    same = (entry >> 4) == (column >> 4)
    return jnp.where(same, 0.25 - 0.5 * parity.astype(F32), 0.0).astype(BF16)


def decoded_table(rotation, codes, scales):
    spread = [jnp.broadcast_to(s, (16, codes.shape[1])) for s in scales]
    scaled = codes.astype(F32) * jnp.concatenate(spread, axis=0)
    upper = scaled.astype(BF16)
    lower = (scaled - upper.astype(F32)).astype(BF16)
    return dot(rotation, jnp.concatenate([upper, lower], axis=0)).astype(BF16)


def lend_kernel(rep_ref, codes_hbm, scales_hbm, out_ref, codes_ref, scales_ref, wide_ref, sems):
    count, width, _ = out_ref.shape
    blocks = scales_ref.shape[0]
    begin = rep_ref[0] * count
    scales_copy = pltpu.make_async_copy(scales_hbm, scales_ref, sems.at[count])
    scales_copy.start()
    copies = []
    for n in range(count):
        copies.append(
            pltpu.make_async_copy(codes_hbm.at[begin + n], codes_ref.at[n], sems.at[n])
        )
        copies[-1].start()
    rotation = rotation_twice(width)
    scales_copy.wait()
    wide_ref[...] = scales_ref[...].astype(F32)
    for n in range(count):
        copies[n].wait()
        scales = [wide_ref[b, pl.ds(begin + n, 1), :] for b in range(blocks)]
        out_ref[n] = decoded_table(rotation, codes_ref[n], scales)


def decode_kernel(lend, rep_ref, codes_hbm, scales_hbm, out_ref, *refs):
    codes_ref, scales_ref, sems = refs[-3:]
    heads, width, _ = codes_ref.shape
    blocks = scales_ref.shape[0]
    scales_copy = pltpu.make_async_copy(scales_hbm, scales_ref, sems.at[heads])
    scales_copy.start()
    copies = []
    for head in range(heads):
        copies.append(
            pltpu.make_async_copy(codes_hbm.at[head], codes_ref.at[head], sems.at[head])
        )
        copies[-1].start()
    rotation = rotation_twice(width)
    scales_copy.wait()
    for head in range(heads):
        copies[head].wait()
        scales = [scales_ref[b, head : head + 1, :].astype(F32) for b in range(blocks)]
        table = decoded_table(rotation, codes_ref[head], scales)
        out_ref[head] = table
        if lend and head >= heads // 2:
            count = heads // 4
            owner, at = divmod(head - heads // 2, count)

            @pl.when(rep_ref[0] == owner)
            def _(table=table, at=at):
                refs[0][at] = table


def picked(local, table):
    hot = to_bf16(iota((table.shape[1], local.shape[1]), 0) == local)
    return dot(table, hot)


def pick_kernel(first, count, scalars_ref, ids_ref, table_ref, *refs):
    out_ref = refs[-1]
    width = table_ref.shape[1]
    ids = ids_ref[...]
    for n in range(count):
        row = ids[first + n : first + n + 1, :]
        value = picked(row - scalars_ref[0], table_ref[first + n])
        if len(refs) > 1:
            side, at = divmod(n, count // 2)
            straight, swapped = refs[0][at], refs[1][at]
            table = jnp.where(scalars_ref[2] == side, straight, swapped)
            value = value + picked(row - scalars_ref[1], table)
        out_ref[n * width : (n + 1) * width, :] = value.astype(BF16)


def merge_kernel(beside_ref, *refs):
    out_ref = refs[-1]
    part = refs[0].shape[0]
    parts = out_ref.shape[0] // part
    for k in range(parts):
        span = slice(k * part, (k + 1) * part)
        total = beside_ref[span, :].astype(F32)
        for other in refs[k:-1:parts]:
            total = total + other[...].astype(F32)
        out_ref[span, :] = total.astype(BF16)


def project_kernel(shifts, count, where_ref, *refs):
    pieces = len(shifts)
    first = 0 in shifts
    rims = refs[:pieces]
    bodies = refs[pieces : 2 * pieces]
    refs = refs[2 * pieces :]
    depth, tokens = bodies[0].shape
    rep = where_ref[0]
    tp = where_ref[1]
    if first:
        weights = refs[:4]
        key_ref, value_ref, rest, held, sems, rest_sems = refs[4:]
        half = held.shape[-1]

        def bring(target, far, which, n, s, sem):
            owner = lax.rem(tp + count - s, count)
            rows = pl.ds(pl.multiple_of(owner * depth, depth), depth)
            copy = pltpu.make_async_copy(
                weights[2 * far + which].at[rows, :],
                target.at[far, which, pl.ds(n * depth, depth), :],
                sem,
            )
            copy.start()
            return copy

        copies = [
            bring(held, far, which, 0, 0, sems.at[2 * far + which])
            for far in range(2)
            for which in (1, 0)
        ]
        later = [
            bring(rest, far, which, n, n + 1, rest_sems.at[(2 * far + which) * (count - 1) + n])
            for far in range(2)
            for which in (1, 0)
            for n in range(count - 1)
        ]
    else:
        later = []
        rest, begun_keys, begun_values, hidden_halo, hidden = refs[:5]
        value_hbm, stats_ref, states, done, done_sems = refs[5:]
        held = rest
        half = held.shape[-1]
        for slot in range(2):
            states[slot, :RIM] = hidden_halo[:, slot * half : (slot + 1) * half]
            states[slot, RIM:] = hidden[:, slot * half : (slot + 1) * half]
    body = jnp.concatenate([b[...].astype(F32) for b in bodies], axis=0).T.astype(BF16)
    rim = jnp.concatenate([r[...].astype(F32) for r in rims], axis=0).T.astype(BF16)
    memory = jnp.concatenate([rim[LANES - RIM :], body], axis=0)
    sums = [0.0] * 4
    for far in range(2):
        slot = rep if far == 0 else 1 - rep
        fields = [None, None]
        for which in (1, 0):
            if first:
                copies[2 * far + 1 - which].wait()
            fields[which] = dot(memory, held[far, which])
            if not first and which == 1:
                done[far] = fields[1] + begun_values[slot]
                copy = pltpu.make_async_copy(done.at[far], value_hbm.at[slot], done_sems.at[far])
                copy.start()
                later.append(copy)
        if first:
            value_ref[slot] = fields[1]
            key_ref[slot] = fields[0]
        else:
            keys = fields[0] + begun_keys[slot]
            values = done[far]
            here = states[slot].astype(F32)
            terms = (here * here, keys * keys, here * keys, values * values)
            sums = [a + jnp.sum(t, axis=1, keepdims=True) for a, t in zip(sums, terms)]
    if not first:
        rows = memory.shape[0]
        lane = iota((rows, 8), 1)
        packed = jnp.zeros((rows, 8), F32)
        for k in range(4):
            packed = jnp.where(lane == k, sums[k], packed)
        stats_ref[...] = dot_nt(unit(8, F32), packed, lax.Precision.HIGHEST)
    for copy in later:
        copy.wait()


def finish_kernel(count, step, keep_ref, *refs):
    stats = refs[:count]
    value_hbm, hidden_ref, taps_ref, out_hbm = refs[count : count + 4]
    gates, factors, value_ref, normed, out_ref, in_sems, sems = refs[count + 4 :]
    rows, half = normed.shape
    tokens, width = out_ref.shape
    arrivals = {}
    chunk = min(step, half)
    for slot in range(2):
        for start in range(0, half, chunk):
            span = pl.ds(start, chunk)
            copy = pltpu.make_async_copy(
                value_hbm.at[slot, :, span], value_ref.at[slot, :, span], in_sems.at[len(arrivals)]
            )
            copy.start()
            arrivals[slot, start] = copy
    total = stats[0][...]
    for other in stats[1:]:
        total = total + other[...]
    inverse_states = lax.rsqrt(total[0:1] / D + EPSILON)
    inverse_keys = lax.rsqrt(total[1:2] / D + EPSILON)
    gate = jax.nn.sigmoid(total[2:3] * inverse_states * inverse_keys / D**0.5)
    factor = gate * lax.rsqrt(gate * gate * total[3:4] / D + EPSILON)
    factor = jnp.where((iota(factor.shape, 1) < RIM) & (keep_ref[0] == 0), 0.0, factor)
    line = iota(total.shape, 0)
    both = jnp.where(line == 0, gate, jnp.where(line == 1, factor, 0.0))
    columns = dot_nt(unit(rows, F32), both, lax.Precision.HIGHEST)
    gates[...] = jnp.broadcast_to(columns[RIM:, 0:1], gates.shape)
    factors[...] = jnp.broadcast_to(columns[:, 1:2], factors.shape)
    copies = []
    for slot in range(2):
        for start in range(0, half, LANES):
            size = min(LANES, half - start)
            span = slice(start, start + size)
            there = slice(slot * half + start, slot * half + start + size)
            if start % chunk == 0:
                arrivals[slot, start].wait()
            values = value_ref[slot, :, span]
            normed[:, span] = values * factors[:, :size]
            conv = None
            for tap in range(KERNEL):
                lag = DILATION * tap
                term = taps_ref[tap : tap + 1, there] * normed[RIM - lag : RIM - lag + tokens, span]
                conv = term if conv is None else conv + term
            gated = values[RIM:] * gates[:, :size]
            out_ref[:, there] = (
                hidden_ref[:, there].astype(F32) + jax.nn.silu(conv) + gated
            ).astype(BF16)
            if there.stop % step == 0:
                ready = pl.ds(there.stop - step, step)
                copy = pltpu.make_async_copy(
                    out_ref.at[:, ready], out_hbm.at[:, ready], sems.at[len(copies)]
                )
                copy.start()
                copies.append(copy)
    for copy in copies:
        copy.wait()


def whole(array):
    return pl.BlockSpec(array.shape, lambda *_: (0,) * array.ndim)


def in_hbm(array):
    return pltpu.with_memory_space_constraint(array, pltpu.HBM)


def after(array, *others):
    return lax.optimization_barrier((array, *others))[0]


def limit(mib):
    return pltpu.CompilerParams(vmem_limit_bytes=mib << 20)


def pick(ids, table, scalars, *near, first=0, count=None):
    heads, width, _ = table.shape
    count = count or heads
    return pl.pallas_call(
        functools.partial(pick_kernel, first, count),
        in_specs=[pl.BlockSpec(memory_space=pltpu.SMEM)]
        + [pl.BlockSpec(memory_space=pltpu.VMEM)] * (2 + len(near)),
        out_shape=jax.ShapeDtypeStruct((count * width, ids.shape[1]), BF16),
        compiler_params=limit(8),
        name="pick_rows",
    )(scalars, ids, table, *near)


def decode(codes, scales, rep, lend):
    heads, width, rows = codes.shape
    shapes = [jax.ShapeDtypeStruct((n, width, rows), BF16) for n in (heads, heads // 4)]
    return pl.pallas_call(
        functools.partial(decode_kernel, lend),
        in_specs=[pl.BlockSpec(memory_space=pltpu.SMEM)] + [pl.BlockSpec(memory_space=pl.ANY)] * 2,
        out_shape=shapes[: 1 + lend],
        scratch_shapes=[
            pltpu.VMEM(codes.shape, BF16),
            pltpu.VMEM(scales.shape, BF16),
            pltpu.SemaphoreType.DMA((heads + 1,)),
        ],
        compiler_params=limit(12),
        name="decode_tables",
    )(rep, in_hbm(codes), in_hbm(scales))


def scattered_sum(stored, codes, scales, here, rep, meanwhile, settled):
    mems = lax.axis_size("mem")
    heads, width, rows = codes.shape
    tokens = stored.shape[1]
    (decoded,) = decode(codes, scales, rep, False)
    asked = lax.all_gather(stored, "mem", axis=0)
    partial = pl.pallas_call(
        functools.partial(pick_kernel, 0, heads),
        grid=(mems,),
        in_specs=[
            pl.BlockSpec(memory_space=pltpu.SMEM),
            pl.BlockSpec((None, heads, tokens), lambda m: (m, 0, 0)),
            whole(decoded),
        ],
        out_specs=pl.BlockSpec((None, heads * width, tokens), lambda m: (m, 0, 0)),
        out_shape=jax.ShapeDtypeStruct((mems, heads * width, tokens), BF16),
        compiler_params=limit(16),
        name="pick_all",
    )((here * rows).astype(I32).reshape(1), asked, decoded)
    total = lax.psum_scatter(partial, "mem", scatter_dimension=0, tiled=False)
    return total, meanwhile(partial), settled


def line_sum(stored, codes, scales, here, rep, meanwhile, settled):
    heads, width, rows = codes.shape
    part = heads // 2
    middle = (here == 1) | (here == 2)
    outer = jnp.where(here < 2, 0, 3)
    scalars = jnp.stack([here * rows, outer * rows, rep[0]]).astype(I32)

    def send(x, *pairs):
        return lax.ppermute(x, "mem", pairs)

    def swap(x):
        return lax.ppermute(x, "rep", [(0, 1), (1, 0)])

    lent = pl.pallas_call(
        lend_kernel,
        in_specs=[pl.BlockSpec(memory_space=pltpu.SMEM)] + [pl.BlockSpec(memory_space=pl.ANY)] * 2,
        out_shape=jax.ShapeDtypeStruct((heads // 4, width, rows), BF16),
        scratch_shapes=[
            pltpu.VMEM((heads // 4, width, rows), BF16),
            pltpu.VMEM(scales.shape, BF16),
            pltpu.VMEM(scales.shape, F32),
            pltpu.SemaphoreType.DMA((heads // 4 + 1,)),
        ],
        compiler_params=limit(4),
        name="lend_tables",
    )(rep, in_hbm(codes), in_hbm(scales))
    near = [send(lent, (0, 1), (3, 2))]
    ids = stored(lent)
    ids_3 = send(ids, (1, 2), (2, 1))
    ids_2 = send(ids, (0, 2), (3, 1))
    decoded, lent = decode(after(codes, ids), scales, rep, True)
    ids_1 = send(after(ids, ids_3), (0, 1), (3, 2))
    lent, settled, ids_1, ids_2, ids_3 = lax.optimization_barrier(
        (lent, settled, ids_1, ids_2, ids_3)
    )
    near.append(send(lent, (0, 1), (3, 2)))

    beside = pick(ids_1, decoded, scalars)
    other = meanwhile(beside)
    beside = send(beside, (1, 0), (2, 3))
    across, onward, own = [], [], []
    for n in range(2):
        near_n = near[n] if n == 0 else after(near[n], own[0])
        held = (near_n, swap(near_n))
        half = dict(first=n * part, count=part)
        rows_3 = pick(ids_3, decoded, scalars, *held, **half)
        across.append(send(rows_3, (1, 2), (2, 1)))
        rows_2 = pick(after(ids_2, rows_3), decoded, scalars, *held, **half)
        if n:
            rows_2 = after(rows_2, across[0], onward[0])
        onward.append(send(rows_2, (1, 3), (2, 0)))
        own.append(pick(after(ids, rows_2), decoded, scalars, *held, **half))
    own[1], other = lax.optimization_barrier((own[1], other))
    memory = pl.pallas_call(
        merge_kernel,
        in_specs=[pl.BlockSpec(memory_space=pltpu.VMEM)] * 7,
        out_shape=jax.ShapeDtypeStruct((heads * width, ids.shape[1]), BF16),
        compiler_params=limit(4),
        name="merge",
    )(beside, *own, *across, *onward)
    return memory, other, settled


def shards(
    hidden, row_ids, row_place, table_codes, table_scales, key_weight, value_weight, conv_weight
):
    mems = lax.axis_size("mem")
    tps = lax.axis_size("tp")
    reps = lax.axis_size("rep")
    blocks = mems * reps
    tokens, heads = row_ids.shape
    rows, width = table_codes.shape[1:]
    depth = heads * width
    half = key_weight.shape[1]
    seq_length = tokens * blocks // SEQS
    assert reps == 2 and seq_length % tokens == 0 and row_place.shape[0] % LANES == 0
    block = lax.axis_index(("mem", "rep"))
    smem = pl.BlockSpec(memory_space=pltpu.SMEM)

    anywhere = pl.BlockSpec(memory_space=pl.ANY)
    resident = pl.BlockSpec(memory_space=pltpu.VMEM)
    places = row_place.reshape(-1, LANES)

    def stored(token=None):
        ids = row_ids.T if token is None else after(row_ids.T, token)
        return pl.pallas_call(
            place_kernel,
            in_specs=[anywhere] * 2,
            out_shape=jax.ShapeDtypeStruct((heads, tokens), I32),
            scratch_shapes=[
                pltpu.VMEM((heads, tokens), I32),
                pltpu.VMEM(places.shape, I32),
                pltpu.SemaphoreType.DMA((2,)),
            ],
            compiler_params=limit(4),
            name="place_rows",
        )(in_hbm(ids), in_hbm(places))

    codes = table_codes.transpose(0, 2, 1)
    scales = table_scales.transpose(2, 0, 1)
    here = lax.axis_index("mem")
    rep = lax.axis_index("rep").astype(I32).reshape(1)
    other_key = lax.ppermute(key_weight, "rep", [(0, 1), (1, 0)])
    other_value = lax.ppermute(value_weight, "rep", [(0, 1), (1, 0)])
    needed = [(i, i + 1) for i in range(blocks - 1) if (i + 1) * tokens % seq_length]

    def meanwhile(token):
        tail = after(hidden[tokens - RIM :], token)
        return lax.ppermute(tail, ("mem", "rep"), needed)

    line = mems == 4 and heads % 4 == 0
    memory, hidden_halo, others = (line_sum if line else scattered_sum)(
        stored if line else stored(),
        codes,
        scales,
        here,
        rep,
        meanwhile,
        (other_key, other_value),
    )
    weights = [in_hbm(w) for w in (key_weight, value_weight, *others)]

    where = jnp.stack([lax.axis_index("rep"), lax.axis_index("tp")]).astype(I32)
    extended = tokens + RIM
    bodies = [memory] + [
        lax.ppermute(memory, "tp", [(i, (i + s) % tps) for i in range(tps)])
        for s in range(1, tps)
    ]

    def next_rim(rim, s):
        pairs = [
            (
                (a // reps * tps + i) * reps + a % reps,
                (b // reps * tps + (i + s) % tps) * reps + b % reps,
            )
            for a, b in needed
            for i in range(tps)
        ]
        return lax.ppermute(rim, ("mem", "tp", "rep"), pairs)

    rim = memory[:, tokens - LANES :]
    rims = [next_rim(rim, s) for s in range(tps)]
    others = tps - 1
    field = jax.ShapeDtypeStruct((2, extended, half), F32)
    *begun, rest = pl.pallas_call(
        functools.partial(project_kernel, (0,), tps),
        in_specs=[smem] + [resident] * 2 + [anywhere] * 4,
        out_specs=(resident,) * 3,
        out_shape=(field, field, pltpu.VMEM((2, 2, others * depth, half), BF16)),
        scratch_shapes=[
            pltpu.VMEM((2, 2, depth, half), BF16),
            pltpu.SemaphoreType.DMA((4,)),
            pltpu.SemaphoreType.DMA((4 * others,)),
        ],
        compiler_params=limit(12),
        name="project_own",
    )(where, rims[0], memory, *weights)
    values, stats = pl.pallas_call(
        functools.partial(project_kernel, tuple(range(1, tps)), tps),
        in_specs=[smem] + [resident] * (2 * others + 5),
        out_specs=(pl.BlockSpec(memory_space=pltpu.HBM), resident),
        out_shape=(pltpu.HBM(field.shape, F32), jax.ShapeDtypeStruct((8, extended), F32)),
        scratch_shapes=[
            pltpu.VMEM((2, extended, half), BF16),
            pltpu.VMEM((2, extended, half), F32),
            pltpu.SemaphoreType.DMA((2,)),
        ],
        compiler_params=limit(14),
        name="project_others",
    )(
        where,
        *rims[1:],
        *bodies[1:],
        rest,
        *begun,
        hidden_halo,
        hidden,
    )

    all_stats = [stats] + [
        lax.ppermute(stats, "tp", [(i, (i + s) % tps) for i in range(tps)]) for s in range(1, tps)
    ]
    keep = (block * tokens % seq_length != 0).astype(I32).reshape(1)
    step = 2 * half
    if half % LANES == 0:
        step = next(c for c in (384, 256, 128) if half % c == 0)
    return pl.pallas_call(
        functools.partial(finish_kernel, tps, step),
        in_specs=[smem] + [resident] * tps + [anywhere] + [resident] * 2,
        out_specs=anywhere,
        out_shape=jax.ShapeDtypeStruct((tokens, 2 * half), BF16),
        scratch_shapes=[
            pltpu.VMEM((tokens, LANES), F32),
            pltpu.VMEM((extended, LANES), F32),
            pltpu.VMEM((2, extended, half), F32),
            pltpu.VMEM((extended, half), F32),
            pltpu.VMEM((tokens, 2 * half), BF16),
            pltpu.SemaphoreType.DMA((2 * half // min(step, half),)),
            pltpu.SemaphoreType.DMA((2 * half // step,)),
        ],
        compiler_params=limit(12),
        name="finish",
    )(keep, *all_stats, in_hbm(values), hidden, conv_weight)


def solution(mesh):
    in_specs = (
        P(("parts", "mem", "rep"), "tp"),
        P(("parts", "mem", "rep"), "tp"),
        P("parts"),
        P(("parts", "tp"), "mem", None),
        P(("parts", "tp"), "mem", None),
        P(None, ("tp", "rep")),
        P(None, ("tp", "rep")),
        P(None, "tp"),
    )
    out_specs = P(("parts", "mem", "rep"), "tp")
    return jax.shard_map(shards, mesh=mesh, in_specs=in_specs, out_specs=out_specs, check_vma=False)
```

```python
import functools

import jax
import jax.numpy as jnp
from jax import lax
from jax.experimental import pallas as pl
from jax.experimental.pallas import tpu as pltpu
from jax.sharding import PartitionSpec as P

D = 4608
KERNEL = 4
DILATION = 3
SEQS = 4
EPSILON = 1e-06
RIM = 16
LANES = 128

F32 = jnp.float32
BF16 = jnp.bfloat16
I32 = jnp.int32


def iota(shape, axis):
    return lax.broadcasted_iota(I32, shape, axis)


def dot(a, b):
    return jnp.dot(a, b, preferred_element_type=F32)


def dot_nt(a, b, precision=None):
    return lax.dot_general(
        a, b, (((1,), (1,)), ((), ())), precision=precision, preferred_element_type=F32
    )


def unit(n, dtype):
    return (iota((n, n), 0) == iota((n, n), 1)).astype(F32).astype(dtype)


def to_bf16(x):
    return x.astype(F32).astype(BF16)


def place_kernel(ids_hbm, place_hbm, out_ref, ids_ref, place_ref, sems):
    copies = [
        pltpu.make_async_copy(place_hbm, place_ref, sems.at[0]),
        pltpu.make_async_copy(ids_hbm, ids_ref, sems.at[1]),
    ]
    for copy in copies:
        copy.start()
    copies[0].wait()
    place = place_ref[...]
    rows = place.shape[0]
    heads, tokens = ids_ref.shape
    eye = unit(LANES, BF16)
    table = jnp.concatenate(
        [dot_nt(eye, to_bf16(place >> 8)), dot_nt(eye, to_bf16(place & 255))], axis=0
    ).astype(BF16)
    copies[1].wait()
    for head in range(heads):
        row = ids_ref[head : head + 1, :]
        hot = to_bf16(iota((rows, tokens), 0) == (row >> 7))
        both = dot(table, hot)
        value = both[:LANES] * 256.0 + both[LANES:]
        chosen = jnp.where(iota(value.shape, 0) == (row & 127), value, 0.0)
        out_ref[head : head + 1, :] = jnp.sum(chosen, axis=0, keepdims=True).astype(I32)


def decode_kernel(codes_hbm, scales_hbm, out_ref, codes_ref, scales_ref, sems):
    heads, width, rows = codes_ref.shape
    blocks = scales_ref.shape[0]
    scales_copy = pltpu.make_async_copy(scales_hbm, scales_ref, sems.at[heads])
    scales_copy.start()
    copies = []
    for head in range(heads):
        copies.append(
            pltpu.make_async_copy(codes_hbm.at[head], codes_ref.at[head], sems.at[head])
        )
        copies[-1].start()
    entry = iota((width, 2 * width), 0)
    column = iota((width, 2 * width), 1)
    column = jnp.where(column < width, column, column - width)
    parity = entry & column & 15
    parity = parity ^ (parity >> 2)
    parity = (parity ^ (parity >> 1)) & 1
    same = (entry >> 4) == (column >> 4)
    rotation = jnp.where(same, 0.25 - 0.5 * parity.astype(F32), 0.0).astype(BF16)
    scales_copy.wait()
    for head in range(heads):
        copies[head].wait()
        factors = jnp.concatenate(
            [
                jnp.broadcast_to(scales_ref[b, head : head + 1, :].astype(F32), (16, rows))
                for b in range(blocks)
            ],
            axis=0,
        )
        scaled = codes_ref[head].astype(F32) * factors
        upper = scaled.astype(BF16)
        lower = (scaled - upper.astype(F32)).astype(BF16)
        out_ref[head] = dot(rotation, jnp.concatenate([upper, lower], axis=0)).astype(BF16)


def picked(local, table_ref, head):
    rows = table_ref.shape[2]
    hot = to_bf16(iota((rows, local.shape[1]), 0) == local[head : head + 1, :])
    return dot(table_ref[head], hot).astype(BF16)


def pick_kernel(base_ref, ids_ref, table_ref, out_ref):
    heads, width, _ = table_ref.shape
    local = ids_ref[...] - base_ref[0]
    for head in range(heads):
        out_ref[head * width : (head + 1) * width, :] = picked(local, table_ref, head)


def merge_kernel(*refs):
    total = refs[0][...].astype(F32)
    for other in refs[1:-1]:
        total = total + other[...].astype(F32)
    refs[-1][...] = total.astype(BF16)


def project_kernel(shifts, count, where_ref, *refs):
    pieces = len(shifts)
    first = 0 in shifts
    rims = refs[:pieces]
    bodies = refs[pieces : 2 * pieces]
    refs = refs[2 * pieces :]
    depth, tokens = bodies[0].shape
    rep = where_ref[0]
    tp = where_ref[1]
    if first:
        weights = refs[:4]
        key_ref, value_ref, rest, held, sems, rest_sems = refs[4:]
        half = held.shape[-1]

        def bring(target, far, which, n, s, sem):
            owner = lax.rem(tp + count - s, count)
            rows = pl.ds(pl.multiple_of(owner * depth, depth), depth)
            copy = pltpu.make_async_copy(
                weights[2 * far + which].at[rows, :],
                target.at[far, which, pl.ds(n * depth, depth), :],
                sem,
            )
            copy.start()
            return copy

        copies = [
            bring(held, far, which, 0, 0, sems.at[2 * far + which])
            for far in range(2)
            for which in (1, 0)
        ]
        later = [
            bring(rest, far, which, n, n + 1, rest_sems.at[(2 * far + which) * (count - 1) + n])
            for far in range(2)
            for which in (1, 0)
            for n in range(count - 1)
        ]
    else:
        later = []
        rest, begun_keys, begun_values, hidden_halo, hidden = refs[:5]
        value_hbm, stats_ref, states, done, done_sems = refs[5:]
        held = rest
        half = held.shape[-1]
        for slot in range(2):
            states[slot, :RIM] = hidden_halo[:, slot * half : (slot + 1) * half]
            states[slot, RIM:] = hidden[:, slot * half : (slot + 1) * half]
    body = jnp.concatenate([b[...].astype(F32) for b in bodies], axis=0).T.astype(BF16)
    rim = jnp.concatenate([r[...].astype(F32) for r in rims], axis=0).T.astype(BF16)
    memory = jnp.concatenate([rim[LANES - RIM :], body], axis=0)
    sums = [0.0] * 4
    for far in range(2):
        slot = rep if far == 0 else 1 - rep
        fields = [None, None]
        for which in (1, 0):
            if first:
                copies[2 * far + 1 - which].wait()
            fields[which] = dot(memory, held[far, which])
            if not first and which == 1:
                done[far] = fields[1] + begun_values[slot]
                copy = pltpu.make_async_copy(done.at[far], value_hbm.at[slot], done_sems.at[far])
                copy.start()
                later.append(copy)
        if first:
            value_ref[slot] = fields[1]
            key_ref[slot] = fields[0]
        else:
            keys = fields[0] + begun_keys[slot]
            values = done[far]
            here = states[slot].astype(F32)
            terms = (here * here, keys * keys, here * keys, values * values)
            sums = [a + jnp.sum(t, axis=1, keepdims=True) for a, t in zip(sums, terms)]
    if not first:
        rows = memory.shape[0]
        lane = iota((rows, 8), 1)
        packed = jnp.zeros((rows, 8), F32)
        for k in range(4):
            packed = jnp.where(lane == k, sums[k], packed)
        stats_ref[...] = dot_nt(unit(8, F32), packed, lax.Precision.HIGHEST)
    for copy in later:
        copy.wait()


def finish_kernel(count, step, keep_ref, *refs):
    stats = refs[:count]
    value_hbm, hidden_ref, taps_ref, out_hbm = refs[count : count + 4]
    gates, factors, value_ref, normed, out_ref, in_sems, sems = refs[count + 4 :]
    rows, half = normed.shape
    tokens, width = out_ref.shape
    arrivals = {}
    chunk = min(step, half)
    for slot in range(2):
        for start in range(0, half, chunk):
            span = pl.ds(start, chunk)
            copy = pltpu.make_async_copy(
                value_hbm.at[slot, :, span], value_ref.at[slot, :, span], in_sems.at[len(arrivals)]
            )
            copy.start()
            arrivals[slot, start] = copy
    total = stats[0][...]
    for other in stats[1:]:
        total = total + other[...]
    inverse_states = lax.rsqrt(total[0:1] / D + EPSILON)
    inverse_keys = lax.rsqrt(total[1:2] / D + EPSILON)
    gate = jax.nn.sigmoid(total[2:3] * inverse_states * inverse_keys / D**0.5)
    factor = gate * lax.rsqrt(gate * gate * total[3:4] / D + EPSILON)
    factor = jnp.where((iota(factor.shape, 1) < RIM) & (keep_ref[0] == 0), 0.0, factor)
    line = iota(total.shape, 0)
    both = jnp.where(line == 0, gate, jnp.where(line == 1, factor, 0.0))
    columns = dot_nt(unit(rows, F32), both, lax.Precision.HIGHEST)
    gates[...] = jnp.broadcast_to(columns[RIM:, 0:1], gates.shape)
    factors[...] = jnp.broadcast_to(columns[:, 1:2], factors.shape)
    copies = []
    for slot in range(2):
        for start in range(0, half, LANES):
            size = min(LANES, half - start)
            span = slice(start, start + size)
            there = slice(slot * half + start, slot * half + start + size)
            if start % chunk == 0:
                arrivals[slot, start].wait()
            values = value_ref[slot, :, span]
            normed[:, span] = values * factors[:, :size]
            conv = None
            for tap in range(KERNEL):
                lag = DILATION * tap
                term = taps_ref[tap : tap + 1, there] * normed[RIM - lag : RIM - lag + tokens, span]
                conv = term if conv is None else conv + term
            gated = values[RIM:] * gates[:, :size]
            out_ref[:, there] = (
                hidden_ref[:, there].astype(F32) + jax.nn.silu(conv) + gated
            ).astype(BF16)
            if there.stop % step == 0:
                ready = pl.ds(there.stop - step, step)
                copy = pltpu.make_async_copy(
                    out_ref.at[:, ready], out_hbm.at[:, ready], sems.at[len(copies)]
                )
                copy.start()
                copies.append(copy)
    for copy in copies:
        copy.wait()


def whole(array):
    return pl.BlockSpec(array.shape, lambda *_: (0,) * array.ndim)


def in_hbm(array):
    return pltpu.with_memory_space_constraint(array, pltpu.HBM)


def after(array, *others):
    return lax.optimization_barrier((array, *others))[0]


def limit(mib):
    return pltpu.CompilerParams(vmem_limit_bytes=mib << 20)


def scattered_sum(stored, decoded, here, meanwhile, settled):
    mems = lax.axis_size("mem")
    heads, width, rows = decoded.shape
    tokens = stored.shape[1]
    asked = lax.all_gather(stored, "mem", axis=0)
    partial = pl.pallas_call(
        pick_kernel,
        grid=(mems,),
        in_specs=[
            pl.BlockSpec(memory_space=pltpu.SMEM),
            pl.BlockSpec((None, heads, tokens), lambda m: (m, 0, 0)),
            whole(decoded),
        ],
        out_specs=pl.BlockSpec((None, heads * width, tokens), lambda m: (m, 0, 0)),
        out_shape=jax.ShapeDtypeStruct((mems, heads * width, tokens), BF16),
        compiler_params=limit(16),
        name="pick_all",
    )((here * rows).astype(I32).reshape(1), asked, decoded)
    total = lax.psum_scatter(partial, "mem", scatter_dimension=0, tiled=False)
    return total, meanwhile(partial), settled


def line_sum(stored, decoded, here, meanwhile, settled):
    heads, width, rows = decoded.shape
    tokens = stored.shape[1]
    base = (here * rows).astype(I32).reshape(1)
    block = jax.ShapeDtypeStruct((heads * width, tokens), BF16)

    def ask(ids, x):
        return lax.ppermute(ids, "mem", [(i, i ^ x) for i in range(4)])

    def crossing(x, pairs):
        return lax.ppermute(x, ("mem", "rep"), [(2 * a + b, 2 * c + d) for a, b, c, d in pairs])

    def pick(ids):
        return pl.pallas_call(
            pick_kernel,
            in_specs=[pl.BlockSpec(memory_space=pltpu.SMEM)]
            + [pl.BlockSpec(memory_space=pltpu.VMEM)] * 2,
            out_shape=block,
            compiler_params=limit(8),
            name="pick_rows",
        )(base, ids, decoded)

    def send(x, *pairs):
        return lax.ppermute(x, "mem", pairs)

    first = ask(stored, 3)
    second = crossing(
        stored,
        [(m, r, m ^ 2, r ^ int(m in (1, 2))) for m in range(4) for r in range(2)],
    )
    first, second = lax.optimization_barrier((first, second))
    rows_3 = pick(first)
    inward = send(rows_3, (0, 1), (3, 2))
    across = send(rows_3, (1, 2), (2, 1))
    rows_2 = pick(after(second, rows_3))
    stored, settled = lax.optimization_barrier((after(stored, rows_2), settled))
    past = crossing(rows_2, [(m, r, m ^ 2, r ^ 1) for m in (0, 3) for r in range(2)])
    rows_1 = pick(ask(stored, 1))
    own = pick(stored)
    beside = send(rows_1, (0, 1), (1, 0), (2, 3), (3, 2))
    onward = after(rows_2, rows_1, own) + inward
    onward = after(onward, across)
    other = meanwhile(onward)
    onward = send(onward, (1, 3), (2, 0))
    own, other = lax.optimization_barrier((own + past + beside, other))
    memory = pl.pallas_call(
        merge_kernel,
        in_specs=[pl.BlockSpec(memory_space=pltpu.VMEM)] * 3,
        out_shape=block,
        compiler_params=limit(4),
        name="merge",
    )(own, across, onward)
    return memory, other, settled


def shards(
    hidden, row_ids, row_place, table_codes, table_scales, key_weight, value_weight, conv_weight
):
    mems = lax.axis_size("mem")
    tps = lax.axis_size("tp")
    reps = lax.axis_size("rep")
    blocks = mems * reps
    tokens, heads = row_ids.shape
    rows, width = table_codes.shape[1:]
    depth = heads * width
    half = key_weight.shape[1]
    seq_length = tokens * blocks // SEQS
    assert reps == 2 and seq_length % tokens == 0 and row_place.shape[0] % LANES == 0
    block = lax.axis_index(("mem", "rep"))
    smem = pl.BlockSpec(memory_space=pltpu.SMEM)

    anywhere = pl.BlockSpec(memory_space=pl.ANY)
    resident = pl.BlockSpec(memory_space=pltpu.VMEM)
    places = row_place.reshape(-1, LANES)
    stored = pl.pallas_call(
        place_kernel,
        in_specs=[anywhere] * 2,
        out_shape=jax.ShapeDtypeStruct((heads, tokens), I32),
        scratch_shapes=[
            pltpu.VMEM((heads, tokens), I32),
            pltpu.VMEM(places.shape, I32),
            pltpu.SemaphoreType.DMA((2,)),
        ],
        compiler_params=limit(4),
        name="place_rows",
    )(in_hbm(row_ids.T), in_hbm(places))
    codes = table_codes.transpose(0, 2, 1)
    scales = table_scales.transpose(2, 0, 1)
    decoded = pl.pallas_call(
        decode_kernel,
        in_specs=[anywhere] * 2,
        out_shape=jax.ShapeDtypeStruct(codes.shape, BF16),
        scratch_shapes=[
            pltpu.VMEM(codes.shape, BF16),
            pltpu.VMEM(scales.shape, BF16),
            pltpu.SemaphoreType.DMA((heads + 1,)),
        ],
        compiler_params=limit(12),
        name="decode_tables",
    )(in_hbm(after(codes, stored)), in_hbm(scales))
    here = lax.axis_index("mem")
    other_key = lax.ppermute(key_weight, "rep", [(0, 1), (1, 0)])
    other_value = lax.ppermute(value_weight, "rep", [(0, 1), (1, 0)])
    needed = [(i, i + 1) for i in range(blocks - 1) if (i + 1) * tokens % seq_length]

    def meanwhile(token):
        tail = after(hidden[tokens - RIM :], token)
        return lax.ppermute(tail, ("mem", "rep"), needed)

    summed = line_sum if mems == 4 else scattered_sum
    memory, hidden_halo, others = summed(
        stored, decoded, here, meanwhile, (other_key, other_value)
    )
    weights = [in_hbm(w) for w in (key_weight, value_weight, *others)]

    where = jnp.stack([lax.axis_index("rep"), lax.axis_index("tp")]).astype(I32)
    extended = tokens + RIM
    bodies = [memory] + [
        lax.ppermute(memory, "tp", [(i, (i + s) % tps) for i in range(tps)])
        for s in range(1, tps)
    ]

    def next_rim(rim, s):
        pairs = [
            (
                (a // reps * tps + i) * reps + a % reps,
                (b // reps * tps + (i + s) % tps) * reps + b % reps,
            )
            for a, b in needed
            for i in range(tps)
        ]
        return lax.ppermute(rim, ("mem", "tp", "rep"), pairs)

    rim = memory[:, tokens - LANES :]
    rims = [next_rim(rim, s) for s in range(tps)]
    others = tps - 1
    field = jax.ShapeDtypeStruct((2, extended, half), F32)
    *begun, rest = pl.pallas_call(
        functools.partial(project_kernel, (0,), tps),
        in_specs=[smem] + [resident] * 2 + [anywhere] * 4,
        out_specs=(resident,) * 3,
        out_shape=(field, field, pltpu.VMEM((2, 2, others * depth, half), BF16)),
        scratch_shapes=[
            pltpu.VMEM((2, 2, depth, half), BF16),
            pltpu.SemaphoreType.DMA((4,)),
            pltpu.SemaphoreType.DMA((4 * others,)),
        ],
        compiler_params=limit(12),
        name="project_own",
    )(where, rims[0], memory, *weights)
    values, stats = pl.pallas_call(
        functools.partial(project_kernel, tuple(range(1, tps)), tps),
        in_specs=[smem] + [resident] * (2 * others + 5),
        out_specs=(pl.BlockSpec(memory_space=pltpu.HBM), resident),
        out_shape=(pltpu.HBM(field.shape, F32), jax.ShapeDtypeStruct((8, extended), F32)),
        scratch_shapes=[
            pltpu.VMEM((2, extended, half), BF16),
            pltpu.VMEM((2, extended, half), F32),
            pltpu.SemaphoreType.DMA((2,)),
        ],
        compiler_params=limit(14),
        name="project_others",
    )(
        where,
        *rims[1:],
        *bodies[1:],
        rest,
        *begun,
        hidden_halo,
        hidden,
    )

    all_stats = [stats] + [
        lax.ppermute(stats, "tp", [(i, (i + s) % tps) for i in range(tps)]) for s in range(1, tps)
    ]
    keep = (block * tokens % seq_length != 0).astype(I32).reshape(1)
    step = 2 * half
    if half % LANES == 0:
        step = next(c for c in (384, 256, 128) if half % c == 0)
    return pl.pallas_call(
        functools.partial(finish_kernel, tps, step),
        in_specs=[smem] + [resident] * tps + [anywhere] + [resident] * 2,
        out_specs=anywhere,
        out_shape=jax.ShapeDtypeStruct((tokens, 2 * half), BF16),
        scratch_shapes=[
            pltpu.VMEM((tokens, LANES), F32),
            pltpu.VMEM((extended, LANES), F32),
            pltpu.VMEM((2, extended, half), F32),
            pltpu.VMEM((extended, half), F32),
            pltpu.VMEM((tokens, 2 * half), BF16),
            pltpu.SemaphoreType.DMA((2 * half // min(step, half),)),
            pltpu.SemaphoreType.DMA((2 * half // step,)),
        ],
        compiler_params=limit(12),
        name="finish",
    )(keep, *all_stats, in_hbm(values), hidden, conv_weight)


def solution(mesh):
    in_specs = (
        P(("parts", "mem", "rep"), "tp"),
        P(("parts", "mem", "rep"), "tp"),
        P("parts"),
        P(("parts", "tp"), "mem", None),
        P(("parts", "tp"), "mem", None),
        P(None, ("tp", "rep")),
        P(None, ("tp", "rep")),
        P(None, "tp"),
    )
    out_specs = P(("parts", "mem", "rep"), "tp")
    return jax.shard_map(shards, mesh=mesh, in_specs=in_specs, out_specs=out_specs, check_vma=False)
```

```python
import functools

import jax
import jax.numpy as jnp
from jax import lax
from jax.experimental import pallas as pl
from jax.experimental.pallas import tpu as pltpu
from jax.sharding import PartitionSpec as P

D = 4608
KERNEL = 4
DILATION = 3
SEQS = 4
EPSILON = 1e-06
RIM = 16
LANES = 128

F32 = jnp.float32
BF16 = jnp.bfloat16
I32 = jnp.int32


def iota(shape, axis):
    return lax.broadcasted_iota(I32, shape, axis)


def dot(a, b):
    return jnp.dot(a, b, preferred_element_type=F32)


def dot_nt(a, b, precision=None):
    return lax.dot_general(
        a, b, (((1,), (1,)), ((), ())), precision=precision, preferred_element_type=F32
    )


def unit(n, dtype):
    return (iota((n, n), 0) == iota((n, n), 1)).astype(F32).astype(dtype)


def to_bf16(x):
    return x.astype(F32).astype(BF16)


def place_kernel(ids_hbm, place_hbm, out_ref, ids_ref, place_ref, sems):
    copies = [
        pltpu.make_async_copy(place_hbm, place_ref, sems.at[0]),
        pltpu.make_async_copy(ids_hbm, ids_ref, sems.at[1]),
    ]
    for copy in copies:
        copy.start()
    copies[0].wait()
    place = place_ref[...]
    rows = place.shape[0]
    heads, tokens = ids_ref.shape
    eye = unit(LANES, BF16)
    table = jnp.concatenate(
        [dot_nt(eye, to_bf16(place >> 8)), dot_nt(eye, to_bf16(place & 255))], axis=0
    ).astype(BF16)
    copies[1].wait()
    for head in range(heads):
        row = ids_ref[head : head + 1, :]
        hot = to_bf16(iota((rows, tokens), 0) == (row >> 7))
        both = dot(table, hot)
        value = both[:LANES] * 256.0 + both[LANES:]
        chosen = jnp.where(iota(value.shape, 0) == (row & 127), value, 0.0)
        out_ref[head : head + 1, :] = jnp.sum(chosen, axis=0, keepdims=True).astype(I32)


def decode_kernel(codes_hbm, scales_hbm, out_ref, codes_ref, scales_ref, sems):
    heads, width, rows = codes_ref.shape
    blocks = scales_ref.shape[0]
    scales_copy = pltpu.make_async_copy(scales_hbm, scales_ref, sems.at[heads])
    scales_copy.start()
    copies = []
    for head in range(heads):
        copies.append(
            pltpu.make_async_copy(codes_hbm.at[head], codes_ref.at[head], sems.at[head])
        )
        copies[-1].start()
    entry = iota((width, 2 * width), 0)
    column = iota((width, 2 * width), 1)
    column = jnp.where(column < width, column, column - width)
    parity = entry & column & 15
    parity = parity ^ (parity >> 2)
    parity = (parity ^ (parity >> 1)) & 1
    same = (entry >> 4) == (column >> 4)
    rotation = jnp.where(same, 0.25 - 0.5 * parity.astype(F32), 0.0).astype(BF16)
    scales_copy.wait()
    for head in range(heads):
        copies[head].wait()
        factors = jnp.concatenate(
            [
                jnp.broadcast_to(scales_ref[b, head : head + 1, :].astype(F32), (16, rows))
                for b in range(blocks)
            ],
            axis=0,
        )
        scaled = codes_ref[head].astype(F32) * factors
        upper = scaled.astype(BF16)
        lower = (scaled - upper.astype(F32)).astype(BF16)
        out_ref[head] = dot(rotation, jnp.concatenate([upper, lower], axis=0)).astype(BF16)


def picked(local, table_ref, head):
    rows = table_ref.shape[2]
    hot = to_bf16(iota((rows, local.shape[1]), 0) == local[head : head + 1, :])
    return dot(table_ref[head], hot).astype(BF16)


def pick_kernel(base_ref, ids_ref, table_ref, out_ref):
    heads, width, _ = table_ref.shape
    local = ids_ref[...] - base_ref[0]
    for head in range(heads):
        out_ref[head * width : (head + 1) * width, :] = picked(local, table_ref, head)


def merge_kernel(*refs):
    total = refs[0][...].astype(F32)
    for other in refs[1:-1]:
        total = total + other[...].astype(F32)
    refs[-1][...] = total.astype(BF16)


def project_kernel(shifts, count, where_ref, *refs):
    pieces = len(shifts)
    first = 0 in shifts
    rims = refs[:pieces]
    bodies = refs[pieces : 2 * pieces]
    refs = refs[2 * pieces :]
    depth, tokens = bodies[0].shape
    rep = where_ref[0]
    tp = where_ref[1]
    if first:
        weights = refs[:4]
        key_ref, value_ref, rest, held, sems, rest_sems = refs[4:]
        half = held.shape[-1]

        def bring(target, far, which, n, s, sem):
            owner = lax.rem(tp + count - s, count)
            rows = pl.ds(pl.multiple_of(owner * depth, depth), depth)
            copy = pltpu.make_async_copy(
                weights[2 * far + which].at[rows, :],
                target.at[far, which, pl.ds(n * depth, depth), :],
                sem,
            )
            copy.start()
            return copy

        copies = [
            bring(held, far, which, 0, 0, sems.at[2 * far + which])
            for far in range(2)
            for which in (1, 0)
        ]
        later = [
            bring(rest, far, which, n, n + 1, rest_sems.at[(2 * far + which) * (count - 1) + n])
            for far in range(2)
            for which in (1, 0)
            for n in range(count - 1)
        ]
    else:
        later = []
        rest, begun_keys, begun_values, hidden_halo, hidden = refs[:5]
        value_hbm, stats_ref, states, done, done_sems = refs[5:]
        held = rest
        half = held.shape[-1]
        for slot in range(2):
            states[slot, :RIM] = hidden_halo[:, slot * half : (slot + 1) * half]
            states[slot, RIM:] = hidden[:, slot * half : (slot + 1) * half]
    body = jnp.concatenate([b[...].astype(F32) for b in bodies], axis=0).T.astype(BF16)
    rim = jnp.concatenate([r[...].astype(F32) for r in rims], axis=0).T.astype(BF16)
    memory = jnp.concatenate([rim[LANES - RIM :], body], axis=0)
    sums = [0.0] * 4
    for far in range(2):
        slot = rep if far == 0 else 1 - rep
        fields = [None, None]
        for which in (1, 0):
            if first:
                copies[2 * far + 1 - which].wait()
            fields[which] = dot(memory, held[far, which])
            if not first and which == 1:
                done[far] = fields[1] + begun_values[slot]
                copy = pltpu.make_async_copy(done.at[far], value_hbm.at[slot], done_sems.at[far])
                copy.start()
                later.append(copy)
        if first:
            value_ref[slot] = fields[1]
            key_ref[slot] = fields[0]
        else:
            keys = fields[0] + begun_keys[slot]
            values = done[far]
            here = states[slot].astype(F32)
            terms = (here * here, keys * keys, here * keys, values * values)
            sums = [a + jnp.sum(t, axis=1, keepdims=True) for a, t in zip(sums, terms)]
    if not first:
        rows = memory.shape[0]
        lane = iota((rows, 8), 1)
        packed = jnp.zeros((rows, 8), F32)
        for k in range(4):
            packed = jnp.where(lane == k, sums[k], packed)
        stats_ref[...] = dot_nt(unit(8, F32), packed, lax.Precision.HIGHEST)
    for copy in later:
        copy.wait()


def finish_kernel(count, step, keep_ref, *refs):
    stats = refs[:count]
    value_hbm, hidden_ref, taps_ref, out_hbm = refs[count : count + 4]
    gates, factors, value_ref, normed, out_ref, in_sems, sems = refs[count + 4 :]
    rows, half = normed.shape
    tokens, width = out_ref.shape
    arrivals = {}
    chunk = min(step, half)
    for slot in range(2):
        for start in range(0, half, chunk):
            span = pl.ds(start, chunk)
            copy = pltpu.make_async_copy(
                value_hbm.at[slot, :, span], value_ref.at[slot, :, span], in_sems.at[len(arrivals)]
            )
            copy.start()
            arrivals[slot, start] = copy
    total = stats[0][...]
    for other in stats[1:]:
        total = total + other[...]
    inverse_states = lax.rsqrt(total[0:1] / D + EPSILON)
    inverse_keys = lax.rsqrt(total[1:2] / D + EPSILON)
    gate = jax.nn.sigmoid(total[2:3] * inverse_states * inverse_keys / D**0.5)
    factor = gate * lax.rsqrt(gate * gate * total[3:4] / D + EPSILON)
    factor = jnp.where((iota(factor.shape, 1) < RIM) & (keep_ref[0] == 0), 0.0, factor)
    line = iota(total.shape, 0)
    both = jnp.where(line == 0, gate, jnp.where(line == 1, factor, 0.0))
    columns = dot_nt(unit(rows, F32), both, lax.Precision.HIGHEST)
    gates[...] = jnp.broadcast_to(columns[RIM:, 0:1], gates.shape)
    factors[...] = jnp.broadcast_to(columns[:, 1:2], factors.shape)
    copies = []
    for slot in range(2):
        for start in range(0, half, LANES):
            size = min(LANES, half - start)
            span = slice(start, start + size)
            there = slice(slot * half + start, slot * half + start + size)
            if start % chunk == 0:
                arrivals[slot, start].wait()
            values = value_ref[slot, :, span]
            normed[:, span] = values * factors[:, :size]
            conv = None
            for tap in range(KERNEL):
                lag = DILATION * tap
                term = taps_ref[tap : tap + 1, there] * normed[RIM - lag : RIM - lag + tokens, span]
                conv = term if conv is None else conv + term
            gated = values[RIM:] * gates[:, :size]
            out_ref[:, there] = (
                hidden_ref[:, there].astype(F32) + jax.nn.silu(conv) + gated
            ).astype(BF16)
            if there.stop % step == 0:
                ready = pl.ds(there.stop - step, step)
                copy = pltpu.make_async_copy(
                    out_ref.at[:, ready], out_hbm.at[:, ready], sems.at[len(copies)]
                )
                copy.start()
                copies.append(copy)
    for copy in copies:
        copy.wait()


def whole(array):
    return pl.BlockSpec(array.shape, lambda *_: (0,) * array.ndim)


def in_hbm(array):
    return pltpu.with_memory_space_constraint(array, pltpu.HBM)


def after(array, *others):
    return lax.optimization_barrier((array, *others))[0]


def limit(mib):
    return pltpu.CompilerParams(vmem_limit_bytes=mib << 20)


def scattered_sum(stored, decoded, here, meanwhile, settled):
    mems = lax.axis_size("mem")
    heads, width, rows = decoded.shape
    tokens = stored.shape[1]
    asked = lax.all_gather(stored, "mem", axis=0)
    partial = pl.pallas_call(
        pick_kernel,
        grid=(mems,),
        in_specs=[
            pl.BlockSpec(memory_space=pltpu.SMEM),
            pl.BlockSpec((None, heads, tokens), lambda m: (m, 0, 0)),
            whole(decoded),
        ],
        out_specs=pl.BlockSpec((None, heads * width, tokens), lambda m: (m, 0, 0)),
        out_shape=jax.ShapeDtypeStruct((mems, heads * width, tokens), BF16),
        compiler_params=limit(16),
        name="pick_all",
    )((here * rows).astype(I32).reshape(1), asked, decoded)
    total = lax.psum_scatter(partial, "mem", scatter_dimension=0, tiled=False)
    return total, meanwhile(partial), settled


def line_sum(stored, decoded, here, meanwhile, settled):
    heads, width, rows = decoded.shape
    tokens = stored.shape[1]
    base = (here * rows).astype(I32).reshape(1)
    block = jax.ShapeDtypeStruct((heads * width, tokens), BF16)

    def ask(ids, x):
        return lax.ppermute(ids, "mem", [(i, i ^ x) for i in range(4)])

    def crossing(x, pairs):
        return lax.ppermute(x, ("mem", "rep"), [(2 * a + b, 2 * c + d) for a, b, c, d in pairs])

    def pick(ids):
        return pl.pallas_call(
            pick_kernel,
            in_specs=[pl.BlockSpec(memory_space=pltpu.SMEM)]
            + [pl.BlockSpec(memory_space=pltpu.VMEM)] * 2,
            out_shape=block,
            compiler_params=limit(8),
            name="pick_rows",
        )(base, ids, decoded)

    def send(x, *pairs):
        return lax.ppermute(x, "mem", pairs)

    first = ask(stored, 3)
    second = crossing(
        stored,
        [(m, r, m ^ 2, r ^ int(m in (1, 2))) for m in range(4) for r in range(2)],
    )
    first, second = lax.optimization_barrier((first, second))
    rows_3 = pick(first)
    inward = send(rows_3, (0, 1), (3, 2))
    across = send(rows_3, (1, 2), (2, 1))
    rows_2 = pick(after(second, rows_3))
    stored, settled = lax.optimization_barrier((after(stored, rows_2), settled))
    past = crossing(rows_2, [(m, r, m ^ 2, r ^ 1) for m in (0, 3) for r in range(2)])
    rows_1 = pick(ask(stored, 1))
    own = pick(stored)
    beside = send(rows_1, (0, 1), (1, 0), (2, 3), (3, 2))
    onward = after(rows_2, rows_1, own, across) + inward
    other = meanwhile(onward)
    onward = send(onward, (1, 3), (2, 0))
    own, other = lax.optimization_barrier((own + past + beside, other))
    memory = pl.pallas_call(
        merge_kernel,
        in_specs=[pl.BlockSpec(memory_space=pltpu.VMEM)] * 3,
        out_shape=block,
        compiler_params=limit(4),
        name="merge",
    )(own, across, onward)
    return memory, other, settled


def shards(
    hidden, row_ids, row_place, table_codes, table_scales, key_weight, value_weight, conv_weight
):
    mems = lax.axis_size("mem")
    tps = lax.axis_size("tp")
    reps = lax.axis_size("rep")
    blocks = mems * reps
    tokens, heads = row_ids.shape
    rows, width = table_codes.shape[1:]
    depth = heads * width
    half = key_weight.shape[1]
    seq_length = tokens * blocks // SEQS
    assert reps == 2 and seq_length % tokens == 0 and row_place.shape[0] % LANES == 0
    block = lax.axis_index(("mem", "rep"))
    smem = pl.BlockSpec(memory_space=pltpu.SMEM)

    anywhere = pl.BlockSpec(memory_space=pl.ANY)
    resident = pl.BlockSpec(memory_space=pltpu.VMEM)
    places = row_place.reshape(-1, LANES)
    stored = pl.pallas_call(
        place_kernel,
        in_specs=[anywhere] * 2,
        out_shape=jax.ShapeDtypeStruct((heads, tokens), I32),
        scratch_shapes=[
            pltpu.VMEM((heads, tokens), I32),
            pltpu.VMEM(places.shape, I32),
            pltpu.SemaphoreType.DMA((2,)),
        ],
        compiler_params=limit(4),
        name="place_rows",
    )(in_hbm(row_ids.T), in_hbm(places))
    codes = table_codes.transpose(0, 2, 1)
    scales = table_scales.transpose(2, 0, 1)
    decoded = pl.pallas_call(
        decode_kernel,
        in_specs=[anywhere] * 2,
        out_shape=jax.ShapeDtypeStruct(codes.shape, BF16),
        scratch_shapes=[
            pltpu.VMEM(codes.shape, BF16),
            pltpu.VMEM(scales.shape, BF16),
            pltpu.SemaphoreType.DMA((heads + 1,)),
        ],
        compiler_params=limit(12),
        name="decode_tables",
    )(in_hbm(after(codes, stored)), in_hbm(scales))
    here = lax.axis_index("mem")
    other_key = lax.ppermute(key_weight, "rep", [(0, 1), (1, 0)])
    other_value = lax.ppermute(value_weight, "rep", [(0, 1), (1, 0)])
    needed = [(i, i + 1) for i in range(blocks - 1) if (i + 1) * tokens % seq_length]

    def meanwhile(token):
        tail = after(hidden[tokens - RIM :], token)
        return lax.ppermute(tail, ("mem", "rep"), needed)

    summed = line_sum if mems == 4 else scattered_sum
    memory, hidden_halo, others = summed(
        stored, decoded, here, meanwhile, (other_key, other_value)
    )
    weights = [in_hbm(w) for w in (key_weight, value_weight, *others)]

    where = jnp.stack([lax.axis_index("rep"), lax.axis_index("tp")]).astype(I32)
    extended = tokens + RIM
    bodies = [memory] + [
        lax.ppermute(memory, "tp", [(i, (i + s) % tps) for i in range(tps)])
        for s in range(1, tps)
    ]

    def next_rim(rim, s):
        pairs = [
            (
                (a // reps * tps + i) * reps + a % reps,
                (b // reps * tps + (i + s) % tps) * reps + b % reps,
            )
            for a, b in needed
            for i in range(tps)
        ]
        return lax.ppermute(rim, ("mem", "tp", "rep"), pairs)

    rim = memory[:, tokens - LANES :]
    rims = [next_rim(rim, s) for s in range(tps)]
    others = tps - 1
    field = jax.ShapeDtypeStruct((2, extended, half), F32)
    *begun, rest = pl.pallas_call(
        functools.partial(project_kernel, (0,), tps),
        in_specs=[smem] + [resident] * 2 + [anywhere] * 4,
        out_specs=(resident,) * 3,
        out_shape=(field, field, pltpu.VMEM((2, 2, others * depth, half), BF16)),
        scratch_shapes=[
            pltpu.VMEM((2, 2, depth, half), BF16),
            pltpu.SemaphoreType.DMA((4,)),
            pltpu.SemaphoreType.DMA((4 * others,)),
        ],
        compiler_params=limit(12),
        name="project_own",
    )(where, rims[0], memory, *weights)
    values, stats = pl.pallas_call(
        functools.partial(project_kernel, tuple(range(1, tps)), tps),
        in_specs=[smem] + [resident] * (2 * others + 5),
        out_specs=(pl.BlockSpec(memory_space=pltpu.HBM), resident),
        out_shape=(pltpu.HBM(field.shape, F32), jax.ShapeDtypeStruct((8, extended), F32)),
        scratch_shapes=[
            pltpu.VMEM((2, extended, half), BF16),
            pltpu.VMEM((2, extended, half), F32),
            pltpu.SemaphoreType.DMA((2,)),
        ],
        compiler_params=limit(14),
        name="project_others",
    )(
        where,
        *rims[1:],
        *bodies[1:],
        rest,
        *begun,
        hidden_halo,
        hidden,
    )

    all_stats = [stats] + [
        lax.ppermute(stats, "tp", [(i, (i + s) % tps) for i in range(tps)]) for s in range(1, tps)
    ]
    keep = (block * tokens % seq_length != 0).astype(I32).reshape(1)
    step = 2 * half
    if half % LANES == 0:
        step = next(c for c in (384, 256, 128) if half % c == 0)
    return pl.pallas_call(
        functools.partial(finish_kernel, tps, step),
        in_specs=[smem] + [resident] * tps + [anywhere] + [resident] * 2,
        out_specs=anywhere,
        out_shape=jax.ShapeDtypeStruct((tokens, 2 * half), BF16),
        scratch_shapes=[
            pltpu.VMEM((tokens, LANES), F32),
            pltpu.VMEM((extended, LANES), F32),
            pltpu.VMEM((2, extended, half), F32),
            pltpu.VMEM((extended, half), F32),
            pltpu.VMEM((tokens, 2 * half), BF16),
            pltpu.SemaphoreType.DMA((2 * half // min(step, half),)),
            pltpu.SemaphoreType.DMA((2 * half // step,)),
        ],
        compiler_params=limit(12),
        name="finish",
    )(keep, *all_stats, in_hbm(values), hidden, conv_weight)


def solution(mesh):
    in_specs = (
        P(("parts", "mem", "rep"), "tp"),
        P(("parts", "mem", "rep"), "tp"),
        P("parts"),
        P(("parts", "tp"), "mem", None),
        P(("parts", "tp"), "mem", None),
        P(None, ("tp", "rep")),
        P(None, ("tp", "rep")),
        P(None, "tp"),
    )
    out_specs = P(("parts", "mem", "rep"), "tp")
    return jax.shard_map(shards, mesh=mesh, in_specs=in_specs, out_specs=out_specs, check_vma=False)
```

```python
import functools

import jax
import jax.numpy as jnp
from jax import lax
from jax.experimental import pallas as pl
from jax.experimental.pallas import tpu as pltpu
from jax.sharding import PartitionSpec as P

D = 4608
KERNEL = 4
DILATION = 3
SEQS = 4
EPSILON = 1e-06
RIM = 16
LANES = 128

F32 = jnp.float32
BF16 = jnp.bfloat16
I32 = jnp.int32


def iota(shape, axis):
    return lax.broadcasted_iota(I32, shape, axis)


def dot(a, b):
    return jnp.dot(a, b, preferred_element_type=F32)


def dot_nt(a, b, precision=None):
    return lax.dot_general(
        a, b, (((1,), (1,)), ((), ())), precision=precision, preferred_element_type=F32
    )


def unit(n, dtype):
    return (iota((n, n), 0) == iota((n, n), 1)).astype(F32).astype(dtype)


def to_bf16(x):
    return x.astype(F32).astype(BF16)


def place_kernel(ids_hbm, place_hbm, out_ref, ids_ref, place_ref, sems):
    copies = [
        pltpu.make_async_copy(place_hbm, place_ref, sems.at[0]),
        pltpu.make_async_copy(ids_hbm, ids_ref, sems.at[1]),
    ]
    for copy in copies:
        copy.start()
    copies[0].wait()
    place = place_ref[...]
    rows = place.shape[0]
    heads, tokens = ids_ref.shape
    eye = unit(LANES, BF16)
    table = jnp.concatenate(
        [dot_nt(eye, to_bf16(place >> 8)), dot_nt(eye, to_bf16(place & 255))], axis=0
    ).astype(BF16)
    copies[1].wait()
    for head in range(heads):
        row = ids_ref[head : head + 1, :]
        hot = to_bf16(iota((rows, tokens), 0) == (row >> 7))
        both = dot(table, hot)
        value = both[:LANES] * 256.0 + both[LANES:]
        chosen = jnp.where(iota(value.shape, 0) == (row & 127), value, 0.0)
        out_ref[head : head + 1, :] = jnp.sum(chosen, axis=0, keepdims=True).astype(I32)


def decode_kernel(codes_hbm, scales_hbm, out_ref, codes_ref, scales_ref, sems):
    heads, width, rows = codes_ref.shape
    blocks = scales_ref.shape[0]
    scales_copy = pltpu.make_async_copy(scales_hbm, scales_ref, sems.at[heads])
    scales_copy.start()
    copies = []
    for head in range(heads):
        copies.append(
            pltpu.make_async_copy(codes_hbm.at[head], codes_ref.at[head], sems.at[head])
        )
        copies[-1].start()
    entry = iota((width, 2 * width), 0)
    column = iota((width, 2 * width), 1)
    column = jnp.where(column < width, column, column - width)
    parity = entry & column & 15
    parity = parity ^ (parity >> 2)
    parity = (parity ^ (parity >> 1)) & 1
    same = (entry >> 4) == (column >> 4)
    rotation = jnp.where(same, 0.25 - 0.5 * parity.astype(F32), 0.0).astype(BF16)
    scales_copy.wait()
    for head in range(heads):
        copies[head].wait()
        factors = jnp.concatenate(
            [
                jnp.broadcast_to(scales_ref[b, head : head + 1, :].astype(F32), (16, rows))
                for b in range(blocks)
            ],
            axis=0,
        )
        scaled = codes_ref[head].astype(F32) * factors
        upper = scaled.astype(BF16)
        lower = (scaled - upper.astype(F32)).astype(BF16)
        out_ref[head] = dot(rotation, jnp.concatenate([upper, lower], axis=0)).astype(BF16)


def picked(local, table_ref, head):
    rows = table_ref.shape[2]
    hot = to_bf16(iota((rows, local.shape[1]), 0) == local[head : head + 1, :])
    return dot(table_ref[head], hot).astype(BF16)


def pick_kernel(base_ref, ids_ref, table_ref, out_ref):
    heads, width, _ = table_ref.shape
    local = ids_ref[...] - base_ref[0]
    for head in range(heads):
        out_ref[head * width : (head + 1) * width, :] = picked(local, table_ref, head)


def merge_kernel(*refs):
    total = refs[0][...].astype(F32)
    for other in refs[1:-1]:
        total = total + other[...].astype(F32)
    refs[-1][...] = total.astype(BF16)


def project_kernel(shifts, count, where_ref, *refs):
    pieces = len(shifts)
    first = 0 in shifts
    rims = refs[:pieces]
    bodies = refs[pieces : 2 * pieces]
    refs = refs[2 * pieces :]
    depth, tokens = bodies[0].shape
    rep = where_ref[0]
    tp = where_ref[1]
    if first:
        weights = refs[:4]
        key_ref, value_ref, rest, held, sems, rest_sems = refs[4:]
        half = held.shape[-1]

        def bring(target, far, which, n, s, sem):
            owner = lax.rem(tp + count - s, count)
            rows = pl.ds(pl.multiple_of(owner * depth, depth), depth)
            copy = pltpu.make_async_copy(
                weights[2 * far + which].at[rows, :],
                target.at[far, which, pl.ds(n * depth, depth), :],
                sem,
            )
            copy.start()
            return copy

        copies = [
            bring(held, far, which, 0, 0, sems.at[2 * far + which])
            for far in range(2)
            for which in (1, 0)
        ]
        later = [
            bring(rest, far, which, n, n + 1, rest_sems.at[(2 * far + which) * (count - 1) + n])
            for far in range(2)
            for which in (1, 0)
            for n in range(count - 1)
        ]
    else:
        later = []
        rest, begun_keys, begun_values, hidden_halo, hidden = refs[:5]
        value_hbm, stats_ref, states, done, done_sems = refs[5:]
        held = rest
        half = held.shape[-1]
        for slot in range(2):
            states[slot, :RIM] = hidden_halo[:, slot * half : (slot + 1) * half]
            states[slot, RIM:] = hidden[:, slot * half : (slot + 1) * half]
    body = jnp.concatenate([b[...].astype(F32) for b in bodies], axis=0).T.astype(BF16)
    rim = jnp.concatenate([r[...].astype(F32) for r in rims], axis=0).T.astype(BF16)
    memory = jnp.concatenate([rim[LANES - RIM :], body], axis=0)
    sums = [0.0] * 4
    for far in range(2):
        slot = rep if far == 0 else 1 - rep
        fields = [None, None]
        for which in (1, 0):
            if first:
                copies[2 * far + 1 - which].wait()
            fields[which] = dot(memory, held[far, which])
            if not first and which == 1:
                done[far] = fields[1] + begun_values[slot]
                copy = pltpu.make_async_copy(done.at[far], value_hbm.at[slot], done_sems.at[far])
                copy.start()
                later.append(copy)
        if first:
            value_ref[slot] = fields[1]
            key_ref[slot] = fields[0]
        else:
            keys = fields[0] + begun_keys[slot]
            values = done[far]
            here = states[slot].astype(F32)
            terms = (here * here, keys * keys, here * keys, values * values)
            sums = [a + jnp.sum(t, axis=1, keepdims=True) for a, t in zip(sums, terms)]
    if not first:
        rows = memory.shape[0]
        lane = iota((rows, 8), 1)
        packed = jnp.zeros((rows, 8), F32)
        for k in range(4):
            packed = jnp.where(lane == k, sums[k], packed)
        stats_ref[...] = dot_nt(unit(8, F32), packed, lax.Precision.HIGHEST)
    for copy in later:
        copy.wait()


def finish_kernel(count, step, keep_ref, *refs):
    stats = refs[:count]
    value_hbm, hidden_ref, taps_ref, out_hbm = refs[count : count + 4]
    gates, factors, value_ref, normed, out_ref, in_sems, sems = refs[count + 4 :]
    rows, half = normed.shape
    tokens, width = out_ref.shape
    arrivals = {}
    chunk = min(step, half)
    for slot in range(2):
        for start in range(0, half, chunk):
            span = pl.ds(start, chunk)
            copy = pltpu.make_async_copy(
                value_hbm.at[slot, :, span], value_ref.at[slot, :, span], in_sems.at[len(arrivals)]
            )
            copy.start()
            arrivals[slot, start] = copy
    total = stats[0][...]
    for other in stats[1:]:
        total = total + other[...]
    inverse_states = lax.rsqrt(total[0:1] / D + EPSILON)
    inverse_keys = lax.rsqrt(total[1:2] / D + EPSILON)
    gate = jax.nn.sigmoid(total[2:3] * inverse_states * inverse_keys / D**0.5)
    factor = gate * lax.rsqrt(gate * gate * total[3:4] / D + EPSILON)
    factor = jnp.where((iota(factor.shape, 1) < RIM) & (keep_ref[0] == 0), 0.0, factor)
    line = iota(total.shape, 0)
    both = jnp.where(line == 0, gate, jnp.where(line == 1, factor, 0.0))
    columns = dot_nt(unit(rows, F32), both, lax.Precision.HIGHEST)
    gates[...] = jnp.broadcast_to(columns[RIM:, 0:1], gates.shape)
    factors[...] = jnp.broadcast_to(columns[:, 1:2], factors.shape)
    copies = []
    for slot in range(2):
        for start in range(0, half, LANES):
            size = min(LANES, half - start)
            span = slice(start, start + size)
            there = slice(slot * half + start, slot * half + start + size)
            if start % chunk == 0:
                arrivals[slot, start].wait()
            values = value_ref[slot, :, span]
            normed[:, span] = values * factors[:, :size]
            conv = None
            for tap in range(KERNEL):
                lag = DILATION * tap
                term = taps_ref[tap : tap + 1, there] * normed[RIM - lag : RIM - lag + tokens, span]
                conv = term if conv is None else conv + term
            gated = values[RIM:] * gates[:, :size]
            out_ref[:, there] = (
                hidden_ref[:, there].astype(F32) + jax.nn.silu(conv) + gated
            ).astype(BF16)
            if there.stop % step == 0:
                ready = pl.ds(there.stop - step, step)
                copy = pltpu.make_async_copy(
                    out_ref.at[:, ready], out_hbm.at[:, ready], sems.at[len(copies)]
                )
                copy.start()
                copies.append(copy)
    for copy in copies:
        copy.wait()


def whole(array):
    return pl.BlockSpec(array.shape, lambda *_: (0,) * array.ndim)


def in_hbm(array):
    return pltpu.with_memory_space_constraint(array, pltpu.HBM)


def after(array, *others):
    return lax.optimization_barrier((array, *others))[0]


def limit(mib):
    return pltpu.CompilerParams(vmem_limit_bytes=mib << 20)


def scattered_sum(stored, decoded, here, meanwhile, settled):
    mems = lax.axis_size("mem")
    heads, width, rows = decoded.shape
    tokens = stored.shape[1]
    asked = lax.all_gather(stored, "mem", axis=0)
    partial = pl.pallas_call(
        pick_kernel,
        grid=(mems,),
        in_specs=[
            pl.BlockSpec(memory_space=pltpu.SMEM),
            pl.BlockSpec((None, heads, tokens), lambda m: (m, 0, 0)),
            whole(decoded),
        ],
        out_specs=pl.BlockSpec((None, heads * width, tokens), lambda m: (m, 0, 0)),
        out_shape=jax.ShapeDtypeStruct((mems, heads * width, tokens), BF16),
        compiler_params=limit(16),
        name="pick_all",
    )((here * rows).astype(I32).reshape(1), asked, decoded)
    total = lax.psum_scatter(partial, "mem", scatter_dimension=0, tiled=False)
    return total, meanwhile(partial), settled


def line_sum(stored, decoded, here, meanwhile, settled):
    heads, width, rows = decoded.shape
    tokens = stored.shape[1]
    base = (here * rows).astype(I32).reshape(1)
    block = jax.ShapeDtypeStruct((heads * width, tokens), BF16)

    def ask(ids, x):
        return lax.ppermute(ids, "mem", [(i, i ^ x) for i in range(4)])

    def crossing(x, pairs):
        return lax.ppermute(x, ("mem", "rep"), [(2 * a + b, 2 * c + d) for a, b, c, d in pairs])

    def pick(ids):
        return pl.pallas_call(
            pick_kernel,
            in_specs=[pl.BlockSpec(memory_space=pltpu.SMEM)]
            + [pl.BlockSpec(memory_space=pltpu.VMEM)] * 2,
            out_shape=block,
            compiler_params=limit(8),
            name="pick_rows",
        )(base, ids, decoded)

    def send(x, *pairs):
        return lax.ppermute(x, "mem", pairs)

    first = ask(stored, 3)
    second = crossing(
        stored,
        [(m, r, m ^ 2, r ^ int(m in (1, 2))) for m in range(4) for r in range(2)],
    )
    third = ask(stored, 1)
    first, second, third = lax.optimization_barrier((first, second, third))
    rows_3 = pick(first)
    inward = send(rows_3, (0, 1), (3, 2))
    across = send(rows_3, (1, 2), (2, 1))
    rows_2 = pick(after(second, rows_3))
    third, settled = lax.optimization_barrier((after(third, rows_2), settled))
    past = crossing(rows_2, [(m, r, m ^ 2, r ^ 1) for m in (0, 3) for r in range(2)])
    rows_1 = pick(third)
    own = pick(after(stored, rows_1))
    beside = send(rows_1, (0, 1), (1, 0), (2, 3), (3, 2))
    onward = after(rows_2, rows_1, own) + inward
    onward = send(onward, (1, 3), (2, 0))
    other = meanwhile(across)
    own, other = lax.optimization_barrier((own + past + beside, other))
    memory = pl.pallas_call(
        merge_kernel,
        in_specs=[pl.BlockSpec(memory_space=pltpu.VMEM)] * 3,
        out_shape=block,
        compiler_params=limit(4),
        name="merge",
    )(own, across, onward)
    return memory, other, settled


def shards(
    hidden, row_ids, row_place, table_codes, table_scales, key_weight, value_weight, conv_weight
):
    mems = lax.axis_size("mem")
    tps = lax.axis_size("tp")
    reps = lax.axis_size("rep")
    blocks = mems * reps
    tokens, heads = row_ids.shape
    rows, width = table_codes.shape[1:]
    depth = heads * width
    half = key_weight.shape[1]
    seq_length = tokens * blocks // SEQS
    assert reps == 2 and seq_length % tokens == 0 and row_place.shape[0] % LANES == 0
    block = lax.axis_index(("mem", "rep"))
    smem = pl.BlockSpec(memory_space=pltpu.SMEM)

    anywhere = pl.BlockSpec(memory_space=pl.ANY)
    resident = pl.BlockSpec(memory_space=pltpu.VMEM)
    places = row_place.reshape(-1, LANES)
    stored = pl.pallas_call(
        place_kernel,
        in_specs=[anywhere] * 2,
        out_shape=jax.ShapeDtypeStruct((heads, tokens), I32),
        scratch_shapes=[
            pltpu.VMEM((heads, tokens), I32),
            pltpu.VMEM(places.shape, I32),
            pltpu.SemaphoreType.DMA((2,)),
        ],
        compiler_params=limit(4),
        name="place_rows",
    )(in_hbm(row_ids.T), in_hbm(places))
    codes = table_codes.transpose(0, 2, 1)
    scales = table_scales.transpose(2, 0, 1)
    decoded = pl.pallas_call(
        decode_kernel,
        in_specs=[anywhere] * 2,
        out_shape=jax.ShapeDtypeStruct(codes.shape, BF16),
        scratch_shapes=[
            pltpu.VMEM(codes.shape, BF16),
            pltpu.VMEM(scales.shape, BF16),
            pltpu.SemaphoreType.DMA((heads + 1,)),
        ],
        compiler_params=limit(12),
        name="decode_tables",
    )(in_hbm(after(codes, stored)), in_hbm(scales))
    here = lax.axis_index("mem")
    other_key = lax.ppermute(key_weight, "rep", [(0, 1), (1, 0)])
    other_value = lax.ppermute(value_weight, "rep", [(0, 1), (1, 0)])
    needed = [(i, i + 1) for i in range(blocks - 1) if (i + 1) * tokens % seq_length]

    def meanwhile(token):
        tail = after(hidden[tokens - RIM :], token)
        return lax.ppermute(tail, ("mem", "rep"), needed)

    summed = line_sum if mems == 4 else scattered_sum
    memory, hidden_halo, others = summed(
        stored, decoded, here, meanwhile, (other_key, other_value)
    )
    weights = [in_hbm(w) for w in (key_weight, value_weight, *others)]

    where = jnp.stack([lax.axis_index("rep"), lax.axis_index("tp")]).astype(I32)
    extended = tokens + RIM
    bodies = [memory] + [
        lax.ppermute(memory, "tp", [(i, (i + s) % tps) for i in range(tps)])
        for s in range(1, tps)
    ]

    def next_rim(rim, s):
        pairs = [
            (
                (a // reps * tps + i) * reps + a % reps,
                (b // reps * tps + (i + s) % tps) * reps + b % reps,
            )
            for a, b in needed
            for i in range(tps)
        ]
        return lax.ppermute(rim, ("mem", "tp", "rep"), pairs)

    rim = memory[:, tokens - LANES :]
    rims = [next_rim(rim, s) for s in range(tps)]
    others = tps - 1
    field = jax.ShapeDtypeStruct((2, extended, half), F32)
    *begun, rest = pl.pallas_call(
        functools.partial(project_kernel, (0,), tps),
        in_specs=[smem] + [resident] * 2 + [anywhere] * 4,
        out_specs=(resident,) * 3,
        out_shape=(field, field, pltpu.VMEM((2, 2, others * depth, half), BF16)),
        scratch_shapes=[
            pltpu.VMEM((2, 2, depth, half), BF16),
            pltpu.SemaphoreType.DMA((4,)),
            pltpu.SemaphoreType.DMA((4 * others,)),
        ],
        compiler_params=limit(12),
        name="project_own",
    )(where, rims[0], memory, *weights)
    values, stats = pl.pallas_call(
        functools.partial(project_kernel, tuple(range(1, tps)), tps),
        in_specs=[smem] + [resident] * (2 * others + 5),
        out_specs=(pl.BlockSpec(memory_space=pltpu.HBM), resident),
        out_shape=(pltpu.HBM(field.shape, F32), jax.ShapeDtypeStruct((8, extended), F32)),
        scratch_shapes=[
            pltpu.VMEM((2, extended, half), BF16),
            pltpu.VMEM((2, extended, half), F32),
            pltpu.SemaphoreType.DMA((2,)),
        ],
        compiler_params=limit(14),
        name="project_others",
    )(
        where,
        *rims[1:],
        *bodies[1:],
        rest,
        *begun,
        hidden_halo,
        hidden,
    )

    all_stats = [stats] + [
        lax.ppermute(stats, "tp", [(i, (i + s) % tps) for i in range(tps)]) for s in range(1, tps)
    ]
    keep = (block * tokens % seq_length != 0).astype(I32).reshape(1)
    step = 2 * half
    if half % LANES == 0:
        step = next(c for c in (384, 256, 128) if half % c == 0)
    return pl.pallas_call(
        functools.partial(finish_kernel, tps, step),
        in_specs=[smem] + [resident] * tps + [anywhere] + [resident] * 2,
        out_specs=anywhere,
        out_shape=jax.ShapeDtypeStruct((tokens, 2 * half), BF16),
        scratch_shapes=[
            pltpu.VMEM((tokens, LANES), F32),
            pltpu.VMEM((extended, LANES), F32),
            pltpu.VMEM((2, extended, half), F32),
            pltpu.VMEM((extended, half), F32),
            pltpu.VMEM((tokens, 2 * half), BF16),
            pltpu.SemaphoreType.DMA((2 * half // min(step, half),)),
            pltpu.SemaphoreType.DMA((2 * half // step,)),
        ],
        compiler_params=limit(12),
        name="finish",
    )(keep, *all_stats, in_hbm(values), hidden, conv_weight)


def solution(mesh):
    in_specs = (
        P(("parts", "mem", "rep"), "tp"),
        P(("parts", "mem", "rep"), "tp"),
        P("parts"),
        P(("parts", "tp"), "mem", None),
        P(("parts", "tp"), "mem", None),
        P(None, ("tp", "rep")),
        P(None, ("tp", "rep")),
        P(None, "tp"),
    )
    out_specs = P(("parts", "mem", "rep"), "tp")
    return jax.shard_map(shards, mesh=mesh, in_specs=in_specs, out_specs=out_specs, check_vma=False)
```

```python
import functools

import jax
import jax.numpy as jnp
from jax import lax
from jax.experimental import pallas as pl
from jax.experimental.pallas import tpu as pltpu
from jax.sharding import PartitionSpec as P

D = 4608
KERNEL = 4
DILATION = 3
SEQS = 4
EPSILON = 1e-06
RIM = 16
LANES = 128

F32 = jnp.float32
BF16 = jnp.bfloat16
I32 = jnp.int32


def iota(shape, axis):
    return lax.broadcasted_iota(I32, shape, axis)


def dot(a, b):
    return jnp.dot(a, b, preferred_element_type=F32)


def dot_nt(a, b, precision=None):
    return lax.dot_general(
        a, b, (((1,), (1,)), ((), ())), precision=precision, preferred_element_type=F32
    )


def unit(n, dtype):
    return (iota((n, n), 0) == iota((n, n), 1)).astype(F32).astype(dtype)


def to_bf16(x):
    return x.astype(F32).astype(BF16)


def place_kernel(ids_hbm, place_hbm, out_ref, ids_ref, place_ref, sems):
    copies = [
        pltpu.make_async_copy(place_hbm, place_ref, sems.at[0]),
        pltpu.make_async_copy(ids_hbm, ids_ref, sems.at[1]),
    ]
    for copy in copies:
        copy.start()
    copies[0].wait()
    place = place_ref[...]
    rows = place.shape[0]
    heads, tokens = ids_ref.shape
    eye = unit(LANES, BF16)
    table = jnp.concatenate(
        [dot_nt(eye, to_bf16(place >> 8)), dot_nt(eye, to_bf16(place & 255))], axis=0
    ).astype(BF16)
    copies[1].wait()
    for head in range(heads):
        row = ids_ref[head : head + 1, :]
        hot = to_bf16(iota((rows, tokens), 0) == (row >> 7))
        both = dot(table, hot)
        value = both[:LANES] * 256.0 + both[LANES:]
        chosen = jnp.where(iota(value.shape, 0) == (row & 127), value, 0.0)
        out_ref[head : head + 1, :] = jnp.sum(chosen, axis=0, keepdims=True).astype(I32)


def decode_kernel(codes_hbm, scales_hbm, out_ref, codes_ref, scales_ref, sems):
    heads, width, rows = codes_ref.shape
    blocks = scales_ref.shape[0]
    scales_copy = pltpu.make_async_copy(scales_hbm, scales_ref, sems.at[heads])
    scales_copy.start()
    copies = []
    for head in range(heads):
        copies.append(
            pltpu.make_async_copy(codes_hbm.at[head], codes_ref.at[head], sems.at[head])
        )
        copies[-1].start()
    entry = iota((width, 2 * width), 0)
    column = iota((width, 2 * width), 1)
    column = jnp.where(column < width, column, column - width)
    parity = entry & column & 15
    parity = parity ^ (parity >> 2)
    parity = (parity ^ (parity >> 1)) & 1
    same = (entry >> 4) == (column >> 4)
    rotation = jnp.where(same, 0.25 - 0.5 * parity.astype(F32), 0.0).astype(BF16)
    scales_copy.wait()
    for head in range(heads):
        copies[head].wait()
        factors = jnp.concatenate(
            [
                jnp.broadcast_to(scales_ref[b, head : head + 1, :].astype(F32), (16, rows))
                for b in range(blocks)
            ],
            axis=0,
        )
        scaled = codes_ref[head].astype(F32) * factors
        upper = scaled.astype(BF16)
        lower = (scaled - upper.astype(F32)).astype(BF16)
        out_ref[head] = dot(rotation, jnp.concatenate([upper, lower], axis=0)).astype(BF16)


def picked(local, table_ref, head):
    rows = table_ref.shape[2]
    hot = to_bf16(iota((rows, local.shape[1]), 0) == local[head : head + 1, :])
    return dot(table_ref[head], hot).astype(BF16)


def pick_kernel(base_ref, ids_ref, table_ref, out_ref):
    heads, width, _ = table_ref.shape
    local = ids_ref[...] - base_ref[0]
    for head in range(heads):
        out_ref[head * width : (head + 1) * width, :] = picked(local, table_ref, head)


def merge_kernel(*refs):
    total = refs[0][...].astype(F32)
    for other in refs[1:-1]:
        total = total + other[...].astype(F32)
    refs[-1][...] = total.astype(BF16)


def project_kernel(shifts, count, where_ref, *refs):
    pieces = len(shifts)
    first = 0 in shifts
    rims = refs[:pieces]
    bodies = refs[pieces : 2 * pieces]
    refs = refs[2 * pieces :]
    depth, tokens = bodies[0].shape
    rep = where_ref[0]
    tp = where_ref[1]
    if first:
        weights = refs[:4]
        key_ref, value_ref, rest, held, sems, rest_sems = refs[4:]
        half = held.shape[-1]

        def bring(target, far, which, n, s, sem):
            owner = lax.rem(tp + count - s, count)
            rows = pl.ds(pl.multiple_of(owner * depth, depth), depth)
            copy = pltpu.make_async_copy(
                weights[2 * far + which].at[rows, :],
                target.at[far, which, pl.ds(n * depth, depth), :],
                sem,
            )
            copy.start()
            return copy

        copies = [
            bring(held, far, which, 0, 0, sems.at[2 * far + which])
            for far in range(2)
            for which in (1, 0)
        ]
        later = [
            bring(rest, far, which, n, n + 1, rest_sems.at[(2 * far + which) * (count - 1) + n])
            for far in range(2)
            for which in (1, 0)
            for n in range(count - 1)
        ]
    else:
        later = []
        rest, begun_keys, begun_values, hidden_halo, hidden = refs[:5]
        value_hbm, stats_ref, states, done, done_sems = refs[5:]
        held = rest
        half = held.shape[-1]
        for slot in range(2):
            states[slot, :RIM] = hidden_halo[:, slot * half : (slot + 1) * half]
            states[slot, RIM:] = hidden[:, slot * half : (slot + 1) * half]
    body = jnp.concatenate([b[...].astype(F32) for b in bodies], axis=0).T.astype(BF16)
    rim = jnp.concatenate([r[...].astype(F32) for r in rims], axis=0).T.astype(BF16)
    memory = jnp.concatenate([rim[LANES - RIM :], body], axis=0)
    sums = [0.0] * 4
    for far in range(2):
        slot = rep if far == 0 else 1 - rep
        fields = [None, None]
        for which in (1, 0):
            if first:
                copies[2 * far + 1 - which].wait()
            fields[which] = dot(memory, held[far, which])
            if not first and which == 1:
                done[far] = fields[1] + begun_values[slot]
                copy = pltpu.make_async_copy(done.at[far], value_hbm.at[slot], done_sems.at[far])
                copy.start()
                later.append(copy)
        if first:
            value_ref[slot] = fields[1]
            key_ref[slot] = fields[0]
        else:
            keys = fields[0] + begun_keys[slot]
            values = done[far]
            here = states[slot].astype(F32)
            terms = (here * here, keys * keys, here * keys, values * values)
            sums = [a + jnp.sum(t, axis=1, keepdims=True) for a, t in zip(sums, terms)]
    if not first:
        rows = memory.shape[0]
        lane = iota((rows, 8), 1)
        packed = jnp.zeros((rows, 8), F32)
        for k in range(4):
            packed = jnp.where(lane == k, sums[k], packed)
        stats_ref[...] = dot_nt(unit(8, F32), packed, lax.Precision.HIGHEST)
    for copy in later:
        copy.wait()


def prepare_kernel(chunk, taps_ref, value_hbm, value_ref, tap_ref, rows_ref, sems):
    half = rows_ref.shape[-1]
    tokens = value_ref.shape[1]
    copies = []
    for slot in range(2):
        for start in range(0, half, chunk):
            span = pl.ds(start, chunk)
            copy = pltpu.make_async_copy(
                value_hbm.at[slot, :, span], rows_ref.at[slot, :, span], sems.at[len(copies)]
            )
            copy.start()
            copies.append(copy)
    for slot in range(2):
        for start in range(0, half, LANES):
            size = min(LANES, half - start)
            span = slice(start, start + size)
            there = slice(slot * half + start, slot * half + start + size)
            if start % chunk == 0:
                copies[(slot * half + start) // chunk].wait()
            value_ref[slot, :, span] = rows_ref[slot, RIM:, span]
            for tap in range(1, KERNEL):
                lag = DILATION * tap
                rows = rows_ref[slot, RIM - lag : RIM - lag + tokens, span]
                tap_ref[tap - 1, slot, :, span] = taps_ref[tap : tap + 1, there] * rows


def finish_kernel(count, step, keep_ref, *refs):
    stats = refs[:count]
    value_ref, tap_ref, hidden_ref, taps_ref, out_hbm = refs[count : count + 5]
    columns, gates, factors, out_ref, sems = refs[count + 5 :]
    half = value_ref.shape[-1]
    tokens, width = out_ref.shape
    total = stats[0][...]
    for other in stats[1:]:
        total = total + other[...]
    inverse_states = lax.rsqrt(total[0:1] / D + EPSILON)
    inverse_keys = lax.rsqrt(total[1:2] / D + EPSILON)
    gate = jax.nn.sigmoid(total[2:3] * inverse_states * inverse_keys / D**0.5)
    factor = gate * lax.rsqrt(gate * gate * total[3:4] / D + EPSILON)
    factor = jnp.where((iota(factor.shape, 1) < RIM) & (keep_ref[0] == 0), 0.0, factor)
    line = iota(total.shape, 0)
    both = jnp.where(line == 0, gate, jnp.where(line == 1, factor, 0.0))
    columns[...] = dot_nt(unit(total.shape[1], F32), both, lax.Precision.HIGHEST)
    gates[...] = jnp.broadcast_to(columns[RIM:, 0:1], gates.shape)
    for tap in range(KERNEL):
        lag = DILATION * tap
        factors[tap] = jnp.broadcast_to(
            columns[RIM - lag : RIM - lag + tokens, 1:2], factors.shape[1:]
        )
    copies = []
    for slot in range(2):
        for start in range(0, half, LANES):
            size = min(LANES, half - start)
            span = slice(start, start + size)
            there = slice(slot * half + start, slot * half + start + size)
            values = value_ref[slot, :, span]
            conv = taps_ref[0:1, there] * values * factors[0, :, :size]
            for tap in range(1, KERNEL):
                conv = conv + tap_ref[tap - 1, slot, :, span] * factors[tap, :, :size]
            gated = values * gates[:, :size]
            out_ref[:, there] = (
                hidden_ref[:, there].astype(F32) + jax.nn.silu(conv) + gated
            ).astype(BF16)
            if there.stop % step == 0:
                ready = pl.ds(there.stop - step, step)
                copy = pltpu.make_async_copy(
                    out_ref.at[:, ready], out_hbm.at[:, ready], sems.at[len(copies)]
                )
                copy.start()
                copies.append(copy)
    for copy in copies:
        copy.wait()


def whole(array):
    return pl.BlockSpec(array.shape, lambda *_: (0,) * array.ndim)


def in_hbm(array):
    return pltpu.with_memory_space_constraint(array, pltpu.HBM)


def after(array, *others):
    return lax.optimization_barrier((array, *others))[0]


def limit(mib):
    return pltpu.CompilerParams(vmem_limit_bytes=mib << 20)


def scattered_sum(stored, decoded, here, meanwhile, settled):
    mems = lax.axis_size("mem")
    heads, width, rows = decoded.shape
    tokens = stored.shape[1]
    asked = lax.all_gather(stored, "mem", axis=0)
    partial = pl.pallas_call(
        pick_kernel,
        grid=(mems,),
        in_specs=[
            pl.BlockSpec(memory_space=pltpu.SMEM),
            pl.BlockSpec((None, heads, tokens), lambda m: (m, 0, 0)),
            whole(decoded),
        ],
        out_specs=pl.BlockSpec((None, heads * width, tokens), lambda m: (m, 0, 0)),
        out_shape=jax.ShapeDtypeStruct((mems, heads * width, tokens), BF16),
        compiler_params=limit(16),
        name="pick_all",
    )((here * rows).astype(I32).reshape(1), asked, decoded)
    total = lax.psum_scatter(partial, "mem", scatter_dimension=0, tiled=False)
    return total, meanwhile(partial), settled


def line_sum(stored, decoded, here, meanwhile, settled):
    heads, width, rows = decoded.shape
    tokens = stored.shape[1]
    base = (here * rows).astype(I32).reshape(1)
    block = jax.ShapeDtypeStruct((heads * width, tokens), BF16)

    def ask(ids, x):
        return lax.ppermute(ids, "mem", [(i, i ^ x) for i in range(4)])

    def crossing(x, pairs):
        return lax.ppermute(x, ("mem", "rep"), [(2 * a + b, 2 * c + d) for a, b, c, d in pairs])

    def pick(ids):
        return pl.pallas_call(
            pick_kernel,
            in_specs=[pl.BlockSpec(memory_space=pltpu.SMEM)]
            + [pl.BlockSpec(memory_space=pltpu.VMEM)] * 2,
            out_shape=block,
            compiler_params=limit(8),
            name="pick_rows",
        )(base, ids, decoded)

    def send(x, *pairs):
        return lax.ppermute(x, "mem", pairs)

    first = ask(stored, 3)
    second = crossing(
        stored,
        [(m, r, m ^ 2, r ^ int(m in (1, 2))) for m in range(4) for r in range(2)],
    )
    third = ask(stored, 1)
    first, second, third = lax.optimization_barrier((first, second, third))
    rows_3 = pick(first)
    inward = send(rows_3, (0, 1), (3, 2))
    across = send(rows_3, (1, 2), (2, 1))
    rows_2 = pick(after(second, rows_3))
    third, settled = lax.optimization_barrier((after(third, rows_2), settled))
    past = crossing(rows_2, [(m, r, m ^ 2, r ^ 1) for m in (0, 3) for r in range(2)])
    rows_1 = pick(third)
    own = pick(after(stored, rows_1))
    beside = send(rows_1, (0, 1), (1, 0), (2, 3), (3, 2))
    onward = after(rows_2, rows_1, own) + inward
    onward = send(onward, (1, 3), (2, 0))
    other = meanwhile(across)
    own, other = lax.optimization_barrier((own + past + beside, other))
    memory = pl.pallas_call(
        merge_kernel,
        in_specs=[pl.BlockSpec(memory_space=pltpu.VMEM)] * 3,
        out_shape=block,
        compiler_params=limit(4),
        name="merge",
    )(own, across, onward)
    return memory, other, settled


def shards(
    hidden, row_ids, row_place, table_codes, table_scales, key_weight, value_weight, conv_weight
):
    mems = lax.axis_size("mem")
    tps = lax.axis_size("tp")
    reps = lax.axis_size("rep")
    blocks = mems * reps
    tokens, heads = row_ids.shape
    rows, width = table_codes.shape[1:]
    depth = heads * width
    half = key_weight.shape[1]
    seq_length = tokens * blocks // SEQS
    assert reps == 2 and seq_length % tokens == 0 and row_place.shape[0] % LANES == 0
    block = lax.axis_index(("mem", "rep"))
    smem = pl.BlockSpec(memory_space=pltpu.SMEM)

    anywhere = pl.BlockSpec(memory_space=pl.ANY)
    resident = pl.BlockSpec(memory_space=pltpu.VMEM)
    places = row_place.reshape(-1, LANES)
    stored = pl.pallas_call(
        place_kernel,
        in_specs=[anywhere] * 2,
        out_shape=jax.ShapeDtypeStruct((heads, tokens), I32),
        scratch_shapes=[
            pltpu.VMEM((heads, tokens), I32),
            pltpu.VMEM(places.shape, I32),
            pltpu.SemaphoreType.DMA((2,)),
        ],
        compiler_params=limit(4),
        name="place_rows",
    )(in_hbm(row_ids.T), in_hbm(places))
    codes = table_codes.transpose(0, 2, 1)
    scales = table_scales.transpose(2, 0, 1)
    decoded = pl.pallas_call(
        decode_kernel,
        in_specs=[anywhere] * 2,
        out_shape=jax.ShapeDtypeStruct(codes.shape, BF16),
        scratch_shapes=[
            pltpu.VMEM(codes.shape, BF16),
            pltpu.VMEM(scales.shape, BF16),
            pltpu.SemaphoreType.DMA((heads + 1,)),
        ],
        compiler_params=limit(12),
        name="decode_tables",
    )(in_hbm(after(codes, stored)), in_hbm(scales))
    here = lax.axis_index("mem")
    other_key = lax.ppermute(key_weight, "rep", [(0, 1), (1, 0)])
    other_value = lax.ppermute(value_weight, "rep", [(0, 1), (1, 0)])
    needed = [(i, i + 1) for i in range(blocks - 1) if (i + 1) * tokens % seq_length]

    def meanwhile(token):
        tail = after(hidden[tokens - RIM :], token)
        return lax.ppermute(tail, ("mem", "rep"), needed)

    summed = line_sum if mems == 4 else scattered_sum
    memory, hidden_halo, others = summed(
        stored, decoded, here, meanwhile, (other_key, other_value)
    )
    weights = [in_hbm(w) for w in (key_weight, value_weight, *others)]

    where = jnp.stack([lax.axis_index("rep"), lax.axis_index("tp")]).astype(I32)
    extended = tokens + RIM
    bodies = [memory] + [
        lax.ppermute(memory, "tp", [(i, (i + s) % tps) for i in range(tps)])
        for s in range(1, tps)
    ]

    def next_rim(rim, s):
        pairs = [
            (
                (a // reps * tps + i) * reps + a % reps,
                (b // reps * tps + (i + s) % tps) * reps + b % reps,
            )
            for a, b in needed
            for i in range(tps)
        ]
        return lax.ppermute(rim, ("mem", "tp", "rep"), pairs)

    rim = memory[:, tokens - LANES :]
    rims = [next_rim(rim, s) for s in range(tps)]
    others = tps - 1
    field = jax.ShapeDtypeStruct((2, extended, half), F32)
    *begun, rest = pl.pallas_call(
        functools.partial(project_kernel, (0,), tps),
        in_specs=[smem] + [resident] * 2 + [anywhere] * 4,
        out_specs=(resident,) * 3,
        out_shape=(field, field, pltpu.VMEM((2, 2, others * depth, half), BF16)),
        scratch_shapes=[
            pltpu.VMEM((2, 2, depth, half), BF16),
            pltpu.SemaphoreType.DMA((4,)),
            pltpu.SemaphoreType.DMA((4 * others,)),
        ],
        compiler_params=limit(12),
        name="project_own",
    )(where, rims[0], memory, *weights)
    values, stats = pl.pallas_call(
        functools.partial(project_kernel, tuple(range(1, tps)), tps),
        in_specs=[smem] + [resident] * (2 * others + 5),
        out_specs=(pl.BlockSpec(memory_space=pltpu.HBM), resident),
        out_shape=(pltpu.HBM(field.shape, F32), jax.ShapeDtypeStruct((8, extended), F32)),
        scratch_shapes=[
            pltpu.VMEM((2, extended, half), BF16),
            pltpu.VMEM((2, extended, half), F32),
            pltpu.SemaphoreType.DMA((2,)),
        ],
        compiler_params=limit(14),
        name="project_others",
    )(
        where,
        *rims[1:],
        *bodies[1:],
        rest,
        *begun,
        hidden_halo,
        hidden,
    )

    all_stats = [stats] + [
        lax.ppermute(stats, "tp", [(i, (i + s) % tps) for i in range(tps)]) for s in range(1, tps)
    ]
    keep = (block * tokens % seq_length != 0).astype(I32).reshape(1)
    step = 2 * half
    if half % LANES == 0:
        step = next(c for c in (384, 256, 128) if half % c == 0)
    chunk = min(step, half)
    body = (2, tokens, half)
    values, products = pl.pallas_call(
        functools.partial(prepare_kernel, chunk),
        in_specs=[resident, anywhere],
        out_specs=(resident,) * 2,
        out_shape=(
            jax.ShapeDtypeStruct(body, F32),
            jax.ShapeDtypeStruct((KERNEL - 1, *body), F32),
        ),
        scratch_shapes=[
            pltpu.VMEM((2, extended, half), F32),
            pltpu.SemaphoreType.DMA((2 * half // chunk,)),
        ],
        compiler_params=limit(6),
        name="prepare",
    )(conv_weight, in_hbm(values))
    return pl.pallas_call(
        functools.partial(finish_kernel, tps, step),
        in_specs=[smem] + [resident] * (tps + 4),
        out_specs=anywhere,
        out_shape=jax.ShapeDtypeStruct((tokens, 2 * half), BF16),
        scratch_shapes=[
            pltpu.VMEM((extended, 8), F32),
            pltpu.VMEM((tokens, LANES), F32),
            pltpu.VMEM((KERNEL, tokens, LANES), F32),
            pltpu.VMEM((tokens, 2 * half), BF16),
            pltpu.SemaphoreType.DMA((2 * half // step,)),
        ],
        compiler_params=limit(6),
        name="finish",
    )(keep, *all_stats, values, products, hidden, conv_weight)


def solution(mesh):
    in_specs = (
        P(("parts", "mem", "rep"), "tp"),
        P(("parts", "mem", "rep"), "tp"),
        P("parts"),
        P(("parts", "tp"), "mem", None),
        P(("parts", "tp"), "mem", None),
        P(None, ("tp", "rep")),
        P(None, ("tp", "rep")),
        P(None, "tp"),
    )
    out_specs = P(("parts", "mem", "rep"), "tp")
    return jax.shard_map(shards, mesh=mesh, in_specs=in_specs, out_specs=out_specs, check_vma=False)
```

```python
import functools

import jax
import jax.numpy as jnp
from jax import lax
from jax.experimental import pallas as pl
from jax.experimental.pallas import tpu as pltpu
from jax.sharding import PartitionSpec as P

D = 4608
KERNEL = 4
DILATION = 3
SEQS = 4
EPSILON = 1e-06
RIM = 16
LANES = 128

F32 = jnp.float32
BF16 = jnp.bfloat16
I32 = jnp.int32


def iota(shape, axis):
    return lax.broadcasted_iota(I32, shape, axis)


def dot(a, b):
    return jnp.dot(a, b, preferred_element_type=F32)


def dot_nt(a, b, precision=None):
    return lax.dot_general(
        a, b, (((1,), (1,)), ((), ())), precision=precision, preferred_element_type=F32
    )


def unit(n, dtype):
    return (iota((n, n), 0) == iota((n, n), 1)).astype(F32).astype(dtype)


def to_bf16(x):
    return x.astype(F32).astype(BF16)


def place_kernel(ids_hbm, place_hbm, out_ref, ids_ref, place_ref, sems):
    copies = [
        pltpu.make_async_copy(place_hbm, place_ref, sems.at[0]),
        pltpu.make_async_copy(ids_hbm, ids_ref, sems.at[1]),
    ]
    for copy in copies:
        copy.start()
    copies[0].wait()
    place = place_ref[...]
    rows = place.shape[0]
    heads, tokens = ids_ref.shape
    eye = unit(LANES, BF16)
    table = jnp.concatenate(
        [dot_nt(eye, to_bf16(place >> 8)), dot_nt(eye, to_bf16(place & 255))], axis=0
    ).astype(BF16)
    copies[1].wait()
    for head in range(heads):
        row = ids_ref[head : head + 1, :]
        hot = to_bf16(iota((rows, tokens), 0) == (row >> 7))
        both = dot(table, hot)
        value = both[:LANES] * 256.0 + both[LANES:]
        chosen = jnp.where(iota(value.shape, 0) == (row & 127), value, 0.0)
        out_ref[head : head + 1, :] = jnp.sum(chosen, axis=0, keepdims=True).astype(I32)


def decode_kernel(codes_hbm, scales_hbm, out_ref, codes_ref, scales_ref, sems):
    heads, width, rows = codes_ref.shape
    blocks = scales_ref.shape[0]
    scales_copy = pltpu.make_async_copy(scales_hbm, scales_ref, sems.at[heads])
    scales_copy.start()
    copies = []
    for head in range(heads):
        copies.append(
            pltpu.make_async_copy(codes_hbm.at[head], codes_ref.at[head], sems.at[head])
        )
        copies[-1].start()
    entry = iota((width, 2 * width), 0)
    column = iota((width, 2 * width), 1)
    column = jnp.where(column < width, column, column - width)
    parity = entry & column & 15
    parity = parity ^ (parity >> 2)
    parity = (parity ^ (parity >> 1)) & 1
    same = (entry >> 4) == (column >> 4)
    rotation = jnp.where(same, 0.25 - 0.5 * parity.astype(F32), 0.0).astype(BF16)
    scales_copy.wait()
    for head in range(heads):
        copies[head].wait()
        factors = jnp.concatenate(
            [
                jnp.broadcast_to(scales_ref[b, head : head + 1, :].astype(F32), (16, rows))
                for b in range(blocks)
            ],
            axis=0,
        )
        scaled = codes_ref[head].astype(F32) * factors
        upper = scaled.astype(BF16)
        lower = (scaled - upper.astype(F32)).astype(BF16)
        out_ref[head] = dot(rotation, jnp.concatenate([upper, lower], axis=0)).astype(BF16)


def picked(local, table_ref, head):
    rows = table_ref.shape[2]
    hot = to_bf16(iota((rows, local.shape[1]), 0) == local[head : head + 1, :])
    return dot(table_ref[head], hot).astype(BF16)


def pick_kernel(base_ref, ids_ref, table_ref, out_ref):
    heads, width, _ = table_ref.shape
    local = ids_ref[...] - base_ref[0]
    for head in range(heads):
        out_ref[head * width : (head + 1) * width, :] = picked(local, table_ref, head)


def merge_kernel(*refs):
    total = refs[0][...].astype(F32)
    for other in refs[1:-1]:
        total = total + other[...].astype(F32)
    refs[-1][...] = total.astype(BF16)


def load_kernel(*refs):
    count = len(refs) // 2
    sources, targets, sems = refs[:count], refs[count : 2 * count], refs[-1]
    pieces = sems.shape[0] // count
    step = sources[0].shape[0] // pieces
    copies = []
    for k in range(count):
        for n in range(pieces):
            span = pl.ds(n * step, step)
            copy = pltpu.make_async_copy(
                sources[k].at[span, :], targets[k].at[span, :], sems.at[k * pieces + n]
            )
            copy.start()
            copies.append(copy)
    for copy in copies:
        copy.wait()


def project_kernel(shifts, count, where_ref, *refs):
    pieces = len(shifts)
    first = 0 in shifts
    rims = refs[:pieces]
    bodies = refs[pieces : 2 * pieces]
    weights = refs[2 * pieces : 2 * pieces + 4]
    refs = refs[2 * pieces + 4 :]
    depth, tokens = bodies[0].shape
    rep = where_ref[0]
    tp = where_ref[1]
    if first:
        key_ref, value_ref = refs
        half = value_ref.shape[-1]
    else:
        begun_keys, begun_values, hidden_halo, hidden, value_ref, stats_ref, states = refs
        half = value_ref.shape[-1]
        for slot in range(2):
            states[slot, :RIM] = hidden_halo[:, slot * half : (slot + 1) * half]
            states[slot, RIM:] = hidden[:, slot * half : (slot + 1) * half]
    body = jnp.concatenate([b[...].astype(F32) for b in bodies], axis=0).T.astype(BF16)
    rim = jnp.concatenate([r[...].astype(F32) for r in rims], axis=0).T.astype(BF16)
    memory = jnp.concatenate([rim[LANES - RIM :], body], axis=0)

    def project(far, which):
        field = None
        for n, s in enumerate(shifts):
            owner = lax.rem(tp + count - s, count)
            rows = pl.ds(pl.multiple_of(owner * depth, depth), depth)
            part = dot(
                memory[:, n * depth : (n + 1) * depth], weights[2 * far + which][rows, :]
            )
            field = part if field is None else field + part
        return field

    sums = [0.0] * 4
    for far in range(2):
        slot = rep if far == 0 else 1 - rep
        if first:
            value_ref[slot] = project(far, 1)
            key_ref[slot] = project(far, 0)
        else:
            values = project(far, 1) + begun_values[slot]
            value_ref[slot] = values
            keys = project(far, 0) + begun_keys[slot]
            here = states[slot].astype(F32)
            terms = (here * here, keys * keys, here * keys, values * values)
            sums = [a + jnp.sum(t, axis=1, keepdims=True) for a, t in zip(sums, terms)]
    if not first:
        rows = memory.shape[0]
        lane = iota((rows, 8), 1)
        packed = jnp.zeros((rows, 8), F32)
        for k in range(4):
            packed = jnp.where(lane == k, sums[k], packed)
        stats_ref[...] = dot_nt(unit(8, F32), packed, lax.Precision.HIGHEST)


def prepare_kernel(taps_ref, rows_ref, tap_ref):
    half = rows_ref.shape[-1]
    tokens = tap_ref.shape[2]
    for slot in range(2):
        for start in range(0, half, LANES):
            size = min(LANES, half - start)
            span = slice(start, start + size)
            there = slice(slot * half + start, slot * half + start + size)
            for tap in range(1, KERNEL):
                lag = DILATION * tap
                rows = rows_ref[slot, RIM - lag : RIM - lag + tokens, span]
                tap_ref[tap - 1, slot, :, span] = taps_ref[tap : tap + 1, there] * rows


def finish_kernel(count, step, keep_ref, *refs):
    stats = refs[:count]
    value_ref, tap_ref, hidden_ref, taps_ref, out_hbm = refs[count : count + 5]
    columns, gates, factors, out_ref, sems = refs[count + 5 :]
    half = value_ref.shape[-1]
    tokens, width = out_ref.shape
    total = stats[0][...]
    for other in stats[1:]:
        total = total + other[...]
    inverse_states = lax.rsqrt(total[0:1] / D + EPSILON)
    inverse_keys = lax.rsqrt(total[1:2] / D + EPSILON)
    gate = jax.nn.sigmoid(total[2:3] * inverse_states * inverse_keys / D**0.5)
    factor = gate * lax.rsqrt(gate * gate * total[3:4] / D + EPSILON)
    factor = jnp.where((iota(factor.shape, 1) < RIM) & (keep_ref[0] == 0), 0.0, factor)
    line = iota(total.shape, 0)
    both = jnp.where(line == 0, gate, jnp.where(line == 1, factor, 0.0))
    columns[...] = dot_nt(unit(total.shape[1], F32), both, lax.Precision.HIGHEST)
    gates[...] = jnp.broadcast_to(columns[RIM:, 0:1], gates.shape)
    for tap in range(KERNEL):
        lag = DILATION * tap
        factors[tap] = jnp.broadcast_to(
            columns[RIM - lag : RIM - lag + tokens, 1:2], factors.shape[1:]
        )
    copies = []
    for slot in range(2):
        for start in range(0, half, LANES):
            size = min(LANES, half - start)
            span = slice(start, start + size)
            there = slice(slot * half + start, slot * half + start + size)
            values = value_ref[slot, RIM:, span]
            conv = taps_ref[0:1, there] * values * factors[0, :, :size]
            for tap in range(1, KERNEL):
                conv = conv + tap_ref[tap - 1, slot, :, span] * factors[tap, :, :size]
            gated = values * gates[:, :size]
            out_ref[:, there] = (
                hidden_ref[:, there].astype(F32) + jax.nn.silu(conv) + gated
            ).astype(BF16)
            if there.stop % step == 0:
                ready = pl.ds(there.stop - step, step)
                copy = pltpu.make_async_copy(
                    out_ref.at[:, ready], out_hbm.at[:, ready], sems.at[len(copies)]
                )
                copy.start()
                copies.append(copy)
    for copy in copies:
        copy.wait()


def whole(array):
    return pl.BlockSpec(array.shape, lambda *_: (0,) * array.ndim)


def in_hbm(array):
    return pltpu.with_memory_space_constraint(array, pltpu.HBM)


def after(array, *others):
    return lax.optimization_barrier((array, *others))[0]


def limit(mib):
    return pltpu.CompilerParams(vmem_limit_bytes=mib << 20)


def scattered_sum(stored, decoded, here, meanwhile, settled):
    mems = lax.axis_size("mem")
    heads, width, rows = decoded.shape
    tokens = stored.shape[1]
    asked = lax.all_gather(stored, "mem", axis=0)
    partial = pl.pallas_call(
        pick_kernel,
        grid=(mems,),
        in_specs=[
            pl.BlockSpec(memory_space=pltpu.SMEM),
            pl.BlockSpec((None, heads, tokens), lambda m: (m, 0, 0)),
            whole(decoded),
        ],
        out_specs=pl.BlockSpec((None, heads * width, tokens), lambda m: (m, 0, 0)),
        out_shape=jax.ShapeDtypeStruct((mems, heads * width, tokens), BF16),
        compiler_params=limit(16),
        name="pick_all",
    )((here * rows).astype(I32).reshape(1), asked, decoded)
    total = lax.psum_scatter(partial, "mem", scatter_dimension=0, tiled=False)
    return total, meanwhile(partial, partial, settled)


def line_sum(stored, decoded, here, meanwhile, settled):
    heads, width, rows = decoded.shape
    tokens = stored.shape[1]
    base = (here * rows).astype(I32).reshape(1)
    block = jax.ShapeDtypeStruct((heads * width, tokens), BF16)

    def ask(ids, x):
        return lax.ppermute(ids, "mem", [(i, i ^ x) for i in range(4)])

    def crossing(x, pairs):
        return lax.ppermute(x, ("mem", "rep"), [(2 * a + b, 2 * c + d) for a, b, c, d in pairs])

    def pick(ids):
        return pl.pallas_call(
            pick_kernel,
            in_specs=[pl.BlockSpec(memory_space=pltpu.SMEM)]
            + [pl.BlockSpec(memory_space=pltpu.VMEM)] * 2,
            out_shape=block,
            compiler_params=limit(8),
            name="pick_rows",
        )(base, ids, decoded)

    def send(x, *pairs):
        return lax.ppermute(x, "mem", pairs)

    first = ask(stored, 3)
    second = crossing(
        stored,
        [(m, r, m ^ 2, r ^ int(m in (1, 2))) for m in range(4) for r in range(2)],
    )
    third = ask(stored, 1)
    first, second, third = lax.optimization_barrier((first, second, third))
    rows_3 = pick(first)
    inward = send(rows_3, (0, 1), (3, 2))
    across = send(rows_3, (1, 2), (2, 1))
    rows_2 = pick(after(second, rows_3))
    third, settled = lax.optimization_barrier((after(third, rows_2), settled))
    past = crossing(rows_2, [(m, r, m ^ 2, r ^ 1) for m in (0, 3) for r in range(2)])
    rows_1 = pick(third)
    own = pick(after(stored, rows_1))
    beside = send(rows_1, (0, 1), (1, 0), (2, 3), (3, 2))
    onward = after(rows_2, rows_1, own) + inward
    other = meanwhile(across, onward, settled)
    onward = send(onward, (1, 3), (2, 0))
    own, other = lax.optimization_barrier((own + past + beside, other))
    memory = pl.pallas_call(
        merge_kernel,
        in_specs=[pl.BlockSpec(memory_space=pltpu.VMEM)] * 3,
        out_shape=block,
        compiler_params=limit(4),
        name="merge",
    )(own, across, onward)
    return memory, other


def shards(
    hidden, row_ids, row_place, table_codes, table_scales, key_weight, value_weight, conv_weight
):
    mems = lax.axis_size("mem")
    tps = lax.axis_size("tp")
    reps = lax.axis_size("rep")
    blocks = mems * reps
    tokens, heads = row_ids.shape
    rows, width = table_codes.shape[1:]
    depth = heads * width
    half = key_weight.shape[1]
    seq_length = tokens * blocks // SEQS
    assert reps == 2 and seq_length % tokens == 0 and row_place.shape[0] % LANES == 0
    block = lax.axis_index(("mem", "rep"))
    smem = pl.BlockSpec(memory_space=pltpu.SMEM)

    anywhere = pl.BlockSpec(memory_space=pl.ANY)
    resident = pl.BlockSpec(memory_space=pltpu.VMEM)
    places = row_place.reshape(-1, LANES)
    stored = pl.pallas_call(
        place_kernel,
        in_specs=[anywhere] * 2,
        out_shape=jax.ShapeDtypeStruct((heads, tokens), I32),
        scratch_shapes=[
            pltpu.VMEM((heads, tokens), I32),
            pltpu.VMEM(places.shape, I32),
            pltpu.SemaphoreType.DMA((2,)),
        ],
        compiler_params=limit(4),
        name="place_rows",
    )(in_hbm(row_ids.T), in_hbm(places))
    codes = table_codes.transpose(0, 2, 1)
    scales = table_scales.transpose(2, 0, 1)
    decoded = pl.pallas_call(
        decode_kernel,
        in_specs=[anywhere] * 2,
        out_shape=jax.ShapeDtypeStruct(codes.shape, BF16),
        scratch_shapes=[
            pltpu.VMEM(codes.shape, BF16),
            pltpu.VMEM(scales.shape, BF16),
            pltpu.SemaphoreType.DMA((heads + 1,)),
        ],
        compiler_params=limit(12),
        name="decode_tables",
    )(in_hbm(after(codes, stored)), in_hbm(scales))
    here = lax.axis_index("mem")
    other_key = lax.ppermute(key_weight, "rep", [(0, 1), (1, 0)])
    other_value = lax.ppermute(value_weight, "rep", [(0, 1), (1, 0)])
    needed = [(i, i + 1) for i in range(blocks - 1) if (i + 1) * tokens % seq_length]

    def meanwhile(token, later, weights):
        tail = after(hidden[tokens - RIM :], token)
        halo = lax.ppermute(tail, ("mem", "rep"), needed)
        weights = lax.optimization_barrier((*weights, later))[:-1]
        held = pl.pallas_call(
            load_kernel,
            in_specs=[anywhere] * 4,
            out_specs=(resident,) * 4,
            out_shape=(pltpu.VMEM(key_weight.shape, BF16),) * 4,
            scratch_shapes=[pltpu.SemaphoreType.DMA((8,))],
            compiler_params=limit(4),
            name="load_weights",
        )(*[in_hbm(w) for w in weights])
        return halo, held

    summed = line_sum if mems == 4 else scattered_sum
    memory, (hidden_halo, weights) = summed(
        stored,
        decoded,
        here,
        meanwhile,
        (key_weight, value_weight, other_key, other_value),
    )

    where = jnp.stack([lax.axis_index("rep"), lax.axis_index("tp")]).astype(I32)
    extended = tokens + RIM
    bodies = [memory] + [
        lax.ppermute(memory, "tp", [(i, (i + s) % tps) for i in range(tps)])
        for s in range(1, tps)
    ]

    def next_rim(rim, s):
        pairs = [
            (
                (a // reps * tps + i) * reps + a % reps,
                (b // reps * tps + (i + s) % tps) * reps + b % reps,
            )
            for a, b in needed
            for i in range(tps)
        ]
        return lax.ppermute(rim, ("mem", "tp", "rep"), pairs)

    rim = memory[:, tokens - LANES :]
    rims = [next_rim(rim, s) for s in range(tps)]
    others = tps - 1
    field = jax.ShapeDtypeStruct((2, extended, half), F32)
    begun = pl.pallas_call(
        functools.partial(project_kernel, (0,), tps),
        in_specs=[smem] + [resident] * 6,
        out_specs=(resident,) * 2,
        out_shape=(field, field),
        compiler_params=limit(8),
        name="project_own",
    )(where, rims[0], memory, *weights)
    values, stats = pl.pallas_call(
        functools.partial(project_kernel, tuple(range(1, tps)), tps),
        in_specs=[smem] + [resident] * (2 * others + 8),
        out_specs=(resident,) * 2,
        out_shape=(field, jax.ShapeDtypeStruct((8, extended), F32)),
        scratch_shapes=[pltpu.VMEM((2, extended, half), BF16)],
        compiler_params=limit(8),
        name="project_others",
    )(where, *rims[1:], *bodies[1:], *weights, *begun, hidden_halo, hidden)

    all_stats = [stats] + [
        lax.ppermute(stats, "tp", [(i, (i + s) % tps) for i in range(tps)]) for s in range(1, tps)
    ]
    keep = (block * tokens % seq_length != 0).astype(I32).reshape(1)
    step = 2 * half
    if half % LANES == 0:
        step = next(c for c in (384, 256, 128) if half % c == 0)
    products = pl.pallas_call(
        prepare_kernel,
        in_specs=[resident] * 2,
        out_specs=resident,
        out_shape=jax.ShapeDtypeStruct((KERNEL - 1, 2, tokens, half), F32),
        compiler_params=limit(4),
        name="prepare",
    )(conv_weight, values)
    return pl.pallas_call(
        functools.partial(finish_kernel, tps, step),
        in_specs=[smem] + [resident] * (tps + 4),
        out_specs=anywhere,
        out_shape=jax.ShapeDtypeStruct((tokens, 2 * half), BF16),
        scratch_shapes=[
            pltpu.VMEM((extended, 8), F32),
            pltpu.VMEM((tokens, LANES), F32),
            pltpu.VMEM((KERNEL, tokens, LANES), F32),
            pltpu.VMEM((tokens, 2 * half), BF16),
            pltpu.SemaphoreType.DMA((2 * half // step,)),
        ],
        compiler_params=limit(6),
        name="finish",
    )(keep, *all_stats, values, products, hidden, conv_weight)


def solution(mesh):
    in_specs = (
        P(("parts", "mem", "rep"), "tp"),
        P(("parts", "mem", "rep"), "tp"),
        P("parts"),
        P(("parts", "tp"), "mem", None),
        P(("parts", "tp"), "mem", None),
        P(None, ("tp", "rep")),
        P(None, ("tp", "rep")),
        P(None, "tp"),
    )
    out_specs = P(("parts", "mem", "rep"), "tp")
    return jax.shard_map(shards, mesh=mesh, in_specs=in_specs, out_specs=out_specs, check_vma=False)
```

```python
import functools

import jax
import jax.numpy as jnp
from jax import lax
from jax.experimental import pallas as pl
from jax.experimental.pallas import tpu as pltpu
from jax.sharding import PartitionSpec as P

D = 4608
KERNEL = 4
DILATION = 3
SEQS = 4
EPSILON = 1e-06
RIM = 16
LANES = 128

F32 = jnp.float32
BF16 = jnp.bfloat16
I32 = jnp.int32


def iota(shape, axis):
    return lax.broadcasted_iota(I32, shape, axis)


def dot(a, b):
    return jnp.dot(a, b, preferred_element_type=F32)


def dot_nt(a, b, precision=None):
    return lax.dot_general(
        a, b, (((1,), (1,)), ((), ())), precision=precision, preferred_element_type=F32
    )


def unit(n, dtype):
    return (iota((n, n), 0) == iota((n, n), 1)).astype(F32).astype(dtype)


def to_bf16(x):
    return x.astype(F32).astype(BF16)


def place_kernel(
    ids_hbm, place_hbm, codes_hbm, scales_hbm, out_ref, codes_ref, scales_ref, ids_ref, place_ref, sems
):
    copies = [
        pltpu.make_async_copy(place_hbm, place_ref, sems.at[0]),
        pltpu.make_async_copy(ids_hbm, ids_ref, sems.at[1]),
        pltpu.make_async_copy(scales_hbm, scales_ref, sems.at[2]),
    ]
    for n in range(codes_ref.shape[0]):
        copies.append(
            pltpu.make_async_copy(codes_hbm.at[n], codes_ref.at[n], sems.at[3 + n])
        )
    for copy in copies:
        copy.start()
    copies[0].wait()
    place = place_ref[...]
    rows = place.shape[0]
    heads, tokens = ids_ref.shape
    eye = unit(LANES, BF16)
    table = jnp.concatenate(
        [dot_nt(eye, to_bf16(place >> 8)), dot_nt(eye, to_bf16(place & 255))], axis=0
    ).astype(BF16)
    copies[1].wait()
    for head in range(heads):
        row = ids_ref[head : head + 1, :]
        hot = to_bf16(iota((rows, tokens), 0) == (row >> 7))
        both = dot(table, hot)
        value = both[:LANES] * 256.0 + both[LANES:]
        chosen = jnp.where(iota(value.shape, 0) == (row & 127), value, 0.0)
        out_ref[head : head + 1, :] = jnp.sum(chosen, axis=0, keepdims=True).astype(I32)
    for copy in copies[2:]:
        copy.wait()


def decode_kernel(codes_ref, scales_ref, out_ref):
    heads, width, rows = codes_ref.shape
    blocks = scales_ref.shape[0]
    entry = iota((width, 2 * width), 0)
    column = iota((width, 2 * width), 1)
    column = jnp.where(column < width, column, column - width)
    parity = entry & column & 15
    parity = parity ^ (parity >> 2)
    parity = (parity ^ (parity >> 1)) & 1
    same = (entry >> 4) == (column >> 4)
    rotation = jnp.where(same, 0.25 - 0.5 * parity.astype(F32), 0.0).astype(BF16)
    for head in range(heads):
        factors = jnp.concatenate(
            [
                jnp.broadcast_to(scales_ref[b, head : head + 1, :].astype(F32), (16, rows))
                for b in range(blocks)
            ],
            axis=0,
        )
        scaled = codes_ref[head].astype(F32) * factors
        upper = scaled.astype(BF16)
        lower = (scaled - upper.astype(F32)).astype(BF16)
        out_ref[head] = dot(rotation, jnp.concatenate([upper, lower], axis=0)).astype(BF16)


def picked(local, table_ref, head):
    rows = table_ref.shape[2]
    hot = to_bf16(iota((rows, local.shape[1]), 0) == local[head : head + 1, :])
    return dot(table_ref[head], hot).astype(BF16)


def pick_kernel(base_ref, ids_ref, table_ref, out_ref):
    heads, width, _ = table_ref.shape
    local = ids_ref[...] - base_ref[0]
    for head in range(heads):
        out_ref[head * width : (head + 1) * width, :] = picked(local, table_ref, head)


def merge_kernel(*refs):
    total = refs[0][...].astype(F32)
    for other in refs[1:-1]:
        total = total + other[...].astype(F32)
    refs[-1][...] = total.astype(BF16)


def project_kernel(shifts, count, where_ref, *refs):
    pieces = len(shifts)
    first = 0 in shifts
    rims = refs[:pieces]
    bodies = refs[pieces : 2 * pieces]
    refs = refs[2 * pieces :]
    depth, tokens = bodies[0].shape
    rep = where_ref[0]
    tp = where_ref[1]
    if first:
        weights = refs[:4]
        key_ref, value_ref, rest, held, sems, rest_sems = refs[4:]
        half = held.shape[-1]

        split = sems.shape[-1]
        size = depth // split

        def bring(target, far, which, n, s, sem):
            owner = lax.rem(tp + count - s, count)
            copies = []
            for k in range(split):
                rows = pl.ds(pl.multiple_of(owner * depth + k * size, size), size)
                copy = pltpu.make_async_copy(
                    weights[2 * far + which].at[rows, :],
                    target.at[far, which, pl.ds(n * depth + k * size, size), :],
                    sem.at[k],
                )
                copy.start()
                copies.append(copy)
            return copies

        copies = [
            bring(held, far, which, 0, 0, sems.at[2 * far + which])
            for far in range(2)
            for which in (1, 0)
        ]
        later = []
        for far in range(2):
            for which in (1, 0):
                for n in range(count - 1):
                    sem = rest_sems.at[(2 * far + which) * (count - 1) + n]
                    later += bring(rest, far, which, n, n + 1, sem)
    else:
        later = []
        rest, begun_keys, begun_values, hidden_halo, hidden = refs[:5]
        value_hbm, stats_ref, states, done, done_sems = refs[5:]
        held = rest
        half = held.shape[-1]
        for slot in range(2):
            states[slot, :RIM] = hidden_halo[:, slot * half : (slot + 1) * half]
            states[slot, RIM:] = hidden[:, slot * half : (slot + 1) * half]
    body = jnp.concatenate([b[...].astype(F32) for b in bodies], axis=0).T.astype(BF16)
    rim = jnp.concatenate([r[...].astype(F32) for r in rims], axis=0).T.astype(BF16)
    memory = jnp.concatenate([rim[LANES - RIM :], body], axis=0)
    sums = [0.0] * 4
    for far in range(2):
        slot = rep if far == 0 else 1 - rep
        fields = [None, None]
        for which in (1, 0):
            if first:
                for copy in copies[2 * far + 1 - which]:
                    copy.wait()
            fields[which] = dot(memory, held[far, which])
            if not first and which == 1:
                done[far] = fields[1] + begun_values[slot]
                copy = pltpu.make_async_copy(done.at[far], value_hbm.at[slot], done_sems.at[far])
                copy.start()
                later.append(copy)
        if first:
            value_ref[slot] = fields[1]
            key_ref[slot] = fields[0]
        else:
            keys = fields[0] + begun_keys[slot]
            values = done[far]
            here = states[slot].astype(F32)
            terms = (here * here, keys * keys, here * keys, values * values)
            sums = [a + jnp.sum(t, axis=1, keepdims=True) for a, t in zip(sums, terms)]
    if not first:
        rows = memory.shape[0]
        lane = iota((rows, 8), 1)
        packed = jnp.zeros((rows, 8), F32)
        for k in range(4):
            packed = jnp.where(lane == k, sums[k], packed)
        stats_ref[...] = dot_nt(unit(8, F32), packed, lax.Precision.HIGHEST)
    for copy in later:
        copy.wait()


def prepare_kernel(chunk, taps_ref, value_hbm, value_ref, tap_ref, rows_ref, sems):
    half = rows_ref.shape[-1]
    tokens = value_ref.shape[1]
    copies = []
    for slot in range(2):
        for start in range(0, half, chunk):
            span = pl.ds(start, chunk)
            copy = pltpu.make_async_copy(
                value_hbm.at[slot, :, span], rows_ref.at[slot, :, span], sems.at[len(copies)]
            )
            copy.start()
            copies.append(copy)
    for slot in range(2):
        for start in range(0, half, LANES):
            size = min(LANES, half - start)
            span = slice(start, start + size)
            there = slice(slot * half + start, slot * half + start + size)
            if start % chunk == 0:
                copies[(slot * half + start) // chunk].wait()
            value_ref[slot, :, span] = rows_ref[slot, RIM:, span]
            for tap in range(1, KERNEL):
                lag = DILATION * tap
                rows = rows_ref[slot, RIM - lag : RIM - lag + tokens, span]
                tap_ref[tap - 1, slot, :, span] = taps_ref[tap : tap + 1, there] * rows


def finish_kernel(count, step, keep_ref, *refs):
    stats = refs[:count]
    value_ref, tap_ref, hidden_ref, taps_ref, out_hbm = refs[count : count + 5]
    columns, gates, factors, out_ref, sems = refs[count + 5 :]
    half = value_ref.shape[-1]
    tokens, width = out_ref.shape
    total = stats[0][...]
    for other in stats[1:]:
        total = total + other[...]
    inverse_states = lax.rsqrt(total[0:1] / D + EPSILON)
    inverse_keys = lax.rsqrt(total[1:2] / D + EPSILON)
    gate = jax.nn.sigmoid(total[2:3] * inverse_states * inverse_keys / D**0.5)
    factor = gate * lax.rsqrt(gate * gate * total[3:4] / D + EPSILON)
    factor = jnp.where((iota(factor.shape, 1) < RIM) & (keep_ref[0] == 0), 0.0, factor)
    line = iota(total.shape, 0)
    both = jnp.where(line == 0, gate, jnp.where(line == 1, factor, 0.0))
    columns[...] = dot_nt(unit(total.shape[1], F32), both, lax.Precision.HIGHEST)
    gates[...] = jnp.broadcast_to(columns[RIM:, 0:1], gates.shape)
    for tap in range(KERNEL):
        lag = DILATION * tap
        factors[tap] = jnp.broadcast_to(
            columns[RIM - lag : RIM - lag + tokens, 1:2], factors.shape[1:]
        )
    copies = []
    for slot in range(2):
        for start in range(0, half, LANES):
            size = min(LANES, half - start)
            span = slice(start, start + size)
            there = slice(slot * half + start, slot * half + start + size)
            values = value_ref[slot, :, span]
            conv = taps_ref[0:1, there] * values * factors[0, :, :size]
            for tap in range(1, KERNEL):
                conv = conv + tap_ref[tap - 1, slot, :, span] * factors[tap, :, :size]
            gated = values * gates[:, :size]
            out_ref[:, there] = (
                hidden_ref[:, there].astype(F32) + jax.nn.silu(conv) + gated
            ).astype(BF16)
            if there.stop % step == 0:
                ready = pl.ds(there.stop - step, step)
                copy = pltpu.make_async_copy(
                    out_ref.at[:, ready], out_hbm.at[:, ready], sems.at[len(copies)]
                )
                copy.start()
                copies.append(copy)
    for copy in copies:
        copy.wait()


def whole(array):
    return pl.BlockSpec(array.shape, lambda *_: (0,) * array.ndim)


def in_hbm(array):
    return pltpu.with_memory_space_constraint(array, pltpu.HBM)


def after(array, *others):
    return lax.optimization_barrier((array, *others))[0]


def limit(mib):
    return pltpu.CompilerParams(vmem_limit_bytes=mib << 20)


def scattered_sum(stored, decoded, here, meanwhile, settled):
    mems = lax.axis_size("mem")
    heads, width, rows = decoded.shape
    tokens = stored.shape[1]
    asked = lax.all_gather(stored, "mem", axis=0)
    partial = pl.pallas_call(
        pick_kernel,
        grid=(mems,),
        in_specs=[
            pl.BlockSpec(memory_space=pltpu.SMEM),
            pl.BlockSpec((None, heads, tokens), lambda m: (m, 0, 0)),
            whole(decoded),
        ],
        out_specs=pl.BlockSpec((None, heads * width, tokens), lambda m: (m, 0, 0)),
        out_shape=jax.ShapeDtypeStruct((mems, heads * width, tokens), BF16),
        compiler_params=limit(16),
        name="pick_all",
    )((here * rows).astype(I32).reshape(1), asked, decoded)
    total = lax.psum_scatter(partial, "mem", scatter_dimension=0, tiled=False)
    return total, meanwhile(partial), settled


def line_sum(stored, decoded, here, meanwhile, settled):
    heads, width, rows = decoded.shape
    tokens = stored.shape[1]
    base = (here * rows).astype(I32).reshape(1)
    block = jax.ShapeDtypeStruct((heads * width, tokens), BF16)

    def ask(ids, x):
        return lax.ppermute(ids, "mem", [(i, i ^ x) for i in range(4)])

    def crossing(x, pairs):
        return lax.ppermute(x, ("mem", "rep"), [(2 * a + b, 2 * c + d) for a, b, c, d in pairs])

    def pick(ids):
        return pl.pallas_call(
            pick_kernel,
            in_specs=[pl.BlockSpec(memory_space=pltpu.SMEM)]
            + [pl.BlockSpec(memory_space=pltpu.VMEM)] * 2,
            out_shape=block,
            compiler_params=limit(8),
            name="pick_rows",
        )(base, ids, decoded)

    def send(x, *pairs):
        return lax.ppermute(x, "mem", pairs)

    first = ask(stored, 3)
    second = crossing(
        stored,
        [(m, r, m ^ 2, r ^ int(m in (1, 2))) for m in range(4) for r in range(2)],
    )
    third = ask(stored, 1)
    first, second, third = lax.optimization_barrier((first, second, third))
    rows_3 = pick(first)
    inward = send(rows_3, (0, 1), (3, 2))
    across = send(rows_3, (1, 2), (2, 1))
    rows_2 = pick(after(second, rows_3))
    third, settled = lax.optimization_barrier((after(third, rows_2), settled))
    past = crossing(rows_2, [(m, r, m ^ 2, r ^ 1) for m in (0, 3) for r in range(2)])
    rows_1 = pick(third)
    own = pick(after(stored, rows_1))
    beside = send(rows_1, (0, 1), (1, 0), (2, 3), (3, 2))
    onward = after(rows_2, rows_1, own) + inward
    onward = send(onward, (1, 3), (2, 0))
    other = meanwhile(across)
    own, other = lax.optimization_barrier((own + past + beside, other))
    memory = pl.pallas_call(
        merge_kernel,
        in_specs=[pl.BlockSpec(memory_space=pltpu.VMEM)] * 3,
        out_shape=block,
        compiler_params=limit(4),
        name="merge",
    )(own, across, onward)
    return memory, other, settled


def shards(
    hidden, row_ids, row_place, table_codes, table_scales, key_weight, value_weight, conv_weight
):
    mems = lax.axis_size("mem")
    tps = lax.axis_size("tp")
    reps = lax.axis_size("rep")
    blocks = mems * reps
    tokens, heads = row_ids.shape
    rows, width = table_codes.shape[1:]
    depth = heads * width
    half = key_weight.shape[1]
    seq_length = tokens * blocks // SEQS
    assert reps == 2 and seq_length % tokens == 0 and row_place.shape[0] % LANES == 0
    block = lax.axis_index(("mem", "rep"))
    smem = pl.BlockSpec(memory_space=pltpu.SMEM)

    anywhere = pl.BlockSpec(memory_space=pl.ANY)
    resident = pl.BlockSpec(memory_space=pltpu.VMEM)
    places = row_place.reshape(-1, LANES)
    codes = table_codes.transpose(0, 2, 1)
    scales = table_scales.transpose(2, 0, 1)
    stored, codes, scales = pl.pallas_call(
        place_kernel,
        in_specs=[anywhere] * 4,
        out_specs=(resident,) * 3,
        out_shape=(
            jax.ShapeDtypeStruct((heads, tokens), I32),
            jax.ShapeDtypeStruct(codes.shape, BF16),
            jax.ShapeDtypeStruct(scales.shape, BF16),
        ),
        scratch_shapes=[
            pltpu.VMEM((heads, tokens), I32),
            pltpu.VMEM(places.shape, I32),
            pltpu.SemaphoreType.DMA((heads + 3,)),
        ],
        compiler_params=limit(4),
        name="place_rows",
    )(*[in_hbm(x) for x in (row_ids.T, places, codes, scales)])
    decoded = pl.pallas_call(
        decode_kernel,
        in_specs=[resident] * 2,
        out_specs=resident,
        out_shape=jax.ShapeDtypeStruct(codes.shape, BF16),
        compiler_params=limit(6),
        name="decode_tables",
    )(codes, scales)
    here = lax.axis_index("mem")
    other_key = lax.ppermute(key_weight, "rep", [(0, 1), (1, 0)])
    other_value = lax.ppermute(value_weight, "rep", [(0, 1), (1, 0)])
    needed = [(i, i + 1) for i in range(blocks - 1) if (i + 1) * tokens % seq_length]

    def meanwhile(token):
        tail = after(hidden[tokens - RIM :], token)
        return lax.ppermute(tail, ("mem", "rep"), needed)

    summed = line_sum if mems == 4 else scattered_sum
    memory, hidden_halo, others = summed(
        stored, decoded, here, meanwhile, (other_key, other_value)
    )
    weights = [in_hbm(w) for w in (key_weight, value_weight, *others)]

    where = jnp.stack([lax.axis_index("rep"), lax.axis_index("tp")]).astype(I32)
    extended = tokens + RIM
    bodies = [memory] + [
        lax.ppermute(memory, "tp", [(i, (i + s) % tps) for i in range(tps)])
        for s in range(1, tps)
    ]

    def next_rim(rim, s):
        pairs = [
            (
                (a // reps * tps + i) * reps + a % reps,
                (b // reps * tps + (i + s) % tps) * reps + b % reps,
            )
            for a, b in needed
            for i in range(tps)
        ]
        return lax.ppermute(rim, ("mem", "tp", "rep"), pairs)

    rim = memory[:, tokens - LANES :]
    rims = [next_rim(rim, s) for s in range(tps)]
    others = tps - 1
    field = jax.ShapeDtypeStruct((2, extended, half), F32)
    *begun, rest = pl.pallas_call(
        functools.partial(project_kernel, (0,), tps),
        in_specs=[smem] + [resident] * 2 + [anywhere] * 4,
        out_specs=(resident,) * 3,
        out_shape=(field, field, pltpu.VMEM((2, 2, others * depth, half), BF16)),
        scratch_shapes=[
            pltpu.VMEM((2, 2, depth, half), BF16),
            pltpu.SemaphoreType.DMA((4, 4)),
            pltpu.SemaphoreType.DMA((4 * others, 4)),
        ],
        compiler_params=limit(12),
        name="project_own",
    )(where, rims[0], memory, *weights)
    values, stats = pl.pallas_call(
        functools.partial(project_kernel, tuple(range(1, tps)), tps),
        in_specs=[smem] + [resident] * (2 * others + 5),
        out_specs=(pl.BlockSpec(memory_space=pltpu.HBM), resident),
        out_shape=(pltpu.HBM(field.shape, F32), jax.ShapeDtypeStruct((8, extended), F32)),
        scratch_shapes=[
            pltpu.VMEM((2, extended, half), BF16),
            pltpu.VMEM((2, extended, half), F32),
            pltpu.SemaphoreType.DMA((2,)),
        ],
        compiler_params=limit(14),
        name="project_others",
    )(
        where,
        *rims[1:],
        *bodies[1:],
        rest,
        *begun,
        hidden_halo,
        hidden,
    )

    all_stats = [stats] + [
        lax.ppermute(stats, "tp", [(i, (i + s) % tps) for i in range(tps)]) for s in range(1, tps)
    ]
    keep = (block * tokens % seq_length != 0).astype(I32).reshape(1)
    step = 2 * half
    if half % LANES == 0:
        step = next(c for c in (384, 256, 128) if half % c == 0)
    chunk = min(step, half)
    body = (2, tokens, half)
    values, products = pl.pallas_call(
        functools.partial(prepare_kernel, chunk),
        in_specs=[resident, anywhere],
        out_specs=(resident,) * 2,
        out_shape=(
            jax.ShapeDtypeStruct(body, F32),
            jax.ShapeDtypeStruct((KERNEL - 1, *body), F32),
        ),
        scratch_shapes=[
            pltpu.VMEM((2, extended, half), F32),
            pltpu.SemaphoreType.DMA((2 * half // chunk,)),
        ],
        compiler_params=limit(6),
        name="prepare",
    )(conv_weight, in_hbm(values))
    return pl.pallas_call(
        functools.partial(finish_kernel, tps, step),
        in_specs=[smem] + [resident] * (tps + 4),
        out_specs=anywhere,
        out_shape=jax.ShapeDtypeStruct((tokens, 2 * half), BF16),
        scratch_shapes=[
            pltpu.VMEM((extended, 8), F32),
            pltpu.VMEM((tokens, LANES), F32),
            pltpu.VMEM((KERNEL, tokens, LANES), F32),
            pltpu.VMEM((tokens, 2 * half), BF16),
            pltpu.SemaphoreType.DMA((2 * half // step,)),
        ],
        compiler_params=limit(6),
        name="finish",
    )(keep, *all_stats, values, products, hidden, conv_weight)


def solution(mesh):
    in_specs = (
        P(("parts", "mem", "rep"), "tp"),
        P(("parts", "mem", "rep"), "tp"),
        P("parts"),
        P(("parts", "tp"), "mem", None),
        P(("parts", "tp"), "mem", None),
        P(None, ("tp", "rep")),
        P(None, ("tp", "rep")),
        P(None, "tp"),
    )
    out_specs = P(("parts", "mem", "rep"), "tp")
    return jax.shard_map(shards, mesh=mesh, in_specs=in_specs, out_specs=out_specs, check_vma=False)
```

```python
import functools

import jax
import jax.numpy as jnp
from jax import lax
from jax.experimental import pallas as pl
from jax.experimental.pallas import tpu as pltpu
from jax.sharding import PartitionSpec as P

D = 4608
KERNEL = 4
DILATION = 3
SEQS = 4
EPSILON = 1e-06
RIM = 16
LANES = 128

F32 = jnp.float32
BF16 = jnp.bfloat16
I32 = jnp.int32


def iota(shape, axis):
    return lax.broadcasted_iota(I32, shape, axis)


def dot(a, b):
    return jnp.dot(a, b, preferred_element_type=F32)


def dot_nt(a, b, precision=None):
    return lax.dot_general(
        a, b, (((1,), (1,)), ((), ())), precision=precision, preferred_element_type=F32
    )


def unit(n, dtype):
    return (iota((n, n), 0) == iota((n, n), 1)).astype(F32).astype(dtype)


def to_bf16(x):
    return x.astype(F32).astype(BF16)


def place_kernel(
    ids_hbm, place_hbm, codes_hbm, scales_hbm, out_ref, codes_ref, scales_ref, ids_ref, place_ref, sems
):
    copies = [
        pltpu.make_async_copy(place_hbm, place_ref, sems.at[0]),
        pltpu.make_async_copy(ids_hbm, ids_ref, sems.at[1]),
        pltpu.make_async_copy(scales_hbm, scales_ref, sems.at[2]),
    ]
    for n in range(codes_ref.shape[0]):
        copies.append(
            pltpu.make_async_copy(codes_hbm.at[n], codes_ref.at[n], sems.at[3 + n])
        )
    for copy in copies:
        copy.start()
    copies[0].wait()
    place = place_ref[...]
    rows = place.shape[0]
    heads, tokens = ids_ref.shape
    eye = unit(LANES, BF16)
    table = jnp.concatenate(
        [dot_nt(eye, to_bf16(place >> 8)), dot_nt(eye, to_bf16(place & 255))], axis=0
    ).astype(BF16)
    copies[1].wait()
    for head in range(heads):
        row = ids_ref[head : head + 1, :]
        hot = to_bf16(iota((rows, tokens), 0) == (row >> 7))
        both = dot(table, hot)
        value = both[:LANES] * 256.0 + both[LANES:]
        chosen = jnp.where(iota(value.shape, 0) == (row & 127), value, 0.0)
        out_ref[head : head + 1, :] = jnp.sum(chosen, axis=0, keepdims=True).astype(I32)
    for copy in copies[2:]:
        copy.wait()


def decode_kernel(codes_ref, scales_ref, out_ref):
    heads, width, rows = codes_ref.shape
    blocks = scales_ref.shape[0]
    entry = iota((width, 2 * width), 0)
    column = iota((width, 2 * width), 1)
    column = jnp.where(column < width, column, column - width)
    parity = entry & column & 15
    parity = parity ^ (parity >> 2)
    parity = (parity ^ (parity >> 1)) & 1
    same = (entry >> 4) == (column >> 4)
    rotation = jnp.where(same, 0.25 - 0.5 * parity.astype(F32), 0.0).astype(BF16)
    for head in range(heads):
        factors = jnp.concatenate(
            [
                jnp.broadcast_to(scales_ref[b, head : head + 1, :].astype(F32), (16, rows))
                for b in range(blocks)
            ],
            axis=0,
        )
        scaled = codes_ref[head].astype(F32) * factors
        upper = scaled.astype(BF16)
        lower = (scaled - upper.astype(F32)).astype(BF16)
        out_ref[head] = dot(rotation, jnp.concatenate([upper, lower], axis=0)).astype(BF16)


def picked(local, table_ref, head):
    rows = table_ref.shape[2]
    hot = to_bf16(iota((rows, local.shape[1]), 0) == local[head : head + 1, :])
    return dot(table_ref[head], hot).astype(BF16)


def pick_kernel(base_ref, ids_ref, table_ref, out_ref):
    heads, width, _ = table_ref.shape
    local = ids_ref[...] - base_ref[0]
    for head in range(heads):
        out_ref[head * width : (head + 1) * width, :] = picked(local, table_ref, head)


def merge_kernel(*refs):
    total = refs[0][...].astype(F32)
    for other in refs[1:-1]:
        total = total + other[...].astype(F32)
    refs[-1][...] = total.astype(BF16)


def project_kernel(shifts, count, where_ref, *refs):
    pieces = len(shifts)
    first = 0 in shifts
    rims = refs[:pieces]
    bodies = refs[pieces : 2 * pieces]
    refs = refs[2 * pieces :]
    depth, tokens = bodies[0].shape
    rep = where_ref[0]
    tp = where_ref[1]
    if first:
        weights = refs[:4]
        key_ref, value_ref, rest, held, sems, rest_sems = refs[4:]
        half = held.shape[-1]

        def bring(target, far, which, n, s, sem):
            owner = lax.rem(tp + count - s, count)
            rows = pl.ds(pl.multiple_of(owner * depth, depth), depth)
            copy = pltpu.make_async_copy(
                weights[2 * far + which].at[rows, :],
                target.at[far, which, pl.ds(n * depth, depth), :],
                sem,
            )
            copy.start()
            return copy

        copies = [
            bring(held, far, which, 0, 0, sems.at[2 * far + which])
            for far in range(2)
            for which in (1, 0)
        ]
        later = []
    else:
        later = []
        rest, begun_keys, begun_values, hidden_halo, hidden = refs[:5]
        value_hbm, stats_ref, states, done, done_sems = refs[5:]
        held = rest
        half = held.shape[-1]
        for slot in range(2):
            states[slot, :RIM] = hidden_halo[:, slot * half : (slot + 1) * half]
            states[slot, RIM:] = hidden[:, slot * half : (slot + 1) * half]
    body = jnp.concatenate([b[...].astype(F32) for b in bodies], axis=0).T.astype(BF16)
    rim = jnp.concatenate([r[...].astype(F32) for r in rims], axis=0).T.astype(BF16)
    memory = jnp.concatenate([rim[LANES - RIM :], body], axis=0)
    sums = [0.0] * 4
    for far in range(2):
        slot = rep if far == 0 else 1 - rep
        fields = [None, None]
        for which in (1, 0):
            if first:
                copies[2 * far + 1 - which].wait()
                if far == 0 and which == 1:
                    later = [
                        bring(rest, f, w, n, n + 1, rest_sems.at[(2 * f + w) * (count - 1) + n])
                        for f in range(2)
                        for w in (1, 0)
                        for n in range(count - 1)
                    ]
            fields[which] = dot(memory, held[far, which])
            if not first and which == 1:
                done[far] = fields[1] + begun_values[slot]
                copy = pltpu.make_async_copy(done.at[far], value_hbm.at[slot], done_sems.at[far])
                copy.start()
                later.append(copy)
        if first:
            value_ref[slot] = fields[1]
            key_ref[slot] = fields[0]
        else:
            keys = fields[0] + begun_keys[slot]
            values = done[far]
            here = states[slot].astype(F32)
            terms = (here * here, keys * keys, here * keys, values * values)
            sums = [a + jnp.sum(t, axis=1, keepdims=True) for a, t in zip(sums, terms)]
    if not first:
        rows = memory.shape[0]
        lane = iota((rows, 8), 1)
        packed = jnp.zeros((rows, 8), F32)
        for k in range(4):
            packed = jnp.where(lane == k, sums[k], packed)
        stats_ref[...] = dot_nt(unit(8, F32), packed, lax.Precision.HIGHEST)
    for copy in later:
        copy.wait()


def prepare_kernel(chunk, taps_ref, value_hbm, value_ref, tap_ref, rows_ref, sems):
    half = rows_ref.shape[-1]
    tokens = value_ref.shape[1]
    copies = []
    for slot in range(2):
        for start in range(0, half, chunk):
            span = pl.ds(start, chunk)
            copy = pltpu.make_async_copy(
                value_hbm.at[slot, :, span], rows_ref.at[slot, :, span], sems.at[len(copies)]
            )
            copy.start()
            copies.append(copy)
    for slot in range(2):
        for start in range(0, half, LANES):
            size = min(LANES, half - start)
            span = slice(start, start + size)
            there = slice(slot * half + start, slot * half + start + size)
            if start % chunk == 0:
                copies[(slot * half + start) // chunk].wait()
            value_ref[slot, :, span] = rows_ref[slot, RIM:, span]
            for tap in range(1, KERNEL):
                lag = DILATION * tap
                rows = rows_ref[slot, RIM - lag : RIM - lag + tokens, span]
                tap_ref[tap - 1, slot, :, span] = taps_ref[tap : tap + 1, there] * rows


def finish_kernel(count, step, keep_ref, *refs):
    stats = refs[:count]
    value_ref, tap_ref, hidden_ref, taps_ref, out_hbm = refs[count : count + 5]
    columns, gates, factors, out_ref, sems = refs[count + 5 :]
    half = value_ref.shape[-1]
    tokens, width = out_ref.shape
    total = stats[0][...]
    for other in stats[1:]:
        total = total + other[...]
    inverse_states = lax.rsqrt(total[0:1] / D + EPSILON)
    inverse_keys = lax.rsqrt(total[1:2] / D + EPSILON)
    gate = jax.nn.sigmoid(total[2:3] * inverse_states * inverse_keys / D**0.5)
    factor = gate * lax.rsqrt(gate * gate * total[3:4] / D + EPSILON)
    factor = jnp.where((iota(factor.shape, 1) < RIM) & (keep_ref[0] == 0), 0.0, factor)
    line = iota(total.shape, 0)
    both = jnp.where(line == 0, gate, jnp.where(line == 1, factor, 0.0))
    columns[...] = dot_nt(unit(total.shape[1], F32), both, lax.Precision.HIGHEST)
    gates[...] = jnp.broadcast_to(columns[RIM:, 0:1], gates.shape)
    for tap in range(KERNEL):
        lag = DILATION * tap
        factors[tap] = jnp.broadcast_to(
            columns[RIM - lag : RIM - lag + tokens, 1:2], factors.shape[1:]
        )
    copies = []
    for slot in range(2):
        for start in range(0, half, LANES):
            size = min(LANES, half - start)
            span = slice(start, start + size)
            there = slice(slot * half + start, slot * half + start + size)
            values = value_ref[slot, :, span]
            conv = taps_ref[0:1, there] * values * factors[0, :, :size]
            for tap in range(1, KERNEL):
                conv = conv + tap_ref[tap - 1, slot, :, span] * factors[tap, :, :size]
            gated = values * gates[:, :size]
            out_ref[:, there] = (
                hidden_ref[:, there].astype(F32) + jax.nn.silu(conv) + gated
            ).astype(BF16)
            if there.stop % step == 0:
                ready = pl.ds(there.stop - step, step)
                copy = pltpu.make_async_copy(
                    out_ref.at[:, ready], out_hbm.at[:, ready], sems.at[len(copies)]
                )
                copy.start()
                copies.append(copy)
    for copy in copies:
        copy.wait()


def whole(array):
    return pl.BlockSpec(array.shape, lambda *_: (0,) * array.ndim)


def in_hbm(array):
    return pltpu.with_memory_space_constraint(array, pltpu.HBM)


def after(array, *others):
    return lax.optimization_barrier((array, *others))[0]


def limit(mib):
    return pltpu.CompilerParams(vmem_limit_bytes=mib << 20)


def scattered_sum(stored, decoded, here, meanwhile, settled):
    mems = lax.axis_size("mem")
    heads, width, rows = decoded.shape
    tokens = stored.shape[1]
    asked = lax.all_gather(stored, "mem", axis=0)
    partial = pl.pallas_call(
        pick_kernel,
        grid=(mems,),
        in_specs=[
            pl.BlockSpec(memory_space=pltpu.SMEM),
            pl.BlockSpec((None, heads, tokens), lambda m: (m, 0, 0)),
            whole(decoded),
        ],
        out_specs=pl.BlockSpec((None, heads * width, tokens), lambda m: (m, 0, 0)),
        out_shape=jax.ShapeDtypeStruct((mems, heads * width, tokens), BF16),
        compiler_params=limit(16),
        name="pick_all",
    )((here * rows).astype(I32).reshape(1), asked, decoded)
    total = lax.psum_scatter(partial, "mem", scatter_dimension=0, tiled=False)
    return total, meanwhile(partial), settled


def line_sum(stored, decoded, here, meanwhile, settled):
    heads, width, rows = decoded.shape
    tokens = stored.shape[1]
    base = (here * rows).astype(I32).reshape(1)
    block = jax.ShapeDtypeStruct((heads * width, tokens), BF16)

    def ask(ids, x):
        return lax.ppermute(ids, "mem", [(i, i ^ x) for i in range(4)])

    def crossing(x, pairs):
        return lax.ppermute(x, ("mem", "rep"), [(2 * a + b, 2 * c + d) for a, b, c, d in pairs])

    def pick(ids):
        return pl.pallas_call(
            pick_kernel,
            in_specs=[pl.BlockSpec(memory_space=pltpu.SMEM)]
            + [pl.BlockSpec(memory_space=pltpu.VMEM)] * 2,
            out_shape=block,
            compiler_params=limit(8),
            name="pick_rows",
        )(base, ids, decoded)

    def send(x, *pairs):
        return lax.ppermute(x, "mem", pairs)

    first = ask(stored, 3)
    second = crossing(
        stored,
        [(m, r, m ^ 2, r ^ int(m in (1, 2))) for m in range(4) for r in range(2)],
    )
    third = ask(stored, 1)
    rows_3 = pick(first)
    rows_3, second, third = lax.optimization_barrier((rows_3, second, third))
    inward = send(rows_3, (0, 1), (3, 2))
    across = send(rows_3, (1, 2), (2, 1))
    rows_2 = pick(after(second, rows_3))
    third, settled = lax.optimization_barrier((after(third, rows_2), settled))
    past = crossing(rows_2, [(m, r, m ^ 2, r ^ 1) for m in (0, 3) for r in range(2)])
    rows_1 = pick(third)
    own = pick(after(stored, rows_1))
    beside = send(rows_1, (0, 1), (1, 0), (2, 3), (3, 2))
    onward = after(rows_2, rows_1, own) + inward
    onward = send(onward, (1, 3), (2, 0))
    other = meanwhile(across)
    own, other = lax.optimization_barrier((own + past + beside, other))
    memory = pl.pallas_call(
        merge_kernel,
        in_specs=[pl.BlockSpec(memory_space=pltpu.VMEM)] * 3,
        out_shape=block,
        compiler_params=limit(4),
        name="merge",
    )(own, across, onward)
    return memory, other, settled


def shards(
    hidden, row_ids, row_place, table_codes, table_scales, key_weight, value_weight, conv_weight
):
    mems = lax.axis_size("mem")
    tps = lax.axis_size("tp")
    reps = lax.axis_size("rep")
    blocks = mems * reps
    tokens, heads = row_ids.shape
    rows, width = table_codes.shape[1:]
    depth = heads * width
    half = key_weight.shape[1]
    seq_length = tokens * blocks // SEQS
    assert reps == 2 and seq_length % tokens == 0 and row_place.shape[0] % LANES == 0
    block = lax.axis_index(("mem", "rep"))
    smem = pl.BlockSpec(memory_space=pltpu.SMEM)

    anywhere = pl.BlockSpec(memory_space=pl.ANY)
    resident = pl.BlockSpec(memory_space=pltpu.VMEM)
    places = row_place.reshape(-1, LANES)
    codes = table_codes.transpose(0, 2, 1)
    scales = table_scales.transpose(2, 0, 1)
    stored, codes, scales = pl.pallas_call(
        place_kernel,
        in_specs=[anywhere] * 4,
        out_specs=(resident,) * 3,
        out_shape=(
            jax.ShapeDtypeStruct((heads, tokens), I32),
            jax.ShapeDtypeStruct(codes.shape, BF16),
            jax.ShapeDtypeStruct(scales.shape, BF16),
        ),
        scratch_shapes=[
            pltpu.VMEM((heads, tokens), I32),
            pltpu.VMEM(places.shape, I32),
            pltpu.SemaphoreType.DMA((heads + 3,)),
        ],
        compiler_params=limit(4),
        name="place_rows",
    )(*[in_hbm(x) for x in (row_ids.T, places, codes, scales)])
    decoded = pl.pallas_call(
        decode_kernel,
        in_specs=[resident] * 2,
        out_specs=resident,
        out_shape=jax.ShapeDtypeStruct(codes.shape, BF16),
        compiler_params=limit(6),
        name="decode_tables",
    )(codes, scales)
    here = lax.axis_index("mem")
    other_key = lax.ppermute(key_weight, "rep", [(0, 1), (1, 0)])
    other_value = lax.ppermute(value_weight, "rep", [(0, 1), (1, 0)])
    needed = [(i, i + 1) for i in range(blocks - 1) if (i + 1) * tokens % seq_length]

    def meanwhile(token):
        tail = after(hidden[tokens - RIM :], token)
        return lax.ppermute(tail, ("mem", "rep"), needed)

    summed = line_sum if mems == 4 else scattered_sum
    memory, hidden_halo, others = summed(
        stored, decoded, here, meanwhile, (other_key, other_value)
    )
    weights = [in_hbm(w) for w in (key_weight, value_weight, *others)]

    where = jnp.stack([lax.axis_index("rep"), lax.axis_index("tp")]).astype(I32)
    extended = tokens + RIM
    bodies = [memory] + [
        lax.ppermute(memory, "tp", [(i, (i + s) % tps) for i in range(tps)])
        for s in range(1, tps)
    ]

    def next_rim(rim, s):
        pairs = [
            (
                (a // reps * tps + i) * reps + a % reps,
                (b // reps * tps + (i + s) % tps) * reps + b % reps,
            )
            for a, b in needed
            for i in range(tps)
        ]
        return lax.ppermute(rim, ("mem", "tp", "rep"), pairs)

    rim = memory[:, tokens - LANES :]
    rims = [next_rim(rim, s) for s in range(tps)]
    others = tps - 1
    field = jax.ShapeDtypeStruct((2, extended, half), F32)
    *begun, rest = pl.pallas_call(
        functools.partial(project_kernel, (0,), tps),
        in_specs=[smem] + [resident] * 2 + [anywhere] * 4,
        out_specs=(resident,) * 3,
        out_shape=(field, field, pltpu.VMEM((2, 2, others * depth, half), BF16)),
        scratch_shapes=[
            pltpu.VMEM((2, 2, depth, half), BF16),
            pltpu.SemaphoreType.DMA((4,)),
            pltpu.SemaphoreType.DMA((4 * others,)),
        ],
        compiler_params=limit(12),
        name="project_own",
    )(where, rims[0], memory, *weights)
    values, stats = pl.pallas_call(
        functools.partial(project_kernel, tuple(range(1, tps)), tps),
        in_specs=[smem] + [resident] * (2 * others + 5),
        out_specs=(pl.BlockSpec(memory_space=pltpu.HBM), resident),
        out_shape=(pltpu.HBM(field.shape, F32), jax.ShapeDtypeStruct((8, extended), F32)),
        scratch_shapes=[
            pltpu.VMEM((2, extended, half), BF16),
            pltpu.VMEM((2, extended, half), F32),
            pltpu.SemaphoreType.DMA((2,)),
        ],
        compiler_params=limit(14),
        name="project_others",
    )(
        where,
        *rims[1:],
        *bodies[1:],
        rest,
        *begun,
        hidden_halo,
        hidden,
    )

    all_stats = [stats] + [
        lax.ppermute(stats, "tp", [(i, (i + s) % tps) for i in range(tps)]) for s in range(1, tps)
    ]
    keep = (block * tokens % seq_length != 0).astype(I32).reshape(1)
    step = 2 * half
    if half % LANES == 0:
        step = next(c for c in (384, 256, 128) if half % c == 0)
    chunk = min(step, half)
    body = (2, tokens, half)
    values, products = pl.pallas_call(
        functools.partial(prepare_kernel, chunk),
        in_specs=[resident, anywhere],
        out_specs=(resident,) * 2,
        out_shape=(
            jax.ShapeDtypeStruct(body, F32),
            jax.ShapeDtypeStruct((KERNEL - 1, *body), F32),
        ),
        scratch_shapes=[
            pltpu.VMEM((2, extended, half), F32),
            pltpu.SemaphoreType.DMA((2 * half // chunk,)),
        ],
        compiler_params=limit(6),
        name="prepare",
    )(conv_weight, in_hbm(values))
    return pl.pallas_call(
        functools.partial(finish_kernel, tps, step),
        in_specs=[smem] + [resident] * (tps + 4),
        out_specs=anywhere,
        out_shape=jax.ShapeDtypeStruct((tokens, 2 * half), BF16),
        scratch_shapes=[
            pltpu.VMEM((extended, 8), F32),
            pltpu.VMEM((tokens, LANES), F32),
            pltpu.VMEM((KERNEL, tokens, LANES), F32),
            pltpu.VMEM((tokens, 2 * half), BF16),
            pltpu.SemaphoreType.DMA((2 * half // step,)),
        ],
        compiler_params=limit(6),
        name="finish",
    )(keep, *all_stats, values, products, hidden, conv_weight)


def solution(mesh):
    in_specs = (
        P(("parts", "mem", "rep"), "tp"),
        P(("parts", "mem", "rep"), "tp"),
        P("parts"),
        P(("parts", "tp"), "mem", None),
        P(("parts", "tp"), "mem", None),
        P(None, ("tp", "rep")),
        P(None, ("tp", "rep")),
        P(None, "tp"),
    )
    out_specs = P(("parts", "mem", "rep"), "tp")
    return jax.shard_map(shards, mesh=mesh, in_specs=in_specs, out_specs=out_specs, check_vma=False)
```

```python
import functools

import jax
import jax.numpy as jnp
from jax import lax
from jax.experimental import pallas as pl
from jax.experimental.pallas import tpu as pltpu
from jax.sharding import PartitionSpec as P

D = 4608
KERNEL = 4
DILATION = 3
SEQS = 4
EPSILON = 1e-06
RIM = 16
LANES = 128

F32 = jnp.float32
BF16 = jnp.bfloat16
I32 = jnp.int32


def iota(shape, axis):
    return lax.broadcasted_iota(I32, shape, axis)


def dot(a, b):
    return jnp.dot(a, b, preferred_element_type=F32)


def dot_nt(a, b, precision=None):
    return lax.dot_general(
        a, b, (((1,), (1,)), ((), ())), precision=precision, preferred_element_type=F32
    )


def unit(n, dtype):
    return (iota((n, n), 0) == iota((n, n), 1)).astype(F32).astype(dtype)


def to_bf16(x):
    return x.astype(F32).astype(BF16)


def place_kernel(
    ids_hbm, place_hbm, codes_hbm, scales_hbm, out_ref, codes_ref, scales_ref, ids_ref, place_ref, sems
):
    copies = [
        pltpu.make_async_copy(place_hbm, place_ref, sems.at[0]),
        pltpu.make_async_copy(ids_hbm, ids_ref, sems.at[1]),
        pltpu.make_async_copy(scales_hbm, scales_ref, sems.at[2]),
    ]
    for n in range(codes_ref.shape[0]):
        copies.append(
            pltpu.make_async_copy(codes_hbm.at[n], codes_ref.at[n], sems.at[3 + n])
        )
    for copy in copies:
        copy.start()
    copies[0].wait()
    place = place_ref[...]
    rows = place.shape[0]
    heads, tokens = ids_ref.shape
    eye = unit(LANES, BF16)
    table = jnp.concatenate(
        [dot_nt(eye, to_bf16(place >> 8)), dot_nt(eye, to_bf16(place & 255))], axis=0
    ).astype(BF16)
    copies[1].wait()
    for head in range(heads):
        row = ids_ref[head : head + 1, :]
        hot = to_bf16(iota((rows, tokens), 0) == (row >> 7))
        both = dot(table, hot)
        value = both[:LANES] * 256.0 + both[LANES:]
        chosen = jnp.where(iota(value.shape, 0) == (row & 127), value, 0.0)
        out_ref[head : head + 1, :] = jnp.sum(chosen, axis=0, keepdims=True).astype(I32)
    for copy in copies[2:]:
        copy.wait()


def decode_kernel(codes_ref, scales_ref, out_ref):
    heads, width, rows = codes_ref.shape
    blocks = scales_ref.shape[0]
    entry = iota((width, 2 * width), 0)
    column = iota((width, 2 * width), 1)
    column = jnp.where(column < width, column, column - width)
    parity = entry & column & 15
    parity = parity ^ (parity >> 2)
    parity = (parity ^ (parity >> 1)) & 1
    same = (entry >> 4) == (column >> 4)
    rotation = jnp.where(same, 0.25 - 0.5 * parity.astype(F32), 0.0).astype(BF16)
    for head in range(heads):
        factors = jnp.concatenate(
            [
                jnp.broadcast_to(scales_ref[b, head : head + 1, :].astype(F32), (16, rows))
                for b in range(blocks)
            ],
            axis=0,
        )
        scaled = codes_ref[head].astype(F32) * factors
        upper = scaled.astype(BF16)
        lower = (scaled - upper.astype(F32)).astype(BF16)
        out_ref[head] = dot(rotation, jnp.concatenate([upper, lower], axis=0)).astype(BF16)


def picked(local, table_ref, head):
    rows = table_ref.shape[2]
    hot = to_bf16(iota((rows, local.shape[1]), 0) == local[head : head + 1, :])
    return dot(table_ref[head], hot).astype(BF16)


def pick_kernel(begin, base_ref, ids_ref, table_ref, out_ref):
    heads, width, _ = table_ref.shape
    local = ids_ref[begin : begin + heads, :] - base_ref[0]
    for head in range(heads):
        out_ref[head * width : (head + 1) * width, :] = picked(local, table_ref, head)


def merge_kernel(*refs):
    total = refs[0][...].astype(F32)
    for other in refs[1:-1]:
        total = total + other[...].astype(F32)
    refs[-1][...] = total.astype(BF16)


def project_kernel(shifts, count, where_ref, *refs):
    pieces = len(shifts)
    first = 0 in shifts
    rims = refs[:pieces]
    bodies = refs[pieces : 2 * pieces]
    refs = refs[2 * pieces :]
    depth, tokens = bodies[0].shape
    rep = where_ref[0]
    tp = where_ref[1]
    if first:
        weights = refs[:4]
        key_ref, value_ref, rest, held, sems, rest_sems = refs[4:]
        half = held.shape[-1]

        def bring(target, far, which, n, s, sem):
            owner = lax.rem(tp + count - s, count)
            rows = pl.ds(pl.multiple_of(owner * depth, depth), depth)
            copy = pltpu.make_async_copy(
                weights[2 * far + which].at[rows, :],
                target.at[far, which, pl.ds(n * depth, depth), :],
                sem,
            )
            copy.start()
            return copy

        copies = [
            bring(held, far, which, 0, 0, sems.at[2 * far + which])
            for far in range(2)
            for which in (1, 0)
        ]
        later = []
    else:
        later = []
        rest, begun_keys, begun_values, hidden_halo, hidden = refs[:5]
        value_hbm, stats_ref, states, done, done_sems = refs[5:]
        held = rest
        half = held.shape[-1]
        for slot in range(2):
            states[slot, :RIM] = hidden_halo[:, slot * half : (slot + 1) * half]
            states[slot, RIM:] = hidden[:, slot * half : (slot + 1) * half]
    body = jnp.concatenate([b[...].astype(F32) for b in bodies], axis=0).T.astype(BF16)
    rim = jnp.concatenate([r[...].astype(F32) for r in rims], axis=0).T.astype(BF16)
    memory = jnp.concatenate([rim[LANES - RIM :], body], axis=0)
    sums = [0.0] * 4
    for far in range(2):
        slot = rep if far == 0 else 1 - rep
        fields = [None, None]
        for which in (1, 0):
            if first:
                copies[2 * far + 1 - which].wait()
                if far == 0 and which == 1:
                    later = [
                        bring(rest, f, w, n, n + 1, rest_sems.at[(2 * f + w) * (count - 1) + n])
                        for f in range(2)
                        for w in (1, 0)
                        for n in range(count - 1)
                    ]
            fields[which] = dot(memory, held[far, which])
            if not first and which == 1:
                done[far] = fields[1] + begun_values[slot]
                copy = pltpu.make_async_copy(done.at[far], value_hbm.at[slot], done_sems.at[far])
                copy.start()
                later.append(copy)
        if first:
            value_ref[slot] = fields[1]
            key_ref[slot] = fields[0]
        else:
            keys = fields[0] + begun_keys[slot]
            values = done[far]
            here = states[slot].astype(F32)
            terms = (here * here, keys * keys, here * keys, values * values)
            sums = [a + jnp.sum(t, axis=1, keepdims=True) for a, t in zip(sums, terms)]
    if not first:
        rows = memory.shape[0]
        lane = iota((rows, 8), 1)
        packed = jnp.zeros((rows, 8), F32)
        for k in range(4):
            packed = jnp.where(lane == k, sums[k], packed)
        stats_ref[...] = dot_nt(unit(8, F32), packed, lax.Precision.HIGHEST)
    for copy in later:
        copy.wait()


def prepare_kernel(chunk, taps_ref, value_hbm, value_ref, tap_ref, rows_ref, sems):
    half = rows_ref.shape[-1]
    tokens = value_ref.shape[1]
    copies = []
    for slot in range(2):
        for start in range(0, half, chunk):
            span = pl.ds(start, chunk)
            copy = pltpu.make_async_copy(
                value_hbm.at[slot, :, span], rows_ref.at[slot, :, span], sems.at[len(copies)]
            )
            copy.start()
            copies.append(copy)
    for slot in range(2):
        for start in range(0, half, LANES):
            size = min(LANES, half - start)
            span = slice(start, start + size)
            there = slice(slot * half + start, slot * half + start + size)
            if start % chunk == 0:
                copies[(slot * half + start) // chunk].wait()
            value_ref[slot, :, span] = rows_ref[slot, RIM:, span]
            for tap in range(1, KERNEL):
                lag = DILATION * tap
                rows = rows_ref[slot, RIM - lag : RIM - lag + tokens, span]
                tap_ref[tap - 1, slot, :, span] = taps_ref[tap : tap + 1, there] * rows


def finish_kernel(count, step, keep_ref, *refs):
    stats = refs[:count]
    value_ref, tap_ref, hidden_ref, taps_ref, out_hbm = refs[count : count + 5]
    columns, gates, factors, out_ref, sems = refs[count + 5 :]
    half = value_ref.shape[-1]
    tokens, width = out_ref.shape
    total = stats[0][...]
    for other in stats[1:]:
        total = total + other[...]
    inverse_states = lax.rsqrt(total[0:1] / D + EPSILON)
    inverse_keys = lax.rsqrt(total[1:2] / D + EPSILON)
    gate = jax.nn.sigmoid(total[2:3] * inverse_states * inverse_keys / D**0.5)
    factor = gate * lax.rsqrt(gate * gate * total[3:4] / D + EPSILON)
    factor = jnp.where((iota(factor.shape, 1) < RIM) & (keep_ref[0] == 0), 0.0, factor)
    line = iota(total.shape, 0)
    both = jnp.where(line == 0, gate, jnp.where(line == 1, factor, 0.0))
    columns[...] = dot_nt(unit(total.shape[1], F32), both, lax.Precision.HIGHEST)
    gates[...] = jnp.broadcast_to(columns[RIM:, 0:1], gates.shape)
    for tap in range(KERNEL):
        lag = DILATION * tap
        factors[tap] = jnp.broadcast_to(
            columns[RIM - lag : RIM - lag + tokens, 1:2], factors.shape[1:]
        )
    copies = []
    for slot in range(2):
        for start in range(0, half, LANES):
            size = min(LANES, half - start)
            span = slice(start, start + size)
            there = slice(slot * half + start, slot * half + start + size)
            values = value_ref[slot, :, span]
            conv = taps_ref[0:1, there] * values * factors[0, :, :size]
            for tap in range(1, KERNEL):
                conv = conv + tap_ref[tap - 1, slot, :, span] * factors[tap, :, :size]
            gated = values * gates[:, :size]
            out_ref[:, there] = (
                hidden_ref[:, there].astype(F32) + jax.nn.silu(conv) + gated
            ).astype(BF16)
            if there.stop % step == 0:
                ready = pl.ds(there.stop - step, step)
                copy = pltpu.make_async_copy(
                    out_ref.at[:, ready], out_hbm.at[:, ready], sems.at[len(copies)]
                )
                copy.start()
                copies.append(copy)
    for copy in copies:
        copy.wait()


def whole(array):
    return pl.BlockSpec(array.shape, lambda *_: (0,) * array.ndim)


def in_hbm(array):
    return pltpu.with_memory_space_constraint(array, pltpu.HBM)


def after(array, *others):
    return lax.optimization_barrier((array, *others))[0]


def limit(mib):
    return pltpu.CompilerParams(vmem_limit_bytes=mib << 20)


def scattered_sum(stored, decoded, here, meanwhile, settled):
    mems = lax.axis_size("mem")
    heads, width, rows = decoded.shape
    tokens = stored.shape[1]
    asked = lax.all_gather(stored, "mem", axis=0)
    partial = pl.pallas_call(
        functools.partial(pick_kernel, 0),
        grid=(mems,),
        in_specs=[
            pl.BlockSpec(memory_space=pltpu.SMEM),
            pl.BlockSpec((None, heads, tokens), lambda m: (m, 0, 0)),
            whole(decoded),
        ],
        out_specs=pl.BlockSpec((None, heads * width, tokens), lambda m: (m, 0, 0)),
        out_shape=jax.ShapeDtypeStruct((mems, heads * width, tokens), BF16),
        compiler_params=limit(16),
        name="pick_all",
    )((here * rows).astype(I32).reshape(1), asked, decoded)
    total = lax.psum_scatter(partial, "mem", scatter_dimension=0, tiled=False)
    return total, meanwhile(partial), settled


def line_sum(stored, decoded, here, meanwhile, settled):
    heads, width, rows = decoded.shape
    tokens = stored.shape[1]
    base = (here * rows).astype(I32).reshape(1)
    block = jax.ShapeDtypeStruct((heads * width, tokens), BF16)

    def crossing(x, pairs):
        return lax.ppermute(x, ("mem", "rep"), [(2 * a + b, 2 * c + d) for a, b, c, d in pairs])

    def pick(ids, begin=0):
        return pl.pallas_call(
            functools.partial(pick_kernel, begin),
            in_specs=[pl.BlockSpec(memory_space=pltpu.SMEM)]
            + [pl.BlockSpec(memory_space=pltpu.VMEM)] * 2,
            out_shape=block,
            compiler_params=limit(8),
            name="pick_rows",
        )(base, ids, decoded)

    def send(x, *pairs):
        return lax.ppermute(x, "mem", pairs)

    first = lax.ppermute(stored, "mem", [(m, m ^ 3) for m in range(4)])
    both = crossing(
        jnp.concatenate([stored, first]),
        [(m, r, m ^ 2, r ^ int(m in (1, 2))) for m in range(4) for r in range(2)],
    )
    rows_3 = pick(first)
    rows_3, both = lax.optimization_barrier((rows_3, both))
    inward = send(rows_3, (0, 1), (3, 2))
    across = send(rows_3, (1, 2), (2, 1))
    rows_2 = pick(both)
    ready, both, settled = lax.optimization_barrier((rows_2, both, settled))
    past = crossing(ready, [(m, r, m ^ 2, r ^ 1) for m in (0, 3) for r in range(2)])
    rows_1 = pick(both, heads)
    own = pick(after(stored, rows_1))
    beside = crossing(
        rows_1, [(m, r, m ^ 1, r ^ int(m in (0, 3))) for m in range(4) for r in range(2)]
    )
    onward = after(rows_2, rows_1, own) + inward
    onward = send(onward, (1, 3), (2, 0))
    other = meanwhile(across)
    own, other = lax.optimization_barrier((own + beside + past, other))
    memory = pl.pallas_call(
        merge_kernel,
        in_specs=[pl.BlockSpec(memory_space=pltpu.VMEM)] * 3,
        out_shape=block,
        compiler_params=limit(4),
        name="merge",
    )(own, across, onward)
    return memory, other, settled


def shards(
    hidden, row_ids, row_place, table_codes, table_scales, key_weight, value_weight, conv_weight
):
    mems = lax.axis_size("mem")
    tps = lax.axis_size("tp")
    reps = lax.axis_size("rep")
    blocks = mems * reps
    tokens, heads = row_ids.shape
    rows, width = table_codes.shape[1:]
    depth = heads * width
    half = key_weight.shape[1]
    seq_length = tokens * blocks // SEQS
    assert reps == 2 and seq_length % tokens == 0 and row_place.shape[0] % LANES == 0
    block = lax.axis_index(("mem", "rep"))
    smem = pl.BlockSpec(memory_space=pltpu.SMEM)

    anywhere = pl.BlockSpec(memory_space=pl.ANY)
    resident = pl.BlockSpec(memory_space=pltpu.VMEM)
    places = row_place.reshape(-1, LANES)
    codes = table_codes.transpose(0, 2, 1)
    scales = table_scales.transpose(2, 0, 1)
    stored, codes, scales = pl.pallas_call(
        place_kernel,
        in_specs=[anywhere] * 4,
        out_specs=(resident,) * 3,
        out_shape=(
            jax.ShapeDtypeStruct((heads, tokens), I32),
            jax.ShapeDtypeStruct(codes.shape, BF16),
            jax.ShapeDtypeStruct(scales.shape, BF16),
        ),
        scratch_shapes=[
            pltpu.VMEM((heads, tokens), I32),
            pltpu.VMEM(places.shape, I32),
            pltpu.SemaphoreType.DMA((heads + 3,)),
        ],
        compiler_params=limit(4),
        name="place_rows",
    )(*[in_hbm(x) for x in (row_ids.T, places, codes, scales)])
    decoded = pl.pallas_call(
        decode_kernel,
        in_specs=[resident] * 2,
        out_specs=resident,
        out_shape=jax.ShapeDtypeStruct(codes.shape, BF16),
        compiler_params=limit(6),
        name="decode_tables",
    )(codes, scales)
    here = lax.axis_index("mem")
    other_key = lax.ppermute(key_weight, "rep", [(0, 1), (1, 0)])
    other_value = lax.ppermute(value_weight, "rep", [(0, 1), (1, 0)])
    needed = [(i, i + 1) for i in range(blocks - 1) if (i + 1) * tokens % seq_length]

    def meanwhile(token):
        tail = after(hidden[tokens - RIM :], token)
        return lax.ppermute(tail, ("mem", "rep"), needed)

    summed = line_sum if mems == 4 else scattered_sum
    memory, hidden_halo, others = summed(
        stored, decoded, here, meanwhile, (other_key, other_value)
    )
    weights = [in_hbm(w) for w in (key_weight, value_weight, *others)]

    where = jnp.stack([lax.axis_index("rep"), lax.axis_index("tp")]).astype(I32)
    extended = tokens + RIM
    bodies = [memory] + [
        lax.ppermute(memory, "tp", [(i, (i + s) % tps) for i in range(tps)])
        for s in range(1, tps)
    ]

    def next_rim(rim, s):
        pairs = [
            (
                (a // reps * tps + i) * reps + a % reps,
                (b // reps * tps + (i + s) % tps) * reps + b % reps,
            )
            for a, b in needed
            for i in range(tps)
        ]
        return lax.ppermute(rim, ("mem", "tp", "rep"), pairs)

    rim = memory[:, tokens - LANES :]
    rims = [next_rim(rim, s) for s in range(tps)]
    others = tps - 1
    field = jax.ShapeDtypeStruct((2, extended, half), F32)
    *begun, rest = pl.pallas_call(
        functools.partial(project_kernel, (0,), tps),
        in_specs=[smem] + [resident] * 2 + [anywhere] * 4,
        out_specs=(resident,) * 3,
        out_shape=(field, field, pltpu.VMEM((2, 2, others * depth, half), BF16)),
        scratch_shapes=[
            pltpu.VMEM((2, 2, depth, half), BF16),
            pltpu.SemaphoreType.DMA((4,)),
            pltpu.SemaphoreType.DMA((4 * others,)),
        ],
        compiler_params=limit(12),
        name="project_own",
    )(where, rims[0], memory, *weights)
    values, stats = pl.pallas_call(
        functools.partial(project_kernel, tuple(range(1, tps)), tps),
        in_specs=[smem] + [resident] * (2 * others + 5),
        out_specs=(pl.BlockSpec(memory_space=pltpu.HBM), resident),
        out_shape=(pltpu.HBM(field.shape, F32), jax.ShapeDtypeStruct((8, extended), F32)),
        scratch_shapes=[
            pltpu.VMEM((2, extended, half), BF16),
            pltpu.VMEM((2, extended, half), F32),
            pltpu.SemaphoreType.DMA((2,)),
        ],
        compiler_params=limit(14),
        name="project_others",
    )(
        where,
        *rims[1:],
        *bodies[1:],
        rest,
        *begun,
        hidden_halo,
        hidden,
    )

    all_stats = [stats] + [
        lax.ppermute(stats, "tp", [(i, (i + s) % tps) for i in range(tps)]) for s in range(1, tps)
    ]
    keep = (block * tokens % seq_length != 0).astype(I32).reshape(1)
    step = 2 * half
    if half % LANES == 0:
        step = next(c for c in (384, 256, 128) if half % c == 0)
    chunk = min(step, half)
    body = (2, tokens, half)
    values, products = pl.pallas_call(
        functools.partial(prepare_kernel, chunk),
        in_specs=[resident, anywhere],
        out_specs=(resident,) * 2,
        out_shape=(
            jax.ShapeDtypeStruct(body, F32),
            jax.ShapeDtypeStruct((KERNEL - 1, *body), F32),
        ),
        scratch_shapes=[
            pltpu.VMEM((2, extended, half), F32),
            pltpu.SemaphoreType.DMA((2 * half // chunk,)),
        ],
        compiler_params=limit(6),
        name="prepare",
    )(conv_weight, in_hbm(values))
    return pl.pallas_call(
        functools.partial(finish_kernel, tps, step),
        in_specs=[smem] + [resident] * (tps + 4),
        out_specs=anywhere,
        out_shape=jax.ShapeDtypeStruct((tokens, 2 * half), BF16),
        scratch_shapes=[
            pltpu.VMEM((extended, 8), F32),
            pltpu.VMEM((tokens, LANES), F32),
            pltpu.VMEM((KERNEL, tokens, LANES), F32),
            pltpu.VMEM((tokens, 2 * half), BF16),
            pltpu.SemaphoreType.DMA((2 * half // step,)),
        ],
        compiler_params=limit(6),
        name="finish",
    )(keep, *all_stats, values, products, hidden, conv_weight)


def solution(mesh):
    in_specs = (
        P(("parts", "mem", "rep"), "tp"),
        P(("parts", "mem", "rep"), "tp"),
        P("parts"),
        P(("parts", "tp"), "mem", None),
        P(("parts", "tp"), "mem", None),
        P(None, ("tp", "rep")),
        P(None, ("tp", "rep")),
        P(None, "tp"),
    )
    out_specs = P(("parts", "mem", "rep"), "tp")
    return jax.shard_map(shards, mesh=mesh, in_specs=in_specs, out_specs=out_specs, check_vma=False)
```

```python
import functools

import jax
import jax.numpy as jnp
from jax import lax
from jax.experimental import pallas as pl
from jax.experimental.pallas import tpu as pltpu
from jax.sharding import PartitionSpec as P

D = 4608
KERNEL = 4
DILATION = 3
SEQS = 4
EPSILON = 1e-06
RIM = 16
LANES = 128

F32 = jnp.float32
BF16 = jnp.bfloat16
I32 = jnp.int32


def iota(shape, axis):
    return lax.broadcasted_iota(I32, shape, axis)


def dot(a, b):
    return jnp.dot(a, b, preferred_element_type=F32)


def dot_nt(a, b, precision=None):
    return lax.dot_general(
        a, b, (((1,), (1,)), ((), ())), precision=precision, preferred_element_type=F32
    )


def unit(n, dtype):
    return (iota((n, n), 0) == iota((n, n), 1)).astype(F32).astype(dtype)


def to_bf16(x):
    return x.astype(F32).astype(BF16)


def place_kernel(
    ids_hbm, place_hbm, codes_hbm, scales_hbm, out_ref, codes_ref, scales_ref, ids_ref, place_ref, sems
):
    copies = [
        pltpu.make_async_copy(place_hbm, place_ref, sems.at[0]),
        pltpu.make_async_copy(ids_hbm, ids_ref, sems.at[1]),
        pltpu.make_async_copy(scales_hbm, scales_ref, sems.at[2]),
    ]
    for n in range(codes_ref.shape[0]):
        copies.append(
            pltpu.make_async_copy(codes_hbm.at[n], codes_ref.at[n], sems.at[3 + n])
        )
    for copy in copies:
        copy.start()
    copies[0].wait()
    place = place_ref[...]
    rows = place.shape[0]
    heads, tokens = ids_ref.shape
    eye = unit(LANES, BF16)
    table = jnp.concatenate(
        [dot_nt(eye, to_bf16(place >> 8)), dot_nt(eye, to_bf16(place & 255))], axis=0
    ).astype(BF16)
    copies[1].wait()
    for head in range(heads):
        row = ids_ref[head : head + 1, :]
        hot = to_bf16(iota((rows, tokens), 0) == (row >> 7))
        both = dot(table, hot)
        value = both[:LANES] * 256.0 + both[LANES:]
        chosen = jnp.where(iota(value.shape, 0) == (row & 127), value, 0.0)
        out_ref[head : head + 1, :] = jnp.sum(chosen, axis=0, keepdims=True).astype(I32)
    for copy in copies[2:]:
        copy.wait()


def decode_kernel(codes_ref, scales_ref, out_ref):
    heads, width, rows = codes_ref.shape
    blocks = scales_ref.shape[0]
    entry = iota((width, 2 * width), 0)
    column = iota((width, 2 * width), 1)
    column = jnp.where(column < width, column, column - width)
    parity = entry & column & 15
    parity = parity ^ (parity >> 2)
    parity = (parity ^ (parity >> 1)) & 1
    same = (entry >> 4) == (column >> 4)
    rotation = jnp.where(same, 0.25 - 0.5 * parity.astype(F32), 0.0).astype(BF16)
    for head in range(heads):
        factors = jnp.concatenate(
            [
                jnp.broadcast_to(scales_ref[b, head : head + 1, :].astype(F32), (16, rows))
                for b in range(blocks)
            ],
            axis=0,
        )
        scaled = codes_ref[head].astype(F32) * factors
        upper = scaled.astype(BF16)
        lower = (scaled - upper.astype(F32)).astype(BF16)
        out_ref[head] = dot(rotation, jnp.concatenate([upper, lower], axis=0)).astype(BF16)


def picked(local, table_ref, head):
    rows = table_ref.shape[2]
    hot = to_bf16(iota((rows, local.shape[1]), 0) == local[head : head + 1, :])
    return dot(table_ref[head], hot).astype(BF16)


def pick_kernel(base_ref, ids_ref, table_ref, out_ref):
    heads, width, _ = table_ref.shape
    local = ids_ref[...] - base_ref[0]
    for head in range(heads):
        out_ref[head * width : (head + 1) * width, :] = picked(local, table_ref, head)


def merge_kernel(*refs):
    total = refs[0][...].astype(F32)
    for other in refs[1:-1]:
        total = total + other[...].astype(F32)
    refs[-1][...] = total.astype(BF16)


def fetch(count, tp, depth, source, target, shifts, sems):
    copies = []
    for n, s in enumerate(shifts):
        owner = lax.rem(tp + count - s, count)
        rows = pl.ds(pl.multiple_of(owner * depth, depth), depth)
        copy = pltpu.make_async_copy(
            source.at[rows, :], target.at[pl.ds(n * depth, depth), :], sems.at[n]
        )
        copy.start()
        copies.append(copy)
    return copies


def await_all(copies):
    for copy in copies:
        copy.wait()


def with_rim(rims, bodies):
    body = jnp.concatenate([b[...].astype(F32) for b in bodies], axis=0).T.astype(BF16)
    rim = jnp.concatenate([r[...].astype(F32) for r in rims], axis=0).T.astype(BF16)
    return jnp.concatenate([rim[LANES - RIM :], body], axis=0)


def project_own_kernel(count, where_ref, rim_ref, body_ref, *refs):
    weights, hidden_halo, hidden = refs[:4], refs[4], refs[5]
    key_ref, value_ref, next_ref, states_ref, power_ref, held, sems, next_sems = refs[6:]
    half = value_ref.shape[-1]
    depth = body_ref.shape[0]
    rep = where_ref[0]
    tp = where_ref[1]
    order = [(far, which) for far in range(2) for which in (1, 0)]
    copies = {
        (far, which): fetch(
            count, tp, depth, weights[2 * far + which], held.at[far, which], (0,),
            sems.at[2 * far + which],
        )
        for far, which in order
    }
    power = 0.0
    for slot in range(2):
        span = slice(slot * half, (slot + 1) * half)
        states_ref[slot, :RIM] = hidden_halo[:, span]
        states_ref[slot, RIM:] = hidden[:, span]
        here = states_ref[slot].astype(F32)
        power = power + jnp.sum(here * here, axis=1, keepdims=True)
    power_ref[...] = jnp.broadcast_to(power, power_ref.shape)
    memory = with_rim([rim_ref], [body_ref])
    later = []
    for far, which in order:
        slot = rep if far == 0 else 1 - rep
        await_all(copies[far, which])
        if not later:
            for w in (1, 0):
                later += fetch(
                    count, tp, depth, weights[w], next_ref.at[w], range(1, count), next_sems.at[w]
                )
        target = value_ref if which == 1 else key_ref
        target[slot] = dot(memory, held[far, which])
    await_all(later)


def project_others_kernel(count, where_ref, *refs):
    pieces = count - 1
    rims, bodies = refs[:pieces], refs[pieces : 2 * pieces]
    weights = refs[2 * pieces : 2 * pieces + 2]
    next_ref, begun_keys, begun_values, states_ref, power_ref = refs[2 * pieces + 2 :][:5]
    value_hbm, stats_ref, held, sems, done, done_sems = refs[2 * pieces + 7 :]
    half = held.shape[-1]
    depth = bodies[0].shape[0]
    rep = where_ref[0]
    tp = where_ref[1]
    copies = {
        which: fetch(
            count, tp, depth, weights[which], held.at[which], range(1, count), sems.at[which]
        )
        for which in (1, 0)
    }
    memory = with_rim(rims, bodies)
    sums = [0.0] * 3
    later = []
    for far in range(2):
        slot = rep if far == 0 else 1 - rep
        fields = [None, None]
        for which in (1, 0):
            if far == 1:
                await_all(copies[which])
            fields[which] = dot(memory, next_ref[which] if far == 0 else held[which])
            if which == 1:
                done[far] = fields[1] + begun_values[slot]
                copy = pltpu.make_async_copy(done.at[far], value_hbm.at[slot], done_sems.at[far])
                copy.start()
                later.append(copy)
        keys = fields[0] + begun_keys[slot]
        values = done[far]
        terms = (keys * keys, states_ref[slot].astype(F32) * keys, values * values)
        sums = [a + jnp.sum(t, axis=1, keepdims=True) for a, t in zip(sums, terms)]
    packed = power_ref[...]
    lane = iota(packed.shape, 1)
    for k in range(3):
        packed = jnp.where(lane == k + 1, sums[k], packed)
    stats_ref[...] = dot_nt(unit(8, F32), packed, lax.Precision.HIGHEST)
    await_all(later)


def prepare_kernel(chunk, taps_ref, value_hbm, value_ref, tap_ref, rows_ref, sems):
    half = rows_ref.shape[-1]
    tokens = value_ref.shape[1]
    copies = []
    for slot in range(2):
        for start in range(0, half, chunk):
            span = pl.ds(start, chunk)
            copy = pltpu.make_async_copy(
                value_hbm.at[slot, :, span], rows_ref.at[slot, :, span], sems.at[len(copies)]
            )
            copy.start()
            copies.append(copy)
    for slot in range(2):
        for start in range(0, half, LANES):
            size = min(LANES, half - start)
            span = slice(start, start + size)
            there = slice(slot * half + start, slot * half + start + size)
            if start % chunk == 0:
                copies[(slot * half + start) // chunk].wait()
            value_ref[slot, :, span] = rows_ref[slot, RIM:, span]
            for tap in range(1, KERNEL):
                lag = DILATION * tap
                rows = rows_ref[slot, RIM - lag : RIM - lag + tokens, span]
                tap_ref[tap - 1, slot, :, span] = taps_ref[tap : tap + 1, there] * rows


def finish_kernel(count, step, keep_ref, *refs):
    stats = refs[:count]
    value_ref, tap_ref, hidden_ref, taps_ref, out_hbm = refs[count : count + 5]
    columns, gates, factors, out_ref, sems = refs[count + 5 :]
    half = value_ref.shape[-1]
    tokens, width = out_ref.shape
    total = stats[0][...]
    for other in stats[1:]:
        total = total + other[...]
    inverse_states = lax.rsqrt(total[0:1] / D + EPSILON)
    inverse_keys = lax.rsqrt(total[1:2] / D + EPSILON)
    gate = jax.nn.sigmoid(total[2:3] * inverse_states * inverse_keys / D**0.5)
    factor = gate * lax.rsqrt(gate * gate * total[3:4] / D + EPSILON)
    factor = jnp.where((iota(factor.shape, 1) < RIM) & (keep_ref[0] == 0), 0.0, factor)
    line = iota(total.shape, 0)
    both = jnp.where(line == 0, gate, jnp.where(line == 1, factor, 0.0))
    columns[...] = dot_nt(unit(total.shape[1], F32), both, lax.Precision.HIGHEST)
    gates[...] = jnp.broadcast_to(columns[RIM:, 0:1], gates.shape)
    for tap in range(KERNEL):
        lag = DILATION * tap
        factors[tap] = jnp.broadcast_to(
            columns[RIM - lag : RIM - lag + tokens, 1:2], factors.shape[1:]
        )
    copies = []
    for slot in range(2):
        for start in range(0, half, LANES):
            size = min(LANES, half - start)
            span = slice(start, start + size)
            there = slice(slot * half + start, slot * half + start + size)
            values = value_ref[slot, :, span]
            conv = taps_ref[0:1, there] * values * factors[0, :, :size]
            for tap in range(1, KERNEL):
                conv = conv + tap_ref[tap - 1, slot, :, span] * factors[tap, :, :size]
            gated = values * gates[:, :size]
            out_ref[:, there] = (
                hidden_ref[:, there].astype(F32) + jax.nn.silu(conv) + gated
            ).astype(BF16)
            if there.stop % step == 0:
                ready = pl.ds(there.stop - step, step)
                copy = pltpu.make_async_copy(
                    out_ref.at[:, ready], out_hbm.at[:, ready], sems.at[len(copies)]
                )
                copy.start()
                copies.append(copy)
    for copy in copies:
        copy.wait()


def whole(array):
    return pl.BlockSpec(array.shape, lambda *_: (0,) * array.ndim)


def in_hbm(array):
    return pltpu.with_memory_space_constraint(array, pltpu.HBM)


def after(array, *others):
    return lax.optimization_barrier((array, *others))[0]


def limit(mib):
    return pltpu.CompilerParams(vmem_limit_bytes=mib << 20)


def scattered_sum(stored, decoded, here, meanwhile, settled):
    mems = lax.axis_size("mem")
    heads, width, rows = decoded.shape
    tokens = stored.shape[1]
    asked = lax.all_gather(stored, "mem", axis=0)
    partial = pl.pallas_call(
        pick_kernel,
        grid=(mems,),
        in_specs=[
            pl.BlockSpec(memory_space=pltpu.SMEM),
            pl.BlockSpec((None, heads, tokens), lambda m: (m, 0, 0)),
            whole(decoded),
        ],
        out_specs=pl.BlockSpec((None, heads * width, tokens), lambda m: (m, 0, 0)),
        out_shape=jax.ShapeDtypeStruct((mems, heads * width, tokens), BF16),
        compiler_params=limit(16),
        name="pick_all",
    )((here * rows).astype(I32).reshape(1), asked, decoded)
    total = lax.psum_scatter(partial, "mem", scatter_dimension=0, tiled=False)
    return total, meanwhile(partial), settled


def line_sum(stored, decoded, here, meanwhile, settled):
    heads, width, rows = decoded.shape
    tokens = stored.shape[1]
    base = (here * rows).astype(I32).reshape(1)
    block = jax.ShapeDtypeStruct((heads * width, tokens), BF16)

    def ask(ids, x):
        return lax.ppermute(ids, "mem", [(i, i ^ x) for i in range(4)])

    def crossing(x, pairs):
        return lax.ppermute(x, ("mem", "rep"), [(2 * a + b, 2 * c + d) for a, b, c, d in pairs])

    def pick(ids):
        return pl.pallas_call(
            pick_kernel,
            in_specs=[pl.BlockSpec(memory_space=pltpu.SMEM)]
            + [pl.BlockSpec(memory_space=pltpu.VMEM)] * 2,
            out_shape=block,
            compiler_params=limit(8),
            name="pick_rows",
        )(base, ids, decoded)

    def send(x, *pairs):
        return lax.ppermute(x, "mem", pairs)

    first = ask(stored, 3)
    second = crossing(
        stored,
        [(m, r, m ^ 2, r ^ int(m in (1, 2))) for m in range(4) for r in range(2)],
    )
    third = ask(stored, 1)
    rows_3 = pick(first)
    rows_3, second, third = lax.optimization_barrier((rows_3, second, third))
    inward = send(rows_3, (0, 1), (3, 2))
    across = send(rows_3, (1, 2), (2, 1))
    rows_2 = pick(after(second, rows_3))
    third, settled = lax.optimization_barrier((after(third, rows_2), settled))
    past = crossing(rows_2, [(m, r, m ^ 2, r ^ 1) for m in (0, 3) for r in range(2)])
    rows_1 = pick(third)
    own = pick(after(stored, rows_1))
    beside = send(rows_1, (0, 1), (1, 0), (2, 3), (3, 2))
    onward = after(rows_2, rows_1, own) + inward
    onward = send(onward, (1, 3), (2, 0))
    other = meanwhile(across)
    own, other = lax.optimization_barrier((own + past + beside, other))
    memory = pl.pallas_call(
        merge_kernel,
        in_specs=[pl.BlockSpec(memory_space=pltpu.VMEM)] * 3,
        out_shape=block,
        compiler_params=limit(4),
        name="merge",
    )(own, across, onward)
    return memory, other, settled


def shards(
    hidden, row_ids, row_place, table_codes, table_scales, key_weight, value_weight, conv_weight
):
    mems = lax.axis_size("mem")
    tps = lax.axis_size("tp")
    reps = lax.axis_size("rep")
    blocks = mems * reps
    tokens, heads = row_ids.shape
    rows, width = table_codes.shape[1:]
    depth = heads * width
    half = key_weight.shape[1]
    seq_length = tokens * blocks // SEQS
    assert reps == 2 and seq_length % tokens == 0 and row_place.shape[0] % LANES == 0
    block = lax.axis_index(("mem", "rep"))
    smem = pl.BlockSpec(memory_space=pltpu.SMEM)

    anywhere = pl.BlockSpec(memory_space=pl.ANY)
    resident = pl.BlockSpec(memory_space=pltpu.VMEM)
    places = row_place.reshape(-1, LANES)
    codes = table_codes.transpose(0, 2, 1)
    scales = table_scales.transpose(2, 0, 1)
    stored, codes, scales = pl.pallas_call(
        place_kernel,
        in_specs=[anywhere] * 4,
        out_specs=(resident,) * 3,
        out_shape=(
            jax.ShapeDtypeStruct((heads, tokens), I32),
            jax.ShapeDtypeStruct(codes.shape, BF16),
            jax.ShapeDtypeStruct(scales.shape, BF16),
        ),
        scratch_shapes=[
            pltpu.VMEM((heads, tokens), I32),
            pltpu.VMEM(places.shape, I32),
            pltpu.SemaphoreType.DMA((heads + 3,)),
        ],
        compiler_params=limit(4),
        name="place_rows",
    )(*[in_hbm(x) for x in (row_ids.T, places, codes, scales)])
    decoded = pl.pallas_call(
        decode_kernel,
        in_specs=[resident] * 2,
        out_specs=resident,
        out_shape=jax.ShapeDtypeStruct(codes.shape, BF16),
        compiler_params=limit(6),
        name="decode_tables",
    )(codes, scales)
    here = lax.axis_index("mem")
    other_key = lax.ppermute(key_weight, "rep", [(0, 1), (1, 0)])
    other_value = lax.ppermute(value_weight, "rep", [(0, 1), (1, 0)])
    needed = [(i, i + 1) for i in range(blocks - 1) if (i + 1) * tokens % seq_length]

    def meanwhile(token):
        tail = after(hidden[tokens - RIM :], token)
        return lax.ppermute(tail, ("mem", "rep"), needed)

    summed = line_sum if mems == 4 else scattered_sum
    memory, hidden_halo, others = summed(
        stored, decoded, here, meanwhile, (other_key, other_value)
    )
    weights = [in_hbm(w) for w in (key_weight, value_weight, *others)]

    where = jnp.stack([lax.axis_index("rep"), lax.axis_index("tp")]).astype(I32)
    extended = tokens + RIM
    bodies = [memory] + [
        lax.ppermute(memory, "tp", [(i, (i + s) % tps) for i in range(tps)])
        for s in range(1, tps)
    ]

    def next_rim(rim, s):
        pairs = [
            (
                (a // reps * tps + i) * reps + a % reps,
                (b // reps * tps + (i + s) % tps) * reps + b % reps,
            )
            for a, b in needed
            for i in range(tps)
        ]
        return lax.ppermute(rim, ("mem", "tp", "rep"), pairs)

    rim = memory[:, tokens - LANES :]
    rims = [next_rim(rim, s) for s in range(tps)]
    others = tps - 1
    field = jax.ShapeDtypeStruct((2, extended, half), F32)
    *begun, following, states, power = pl.pallas_call(
        functools.partial(project_own_kernel, tps),
        in_specs=[smem] + [resident] * 2 + [anywhere] * 4 + [resident] * 2,
        out_specs=(resident,) * 5,
        out_shape=(
            field,
            field,
            pltpu.VMEM((2, others * depth, half), BF16),
            jax.ShapeDtypeStruct((2, extended, half), BF16),
            jax.ShapeDtypeStruct((extended, 8), F32),
        ),
        scratch_shapes=[
            pltpu.VMEM((2, 2, depth, half), BF16),
            pltpu.SemaphoreType.DMA((4, 1)),
            pltpu.SemaphoreType.DMA((2, others)),
        ],
        compiler_params=limit(12),
        name="project_own",
    )(where, rims[0], memory, *weights, hidden_halo, hidden)
    values, stats = pl.pallas_call(
        functools.partial(project_others_kernel, tps),
        in_specs=[smem] + [resident] * (2 * others) + [anywhere] * 2 + [resident] * 5,
        out_specs=(pl.BlockSpec(memory_space=pltpu.HBM), resident),
        out_shape=(pltpu.HBM(field.shape, F32), jax.ShapeDtypeStruct((8, extended), F32)),
        scratch_shapes=[
            pltpu.VMEM((2, others * depth, half), BF16),
            pltpu.SemaphoreType.DMA((2, others)),
            pltpu.VMEM((2, extended, half), F32),
            pltpu.SemaphoreType.DMA((2,)),
        ],
        compiler_params=limit(14),
        name="project_others",
    )(where, *rims[1:], *bodies[1:], *weights[2:], following, *begun, states, power)

    all_stats = [stats] + [
        lax.ppermute(stats, "tp", [(i, (i + s) % tps) for i in range(tps)]) for s in range(1, tps)
    ]
    keep = (block * tokens % seq_length != 0).astype(I32).reshape(1)
    step = 2 * half
    if half % LANES == 0:
        step = next(c for c in (384, 256, 128) if half % c == 0)
    chunk = min(step, half)
    body = (2, tokens, half)
    values, products = pl.pallas_call(
        functools.partial(prepare_kernel, chunk),
        in_specs=[resident, anywhere],
        out_specs=(resident,) * 2,
        out_shape=(
            jax.ShapeDtypeStruct(body, F32),
            jax.ShapeDtypeStruct((KERNEL - 1, *body), F32),
        ),
        scratch_shapes=[
            pltpu.VMEM((2, extended, half), F32),
            pltpu.SemaphoreType.DMA((2 * half // chunk,)),
        ],
        compiler_params=limit(6),
        name="prepare",
    )(conv_weight, in_hbm(values))
    return pl.pallas_call(
        functools.partial(finish_kernel, tps, step),
        in_specs=[smem] + [resident] * (tps + 4),
        out_specs=anywhere,
        out_shape=jax.ShapeDtypeStruct((tokens, 2 * half), BF16),
        scratch_shapes=[
            pltpu.VMEM((extended, 8), F32),
            pltpu.VMEM((tokens, LANES), F32),
            pltpu.VMEM((KERNEL, tokens, LANES), F32),
            pltpu.VMEM((tokens, 2 * half), BF16),
            pltpu.SemaphoreType.DMA((2 * half // step,)),
        ],
        compiler_params=limit(6),
        name="finish",
    )(keep, *all_stats, values, products, hidden, conv_weight)


def solution(mesh):
    in_specs = (
        P(("parts", "mem", "rep"), "tp"),
        P(("parts", "mem", "rep"), "tp"),
        P("parts"),
        P(("parts", "tp"), "mem", None),
        P(("parts", "tp"), "mem", None),
        P(None, ("tp", "rep")),
        P(None, ("tp", "rep")),
        P(None, "tp"),
    )
    out_specs = P(("parts", "mem", "rep"), "tp")
    return jax.shard_map(shards, mesh=mesh, in_specs=in_specs, out_specs=out_specs, check_vma=False)
```

```python
import functools

import jax
import jax.numpy as jnp
from jax import lax
from jax.experimental import pallas as pl
from jax.experimental.pallas import tpu as pltpu
from jax.sharding import PartitionSpec as P

D = 4608
KERNEL = 4
DILATION = 3
SEQS = 4
EPSILON = 1e-06
RIM = 16
LANES = 128

F32 = jnp.float32
BF16 = jnp.bfloat16
I32 = jnp.int32


def iota(shape, axis):
    return lax.broadcasted_iota(I32, shape, axis)


def dot(a, b):
    return jnp.dot(a, b, preferred_element_type=F32)


def dot_nt(a, b, precision=None):
    return lax.dot_general(
        a, b, (((1,), (1,)), ((), ())), precision=precision, preferred_element_type=F32
    )


def unit(n, dtype):
    return (iota((n, n), 0) == iota((n, n), 1)).astype(F32).astype(dtype)


def to_bf16(x):
    return x.astype(F32).astype(BF16)


def place_kernel(
    ids_hbm, place_hbm, codes_hbm, scales_hbm, out_ref, codes_ref, scales_ref, ids_ref, place_ref, sems
):
    copies = [
        pltpu.make_async_copy(place_hbm, place_ref, sems.at[0]),
        pltpu.make_async_copy(ids_hbm, ids_ref, sems.at[1]),
        pltpu.make_async_copy(scales_hbm, scales_ref, sems.at[2]),
    ]
    for n in range(codes_ref.shape[0]):
        copies.append(
            pltpu.make_async_copy(codes_hbm.at[n], codes_ref.at[n], sems.at[3 + n])
        )
    for copy in copies:
        copy.start()
    copies[0].wait()
    place = place_ref[...]
    rows = place.shape[0]
    heads, tokens = ids_ref.shape
    eye = unit(LANES, BF16)
    table = jnp.concatenate(
        [dot_nt(eye, to_bf16(place >> 8)), dot_nt(eye, to_bf16(place & 255))], axis=0
    ).astype(BF16)
    copies[1].wait()
    for head in range(heads):
        row = ids_ref[head : head + 1, :]
        hot = to_bf16(iota((rows, tokens), 0) == (row >> 7))
        both = dot(table, hot)
        value = both[:LANES] * 256.0 + both[LANES:]
        chosen = jnp.where(iota(value.shape, 0) == (row & 127), value, 0.0)
        out_ref[head : head + 1, :] = jnp.sum(chosen, axis=0, keepdims=True).astype(I32)
    for copy in copies[2:]:
        copy.wait()


def decode_kernel(codes_ref, scales_ref, out_ref):
    heads, width, rows = codes_ref.shape
    blocks = scales_ref.shape[0]
    entry = iota((width, 2 * width), 0)
    column = iota((width, 2 * width), 1)
    column = jnp.where(column < width, column, column - width)
    parity = entry & column & 15
    parity = parity ^ (parity >> 2)
    parity = (parity ^ (parity >> 1)) & 1
    same = (entry >> 4) == (column >> 4)
    rotation = jnp.where(same, 0.25 - 0.5 * parity.astype(F32), 0.0).astype(BF16)
    for head in range(heads):
        factors = jnp.concatenate(
            [
                jnp.broadcast_to(scales_ref[b, head : head + 1, :].astype(F32), (16, rows))
                for b in range(blocks)
            ],
            axis=0,
        )
        scaled = codes_ref[head].astype(F32) * factors
        upper = scaled.astype(BF16)
        lower = (scaled - upper.astype(F32)).astype(BF16)
        out_ref[head] = dot(rotation, jnp.concatenate([upper, lower], axis=0)).astype(BF16)


def picked(local, table_ref, head):
    rows = table_ref.shape[2]
    hot = to_bf16(iota((rows, local.shape[1]), 0) == local[head : head + 1, :])
    return dot(table_ref[head], hot).astype(BF16)


def pick_kernel(base_ref, ids_ref, table_ref, out_ref):
    heads, width, _ = table_ref.shape
    local = ids_ref[...] - base_ref[0]
    for head in range(heads):
        out_ref[head * width : (head + 1) * width, :] = picked(local, table_ref, head)


def merge_kernel(*refs):
    total = refs[0][...].astype(F32)
    for other in refs[1:-1]:
        total = total + other[...].astype(F32)
    refs[-1][...] = total.astype(BF16)


def fetch(count, tp, depth, source, target, shifts, sems):
    copies = []
    for n, s in enumerate(shifts):
        owner = lax.rem(tp + count - s, count)
        rows = pl.ds(pl.multiple_of(owner * depth, depth), depth)
        copy = pltpu.make_async_copy(
            source.at[rows, :], target.at[pl.ds(n * depth, depth), :], sems.at[n]
        )
        copy.start()
        copies.append(copy)
    return copies


def await_all(copies):
    for copy in copies:
        copy.wait()


def with_rim(rims, bodies):
    body = jnp.concatenate([b[...].astype(F32) for b in bodies], axis=0).T.astype(BF16)
    rim = jnp.concatenate([r[...].astype(F32) for r in rims], axis=0).T.astype(BF16)
    return jnp.concatenate([rim[LANES - RIM :], body], axis=0)


def project_own_kernel(count, where_ref, rim_ref, body_ref, *refs):
    weights, hidden_halo, hidden = refs[:4], refs[4], refs[5]
    key_ref, value_ref, next_ref, states_ref, power_ref, held, sems, next_sems = refs[6:]
    half = value_ref.shape[-1]
    depth = body_ref.shape[0]
    rep = where_ref[0]
    tp = where_ref[1]
    order = [(far, which) for far in range(2) for which in (1, 0)]
    copies = {
        (far, which): fetch(
            count, tp, depth, weights[2 * far + which], held.at[far, which], (0,),
            sems.at[2 * far + which],
        )
        for far, which in order
    }
    power = 0.0
    for slot in range(2):
        span = slice(slot * half, (slot + 1) * half)
        states_ref[slot, :RIM] = hidden_halo[:, span]
        states_ref[slot, RIM:] = hidden[:, span]
        here = states_ref[slot].astype(F32)
        power = power + jnp.sum(here * here, axis=1, keepdims=True)
    power_ref[...] = jnp.broadcast_to(power, power_ref.shape)
    memory = with_rim([rim_ref], [body_ref])
    later = []
    for far, which in order:
        slot = rep if far == 0 else 1 - rep
        await_all(copies[far, which])
        if not later:
            for f, w in order:
                later += fetch(
                    count, tp, depth, weights[2 * f + w], next_ref.at[f, w], range(1, count),
                    next_sems.at[2 * f + w],
                )
        target = value_ref if which == 1 else key_ref
        target[slot] = dot(memory, held[far, which])
    await_all(later)


def project_others_kernel(count, where_ref, *refs):
    pieces = count - 1
    rims, bodies = refs[:pieces], refs[pieces : 2 * pieces]
    held, begun_keys, begun_values, states_ref, power_ref = refs[2 * pieces :][:5]
    value_hbm, stats_ref, done, done_sems = refs[2 * pieces + 5 :]
    rep = where_ref[0]
    memory = with_rim(rims, bodies)
    sums = [0.0] * 3
    later = []
    for far in range(2):
        slot = rep if far == 0 else 1 - rep
        fields = [None, None]
        for which in (1, 0):
            fields[which] = dot(memory, held[far, which])
            if which == 1:
                done[far] = fields[1] + begun_values[slot]
                copy = pltpu.make_async_copy(done.at[far], value_hbm.at[slot], done_sems.at[far])
                copy.start()
                later.append(copy)
        keys = fields[0] + begun_keys[slot]
        values = done[far]
        terms = (keys * keys, states_ref[slot].astype(F32) * keys, values * values)
        sums = [a + jnp.sum(t, axis=1, keepdims=True) for a, t in zip(sums, terms)]
    packed = power_ref[...]
    lane = iota(packed.shape, 1)
    for k in range(3):
        packed = jnp.where(lane == k + 1, sums[k], packed)
    stats_ref[...] = dot_nt(unit(8, F32), packed, lax.Precision.HIGHEST)
    await_all(later)


def prepare_kernel(chunk, taps_ref, value_hbm, value_ref, tap_ref, rows_ref, sems):
    half = rows_ref.shape[-1]
    tokens = value_ref.shape[1]
    copies = []
    for slot in range(2):
        for start in range(0, half, chunk):
            span = pl.ds(start, chunk)
            copy = pltpu.make_async_copy(
                value_hbm.at[slot, :, span], rows_ref.at[slot, :, span], sems.at[len(copies)]
            )
            copy.start()
            copies.append(copy)
    for slot in range(2):
        for start in range(0, half, LANES):
            size = min(LANES, half - start)
            span = slice(start, start + size)
            there = slice(slot * half + start, slot * half + start + size)
            if start % chunk == 0:
                copies[(slot * half + start) // chunk].wait()
            value_ref[slot, :, span] = rows_ref[slot, RIM:, span]
            for tap in range(1, KERNEL):
                lag = DILATION * tap
                rows = rows_ref[slot, RIM - lag : RIM - lag + tokens, span]
                tap_ref[tap - 1, slot, :, span] = taps_ref[tap : tap + 1, there] * rows


def finish_kernel(count, step, keep_ref, *refs):
    stats = refs[:count]
    value_ref, tap_ref, hidden_ref, taps_ref, out_hbm = refs[count : count + 5]
    columns, gates, factors, out_ref, sems = refs[count + 5 :]
    half = value_ref.shape[-1]
    tokens, width = out_ref.shape
    total = stats[0][...]
    for other in stats[1:]:
        total = total + other[...]
    inverse_states = lax.rsqrt(total[0:1] / D + EPSILON)
    inverse_keys = lax.rsqrt(total[1:2] / D + EPSILON)
    gate = jax.nn.sigmoid(total[2:3] * inverse_states * inverse_keys / D**0.5)
    factor = gate * lax.rsqrt(gate * gate * total[3:4] / D + EPSILON)
    factor = jnp.where((iota(factor.shape, 1) < RIM) & (keep_ref[0] == 0), 0.0, factor)
    line = iota(total.shape, 0)
    both = jnp.where(line == 0, gate, jnp.where(line == 1, factor, 0.0))
    columns[...] = dot_nt(unit(total.shape[1], F32), both, lax.Precision.HIGHEST)
    gates[...] = jnp.broadcast_to(columns[RIM:, 0:1], gates.shape)
    for tap in range(KERNEL):
        lag = DILATION * tap
        factors[tap] = jnp.broadcast_to(
            columns[RIM - lag : RIM - lag + tokens, 1:2], factors.shape[1:]
        )
    copies = []
    for slot in range(2):
        for start in range(0, half, LANES):
            size = min(LANES, half - start)
            span = slice(start, start + size)
            there = slice(slot * half + start, slot * half + start + size)
            values = value_ref[slot, :, span]
            conv = taps_ref[0:1, there] * values * factors[0, :, :size]
            for tap in range(1, KERNEL):
                conv = conv + tap_ref[tap - 1, slot, :, span] * factors[tap, :, :size]
            gated = values * gates[:, :size]
            out_ref[:, there] = (
                hidden_ref[:, there].astype(F32) + jax.nn.silu(conv) + gated
            ).astype(BF16)
            if there.stop % step == 0:
                ready = pl.ds(there.stop - step, step)
                copy = pltpu.make_async_copy(
                    out_ref.at[:, ready], out_hbm.at[:, ready], sems.at[len(copies)]
                )
                copy.start()
                copies.append(copy)
    for copy in copies:
        copy.wait()


def whole(array):
    return pl.BlockSpec(array.shape, lambda *_: (0,) * array.ndim)


def in_hbm(array):
    return pltpu.with_memory_space_constraint(array, pltpu.HBM)


def after(array, *others):
    return lax.optimization_barrier((array, *others))[0]


def limit(mib):
    return pltpu.CompilerParams(vmem_limit_bytes=mib << 20)


def scattered_sum(stored, decoded, here, meanwhile, settled):
    mems = lax.axis_size("mem")
    heads, width, rows = decoded.shape
    tokens = stored.shape[1]
    asked = lax.all_gather(stored, "mem", axis=0)
    partial = pl.pallas_call(
        pick_kernel,
        grid=(mems,),
        in_specs=[
            pl.BlockSpec(memory_space=pltpu.SMEM),
            pl.BlockSpec((None, heads, tokens), lambda m: (m, 0, 0)),
            whole(decoded),
        ],
        out_specs=pl.BlockSpec((None, heads * width, tokens), lambda m: (m, 0, 0)),
        out_shape=jax.ShapeDtypeStruct((mems, heads * width, tokens), BF16),
        compiler_params=limit(16),
        name="pick_all",
    )((here * rows).astype(I32).reshape(1), asked, decoded)
    total = lax.psum_scatter(partial, "mem", scatter_dimension=0, tiled=False)
    return total, meanwhile(partial), settled


def line_sum(stored, decoded, here, meanwhile, settled):
    heads, width, rows = decoded.shape
    tokens = stored.shape[1]
    base = (here * rows).astype(I32).reshape(1)
    block = jax.ShapeDtypeStruct((heads * width, tokens), BF16)

    def ask(ids, x):
        return lax.ppermute(ids, "mem", [(i, i ^ x) for i in range(4)])

    def crossing(x, pairs):
        return lax.ppermute(x, ("mem", "rep"), [(2 * a + b, 2 * c + d) for a, b, c, d in pairs])

    def pick(ids):
        return pl.pallas_call(
            pick_kernel,
            in_specs=[pl.BlockSpec(memory_space=pltpu.SMEM)]
            + [pl.BlockSpec(memory_space=pltpu.VMEM)] * 2,
            out_shape=block,
            compiler_params=limit(8),
            name="pick_rows",
        )(base, ids, decoded)

    def send(x, *pairs):
        return lax.ppermute(x, "mem", pairs)

    first = ask(stored, 3)
    second = crossing(
        stored,
        [(m, r, m ^ 2, r ^ int(m in (1, 2))) for m in range(4) for r in range(2)],
    )
    third = ask(stored, 1)
    rows_3 = pick(first)
    rows_3, second, third = lax.optimization_barrier((rows_3, second, third))
    inward = send(rows_3, (0, 1), (3, 2))
    across = send(rows_3, (1, 2), (2, 1))
    rows_2 = pick(after(second, rows_3))
    third, settled = lax.optimization_barrier((after(third, rows_2), settled))
    past = crossing(rows_2, [(m, r, m ^ 2, r ^ 1) for m in (0, 3) for r in range(2)])
    rows_1 = pick(third)
    own = pick(after(stored, rows_1))
    beside = send(rows_1, (0, 1), (1, 0), (2, 3), (3, 2))
    onward = after(rows_2, rows_1, own) + inward
    onward = send(onward, (1, 3), (2, 0))
    other = meanwhile(across)
    own, other = lax.optimization_barrier((own + past + beside, other))
    memory = pl.pallas_call(
        merge_kernel,
        in_specs=[pl.BlockSpec(memory_space=pltpu.VMEM)] * 3,
        out_shape=block,
        compiler_params=limit(4),
        name="merge",
    )(own, across, onward)
    return memory, other, settled


def shards(
    hidden, row_ids, row_place, table_codes, table_scales, key_weight, value_weight, conv_weight
):
    mems = lax.axis_size("mem")
    tps = lax.axis_size("tp")
    reps = lax.axis_size("rep")
    blocks = mems * reps
    tokens, heads = row_ids.shape
    rows, width = table_codes.shape[1:]
    depth = heads * width
    half = key_weight.shape[1]
    seq_length = tokens * blocks // SEQS
    assert reps == 2 and seq_length % tokens == 0 and row_place.shape[0] % LANES == 0
    block = lax.axis_index(("mem", "rep"))
    smem = pl.BlockSpec(memory_space=pltpu.SMEM)

    anywhere = pl.BlockSpec(memory_space=pl.ANY)
    resident = pl.BlockSpec(memory_space=pltpu.VMEM)
    places = row_place.reshape(-1, LANES)
    codes = table_codes.transpose(0, 2, 1)
    scales = table_scales.transpose(2, 0, 1)
    stored, codes, scales = pl.pallas_call(
        place_kernel,
        in_specs=[anywhere] * 4,
        out_specs=(resident,) * 3,
        out_shape=(
            jax.ShapeDtypeStruct((heads, tokens), I32),
            jax.ShapeDtypeStruct(codes.shape, BF16),
            jax.ShapeDtypeStruct(scales.shape, BF16),
        ),
        scratch_shapes=[
            pltpu.VMEM((heads, tokens), I32),
            pltpu.VMEM(places.shape, I32),
            pltpu.SemaphoreType.DMA((heads + 3,)),
        ],
        compiler_params=limit(4),
        name="place_rows",
    )(*[in_hbm(x) for x in (row_ids.T, places, codes, scales)])
    decoded = pl.pallas_call(
        decode_kernel,
        in_specs=[resident] * 2,
        out_specs=resident,
        out_shape=jax.ShapeDtypeStruct(codes.shape, BF16),
        compiler_params=limit(6),
        name="decode_tables",
    )(codes, scales)
    here = lax.axis_index("mem")
    other_key = lax.ppermute(key_weight, "rep", [(0, 1), (1, 0)])
    other_value = lax.ppermute(value_weight, "rep", [(0, 1), (1, 0)])
    needed = [(i, i + 1) for i in range(blocks - 1) if (i + 1) * tokens % seq_length]

    def meanwhile(token):
        tail = after(hidden[tokens - RIM :], token)
        return lax.ppermute(tail, ("mem", "rep"), needed)

    summed = line_sum if mems == 4 else scattered_sum
    memory, hidden_halo, others = summed(
        stored, decoded, here, meanwhile, (other_key, other_value)
    )
    weights = [in_hbm(w) for w in (key_weight, value_weight, *others)]

    where = jnp.stack([lax.axis_index("rep"), lax.axis_index("tp")]).astype(I32)
    extended = tokens + RIM
    bodies = [memory] + [
        lax.ppermute(memory, "tp", [(i, (i + s) % tps) for i in range(tps)])
        for s in range(1, tps)
    ]

    def next_rim(rim, s):
        pairs = [
            (
                (a // reps * tps + i) * reps + a % reps,
                (b // reps * tps + (i + s) % tps) * reps + b % reps,
            )
            for a, b in needed
            for i in range(tps)
        ]
        return lax.ppermute(rim, ("mem", "tp", "rep"), pairs)

    rim = memory[:, tokens - LANES :]
    rims = [next_rim(rim, s) for s in range(tps)]
    others = tps - 1
    field = jax.ShapeDtypeStruct((2, extended, half), F32)
    *begun, following, states, power = pl.pallas_call(
        functools.partial(project_own_kernel, tps),
        in_specs=[smem] + [resident] * 2 + [anywhere] * 4 + [resident] * 2,
        out_specs=(resident,) * 5,
        out_shape=(
            field,
            field,
            pltpu.VMEM((2, 2, others * depth, half), BF16),
            jax.ShapeDtypeStruct((2, extended, half), BF16),
            jax.ShapeDtypeStruct((extended, 8), F32),
        ),
        scratch_shapes=[
            pltpu.VMEM((2, 2, depth, half), BF16),
            pltpu.SemaphoreType.DMA((4, 1)),
            pltpu.SemaphoreType.DMA((4, others)),
        ],
        compiler_params=limit(12),
        name="project_own",
    )(where, rims[0], memory, *weights, hidden_halo, hidden)
    values, stats = pl.pallas_call(
        functools.partial(project_others_kernel, tps),
        in_specs=[smem] + [resident] * (2 * others + 5),
        out_specs=(pl.BlockSpec(memory_space=pltpu.HBM), resident),
        out_shape=(pltpu.HBM(field.shape, F32), jax.ShapeDtypeStruct((8, extended), F32)),
        scratch_shapes=[
            pltpu.VMEM((2, extended, half), F32),
            pltpu.SemaphoreType.DMA((2,)),
        ],
        compiler_params=limit(14),
        name="project_others",
    )(where, *rims[1:], *bodies[1:], following, *begun, states, power)

    all_stats = [stats] + [
        lax.ppermute(stats, "tp", [(i, (i + s) % tps) for i in range(tps)]) for s in range(1, tps)
    ]
    keep = (block * tokens % seq_length != 0).astype(I32).reshape(1)
    step = 2 * half
    if half % LANES == 0:
        step = next(c for c in (384, 256, 128) if half % c == 0)
    chunk = min(step, half)
    body = (2, tokens, half)
    values, products = pl.pallas_call(
        functools.partial(prepare_kernel, chunk),
        in_specs=[resident, anywhere],
        out_specs=(resident,) * 2,
        out_shape=(
            jax.ShapeDtypeStruct(body, F32),
            jax.ShapeDtypeStruct((KERNEL - 1, *body), F32),
        ),
        scratch_shapes=[
            pltpu.VMEM((2, extended, half), F32),
            pltpu.SemaphoreType.DMA((2 * half // chunk,)),
        ],
        compiler_params=limit(6),
        name="prepare",
    )(conv_weight, in_hbm(values))
    return pl.pallas_call(
        functools.partial(finish_kernel, tps, step),
        in_specs=[smem] + [resident] * (tps + 4),
        out_specs=anywhere,
        out_shape=jax.ShapeDtypeStruct((tokens, 2 * half), BF16),
        scratch_shapes=[
            pltpu.VMEM((extended, 8), F32),
            pltpu.VMEM((tokens, LANES), F32),
            pltpu.VMEM((KERNEL, tokens, LANES), F32),
            pltpu.VMEM((tokens, 2 * half), BF16),
            pltpu.SemaphoreType.DMA((2 * half // step,)),
        ],
        compiler_params=limit(6),
        name="finish",
    )(keep, *all_stats, values, products, hidden, conv_weight)


def solution(mesh):
    in_specs = (
        P(("parts", "mem", "rep"), "tp"),
        P(("parts", "mem", "rep"), "tp"),
        P("parts"),
        P(("parts", "tp"), "mem", None),
        P(("parts", "tp"), "mem", None),
        P(None, ("tp", "rep")),
        P(None, ("tp", "rep")),
        P(None, "tp"),
    )
    out_specs = P(("parts", "mem", "rep"), "tp")
    return jax.shard_map(shards, mesh=mesh, in_specs=in_specs, out_specs=out_specs, check_vma=False)
```

```python
import functools

import jax
import jax.numpy as jnp
from jax import lax
from jax.experimental import pallas as pl
from jax.experimental.pallas import tpu as pltpu
from jax.sharding import PartitionSpec as P

D = 4608
KERNEL = 4
DILATION = 3
SEQS = 4
EPSILON = 1e-06
RIM = 16
LANES = 128

F32 = jnp.float32
BF16 = jnp.bfloat16
I32 = jnp.int32


def iota(shape, axis):
    return lax.broadcasted_iota(I32, shape, axis)


def dot(a, b):
    return jnp.dot(a, b, preferred_element_type=F32)


def dot_nt(a, b, precision=None):
    return lax.dot_general(
        a, b, (((1,), (1,)), ((), ())), precision=precision, preferred_element_type=F32
    )


def unit(n, dtype):
    return (iota((n, n), 0) == iota((n, n), 1)).astype(F32).astype(dtype)


def to_bf16(x):
    return x.astype(F32).astype(BF16)


def place_kernel(
    ids_hbm, place_hbm, codes_hbm, scales_hbm, out_ref, codes_ref, scales_ref, ids_ref, place_ref, sems
):
    copies = [
        pltpu.make_async_copy(place_hbm, place_ref, sems.at[0]),
        pltpu.make_async_copy(ids_hbm, ids_ref, sems.at[1]),
        pltpu.make_async_copy(scales_hbm, scales_ref, sems.at[2]),
    ]
    for n in range(codes_ref.shape[0]):
        copies.append(
            pltpu.make_async_copy(codes_hbm.at[n], codes_ref.at[n], sems.at[3 + n])
        )
    for copy in copies:
        copy.start()
    copies[0].wait()
    place = place_ref[...]
    rows = place.shape[0]
    heads, tokens = ids_ref.shape
    eye = unit(LANES, BF16)
    table = jnp.concatenate(
        [dot_nt(eye, to_bf16(place >> 8)), dot_nt(eye, to_bf16(place & 255))], axis=0
    ).astype(BF16)
    copies[1].wait()
    for head in range(heads):
        row = ids_ref[head : head + 1, :]
        hot = to_bf16(iota((rows, tokens), 0) == (row >> 7))
        both = dot(table, hot)
        value = both[:LANES] * 256.0 + both[LANES:]
        chosen = jnp.where(iota(value.shape, 0) == (row & 127), value, 0.0)
        out_ref[head : head + 1, :] = jnp.sum(chosen, axis=0, keepdims=True).astype(I32)
    for copy in copies[2:]:
        copy.wait()


def decode_kernel(codes_ref, scales_ref, out_ref):
    heads, width, rows = codes_ref.shape
    blocks = scales_ref.shape[0]
    entry = iota((width, 2 * width), 0)
    column = iota((width, 2 * width), 1)
    column = jnp.where(column < width, column, column - width)
    parity = entry & column & 15
    parity = parity ^ (parity >> 2)
    parity = (parity ^ (parity >> 1)) & 1
    same = (entry >> 4) == (column >> 4)
    rotation = jnp.where(same, 0.25 - 0.5 * parity.astype(F32), 0.0).astype(BF16)
    for head in range(heads):
        factors = jnp.concatenate(
            [
                jnp.broadcast_to(scales_ref[b, head : head + 1, :].astype(F32), (16, rows))
                for b in range(blocks)
            ],
            axis=0,
        )
        scaled = codes_ref[head].astype(F32) * factors
        upper = scaled.astype(BF16)
        lower = (scaled - upper.astype(F32)).astype(BF16)
        out_ref[head] = dot(rotation, jnp.concatenate([upper, lower], axis=0)).astype(BF16)


def picked(local, table_ref, head):
    rows = table_ref.shape[2]
    hot = to_bf16(iota((rows, local.shape[1]), 0) == local[head : head + 1, :])
    return dot(table_ref[head], hot).astype(BF16)


def pick_kernel(base_ref, ids_ref, table_ref, out_ref):
    heads, width, _ = table_ref.shape
    local = ids_ref[...] - base_ref[0]
    for head in range(heads):
        out_ref[head * width : (head + 1) * width, :] = picked(local, table_ref, head)


def merge_kernel(*refs):
    total = refs[0][...].astype(F32)
    for other in refs[1:-1]:
        total = total + other[...].astype(F32)
    refs[-1][...] = total.astype(BF16)


def fetch(count, tp, depth, source, target, parts, sems):
    copies = []
    start = 0
    for n, (shift, begin, size) in enumerate(parts):
        owner = lax.rem(tp + count - shift, count)
        rows = pl.ds(pl.multiple_of(owner * depth + begin, 16), size)
        copy = pltpu.make_async_copy(
            source.at[rows, :], target.at[pl.ds(start, size), :], sems.at[n]
        )
        copy.start()
        copies.append(copy)
        start += size
    return copies


def await_all(copies):
    for copy in copies:
        copy.wait()


def with_rim(rims, bodies):
    body = jnp.concatenate([b.astype(F32) for b in bodies], axis=0).T.astype(BF16)
    rim = jnp.concatenate([r.astype(F32) for r in rims], axis=0).T.astype(BF16)
    return jnp.concatenate([rim[LANES - RIM :], body], axis=0)


def project_own_kernel(count, where_ref, rim_ref, body_ref, *refs):
    weights, hidden_halo, hidden = refs[:4], refs[4], refs[5]
    key_ref, value_ref, next_ref, states_ref, power_ref, held, sems, next_sems = refs[6:]
    half = value_ref.shape[-1]
    depth = body_ref.shape[0]
    split = held.shape[2]
    remainder = [(0, split, depth - split)] + [(n, 0, depth) for n in range(1, count)]
    rep = where_ref[0]
    tp = where_ref[1]
    order = [(far, which) for far in range(2) for which in (1, 0)]
    copies = {
        (far, which): fetch(
            count, tp, depth, weights[2 * far + which], held.at[far, which], [(0, 0, split)],
            sems.at[2 * far + which],
        )
        for far, which in order
    }
    power = 0.0
    for slot in range(2):
        span = slice(slot * half, (slot + 1) * half)
        states_ref[slot, :RIM] = hidden_halo[:, span]
        states_ref[slot, RIM:] = hidden[:, span]
        here = states_ref[slot].astype(F32)
        power = power + jnp.sum(here * here, axis=1, keepdims=True)
    power_ref[...] = jnp.broadcast_to(power, power_ref.shape)
    memory = with_rim([rim_ref[:split]], [body_ref[:split]])
    later = []
    for far, which in order:
        slot = rep if far == 0 else 1 - rep
        await_all(copies[far, which])
        if not later:
            for f, w in order:
                later += fetch(
                    count, tp, depth, weights[2 * f + w], next_ref.at[f, w], remainder,
                    next_sems.at[2 * f + w],
                )
        target = value_ref if which == 1 else key_ref
        target[slot] = dot(memory, held[far, which])
    await_all(later)


def project_others_kernel(count, where_ref, *refs):
    rims, bodies = refs[:count], refs[count : 2 * count]
    held, begun_keys, begun_values, states_ref, power_ref = refs[2 * count :][:5]
    value_hbm, stats_ref, done, done_sems = refs[2 * count + 5 :]
    rep = where_ref[0]
    split = count * bodies[0].shape[0] - held.shape[2]
    rims = [r[split if n == 0 else 0 :] for n, r in enumerate(rims)]
    bodies = [b[split if n == 0 else 0 :] for n, b in enumerate(bodies)]
    memory = with_rim(rims, bodies)
    sums = [0.0] * 3
    later = []
    for far in range(2):
        slot = rep if far == 0 else 1 - rep
        fields = [None, None]
        for which in (1, 0):
            fields[which] = dot(memory, held[far, which])
            if which == 1:
                done[far] = fields[1] + begun_values[slot]
                copy = pltpu.make_async_copy(done.at[far], value_hbm.at[slot], done_sems.at[far])
                copy.start()
                later.append(copy)
        keys = fields[0] + begun_keys[slot]
        values = done[far]
        terms = (keys * keys, states_ref[slot].astype(F32) * keys, values * values)
        sums = [a + jnp.sum(t, axis=1, keepdims=True) for a, t in zip(sums, terms)]
    packed = power_ref[...]
    lane = iota(packed.shape, 1)
    for k in range(3):
        packed = jnp.where(lane == k + 1, sums[k], packed)
    stats_ref[...] = dot_nt(unit(8, F32), packed, lax.Precision.HIGHEST)
    await_all(later)


def prepare_kernel(chunk, taps_ref, value_hbm, value_ref, tap_ref, rows_ref, sems):
    half = rows_ref.shape[-1]
    tokens = value_ref.shape[1]
    copies = []
    for slot in range(2):
        for start in range(0, half, chunk):
            span = pl.ds(start, chunk)
            copy = pltpu.make_async_copy(
                value_hbm.at[slot, :, span], rows_ref.at[slot, :, span], sems.at[len(copies)]
            )
            copy.start()
            copies.append(copy)
    for slot in range(2):
        for start in range(0, half, LANES):
            size = min(LANES, half - start)
            span = slice(start, start + size)
            there = slice(slot * half + start, slot * half + start + size)
            if start % chunk == 0:
                copies[(slot * half + start) // chunk].wait()
            value_ref[slot, :, span] = rows_ref[slot, RIM:, span]
            for tap in range(1, KERNEL):
                lag = DILATION * tap
                rows = rows_ref[slot, RIM - lag : RIM - lag + tokens, span]
                tap_ref[tap - 1, slot, :, span] = taps_ref[tap : tap + 1, there] * rows


def finish_kernel(count, step, keep_ref, *refs):
    stats = refs[:count]
    value_ref, tap_ref, hidden_ref, taps_ref, out_hbm = refs[count : count + 5]
    columns, gates, factors, out_ref, sems = refs[count + 5 :]
    half = value_ref.shape[-1]
    tokens, width = out_ref.shape
    total = stats[0][...]
    for other in stats[1:]:
        total = total + other[...]
    inverse_states = lax.rsqrt(total[0:1] / D + EPSILON)
    inverse_keys = lax.rsqrt(total[1:2] / D + EPSILON)
    gate = jax.nn.sigmoid(total[2:3] * inverse_states * inverse_keys / D**0.5)
    factor = gate * lax.rsqrt(gate * gate * total[3:4] / D + EPSILON)
    factor = jnp.where((iota(factor.shape, 1) < RIM) & (keep_ref[0] == 0), 0.0, factor)
    line = iota(total.shape, 0)
    both = jnp.where(line == 0, gate, jnp.where(line == 1, factor, 0.0))
    columns[...] = dot_nt(unit(total.shape[1], F32), both, lax.Precision.HIGHEST)
    gates[...] = jnp.broadcast_to(columns[RIM:, 0:1], gates.shape)
    for tap in range(KERNEL):
        lag = DILATION * tap
        factors[tap] = jnp.broadcast_to(
            columns[RIM - lag : RIM - lag + tokens, 1:2], factors.shape[1:]
        )
    copies = []
    for slot in range(2):
        for start in range(0, half, LANES):
            size = min(LANES, half - start)
            span = slice(start, start + size)
            there = slice(slot * half + start, slot * half + start + size)
            values = value_ref[slot, :, span]
            conv = taps_ref[0:1, there] * values * factors[0, :, :size]
            for tap in range(1, KERNEL):
                conv = conv + tap_ref[tap - 1, slot, :, span] * factors[tap, :, :size]
            gated = values * gates[:, :size]
            out_ref[:, there] = (
                hidden_ref[:, there].astype(F32) + jax.nn.silu(conv) + gated
            ).astype(BF16)
            if there.stop % step == 0:
                ready = pl.ds(there.stop - step, step)
                copy = pltpu.make_async_copy(
                    out_ref.at[:, ready], out_hbm.at[:, ready], sems.at[len(copies)]
                )
                copy.start()
                copies.append(copy)
    for copy in copies:
        copy.wait()


def whole(array):
    return pl.BlockSpec(array.shape, lambda *_: (0,) * array.ndim)


def in_hbm(array):
    return pltpu.with_memory_space_constraint(array, pltpu.HBM)


def after(array, *others):
    return lax.optimization_barrier((array, *others))[0]


def limit(mib):
    return pltpu.CompilerParams(vmem_limit_bytes=mib << 20)


def scattered_sum(stored, decoded, here, meanwhile, settled):
    mems = lax.axis_size("mem")
    heads, width, rows = decoded.shape
    tokens = stored.shape[1]
    asked = lax.all_gather(stored, "mem", axis=0)
    partial = pl.pallas_call(
        pick_kernel,
        grid=(mems,),
        in_specs=[
            pl.BlockSpec(memory_space=pltpu.SMEM),
            pl.BlockSpec((None, heads, tokens), lambda m: (m, 0, 0)),
            whole(decoded),
        ],
        out_specs=pl.BlockSpec((None, heads * width, tokens), lambda m: (m, 0, 0)),
        out_shape=jax.ShapeDtypeStruct((mems, heads * width, tokens), BF16),
        compiler_params=limit(16),
        name="pick_all",
    )((here * rows).astype(I32).reshape(1), asked, decoded)
    total = lax.psum_scatter(partial, "mem", scatter_dimension=0, tiled=False)
    return total, meanwhile(partial), settled


def line_sum(stored, decoded, here, meanwhile, settled):
    heads, width, rows = decoded.shape
    tokens = stored.shape[1]
    base = (here * rows).astype(I32).reshape(1)
    block = jax.ShapeDtypeStruct((heads * width, tokens), BF16)

    def ask(ids, x):
        return lax.ppermute(ids, "mem", [(i, i ^ x) for i in range(4)])

    def crossing(x, pairs):
        return lax.ppermute(x, ("mem", "rep"), [(2 * a + b, 2 * c + d) for a, b, c, d in pairs])

    def pick(ids):
        return pl.pallas_call(
            pick_kernel,
            in_specs=[pl.BlockSpec(memory_space=pltpu.SMEM)]
            + [pl.BlockSpec(memory_space=pltpu.VMEM)] * 2,
            out_shape=block,
            compiler_params=limit(8),
            name="pick_rows",
        )(base, ids, decoded)

    def send(x, *pairs):
        return lax.ppermute(x, "mem", pairs)

    first = ask(stored, 3)
    second = crossing(
        stored,
        [(m, r, m ^ 2, r ^ int(m in (1, 2))) for m in range(4) for r in range(2)],
    )
    third = ask(stored, 1)
    rows_3 = pick(first)
    rows_3, second, third = lax.optimization_barrier((rows_3, second, third))
    inward = send(rows_3, (0, 1), (3, 2))
    across = send(rows_3, (1, 2), (2, 1))
    rows_2 = pick(after(second, rows_3))
    third, settled = lax.optimization_barrier((after(third, rows_2), settled))
    past = crossing(rows_2, [(m, r, m ^ 2, r ^ 1) for m in (0, 3) for r in range(2)])
    rows_1 = pick(third)
    own = pick(after(stored, rows_1))
    beside = send(rows_1, (0, 1), (1, 0), (2, 3), (3, 2))
    onward = after(rows_2, rows_1, own) + inward
    onward = send(onward, (1, 3), (2, 0))
    other = meanwhile(across)
    own, other = lax.optimization_barrier((own + past + beside, other))
    memory = pl.pallas_call(
        merge_kernel,
        in_specs=[pl.BlockSpec(memory_space=pltpu.VMEM)] * 3,
        out_shape=block,
        compiler_params=limit(4),
        name="merge",
    )(own, across, onward)
    return memory, other, settled


def shards(
    hidden, row_ids, row_place, table_codes, table_scales, key_weight, value_weight, conv_weight
):
    mems = lax.axis_size("mem")
    tps = lax.axis_size("tp")
    reps = lax.axis_size("rep")
    blocks = mems * reps
    tokens, heads = row_ids.shape
    rows, width = table_codes.shape[1:]
    depth = heads * width
    half = key_weight.shape[1]
    seq_length = tokens * blocks // SEQS
    assert reps == 2 and seq_length % tokens == 0 and row_place.shape[0] % LANES == 0
    block = lax.axis_index(("mem", "rep"))
    smem = pl.BlockSpec(memory_space=pltpu.SMEM)

    anywhere = pl.BlockSpec(memory_space=pl.ANY)
    resident = pl.BlockSpec(memory_space=pltpu.VMEM)
    places = row_place.reshape(-1, LANES)
    codes = table_codes.transpose(0, 2, 1)
    scales = table_scales.transpose(2, 0, 1)
    stored, codes, scales = pl.pallas_call(
        place_kernel,
        in_specs=[anywhere] * 4,
        out_specs=(resident,) * 3,
        out_shape=(
            jax.ShapeDtypeStruct((heads, tokens), I32),
            jax.ShapeDtypeStruct(codes.shape, BF16),
            jax.ShapeDtypeStruct(scales.shape, BF16),
        ),
        scratch_shapes=[
            pltpu.VMEM((heads, tokens), I32),
            pltpu.VMEM(places.shape, I32),
            pltpu.SemaphoreType.DMA((heads + 3,)),
        ],
        compiler_params=limit(4),
        name="place_rows",
    )(*[in_hbm(x) for x in (row_ids.T, places, codes, scales)])
    decoded = pl.pallas_call(
        decode_kernel,
        in_specs=[resident] * 2,
        out_specs=resident,
        out_shape=jax.ShapeDtypeStruct(codes.shape, BF16),
        compiler_params=limit(6),
        name="decode_tables",
    )(codes, scales)
    here = lax.axis_index("mem")
    other_key = lax.ppermute(key_weight, "rep", [(0, 1), (1, 0)])
    other_value = lax.ppermute(value_weight, "rep", [(0, 1), (1, 0)])
    needed = [(i, i + 1) for i in range(blocks - 1) if (i + 1) * tokens % seq_length]

    def meanwhile(token):
        tail = after(hidden[tokens - RIM :], token)
        return lax.ppermute(tail, ("mem", "rep"), needed)

    summed = line_sum if mems == 4 else scattered_sum
    memory, hidden_halo, others = summed(
        stored, decoded, here, meanwhile, (other_key, other_value)
    )
    weights = [in_hbm(w) for w in (key_weight, value_weight, *others)]

    where = jnp.stack([lax.axis_index("rep"), lax.axis_index("tp")]).astype(I32)
    extended = tokens + RIM
    bodies = [memory] + [
        lax.ppermute(memory, "tp", [(i, (i + s) % tps) for i in range(tps)])
        for s in range(1, tps)
    ]

    def next_rim(rim, s):
        pairs = [
            (
                (a // reps * tps + i) * reps + a % reps,
                (b // reps * tps + (i + s) % tps) * reps + b % reps,
            )
            for a, b in needed
            for i in range(tps)
        ]
        return lax.ppermute(rim, ("mem", "tp", "rep"), pairs)

    rim = memory[:, tokens - LANES :]
    rims = [next_rim(rim, s) for s in range(tps)]
    field = jax.ShapeDtypeStruct((2, extended, half), F32)
    split = max(depth // 256 * 256, depth // 2)
    *begun, following, states, power = pl.pallas_call(
        functools.partial(project_own_kernel, tps),
        in_specs=[smem] + [resident] * 2 + [anywhere] * 4 + [resident] * 2,
        out_specs=(resident,) * 5,
        out_shape=(
            field,
            field,
            pltpu.VMEM((2, 2, tps * depth - split, half), BF16),
            jax.ShapeDtypeStruct((2, extended, half), BF16),
            jax.ShapeDtypeStruct((extended, 8), F32),
        ),
        scratch_shapes=[
            pltpu.VMEM((2, 2, split, half), BF16),
            pltpu.SemaphoreType.DMA((4, 1)),
            pltpu.SemaphoreType.DMA((4, tps)),
        ],
        compiler_params=limit(12),
        name="project_own",
    )(where, rims[0], memory, *weights, hidden_halo, hidden)
    values, stats = pl.pallas_call(
        functools.partial(project_others_kernel, tps),
        in_specs=[smem] + [resident] * (2 * tps + 5),
        out_specs=(pl.BlockSpec(memory_space=pltpu.HBM), resident),
        out_shape=(pltpu.HBM(field.shape, F32), jax.ShapeDtypeStruct((8, extended), F32)),
        scratch_shapes=[
            pltpu.VMEM((2, extended, half), F32),
            pltpu.SemaphoreType.DMA((2,)),
        ],
        compiler_params=limit(14),
        name="project_others",
    )(where, *rims, *bodies, following, *begun, states, power)

    all_stats = [stats] + [
        lax.ppermute(stats, "tp", [(i, (i + s) % tps) for i in range(tps)]) for s in range(1, tps)
    ]
    keep = (block * tokens % seq_length != 0).astype(I32).reshape(1)
    step = 2 * half
    if half % LANES == 0:
        step = next(c for c in (384, 256, 128) if half % c == 0)
    chunk = min(step, half)
    body = (2, tokens, half)
    values, products = pl.pallas_call(
        functools.partial(prepare_kernel, chunk),
        in_specs=[resident, anywhere],
        out_specs=(resident,) * 2,
        out_shape=(
            jax.ShapeDtypeStruct(body, F32),
            jax.ShapeDtypeStruct((KERNEL - 1, *body), F32),
        ),
        scratch_shapes=[
            pltpu.VMEM((2, extended, half), F32),
            pltpu.SemaphoreType.DMA((2 * half // chunk,)),
        ],
        compiler_params=limit(6),
        name="prepare",
    )(conv_weight, in_hbm(values))
    return pl.pallas_call(
        functools.partial(finish_kernel, tps, step),
        in_specs=[smem] + [resident] * (tps + 4),
        out_specs=anywhere,
        out_shape=jax.ShapeDtypeStruct((tokens, 2 * half), BF16),
        scratch_shapes=[
            pltpu.VMEM((extended, 8), F32),
            pltpu.VMEM((tokens, LANES), F32),
            pltpu.VMEM((KERNEL, tokens, LANES), F32),
            pltpu.VMEM((tokens, 2 * half), BF16),
            pltpu.SemaphoreType.DMA((2 * half // step,)),
        ],
        compiler_params=limit(6),
        name="finish",
    )(keep, *all_stats, values, products, hidden, conv_weight)


def solution(mesh):
    in_specs = (
        P(("parts", "mem", "rep"), "tp"),
        P(("parts", "mem", "rep"), "tp"),
        P("parts"),
        P(("parts", "tp"), "mem", None),
        P(("parts", "tp"), "mem", None),
        P(None, ("tp", "rep")),
        P(None, ("tp", "rep")),
        P(None, "tp"),
    )
    out_specs = P(("parts", "mem", "rep"), "tp")
    return jax.shard_map(shards, mesh=mesh, in_specs=in_specs, out_specs=out_specs, check_vma=False)
```

```python
import functools

import jax
import jax.numpy as jnp
from jax import lax
from jax.experimental import pallas as pl
from jax.experimental.pallas import tpu as pltpu
from jax.sharding import PartitionSpec as P

D = 4608
KERNEL = 4
DILATION = 3
SEQS = 4
EPSILON = 1e-06
RIM = 16
LANES = 128

F32 = jnp.float32
BF16 = jnp.bfloat16
I32 = jnp.int32


def iota(shape, axis):
    return lax.broadcasted_iota(I32, shape, axis)


def dot(a, b):
    return jnp.dot(a, b, preferred_element_type=F32)


def dot_nt(a, b, precision=None):
    return lax.dot_general(
        a, b, (((1,), (1,)), ((), ())), precision=precision, preferred_element_type=F32
    )


def unit(n, dtype):
    return (iota((n, n), 0) == iota((n, n), 1)).astype(F32).astype(dtype)


def to_bf16(x):
    return x.astype(F32).astype(BF16)


def place_kernel(
    ids_hbm, place_hbm, codes_hbm, scales_hbm, out_ref, codes_ref, scales_ref, ids_ref, place_ref, sems
):
    copies = [
        pltpu.make_async_copy(place_hbm, place_ref, sems.at[0]),
        pltpu.make_async_copy(ids_hbm, ids_ref, sems.at[1]),
        pltpu.make_async_copy(scales_hbm, scales_ref, sems.at[2]),
    ]
    for n in range(codes_ref.shape[0]):
        copies.append(
            pltpu.make_async_copy(codes_hbm.at[n], codes_ref.at[n], sems.at[3 + n])
        )
    for copy in copies:
        copy.start()
    copies[0].wait()
    place = place_ref[...]
    rows = place.shape[0]
    heads, tokens = ids_ref.shape
    eye = unit(LANES, BF16)
    table = jnp.concatenate(
        [dot_nt(eye, to_bf16(place >> 8)), dot_nt(eye, to_bf16(place & 255))], axis=0
    ).astype(BF16)
    copies[1].wait()
    for head in range(heads):
        row = ids_ref[head : head + 1, :]
        hot = to_bf16(iota((rows, tokens), 0) == (row >> 7))
        both = dot(table, hot)
        value = both[:LANES] * 256.0 + both[LANES:]
        chosen = jnp.where(iota(value.shape, 0) == (row & 127), value, 0.0)
        out_ref[head : head + 1, :] = jnp.sum(chosen, axis=0, keepdims=True).astype(I32)
    for copy in copies[2:]:
        copy.wait()


def decode_kernel(codes_ref, scales_ref, out_ref):
    heads, width, rows = codes_ref.shape
    blocks = scales_ref.shape[0]
    entry = iota((width, 2 * width), 0)
    column = iota((width, 2 * width), 1)
    column = jnp.where(column < width, column, column - width)
    parity = entry & column & 15
    parity = parity ^ (parity >> 2)
    parity = (parity ^ (parity >> 1)) & 1
    same = (entry >> 4) == (column >> 4)
    rotation = jnp.where(same, 0.25 - 0.5 * parity.astype(F32), 0.0).astype(BF16)
    for head in range(heads):
        factors = jnp.concatenate(
            [
                jnp.broadcast_to(scales_ref[b, head : head + 1, :].astype(F32), (16, rows))
                for b in range(blocks)
            ],
            axis=0,
        )
        scaled = codes_ref[head].astype(F32) * factors
        upper = scaled.astype(BF16)
        lower = (scaled - upper.astype(F32)).astype(BF16)
        out_ref[head] = dot(rotation, jnp.concatenate([upper, lower], axis=0)).astype(BF16)


def picked(local, table_ref, head):
    rows = table_ref.shape[2]
    hot = to_bf16(iota((rows, local.shape[1]), 0) == local[head : head + 1, :])
    return dot(table_ref[head], hot).astype(BF16)


def pick_kernel(base_ref, ids_ref, table_ref, out_ref):
    heads, width, _ = table_ref.shape
    local = ids_ref[...] - base_ref[0]
    for head in range(heads):
        out_ref[head * width : (head + 1) * width, :] = picked(local, table_ref, head)


def merge_kernel(*refs):
    total = refs[0][...].astype(F32)
    for other in refs[1:-1]:
        total = total + other[...].astype(F32)
    refs[-1][...] = total.astype(BF16)


def fetch(count, tp, depth, source, target, shifts, sems):
    copies = []
    for n, s in enumerate(shifts):
        owner = lax.rem(tp + count - s, count)
        rows = pl.ds(pl.multiple_of(owner * depth, depth), depth)
        copy = pltpu.make_async_copy(
            source.at[rows, :], target.at[pl.ds(n * depth, depth), :], sems.at[n]
        )
        copy.start()
        copies.append(copy)
    return copies


def await_all(copies):
    for copy in copies:
        copy.wait()


def with_rim(rims, bodies):
    body = jnp.concatenate([b[...].astype(F32) for b in bodies], axis=0).T.astype(BF16)
    rim = jnp.concatenate([r[...].astype(F32) for r in rims], axis=0).T.astype(BF16)
    return jnp.concatenate([rim[LANES - RIM :], body], axis=0)


def load_kernel(count, where_ref, key_hbm, value_hbm, out_ref, sems):
    copies = []
    for which, source in enumerate((key_hbm, value_hbm)):
        depth = out_ref.shape[1]
        copies += fetch(
            count, where_ref[1], depth, source, out_ref.at[which], (0,), sems.at[which]
        )
    await_all(copies)


def project_own_kernel(count, where_ref, rim_ref, body_ref, *refs):
    weights, ready, hidden_halo, hidden = refs[:4], refs[4], refs[5], refs[6]
    key_ref, value_ref, next_ref, states_ref, power_ref, held, sems, next_sems = refs[7:]
    half = value_ref.shape[-1]
    depth = body_ref.shape[0]
    rep = where_ref[0]
    tp = where_ref[1]
    order = [(far, which) for far in range(2) for which in (1, 0)]
    copies = {
        (1, which): fetch(
            count, tp, depth, weights[2 + which], held.at[which], (0,), sems.at[which]
        )
        for which in (1, 0)
    }
    later = []
    for f, w in order:
        later += fetch(
            count, tp, depth, weights[2 * f + w], next_ref.at[f, w], range(1, count),
            next_sems.at[2 * f + w],
        )
    power = 0.0
    for slot in range(2):
        span = slice(slot * half, (slot + 1) * half)
        states_ref[slot, :RIM] = hidden_halo[:, span]
        states_ref[slot, RIM:] = hidden[:, span]
        here = states_ref[slot].astype(F32)
        power = power + jnp.sum(here * here, axis=1, keepdims=True)
    power_ref[...] = jnp.broadcast_to(power, power_ref.shape)
    memory = with_rim([rim_ref], [body_ref])
    for far, which in order:
        slot = rep if far == 0 else 1 - rep
        await_all(copies.get((far, which), ()))
        target = value_ref if which == 1 else key_ref
        target[slot] = dot(memory, ready[which] if far == 0 else held[which])
    await_all(later)


def project_others_kernel(count, where_ref, *refs):
    pieces = count - 1
    rims, bodies = refs[:pieces], refs[pieces : 2 * pieces]
    held, begun_keys, begun_values, states_ref, power_ref = refs[2 * pieces :][:5]
    value_hbm, stats_ref, done, done_sems = refs[2 * pieces + 5 :]
    rep = where_ref[0]
    memory = with_rim(rims, bodies)
    sums = [0.0] * 3
    later = []
    for far in range(2):
        slot = rep if far == 0 else 1 - rep
        fields = [None, None]
        for which in (1, 0):
            fields[which] = dot(memory, held[far, which])
            if which == 1:
                done[far] = fields[1] + begun_values[slot]
                copy = pltpu.make_async_copy(done.at[far], value_hbm.at[slot], done_sems.at[far])
                copy.start()
                later.append(copy)
        keys = fields[0] + begun_keys[slot]
        values = done[far]
        terms = (keys * keys, states_ref[slot].astype(F32) * keys, values * values)
        sums = [a + jnp.sum(t, axis=1, keepdims=True) for a, t in zip(sums, terms)]
    packed = power_ref[...]
    lane = iota(packed.shape, 1)
    for k in range(3):
        packed = jnp.where(lane == k + 1, sums[k], packed)
    stats_ref[...] = dot_nt(unit(8, F32), packed, lax.Precision.HIGHEST)
    await_all(later)


def prepare_kernel(chunk, taps_ref, value_hbm, value_ref, tap_ref, rows_ref, sems):
    half = rows_ref.shape[-1]
    tokens = value_ref.shape[1]
    copies = []
    for slot in range(2):
        for start in range(0, half, chunk):
            span = pl.ds(start, chunk)
            copy = pltpu.make_async_copy(
                value_hbm.at[slot, :, span], rows_ref.at[slot, :, span], sems.at[len(copies)]
            )
            copy.start()
            copies.append(copy)
    for slot in range(2):
        for start in range(0, half, LANES):
            size = min(LANES, half - start)
            span = slice(start, start + size)
            there = slice(slot * half + start, slot * half + start + size)
            if start % chunk == 0:
                copies[(slot * half + start) // chunk].wait()
            value_ref[slot, :, span] = rows_ref[slot, RIM:, span]
            for tap in range(1, KERNEL):
                lag = DILATION * tap
                rows = rows_ref[slot, RIM - lag : RIM - lag + tokens, span]
                tap_ref[tap - 1, slot, :, span] = taps_ref[tap : tap + 1, there] * rows


def finish_kernel(count, step, keep_ref, *refs):
    stats = refs[:count]
    value_ref, tap_ref, hidden_ref, taps_ref, out_hbm = refs[count : count + 5]
    columns, gates, factors, out_ref, sems = refs[count + 5 :]
    half = value_ref.shape[-1]
    tokens, width = out_ref.shape
    total = stats[0][...]
    for other in stats[1:]:
        total = total + other[...]
    inverse_states = lax.rsqrt(total[0:1] / D + EPSILON)
    inverse_keys = lax.rsqrt(total[1:2] / D + EPSILON)
    gate = jax.nn.sigmoid(total[2:3] * inverse_states * inverse_keys / D**0.5)
    factor = gate * lax.rsqrt(gate * gate * total[3:4] / D + EPSILON)
    factor = jnp.where((iota(factor.shape, 1) < RIM) & (keep_ref[0] == 0), 0.0, factor)
    line = iota(total.shape, 0)
    both = jnp.where(line == 0, gate, jnp.where(line == 1, factor, 0.0))
    columns[...] = dot_nt(unit(total.shape[1], F32), both, lax.Precision.HIGHEST)
    gates[...] = jnp.broadcast_to(columns[RIM:, 0:1], gates.shape)
    for tap in range(KERNEL):
        lag = DILATION * tap
        factors[tap] = jnp.broadcast_to(
            columns[RIM - lag : RIM - lag + tokens, 1:2], factors.shape[1:]
        )
    copies = []
    for slot in range(2):
        for start in range(0, half, LANES):
            size = min(LANES, half - start)
            span = slice(start, start + size)
            there = slice(slot * half + start, slot * half + start + size)
            values = value_ref[slot, :, span]
            conv = taps_ref[0:1, there] * values * factors[0, :, :size]
            for tap in range(1, KERNEL):
                conv = conv + tap_ref[tap - 1, slot, :, span] * factors[tap, :, :size]
            gated = values * gates[:, :size]
            out_ref[:, there] = (
                hidden_ref[:, there].astype(F32) + jax.nn.silu(conv) + gated
            ).astype(BF16)
            if there.stop % step == 0:
                ready = pl.ds(there.stop - step, step)
                copy = pltpu.make_async_copy(
                    out_ref.at[:, ready], out_hbm.at[:, ready], sems.at[len(copies)]
                )
                copy.start()
                copies.append(copy)
    for copy in copies:
        copy.wait()


def whole(array):
    return pl.BlockSpec(array.shape, lambda *_: (0,) * array.ndim)


def in_hbm(array):
    return pltpu.with_memory_space_constraint(array, pltpu.HBM)


def after(array, *others):
    return lax.optimization_barrier((array, *others))[0]


def limit(mib):
    return pltpu.CompilerParams(vmem_limit_bytes=mib << 20)


def scattered_sum(stored, decoded, here, meanwhile, settled):
    mems = lax.axis_size("mem")
    heads, width, rows = decoded.shape
    tokens = stored.shape[1]
    asked = lax.all_gather(stored, "mem", axis=0)
    partial = pl.pallas_call(
        pick_kernel,
        grid=(mems,),
        in_specs=[
            pl.BlockSpec(memory_space=pltpu.SMEM),
            pl.BlockSpec((None, heads, tokens), lambda m: (m, 0, 0)),
            whole(decoded),
        ],
        out_specs=pl.BlockSpec((None, heads * width, tokens), lambda m: (m, 0, 0)),
        out_shape=jax.ShapeDtypeStruct((mems, heads * width, tokens), BF16),
        compiler_params=limit(16),
        name="pick_all",
    )((here * rows).astype(I32).reshape(1), asked, decoded)
    total = lax.psum_scatter(partial, "mem", scatter_dimension=0, tiled=False)
    return total, meanwhile(partial, partial), settled


def line_sum(stored, decoded, here, meanwhile, settled):
    heads, width, rows = decoded.shape
    tokens = stored.shape[1]
    base = (here * rows).astype(I32).reshape(1)
    block = jax.ShapeDtypeStruct((heads * width, tokens), BF16)

    def ask(ids, x):
        return lax.ppermute(ids, "mem", [(i, i ^ x) for i in range(4)])

    def crossing(x, pairs):
        return lax.ppermute(x, ("mem", "rep"), [(2 * a + b, 2 * c + d) for a, b, c, d in pairs])

    def pick(ids):
        return pl.pallas_call(
            pick_kernel,
            in_specs=[pl.BlockSpec(memory_space=pltpu.SMEM)]
            + [pl.BlockSpec(memory_space=pltpu.VMEM)] * 2,
            out_shape=block,
            compiler_params=limit(8),
            name="pick_rows",
        )(base, ids, decoded)

    def send(x, *pairs):
        return lax.ppermute(x, "mem", pairs)

    first = ask(stored, 3)
    second = crossing(
        stored,
        [(m, r, m ^ 2, r ^ int(m in (1, 2))) for m in range(4) for r in range(2)],
    )
    third = ask(stored, 1)
    rows_3 = pick(first)
    rows_3, second, third = lax.optimization_barrier((rows_3, second, third))
    inward = send(rows_3, (0, 1), (3, 2))
    across = send(rows_3, (1, 2), (2, 1))
    rows_2 = pick(after(second, rows_3))
    third, settled = lax.optimization_barrier((after(third, rows_2), settled))
    past = crossing(rows_2, [(m, r, m ^ 2, r ^ 1) for m in (0, 3) for r in range(2)])
    rows_1 = pick(third)
    own = pick(after(stored, rows_1))
    beside = send(rows_1, (0, 1), (1, 0), (2, 3), (3, 2))
    onward = after(rows_2, rows_1, own) + inward
    onward_sum = onward
    onward = send(onward, (1, 3), (2, 0))
    other = meanwhile(across, onward_sum)
    own, other = lax.optimization_barrier((own + past + beside, other))
    memory = pl.pallas_call(
        merge_kernel,
        in_specs=[pl.BlockSpec(memory_space=pltpu.VMEM)] * 3,
        out_shape=block,
        compiler_params=limit(4),
        name="merge",
    )(own, across, onward)
    return memory, other, settled


def shards(
    hidden, row_ids, row_place, table_codes, table_scales, key_weight, value_weight, conv_weight
):
    mems = lax.axis_size("mem")
    tps = lax.axis_size("tp")
    reps = lax.axis_size("rep")
    blocks = mems * reps
    tokens, heads = row_ids.shape
    rows, width = table_codes.shape[1:]
    depth = heads * width
    half = key_weight.shape[1]
    seq_length = tokens * blocks // SEQS
    assert reps == 2 and seq_length % tokens == 0 and row_place.shape[0] % LANES == 0
    block = lax.axis_index(("mem", "rep"))
    smem = pl.BlockSpec(memory_space=pltpu.SMEM)

    anywhere = pl.BlockSpec(memory_space=pl.ANY)
    resident = pl.BlockSpec(memory_space=pltpu.VMEM)
    places = row_place.reshape(-1, LANES)
    codes = table_codes.transpose(0, 2, 1)
    scales = table_scales.transpose(2, 0, 1)
    stored, codes, scales = pl.pallas_call(
        place_kernel,
        in_specs=[anywhere] * 4,
        out_specs=(resident,) * 3,
        out_shape=(
            jax.ShapeDtypeStruct((heads, tokens), I32),
            jax.ShapeDtypeStruct(codes.shape, BF16),
            jax.ShapeDtypeStruct(scales.shape, BF16),
        ),
        scratch_shapes=[
            pltpu.VMEM((heads, tokens), I32),
            pltpu.VMEM(places.shape, I32),
            pltpu.SemaphoreType.DMA((heads + 3,)),
        ],
        compiler_params=limit(4),
        name="place_rows",
    )(*[in_hbm(x) for x in (row_ids.T, places, codes, scales)])
    decoded = pl.pallas_call(
        decode_kernel,
        in_specs=[resident] * 2,
        out_specs=resident,
        out_shape=jax.ShapeDtypeStruct(codes.shape, BF16),
        compiler_params=limit(6),
        name="decode_tables",
    )(codes, scales)
    here = lax.axis_index("mem")
    other_key = lax.ppermute(key_weight, "rep", [(0, 1), (1, 0)])
    other_value = lax.ppermute(value_weight, "rep", [(0, 1), (1, 0)])
    needed = [(i, i + 1) for i in range(blocks - 1) if (i + 1) * tokens % seq_length]

    where = jnp.stack([lax.axis_index("rep"), lax.axis_index("tp")]).astype(I32)

    def meanwhile(token, later):
        tail = after(hidden[tokens - RIM :], token)
        halo = lax.ppermute(tail, ("mem", "rep"), needed)
        ready = pl.pallas_call(
            functools.partial(load_kernel, tps),
            in_specs=[smem] + [anywhere] * 2,
            out_specs=resident,
            out_shape=pltpu.VMEM((2, depth, half), BF16),
            scratch_shapes=[pltpu.SemaphoreType.DMA((2, 1))],
            compiler_params=limit(4),
            name="load_weights",
        )(where, *[in_hbm(after(w, later)) for w in (key_weight, value_weight)])
        return halo, ready

    summed = line_sum if mems == 4 else scattered_sum
    memory, (hidden_halo, ready), others = summed(
        stored, decoded, here, meanwhile, (other_key, other_value)
    )
    weights = [in_hbm(w) for w in (key_weight, value_weight, *others)]

    extended = tokens + RIM
    bodies = [memory] + [
        lax.ppermute(memory, "tp", [(i, (i + s) % tps) for i in range(tps)])
        for s in range(1, tps)
    ]

    def next_rim(rim, s):
        pairs = [
            (
                (a // reps * tps + i) * reps + a % reps,
                (b // reps * tps + (i + s) % tps) * reps + b % reps,
            )
            for a, b in needed
            for i in range(tps)
        ]
        return lax.ppermute(rim, ("mem", "tp", "rep"), pairs)

    rim = memory[:, tokens - LANES :]
    rims = [next_rim(rim, s) for s in range(tps)]
    others = tps - 1
    field = jax.ShapeDtypeStruct((2, extended, half), F32)
    *begun, following, states, power = pl.pallas_call(
        functools.partial(project_own_kernel, tps),
        in_specs=[smem] + [resident] * 2 + [anywhere] * 4 + [resident] * 3,
        out_specs=(resident,) * 5,
        out_shape=(
            field,
            field,
            pltpu.VMEM((2, 2, others * depth, half), BF16),
            jax.ShapeDtypeStruct((2, extended, half), BF16),
            jax.ShapeDtypeStruct((extended, 8), F32),
        ),
        scratch_shapes=[
            pltpu.VMEM((2, depth, half), BF16),
            pltpu.SemaphoreType.DMA((2, 1)),
            pltpu.SemaphoreType.DMA((4, others)),
        ],
        compiler_params=limit(12),
        name="project_own",
    )(where, rims[0], memory, *weights, ready, hidden_halo, hidden)
    values, stats = pl.pallas_call(
        functools.partial(project_others_kernel, tps),
        in_specs=[smem] + [resident] * (2 * others + 5),
        out_specs=(pl.BlockSpec(memory_space=pltpu.HBM), resident),
        out_shape=(pltpu.HBM(field.shape, F32), jax.ShapeDtypeStruct((8, extended), F32)),
        scratch_shapes=[
            pltpu.VMEM((2, extended, half), F32),
            pltpu.SemaphoreType.DMA((2,)),
        ],
        compiler_params=limit(14),
        name="project_others",
    )(where, *rims[1:], *bodies[1:], following, *begun, states, power)

    all_stats = [stats] + [
        lax.ppermute(stats, "tp", [(i, (i + s) % tps) for i in range(tps)]) for s in range(1, tps)
    ]
    keep = (block * tokens % seq_length != 0).astype(I32).reshape(1)
    step = 2 * half
    if half % LANES == 0:
        step = next(c for c in (384, 256, 128) if half % c == 0)
    chunk = min(step, half)
    body = (2, tokens, half)
    values, products = pl.pallas_call(
        functools.partial(prepare_kernel, chunk),
        in_specs=[resident, anywhere],
        out_specs=(resident,) * 2,
        out_shape=(
            jax.ShapeDtypeStruct(body, F32),
            jax.ShapeDtypeStruct((KERNEL - 1, *body), F32),
        ),
        scratch_shapes=[
            pltpu.VMEM((2, extended, half), F32),
            pltpu.SemaphoreType.DMA((2 * half // chunk,)),
        ],
        compiler_params=limit(6),
        name="prepare",
    )(conv_weight, in_hbm(values))
    return pl.pallas_call(
        functools.partial(finish_kernel, tps, step),
        in_specs=[smem] + [resident] * (tps + 4),
        out_specs=anywhere,
        out_shape=jax.ShapeDtypeStruct((tokens, 2 * half), BF16),
        scratch_shapes=[
            pltpu.VMEM((extended, 8), F32),
            pltpu.VMEM((tokens, LANES), F32),
            pltpu.VMEM((KERNEL, tokens, LANES), F32),
            pltpu.VMEM((tokens, 2 * half), BF16),
            pltpu.SemaphoreType.DMA((2 * half // step,)),
        ],
        compiler_params=limit(6),
        name="finish",
    )(keep, *all_stats, values, products, hidden, conv_weight)


def solution(mesh):
    in_specs = (
        P(("parts", "mem", "rep"), "tp"),
        P(("parts", "mem", "rep"), "tp"),
        P("parts"),
        P(("parts", "tp"), "mem", None),
        P(("parts", "tp"), "mem", None),
        P(None, ("tp", "rep")),
        P(None, ("tp", "rep")),
        P(None, "tp"),
    )
    out_specs = P(("parts", "mem", "rep"), "tp")
    return jax.shard_map(shards, mesh=mesh, in_specs=in_specs, out_specs=out_specs, check_vma=False)
```

```python
import functools

import jax
import jax.numpy as jnp
from jax import lax
from jax.experimental import pallas as pl
from jax.experimental.pallas import tpu as pltpu
from jax.sharding import PartitionSpec as P

D = 4608
KERNEL = 4
DILATION = 3
SEQS = 4
EPSILON = 1e-06
RIM = 16
LANES = 128

F32 = jnp.float32
BF16 = jnp.bfloat16
I32 = jnp.int32


def iota(shape, axis):
    return lax.broadcasted_iota(I32, shape, axis)


def dot(a, b):
    return jnp.dot(a, b, preferred_element_type=F32)


def dot_nt(a, b, precision=None):
    return lax.dot_general(
        a, b, (((1,), (1,)), ((), ())), precision=precision, preferred_element_type=F32
    )


def unit(n, dtype):
    return (iota((n, n), 0) == iota((n, n), 1)).astype(F32).astype(dtype)


def to_bf16(x):
    return x.astype(F32).astype(BF16)


def place_kernel(
    ids_hbm, place_hbm, codes_hbm, scales_hbm, out_ref, codes_ref, scales_ref, ids_ref, place_ref, sems
):
    copies = [
        pltpu.make_async_copy(place_hbm, place_ref, sems.at[0]),
        pltpu.make_async_copy(ids_hbm, ids_ref, sems.at[1]),
        pltpu.make_async_copy(scales_hbm, scales_ref, sems.at[2]),
    ]
    for n in range(codes_ref.shape[0]):
        copies.append(
            pltpu.make_async_copy(codes_hbm.at[n], codes_ref.at[n], sems.at[3 + n])
        )
    for copy in copies:
        copy.start()
    copies[0].wait()
    place = place_ref[...]
    rows = place.shape[0]
    heads, tokens = ids_ref.shape
    eye = unit(LANES, BF16)
    table = jnp.concatenate(
        [dot_nt(eye, to_bf16(place >> 8)), dot_nt(eye, to_bf16(place & 255))], axis=0
    ).astype(BF16)
    copies[1].wait()
    for head in range(heads):
        row = ids_ref[head : head + 1, :]
        hot = to_bf16(iota((rows, tokens), 0) == (row >> 7))
        both = dot(table, hot)
        value = both[:LANES] * 256.0 + both[LANES:]
        chosen = jnp.where(iota(value.shape, 0) == (row & 127), value, 0.0)
        out_ref[head : head + 1, :] = jnp.sum(chosen, axis=0, keepdims=True).astype(I32)
    for copy in copies[2:]:
        copy.wait()


def decode_kernel(codes_ref, scales_ref, out_ref):
    heads, width, rows = codes_ref.shape
    blocks = scales_ref.shape[0]
    entry = iota((width, 2 * width), 0)
    column = iota((width, 2 * width), 1)
    column = jnp.where(column < width, column, column - width)
    parity = entry & column & 15
    parity = parity ^ (parity >> 2)
    parity = (parity ^ (parity >> 1)) & 1
    same = (entry >> 4) == (column >> 4)
    rotation = jnp.where(same, 0.25 - 0.5 * parity.astype(F32), 0.0).astype(BF16)
    for head in range(heads):
        factors = jnp.concatenate(
            [
                jnp.broadcast_to(scales_ref[b, head : head + 1, :].astype(F32), (16, rows))
                for b in range(blocks)
            ],
            axis=0,
        )
        scaled = codes_ref[head].astype(F32) * factors
        upper = scaled.astype(BF16)
        lower = (scaled - upper.astype(F32)).astype(BF16)
        out_ref[head] = dot(rotation, jnp.concatenate([upper, lower], axis=0)).astype(BF16)


def picked(local, table_ref, head):
    rows = table_ref.shape[2]
    hot = to_bf16(iota((rows, local.shape[1]), 0) == local[head : head + 1, :])
    return dot(table_ref[head], hot).astype(BF16)


def pick_kernel(base_ref, ids_ref, table_ref, out_ref):
    heads, width, _ = table_ref.shape
    local = ids_ref[...] - base_ref[0]
    for head in range(heads):
        out_ref[head * width : (head + 1) * width, :] = picked(local, table_ref, head)


def merge_kernel(*refs):
    total = refs[0][...].astype(F32)
    for other in refs[1:-1]:
        total = total + other[...].astype(F32)
    refs[-1][...] = total.astype(BF16)


def fetch(count, tp, depth, source, target, shifts, sems):
    copies = []
    for n, s in enumerate(shifts):
        owner = lax.rem(tp + count - s, count)
        rows = pl.ds(pl.multiple_of(owner * depth, depth), depth)
        copy = pltpu.make_async_copy(
            source.at[rows, :], target.at[pl.ds(n * depth, depth), :], sems.at[n]
        )
        copy.start()
        copies.append(copy)
    return copies


def await_all(copies):
    for copy in copies:
        copy.wait()


def with_rim(rims, bodies):
    body = jnp.concatenate([b[...].astype(F32) for b in bodies], axis=0).T.astype(BF16)
    rim = jnp.concatenate([r[...].astype(F32) for r in rims], axis=0).T.astype(BF16)
    return jnp.concatenate([rim[LANES - RIM :], body], axis=0)


def project_own_kernel(count, where_ref, rim_ref, body_ref, *refs):
    weights, hidden_halo, hidden = refs[:4], refs[4], refs[5]
    key_ref, value_ref, next_ref, states_ref, power_ref, held, sems, next_sems = refs[6:]
    half = value_ref.shape[-1]
    depth = body_ref.shape[0]
    rep = where_ref[0]
    tp = where_ref[1]
    order = [(far, which) for far in range(2) for which in (1, 0)]
    copies = {
        (far, which): fetch(
            count, tp, depth, weights[2 * far + which], held.at[far, which], (0,),
            sems.at[2 * far + which],
        )
        for far, which in order
    }
    power = 0.0
    for slot in range(2):
        span = slice(slot * half, (slot + 1) * half)
        states_ref[slot, :RIM] = hidden_halo[:, span]
        states_ref[slot, RIM:] = hidden[:, span]
        here = states_ref[slot].astype(F32)
        power = power + jnp.sum(here * here, axis=1, keepdims=True)
    power_ref[...] = jnp.broadcast_to(power, power_ref.shape)
    memory = with_rim([rim_ref], [body_ref])
    later = []
    for far, which in order:
        slot = rep if far == 0 else 1 - rep
        await_all(copies[far, which])
        if (far, which) == (0, 0):
            for f, w in order:
                later += fetch(
                    count, tp, depth, weights[2 * f + w], next_ref.at[f, w], range(1, count),
                    next_sems.at[2 * f + w],
                )
        target = value_ref if which == 1 else key_ref
        target[slot] = dot(memory, held[far, which])
    await_all(later)


def project_others_kernel(count, where_ref, *refs):
    pieces = count - 1
    rims, bodies = refs[:pieces], refs[pieces : 2 * pieces]
    held, begun_keys, begun_values, states_ref, power_ref = refs[2 * pieces :][:5]
    value_hbm, stats_ref, done, done_sems = refs[2 * pieces + 5 :]
    rep = where_ref[0]
    memory = with_rim(rims, bodies)
    sums = [0.0] * 3
    later = []
    for far in range(2):
        slot = rep if far == 0 else 1 - rep
        fields = [None, None]
        for which in (1, 0):
            fields[which] = dot(memory, held[far, which])
            if which == 1:
                done[far] = fields[1] + begun_values[slot]
                copy = pltpu.make_async_copy(done.at[far], value_hbm.at[slot], done_sems.at[far])
                copy.start()
                later.append(copy)
        keys = fields[0] + begun_keys[slot]
        values = done[far]
        terms = (keys * keys, states_ref[slot].astype(F32) * keys, values * values)
        sums = [a + jnp.sum(t, axis=1, keepdims=True) for a, t in zip(sums, terms)]
    packed = power_ref[...]
    lane = iota(packed.shape, 1)
    for k in range(3):
        packed = jnp.where(lane == k + 1, sums[k], packed)
    stats_ref[...] = dot_nt(unit(8, F32), packed, lax.Precision.HIGHEST)
    await_all(later)


def prepare_kernel(chunk, taps_ref, value_hbm, value_ref, tap_ref, rows_ref, sems):
    half = rows_ref.shape[-1]
    tokens = value_ref.shape[1]
    copies = []
    for slot in range(2):
        for start in range(0, half, chunk):
            span = pl.ds(start, chunk)
            copy = pltpu.make_async_copy(
                value_hbm.at[slot, :, span], rows_ref.at[slot, :, span], sems.at[len(copies)]
            )
            copy.start()
            copies.append(copy)
    for slot in range(2):
        for start in range(0, half, LANES):
            size = min(LANES, half - start)
            span = slice(start, start + size)
            there = slice(slot * half + start, slot * half + start + size)
            if start % chunk == 0:
                copies[(slot * half + start) // chunk].wait()
            value_ref[slot, :, span] = rows_ref[slot, RIM:, span]
            for tap in range(1, KERNEL):
                lag = DILATION * tap
                rows = rows_ref[slot, RIM - lag : RIM - lag + tokens, span]
                tap_ref[tap - 1, slot, :, span] = taps_ref[tap : tap + 1, there] * rows


def finish_kernel(count, step, keep_ref, *refs):
    stats = refs[:count]
    value_ref, tap_ref, hidden_ref, taps_ref, out_hbm = refs[count : count + 5]
    columns, gates, factors, out_ref, sems = refs[count + 5 :]
    half = value_ref.shape[-1]
    tokens, width = out_ref.shape
    total = stats[0][...]
    for other in stats[1:]:
        total = total + other[...]
    inverse_states = lax.rsqrt(total[0:1] / D + EPSILON)
    inverse_keys = lax.rsqrt(total[1:2] / D + EPSILON)
    gate = jax.nn.sigmoid(total[2:3] * inverse_states * inverse_keys / D**0.5)
    factor = gate * lax.rsqrt(gate * gate * total[3:4] / D + EPSILON)
    factor = jnp.where((iota(factor.shape, 1) < RIM) & (keep_ref[0] == 0), 0.0, factor)
    line = iota(total.shape, 0)
    both = jnp.where(line == 0, gate, jnp.where(line == 1, factor, 0.0))
    columns[...] = dot_nt(unit(total.shape[1], F32), both, lax.Precision.HIGHEST)
    gates[...] = jnp.broadcast_to(columns[RIM:, 0:1], gates.shape)
    for tap in range(KERNEL):
        lag = DILATION * tap
        factors[tap] = jnp.broadcast_to(
            columns[RIM - lag : RIM - lag + tokens, 1:2], factors.shape[1:]
        )
    copies = []
    for slot in range(2):
        for start in range(0, half, LANES):
            size = min(LANES, half - start)
            span = slice(start, start + size)
            there = slice(slot * half + start, slot * half + start + size)
            values = value_ref[slot, :, span]
            conv = taps_ref[0:1, there] * values * factors[0, :, :size]
            for tap in range(1, KERNEL):
                conv = conv + tap_ref[tap - 1, slot, :, span] * factors[tap, :, :size]
            gated = values * gates[:, :size]
            out_ref[:, there] = (
                hidden_ref[:, there].astype(F32) + jax.nn.silu(conv) + gated
            ).astype(BF16)
            if there.stop % step == 0:
                ready = pl.ds(there.stop - step, step)
                copy = pltpu.make_async_copy(
                    out_ref.at[:, ready], out_hbm.at[:, ready], sems.at[len(copies)]
                )
                copy.start()
                copies.append(copy)
    for copy in copies:
        copy.wait()


def whole(array):
    return pl.BlockSpec(array.shape, lambda *_: (0,) * array.ndim)


def in_hbm(array):
    return pltpu.with_memory_space_constraint(array, pltpu.HBM)


def after(array, *others):
    return lax.optimization_barrier((array, *others))[0]


def limit(mib):
    return pltpu.CompilerParams(vmem_limit_bytes=mib << 20)


def scattered_sum(stored, decoded, here, meanwhile, settled):
    mems = lax.axis_size("mem")
    heads, width, rows = decoded.shape
    tokens = stored.shape[1]
    asked = lax.all_gather(stored, "mem", axis=0)
    partial = pl.pallas_call(
        pick_kernel,
        grid=(mems,),
        in_specs=[
            pl.BlockSpec(memory_space=pltpu.SMEM),
            pl.BlockSpec((None, heads, tokens), lambda m: (m, 0, 0)),
            whole(decoded),
        ],
        out_specs=pl.BlockSpec((None, heads * width, tokens), lambda m: (m, 0, 0)),
        out_shape=jax.ShapeDtypeStruct((mems, heads * width, tokens), BF16),
        compiler_params=limit(16),
        name="pick_all",
    )((here * rows).astype(I32).reshape(1), asked, decoded)
    total = lax.psum_scatter(partial, "mem", scatter_dimension=0, tiled=False)
    return total, meanwhile(partial), settled


def line_sum(stored, decoded, here, meanwhile, settled):
    heads, width, rows = decoded.shape
    tokens = stored.shape[1]
    base = (here * rows).astype(I32).reshape(1)
    block = jax.ShapeDtypeStruct((heads * width, tokens), BF16)

    def ask(ids, x):
        return lax.ppermute(ids, "mem", [(i, i ^ x) for i in range(4)])

    def crossing(x, pairs):
        return lax.ppermute(x, ("mem", "rep"), [(2 * a + b, 2 * c + d) for a, b, c, d in pairs])

    def pick(ids):
        return pl.pallas_call(
            pick_kernel,
            in_specs=[pl.BlockSpec(memory_space=pltpu.SMEM)]
            + [pl.BlockSpec(memory_space=pltpu.VMEM)] * 2,
            out_shape=block,
            compiler_params=limit(8),
            name="pick_rows",
        )(base, ids, decoded)

    def send(x, *pairs):
        return lax.ppermute(x, "mem", pairs)

    first = ask(stored, 3)
    second = crossing(
        stored,
        [(m, r, m ^ 2, r ^ int(m in (1, 2))) for m in range(4) for r in range(2)],
    )
    third = ask(stored, 1)
    rows_3 = pick(first)
    rows_3, second, third = lax.optimization_barrier((rows_3, second, third))
    inward = send(rows_3, (0, 1), (3, 2))
    across = send(rows_3, (1, 2), (2, 1))
    rows_2 = pick(after(second, rows_3))
    third, settled = lax.optimization_barrier((after(third, rows_2), settled))
    past = crossing(rows_2, [(m, r, m ^ 2, r ^ 1) for m in (0, 3) for r in range(2)])
    rows_1 = pick(third)
    own = pick(after(stored, rows_1))
    beside = send(rows_1, (0, 1), (1, 0), (2, 3), (3, 2))
    onward = after(rows_2, rows_1, own) + inward
    onward = send(onward, (1, 3), (2, 0))
    other = meanwhile(across)
    own, other = lax.optimization_barrier((own + past + beside, other))
    memory = pl.pallas_call(
        merge_kernel,
        in_specs=[pl.BlockSpec(memory_space=pltpu.VMEM)] * 3,
        out_shape=block,
        compiler_params=limit(4),
        name="merge",
    )(own, across, onward)
    return memory, other, settled


def shards(
    hidden, row_ids, row_place, table_codes, table_scales, key_weight, value_weight, conv_weight
):
    mems = lax.axis_size("mem")
    tps = lax.axis_size("tp")
    reps = lax.axis_size("rep")
    blocks = mems * reps
    tokens, heads = row_ids.shape
    rows, width = table_codes.shape[1:]
    depth = heads * width
    half = key_weight.shape[1]
    seq_length = tokens * blocks // SEQS
    assert reps == 2 and seq_length % tokens == 0 and row_place.shape[0] % LANES == 0
    block = lax.axis_index(("mem", "rep"))
    smem = pl.BlockSpec(memory_space=pltpu.SMEM)

    anywhere = pl.BlockSpec(memory_space=pl.ANY)
    resident = pl.BlockSpec(memory_space=pltpu.VMEM)
    places = row_place.reshape(-1, LANES)
    codes = table_codes.transpose(0, 2, 1)
    scales = table_scales.transpose(2, 0, 1)
    stored, codes, scales = pl.pallas_call(
        place_kernel,
        in_specs=[anywhere] * 4,
        out_specs=(resident,) * 3,
        out_shape=(
            jax.ShapeDtypeStruct((heads, tokens), I32),
            jax.ShapeDtypeStruct(codes.shape, BF16),
            jax.ShapeDtypeStruct(scales.shape, BF16),
        ),
        scratch_shapes=[
            pltpu.VMEM((heads, tokens), I32),
            pltpu.VMEM(places.shape, I32),
            pltpu.SemaphoreType.DMA((heads + 3,)),
        ],
        compiler_params=limit(4),
        name="place_rows",
    )(*[in_hbm(x) for x in (row_ids.T, places, codes, scales)])
    decoded = pl.pallas_call(
        decode_kernel,
        in_specs=[resident] * 2,
        out_specs=resident,
        out_shape=jax.ShapeDtypeStruct(codes.shape, BF16),
        compiler_params=limit(6),
        name="decode_tables",
    )(codes, scales)
    here = lax.axis_index("mem")
    other_key = lax.ppermute(key_weight, "rep", [(0, 1), (1, 0)])
    other_value = lax.ppermute(value_weight, "rep", [(0, 1), (1, 0)])
    needed = [(i, i + 1) for i in range(blocks - 1) if (i + 1) * tokens % seq_length]

    def meanwhile(token):
        tail = after(hidden[tokens - RIM :], token)
        return lax.ppermute(tail, ("mem", "rep"), needed)

    summed = line_sum if mems == 4 else scattered_sum
    memory, hidden_halo, others = summed(
        stored, decoded, here, meanwhile, (other_key, other_value)
    )
    weights = [in_hbm(w) for w in (key_weight, value_weight, *others)]

    where = jnp.stack([lax.axis_index("rep"), lax.axis_index("tp")]).astype(I32)
    extended = tokens + RIM
    bodies = [memory] + [
        lax.ppermute(memory, "tp", [(i, (i + s) % tps) for i in range(tps)])
        for s in range(1, tps)
    ]

    def next_rim(rim, s):
        pairs = [
            (
                (a // reps * tps + i) * reps + a % reps,
                (b // reps * tps + (i + s) % tps) * reps + b % reps,
            )
            for a, b in needed
            for i in range(tps)
        ]
        return lax.ppermute(rim, ("mem", "tp", "rep"), pairs)

    rim = memory[:, tokens - LANES :]
    rims = [next_rim(rim, s) for s in range(tps)]
    others = tps - 1
    field = jax.ShapeDtypeStruct((2, extended, half), F32)
    *begun, following, states, power = pl.pallas_call(
        functools.partial(project_own_kernel, tps),
        in_specs=[smem] + [resident] * 2 + [anywhere] * 4 + [resident] * 2,
        out_specs=(resident,) * 5,
        out_shape=(
            field,
            field,
            pltpu.VMEM((2, 2, others * depth, half), BF16),
            jax.ShapeDtypeStruct((2, extended, half), BF16),
            jax.ShapeDtypeStruct((extended, 8), F32),
        ),
        scratch_shapes=[
            pltpu.VMEM((2, 2, depth, half), BF16),
            pltpu.SemaphoreType.DMA((4, 1)),
            pltpu.SemaphoreType.DMA((4, others)),
        ],
        compiler_params=limit(12),
        name="project_own",
    )(where, rims[0], memory, *weights, hidden_halo, hidden)
    values, stats = pl.pallas_call(
        functools.partial(project_others_kernel, tps),
        in_specs=[smem] + [resident] * (2 * others + 5),
        out_specs=(pl.BlockSpec(memory_space=pltpu.HBM), resident),
        out_shape=(pltpu.HBM(field.shape, F32), jax.ShapeDtypeStruct((8, extended), F32)),
        scratch_shapes=[
            pltpu.VMEM((2, extended, half), F32),
            pltpu.SemaphoreType.DMA((2,)),
        ],
        compiler_params=limit(14),
        name="project_others",
    )(where, *rims[1:], *bodies[1:], following, *begun, states, power)

    all_stats = [stats] + [
        lax.ppermute(stats, "tp", [(i, (i + s) % tps) for i in range(tps)]) for s in range(1, tps)
    ]
    keep = (block * tokens % seq_length != 0).astype(I32).reshape(1)
    step = 2 * half
    if half % LANES == 0:
        step = next(c for c in (384, 256, 128) if half % c == 0)
    chunk = min(step, half)
    body = (2, tokens, half)
    values, products = pl.pallas_call(
        functools.partial(prepare_kernel, chunk),
        in_specs=[resident, anywhere],
        out_specs=(resident,) * 2,
        out_shape=(
            jax.ShapeDtypeStruct(body, F32),
            jax.ShapeDtypeStruct((KERNEL - 1, *body), F32),
        ),
        scratch_shapes=[
            pltpu.VMEM((2, extended, half), F32),
            pltpu.SemaphoreType.DMA((2 * half // chunk,)),
        ],
        compiler_params=limit(6),
        name="prepare",
    )(conv_weight, in_hbm(values))
    return pl.pallas_call(
        functools.partial(finish_kernel, tps, step),
        in_specs=[smem] + [resident] * (tps + 4),
        out_specs=anywhere,
        out_shape=jax.ShapeDtypeStruct((tokens, 2 * half), BF16),
        scratch_shapes=[
            pltpu.VMEM((extended, 8), F32),
            pltpu.VMEM((tokens, LANES), F32),
            pltpu.VMEM((KERNEL, tokens, LANES), F32),
            pltpu.VMEM((tokens, 2 * half), BF16),
            pltpu.SemaphoreType.DMA((2 * half // step,)),
        ],
        compiler_params=limit(6),
        name="finish",
    )(keep, *all_stats, values, products, hidden, conv_weight)


def solution(mesh):
    in_specs = (
        P(("parts", "mem", "rep"), "tp"),
        P(("parts", "mem", "rep"), "tp"),
        P("parts"),
        P(("parts", "tp"), "mem", None),
        P(("parts", "tp"), "mem", None),
        P(None, ("tp", "rep")),
        P(None, ("tp", "rep")),
        P(None, "tp"),
    )
    out_specs = P(("parts", "mem", "rep"), "tp")
    return jax.shard_map(shards, mesh=mesh, in_specs=in_specs, out_specs=out_specs, check_vma=False)
```

```python
import functools

import jax
import jax.numpy as jnp
from jax import lax
from jax.experimental import pallas as pl
from jax.experimental.pallas import tpu as pltpu
from jax.sharding import PartitionSpec as P

D = 4608
KERNEL = 4
DILATION = 3
SEQS = 4
EPSILON = 1e-06
RIM = 16
LANES = 128

F32 = jnp.float32
BF16 = jnp.bfloat16
I32 = jnp.int32


def iota(shape, axis):
    return lax.broadcasted_iota(I32, shape, axis)


def dot(a, b):
    return jnp.dot(a, b, preferred_element_type=F32)


def dot_nt(a, b, precision=None):
    return lax.dot_general(
        a, b, (((1,), (1,)), ((), ())), precision=precision, preferred_element_type=F32
    )


def unit(n, dtype):
    return (iota((n, n), 0) == iota((n, n), 1)).astype(F32).astype(dtype)


def to_bf16(x):
    return x.astype(F32).astype(BF16)


def place_ids(ids, place, out_ref):
    rows = place.shape[0]
    heads, tokens = ids.shape
    eye = unit(LANES, BF16)
    table = jnp.concatenate(
        [dot_nt(eye, to_bf16(place >> 8)), dot_nt(eye, to_bf16(place & 255))], axis=0
    ).astype(BF16)
    for head in range(heads):
        row = ids[head : head + 1, :]
        hot = to_bf16(iota((rows, tokens), 0) == (row >> 7))
        both = dot(table, hot)
        value = both[:LANES] * 256.0 + both[LANES:]
        chosen = jnp.where(iota(value.shape, 0) == (row & 127), value, 0.0)
        out_ref[head : head + 1, :] = jnp.sum(chosen, axis=0, keepdims=True).astype(I32)


def place_kernel(ids_ref, place_ref, out_ref):
    place_ids(ids_ref[...], place_ref[...], out_ref)


def fetch_kernel(
    place_hbm, ids_hbm, codes_hbm, scales_hbm, place_ref, codes_ref, scales_ref, out_ref, ids_ref, sems
):
    pairs = [(place_hbm, place_ref), (ids_hbm, ids_ref), (scales_hbm, scales_ref)]
    pairs += [(codes_hbm.at[n], codes_ref.at[n]) for n in range(codes_ref.shape[0])]
    copies = []
    for source, target in pairs:
        copies.append(pltpu.make_async_copy(source, target, sems.at[len(copies)]))
        copies[-1].start()
    await_all(copies[:2])
    place_ids(ids_ref[...], place_ref[...], out_ref)
    await_all(copies[2:])


def decode_kernel(codes_ref, scales_ref, out_ref):
    heads, width, rows = codes_ref.shape
    blocks = scales_ref.shape[0]
    entry = iota((width, 2 * width), 0)
    column = iota((width, 2 * width), 1)
    column = jnp.where(column < width, column, column - width)
    parity = entry & column & 15
    parity = parity ^ (parity >> 2)
    parity = (parity ^ (parity >> 1)) & 1
    same = (entry >> 4) == (column >> 4)
    rotation = jnp.where(same, 0.25 - 0.5 * parity.astype(F32), 0.0).astype(BF16)
    for head in range(heads):
        factors = jnp.concatenate(
            [
                jnp.broadcast_to(scales_ref[b, head : head + 1, :].astype(F32), (16, rows))
                for b in range(blocks)
            ],
            axis=0,
        )
        scaled = codes_ref[head].astype(F32) * factors
        upper = scaled.astype(BF16)
        lower = (scaled - upper.astype(F32)).astype(BF16)
        out_ref[head] = dot(rotation, jnp.concatenate([upper, lower], axis=0)).astype(BF16)


def picked(local, table_ref, head):
    rows = table_ref.shape[2]
    hot = to_bf16(iota((rows, local.shape[1]), 0) == local[head : head + 1, :])
    return dot(table_ref[head], hot).astype(BF16)


def pick_kernel(base_ref, ids_ref, table_ref, out_ref):
    heads, width, _ = table_ref.shape
    local = ids_ref[...] - base_ref[0]
    for head in range(heads):
        out_ref[head * width : (head + 1) * width, :] = picked(local, table_ref, head)


def merge_kernel(*refs):
    total = refs[0][...].astype(F32)
    for other in refs[1:-1]:
        total = total + other[...].astype(F32)
    refs[-1][...] = total.astype(BF16)


def fetch(count, tp, depth, source, target, shifts, sems):
    copies = []
    for n, s in enumerate(shifts):
        owner = lax.rem(tp + count - s, count)
        rows = pl.ds(pl.multiple_of(owner * depth, depth), depth)
        copy = pltpu.make_async_copy(
            source.at[rows, :], target.at[pl.ds(n * depth, depth), :], sems.at[n]
        )
        copy.start()
        copies.append(copy)
    return copies


def await_all(copies):
    for copy in copies:
        copy.wait()


def with_rim(rims, bodies):
    body = jnp.concatenate([b[...].astype(F32) for b in bodies], axis=0).T.astype(BF16)
    rim = jnp.concatenate([r[...].astype(F32) for r in rims], axis=0).T.astype(BF16)
    return jnp.concatenate([rim[LANES - RIM :], body], axis=0)


def project_own_kernel(count, where_ref, rim_ref, body_ref, *refs):
    weights, hidden_halo, hidden = refs[:4], refs[4], refs[5]
    key_ref, value_ref, next_ref, states_ref, power_ref, held, sems, next_sems = refs[6:]
    half = value_ref.shape[-1]
    depth = body_ref.shape[0]
    rep = where_ref[0]
    tp = where_ref[1]
    order = [(far, which) for far in range(2) for which in (1, 0)]
    copies = {
        (far, which): fetch(
            count, tp, depth, weights[2 * far + which], held.at[far, which], (0,),
            sems.at[2 * far + which],
        )
        for far, which in order
    }
    power = 0.0
    for slot in range(2):
        span = slice(slot * half, (slot + 1) * half)
        states_ref[slot, :RIM] = hidden_halo[:, span]
        states_ref[slot, RIM:] = hidden[:, span]
        here = states_ref[slot].astype(F32)
        power = power + jnp.sum(here * here, axis=1, keepdims=True)
    power_ref[...] = jnp.broadcast_to(power, power_ref.shape)
    memory = with_rim([rim_ref], [body_ref])
    later = []
    for far, which in order:
        slot = rep if far == 0 else 1 - rep
        await_all(copies[far, which])
        if not later:
            for f, w in order:
                later += fetch(
                    count, tp, depth, weights[2 * f + w], next_ref.at[f, w], range(1, count),
                    next_sems.at[2 * f + w],
                )
        target = value_ref if which == 1 else key_ref
        target[slot] = dot(memory, held[far, which])
    await_all(later)


def project_others_kernel(count, where_ref, *refs):
    pieces = count - 1
    rims, bodies = refs[:pieces], refs[pieces : 2 * pieces]
    held, begun_keys, begun_values, states_ref, power_ref = refs[2 * pieces :][:5]
    value_hbm, stats_ref, done, done_sems = refs[2 * pieces + 5 :]
    rep = where_ref[0]
    memory = with_rim(rims, bodies)
    sums = [0.0] * 3
    later = []
    for far in range(2):
        slot = rep if far == 0 else 1 - rep
        fields = [None, None]
        for which in (1, 0):
            fields[which] = dot(memory, held[far, which])
            if which == 1:
                done[far] = fields[1] + begun_values[slot]
                copy = pltpu.make_async_copy(done.at[far], value_hbm.at[slot], done_sems.at[far])
                copy.start()
                later.append(copy)
        keys = fields[0] + begun_keys[slot]
        values = done[far]
        terms = (keys * keys, states_ref[slot].astype(F32) * keys, values * values)
        sums = [a + jnp.sum(t, axis=1, keepdims=True) for a, t in zip(sums, terms)]
    packed = power_ref[...]
    lane = iota(packed.shape, 1)
    for k in range(3):
        packed = jnp.where(lane == k + 1, sums[k], packed)
    stats_ref[...] = dot_nt(unit(8, F32), packed, lax.Precision.HIGHEST)
    await_all(later)


def prepare_kernel(chunk, taps_ref, value_hbm, value_ref, tap_ref, rows_ref, sems):
    half = rows_ref.shape[-1]
    tokens = value_ref.shape[1]
    copies = []
    for slot in range(2):
        for start in range(0, half, chunk):
            span = pl.ds(start, chunk)
            copy = pltpu.make_async_copy(
                value_hbm.at[slot, :, span], rows_ref.at[slot, :, span], sems.at[len(copies)]
            )
            copy.start()
            copies.append(copy)
    for slot in range(2):
        for start in range(0, half, LANES):
            size = min(LANES, half - start)
            span = slice(start, start + size)
            there = slice(slot * half + start, slot * half + start + size)
            if start % chunk == 0:
                copies[(slot * half + start) // chunk].wait()
            value_ref[slot, :, span] = rows_ref[slot, RIM:, span]
            for tap in range(1, KERNEL):
                lag = DILATION * tap
                rows = rows_ref[slot, RIM - lag : RIM - lag + tokens, span]
                tap_ref[tap - 1, slot, :, span] = taps_ref[tap : tap + 1, there] * rows


def finish_kernel(count, step, keep_ref, *refs):
    stats = refs[:count]
    value_ref, tap_ref, hidden_ref, taps_ref, out_hbm = refs[count : count + 5]
    columns, gates, factors, out_ref, sems = refs[count + 5 :]
    half = value_ref.shape[-1]
    tokens, width = out_ref.shape
    total = stats[0][...]
    for other in stats[1:]:
        total = total + other[...]
    inverse_states = lax.rsqrt(total[0:1] / D + EPSILON)
    inverse_keys = lax.rsqrt(total[1:2] / D + EPSILON)
    gate = jax.nn.sigmoid(total[2:3] * inverse_states * inverse_keys / D**0.5)
    factor = gate * lax.rsqrt(gate * gate * total[3:4] / D + EPSILON)
    factor = jnp.where((iota(factor.shape, 1) < RIM) & (keep_ref[0] == 0), 0.0, factor)
    line = iota(total.shape, 0)
    both = jnp.where(line == 0, gate, jnp.where(line == 1, factor, 0.0))
    columns[...] = dot_nt(unit(total.shape[1], F32), both, lax.Precision.HIGHEST)
    gates[...] = jnp.broadcast_to(columns[RIM:, 0:1], gates.shape)
    for tap in range(KERNEL):
        lag = DILATION * tap
        factors[tap] = jnp.broadcast_to(
            columns[RIM - lag : RIM - lag + tokens, 1:2], factors.shape[1:]
        )
    copies = []
    for slot in range(2):
        for start in range(0, half, LANES):
            size = min(LANES, half - start)
            span = slice(start, start + size)
            there = slice(slot * half + start, slot * half + start + size)
            values = value_ref[slot, :, span]
            conv = taps_ref[0:1, there] * values * factors[0, :, :size]
            for tap in range(1, KERNEL):
                conv = conv + tap_ref[tap - 1, slot, :, span] * factors[tap, :, :size]
            gated = values * gates[:, :size]
            out_ref[:, there] = (
                hidden_ref[:, there].astype(F32) + jax.nn.silu(conv) + gated
            ).astype(BF16)
            if there.stop % step == 0:
                ready = pl.ds(there.stop - step, step)
                copy = pltpu.make_async_copy(
                    out_ref.at[:, ready], out_hbm.at[:, ready], sems.at[len(copies)]
                )
                copy.start()
                copies.append(copy)
    for copy in copies:
        copy.wait()


def whole(array):
    return pl.BlockSpec(array.shape, lambda *_: (0,) * array.ndim)


def in_hbm(array):
    return pltpu.with_memory_space_constraint(array, pltpu.HBM)


def after(array, *others):
    return lax.optimization_barrier((array, *others))[0]


def limit(mib):
    return pltpu.CompilerParams(vmem_limit_bytes=mib << 20)


def scattered_sum(raw, place, stored, decoded, here, meanwhile, settled):
    mems = lax.axis_size("mem")
    heads, width, rows = decoded.shape
    tokens = stored.shape[1]
    asked = lax.all_gather(stored, "mem", axis=0)
    partial = pl.pallas_call(
        pick_kernel,
        grid=(mems,),
        in_specs=[
            pl.BlockSpec(memory_space=pltpu.SMEM),
            pl.BlockSpec((None, heads, tokens), lambda m: (m, 0, 0)),
            whole(decoded),
        ],
        out_specs=pl.BlockSpec((None, heads * width, tokens), lambda m: (m, 0, 0)),
        out_shape=jax.ShapeDtypeStruct((mems, heads * width, tokens), BF16),
        compiler_params=limit(16),
        name="pick_all",
    )((here * rows).astype(I32).reshape(1), asked, decoded)
    total = lax.psum_scatter(partial, "mem", scatter_dimension=0, tiled=False)
    return total, meanwhile(partial), settled


def line_sum(raw, place, stored, decoded, here, meanwhile, settled):
    heads, width, rows = decoded.shape
    tokens = stored.shape[1]
    base = (here * rows).astype(I32).reshape(1)
    block = jax.ShapeDtypeStruct((heads * width, tokens), BF16)

    def ask(ids, x):
        return lax.ppermute(ids, "mem", [(i, i ^ x) for i in range(4)])

    def crossing(x, pairs):
        return lax.ppermute(x, ("mem", "rep"), [(2 * a + b, 2 * c + d) for a, b, c, d in pairs])

    def pick(ids):
        return pl.pallas_call(
            pick_kernel,
            in_specs=[pl.BlockSpec(memory_space=pltpu.SMEM)]
            + [pl.BlockSpec(memory_space=pltpu.VMEM)] * 2,
            out_shape=block,
            compiler_params=limit(8),
            name="pick_rows",
        )(base, ids, decoded)

    def send(x, *pairs):
        return lax.ppermute(x, "mem", pairs)

    first = ask(raw, 3)
    second = crossing(
        raw,
        [(m, r, m ^ 2, r ^ int(m in (1, 2))) for m in range(4) for r in range(2)],
    )
    third = ask(raw, 1)
    rows_3 = pick(place(first))
    rows_3, second, third = lax.optimization_barrier((rows_3, second, third))
    inward = send(rows_3, (0, 1), (3, 2))
    across = send(rows_3, (1, 2), (2, 1))
    rows_2 = pick(place(after(second, rows_3)))
    third, settled = lax.optimization_barrier((after(third, rows_2), settled))
    past = crossing(rows_2, [(m, r, m ^ 2, r ^ 1) for m in (0, 3) for r in range(2)])
    rows_1 = pick(place(third))
    own = pick(after(stored, rows_1))
    beside = send(rows_1, (0, 1), (1, 0), (2, 3), (3, 2))
    onward = after(rows_2, rows_1, own) + inward
    onward = send(onward, (1, 3), (2, 0))
    other = meanwhile(across)
    own, other = lax.optimization_barrier((own + past + beside, other))
    memory = pl.pallas_call(
        merge_kernel,
        in_specs=[pl.BlockSpec(memory_space=pltpu.VMEM)] * 3,
        out_shape=block,
        compiler_params=limit(4),
        name="merge",
    )(own, across, onward)
    return memory, other, settled


def shards(
    hidden, row_ids, row_place, table_codes, table_scales, key_weight, value_weight, conv_weight
):
    mems = lax.axis_size("mem")
    tps = lax.axis_size("tp")
    reps = lax.axis_size("rep")
    blocks = mems * reps
    tokens, heads = row_ids.shape
    rows, width = table_codes.shape[1:]
    depth = heads * width
    half = key_weight.shape[1]
    seq_length = tokens * blocks // SEQS
    assert reps == 2 and seq_length % tokens == 0 and row_place.shape[0] % LANES == 0
    block = lax.axis_index(("mem", "rep"))
    smem = pl.BlockSpec(memory_space=pltpu.SMEM)

    anywhere = pl.BlockSpec(memory_space=pl.ANY)
    resident = pl.BlockSpec(memory_space=pltpu.VMEM)
    places = row_place.reshape(-1, LANES)
    codes = table_codes.transpose(0, 2, 1)
    scales = table_scales.transpose(2, 0, 1)
    raw = row_ids.T
    placed = jax.ShapeDtypeStruct(raw.shape, I32)
    places, codes, scales, stored = pl.pallas_call(
        fetch_kernel,
        in_specs=[anywhere] * 4,
        out_specs=(resident,) * 4,
        out_shape=(
            jax.ShapeDtypeStruct(places.shape, I32),
            jax.ShapeDtypeStruct(codes.shape, BF16),
            jax.ShapeDtypeStruct(scales.shape, BF16),
            placed,
        ),
        scratch_shapes=[
            pltpu.VMEM(raw.shape, I32),
            pltpu.SemaphoreType.DMA((heads + 3,)),
        ],
        compiler_params=limit(4),
        name="fetch_tables",
    )(*[in_hbm(x) for x in (places, raw, codes, scales)])

    def place(ids):
        return pl.pallas_call(
            place_kernel,
            in_specs=[resident] * 2,
            out_specs=resident,
            out_shape=placed,
            compiler_params=limit(4),
            name="place_rows",
        )(ids, places)

    decoded = pl.pallas_call(
        decode_kernel,
        in_specs=[resident] * 2,
        out_specs=resident,
        out_shape=jax.ShapeDtypeStruct(codes.shape, BF16),
        compiler_params=limit(6),
        name="decode_tables",
    )(codes, scales)
    here = lax.axis_index("mem")
    other_key = lax.ppermute(key_weight, "rep", [(0, 1), (1, 0)])
    other_value = lax.ppermute(value_weight, "rep", [(0, 1), (1, 0)])
    needed = [(i, i + 1) for i in range(blocks - 1) if (i + 1) * tokens % seq_length]

    def meanwhile(token):
        tail = after(hidden[tokens - RIM :], token)
        return lax.ppermute(tail, ("mem", "rep"), needed)

    summed = line_sum if mems == 4 else scattered_sum
    memory, hidden_halo, others = summed(
        raw, place, stored, decoded, here, meanwhile, (other_key, other_value)
    )
    weights = [in_hbm(w) for w in (key_weight, value_weight, *others)]

    where = jnp.stack([lax.axis_index("rep"), lax.axis_index("tp")]).astype(I32)
    extended = tokens + RIM
    bodies = [memory] + [
        lax.ppermute(memory, "tp", [(i, (i + s) % tps) for i in range(tps)])
        for s in range(1, tps)
    ]

    def next_rim(rim, s):
        pairs = [
            (
                (a // reps * tps + i) * reps + a % reps,
                (b // reps * tps + (i + s) % tps) * reps + b % reps,
            )
            for a, b in needed
            for i in range(tps)
        ]
        return lax.ppermute(rim, ("mem", "tp", "rep"), pairs)

    rim = memory[:, tokens - LANES :]
    rims = [next_rim(rim, s) for s in range(tps)]
    others = tps - 1
    field = jax.ShapeDtypeStruct((2, extended, half), F32)
    *begun, following, states, power = pl.pallas_call(
        functools.partial(project_own_kernel, tps),
        in_specs=[smem] + [resident] * 2 + [anywhere] * 4 + [resident] * 2,
        out_specs=(resident,) * 5,
        out_shape=(
            field,
            field,
            pltpu.VMEM((2, 2, others * depth, half), BF16),
            jax.ShapeDtypeStruct((2, extended, half), BF16),
            jax.ShapeDtypeStruct((extended, 8), F32),
        ),
        scratch_shapes=[
            pltpu.VMEM((2, 2, depth, half), BF16),
            pltpu.SemaphoreType.DMA((4, 1)),
            pltpu.SemaphoreType.DMA((4, others)),
        ],
        compiler_params=limit(12),
        name="project_own",
    )(where, rims[0], memory, *weights, hidden_halo, hidden)
    values, stats = pl.pallas_call(
        functools.partial(project_others_kernel, tps),
        in_specs=[smem] + [resident] * (2 * others + 5),
        out_specs=(pl.BlockSpec(memory_space=pltpu.HBM), resident),
        out_shape=(pltpu.HBM(field.shape, F32), jax.ShapeDtypeStruct((8, extended), F32)),
        scratch_shapes=[
            pltpu.VMEM((2, extended, half), F32),
            pltpu.SemaphoreType.DMA((2,)),
        ],
        compiler_params=limit(14),
        name="project_others",
    )(where, *rims[1:], *bodies[1:], following, *begun, states, power)

    all_stats = [stats] + [
        lax.ppermute(stats, "tp", [(i, (i + s) % tps) for i in range(tps)]) for s in range(1, tps)
    ]
    keep = (block * tokens % seq_length != 0).astype(I32).reshape(1)
    step = 2 * half
    if half % LANES == 0:
        step = next(c for c in (384, 256, 128) if half % c == 0)
    chunk = min(step, half)
    body = (2, tokens, half)
    values, products = pl.pallas_call(
        functools.partial(prepare_kernel, chunk),
        in_specs=[resident, anywhere],
        out_specs=(resident,) * 2,
        out_shape=(
            jax.ShapeDtypeStruct(body, F32),
            jax.ShapeDtypeStruct((KERNEL - 1, *body), F32),
        ),
        scratch_shapes=[
            pltpu.VMEM((2, extended, half), F32),
            pltpu.SemaphoreType.DMA((2 * half // chunk,)),
        ],
        compiler_params=limit(6),
        name="prepare",
    )(conv_weight, in_hbm(values))
    return pl.pallas_call(
        functools.partial(finish_kernel, tps, step),
        in_specs=[smem] + [resident] * (tps + 4),
        out_specs=anywhere,
        out_shape=jax.ShapeDtypeStruct((tokens, 2 * half), BF16),
        scratch_shapes=[
            pltpu.VMEM((extended, 8), F32),
            pltpu.VMEM((tokens, LANES), F32),
            pltpu.VMEM((KERNEL, tokens, LANES), F32),
            pltpu.VMEM((tokens, 2 * half), BF16),
            pltpu.SemaphoreType.DMA((2 * half // step,)),
        ],
        compiler_params=limit(6),
        name="finish",
    )(keep, *all_stats, values, products, hidden, conv_weight)


def solution(mesh):
    in_specs = (
        P(("parts", "mem", "rep"), "tp"),
        P(("parts", "mem", "rep"), "tp"),
        P("parts"),
        P(("parts", "tp"), "mem", None),
        P(("parts", "tp"), "mem", None),
        P(None, ("tp", "rep")),
        P(None, ("tp", "rep")),
        P(None, "tp"),
    )
    out_specs = P(("parts", "mem", "rep"), "tp")
    return jax.shard_map(shards, mesh=mesh, in_specs=in_specs, out_specs=out_specs, check_vma=False)
```

```python
import functools

import jax
import jax.numpy as jnp
from jax import lax
from jax.experimental import pallas as pl
from jax.experimental.pallas import tpu as pltpu
from jax.sharding import PartitionSpec as P

D = 4608
KERNEL = 4
DILATION = 3
SEQS = 4
EPSILON = 1e-06
RIM = 16
LANES = 128

F32 = jnp.float32
BF16 = jnp.bfloat16
I32 = jnp.int32


def iota(shape, axis):
    return lax.broadcasted_iota(I32, shape, axis)


def dot(a, b):
    return jnp.dot(a, b, preferred_element_type=F32)


def dot_nt(a, b, precision=None):
    return lax.dot_general(
        a, b, (((1,), (1,)), ((), ())), precision=precision, preferred_element_type=F32
    )


def unit(n, dtype):
    return (iota((n, n), 0) == iota((n, n), 1)).astype(F32).astype(dtype)


def to_bf16(x):
    return x.astype(F32).astype(BF16)


def place_ids(ids, place, out_ref):
    rows = place.shape[0]
    heads, tokens = ids.shape
    eye = unit(LANES, BF16)
    table = jnp.concatenate(
        [dot_nt(eye, to_bf16(place >> 8)), dot_nt(eye, to_bf16(place & 255))], axis=0
    ).astype(BF16)
    for head in range(heads):
        row = ids[head : head + 1, :]
        hot = to_bf16(iota((rows, tokens), 0) == (row >> 7))
        both = dot(table, hot)
        value = both[:LANES] * 256.0 + both[LANES:]
        chosen = jnp.where(iota(value.shape, 0) == (row & 127), value, 0.0)
        out_ref[head : head + 1, :] = jnp.sum(chosen, axis=0, keepdims=True).astype(I32)


def place_kernel(ids_ref, place_ref, out_ref):
    place_ids(ids_ref[...], place_ref[...], out_ref)


def fetch_kernel(
    place_hbm, ids_hbm, codes_hbm, scales_hbm, place_ref, codes_ref, scales_ref, out_ref, ids_ref, sems
):
    pairs = [(place_hbm, place_ref), (ids_hbm, ids_ref), (scales_hbm, scales_ref)]
    pairs += [(codes_hbm.at[n], codes_ref.at[n]) for n in range(codes_ref.shape[0])]
    copies = []
    for source, target in pairs:
        copies.append(pltpu.make_async_copy(source, target, sems.at[len(copies)]))
        copies[-1].start()
    await_all(copies[:2])
    place_ids(ids_ref[...], place_ref[...], out_ref)
    await_all(copies[2:])


def decode_kernel(codes_ref, scales_ref, out_ref):
    heads, width, rows = codes_ref.shape
    blocks = scales_ref.shape[0]
    entry = iota((width, 2 * width), 0)
    column = iota((width, 2 * width), 1)
    column = jnp.where(column < width, column, column - width)
    parity = entry & column & 15
    parity = parity ^ (parity >> 2)
    parity = (parity ^ (parity >> 1)) & 1
    same = (entry >> 4) == (column >> 4)
    rotation = jnp.where(same, 0.25 - 0.5 * parity.astype(F32), 0.0).astype(BF16)
    for head in range(heads):
        factors = jnp.concatenate(
            [
                jnp.broadcast_to(scales_ref[b, head : head + 1, :].astype(F32), (16, rows))
                for b in range(blocks)
            ],
            axis=0,
        )
        scaled = codes_ref[head].astype(F32) * factors
        upper = scaled.astype(BF16)
        lower = (scaled - upper.astype(F32)).astype(BF16)
        out_ref[head] = dot(rotation, jnp.concatenate([upper, lower], axis=0)).astype(BF16)


def picked(local, table_ref, head):
    rows = table_ref.shape[2]
    hot = to_bf16(iota((rows, local.shape[1]), 0) == local[head : head + 1, :])
    return dot(table_ref[head], hot).astype(BF16)


def pick_kernel(base_ref, ids_ref, table_ref, out_ref):
    heads, width, _ = table_ref.shape
    local = ids_ref[...] - base_ref[0]
    for head in range(heads):
        out_ref[head * width : (head + 1) * width, :] = picked(local, table_ref, head)


def merge_kernel(*refs):
    total = refs[0][...].astype(F32)
    for other in refs[1:-1]:
        total = total + other[...].astype(F32)
    refs[-1][...] = total.astype(BF16)


def fetch(count, tp, depth, source, target, shifts, sems):
    copies = []
    for n, s in enumerate(shifts):
        owner = lax.rem(tp + count - s, count)
        rows = pl.ds(pl.multiple_of(owner * depth, depth), depth)
        copy = pltpu.make_async_copy(
            source.at[rows, :], target.at[pl.ds(n * depth, depth), :], sems.at[n]
        )
        copy.start()
        copies.append(copy)
    return copies


def await_all(copies):
    for copy in copies:
        copy.wait()


def with_rim(rims, bodies):
    body = jnp.concatenate([b[...].astype(F32) for b in bodies], axis=0).T.astype(BF16)
    rim = jnp.concatenate([r[...].astype(F32) for r in rims], axis=0).T.astype(BF16)
    return jnp.concatenate([rim[LANES - RIM :], body], axis=0)


def project_own_kernel(count, where_ref, rim_ref, body_ref, *refs):
    weights, hidden_halo, hidden = refs[:4], refs[4], refs[5]
    key_ref, value_ref, next_ref, states_ref, power_ref, held, sems, next_sems = refs[6:]
    half = value_ref.shape[-1]
    depth = body_ref.shape[0]
    rep = where_ref[0]
    tp = where_ref[1]
    order = [(far, which) for far in range(2) for which in (1, 0)]
    copies = {
        (far, which): fetch(
            count, tp, depth, weights[2 * far + which], held.at[far, which], (0,),
            sems.at[2 * far + which],
        )
        for far, which in order
    }
    power = 0.0
    for slot in range(2):
        span = slice(slot * half, (slot + 1) * half)
        states_ref[slot, :RIM] = hidden_halo[:, span]
        states_ref[slot, RIM:] = hidden[:, span]
        here = states_ref[slot].astype(F32)
        power = power + jnp.sum(here * here, axis=1, keepdims=True)
    power_ref[...] = jnp.broadcast_to(power, power_ref.shape)
    memory = with_rim([rim_ref], [body_ref])
    later = []
    for far, which in order:
        slot = rep if far == 0 else 1 - rep
        await_all(copies[far, which])
        if not later:
            for f, w in order:
                later += fetch(
                    count, tp, depth, weights[2 * f + w], next_ref.at[f, w], range(1, count),
                    next_sems.at[2 * f + w],
                )
        target = value_ref if which == 1 else key_ref
        target[slot] = dot(memory, held[far, which])
    await_all(later)


def project_others_kernel(count, where_ref, *refs):
    pieces = count - 1
    rims, bodies = refs[:pieces], refs[pieces : 2 * pieces]
    held, begun_keys, begun_values, states_ref, power_ref = refs[2 * pieces :][:5]
    value_hbm, stats_ref, done, done_sems = refs[2 * pieces + 5 :]
    rep = where_ref[0]
    memory = with_rim(rims, bodies)
    sums = [0.0] * 3
    later = []
    for far in range(2):
        slot = rep if far == 0 else 1 - rep
        fields = [None, None]
        for which in (1, 0):
            fields[which] = dot(memory, held[far, which])
            if which == 1:
                done[far] = fields[1] + begun_values[slot]
                copy = pltpu.make_async_copy(done.at[far], value_hbm.at[slot], done_sems.at[far])
                copy.start()
                later.append(copy)
        keys = fields[0] + begun_keys[slot]
        values = done[far]
        terms = (keys * keys, states_ref[slot].astype(F32) * keys, values * values)
        sums = [a + jnp.sum(t, axis=1, keepdims=True) for a, t in zip(sums, terms)]
    packed = power_ref[...]
    lane = iota(packed.shape, 1)
    for k in range(3):
        packed = jnp.where(lane == k + 1, sums[k], packed)
    stats_ref[...] = dot_nt(unit(8, F32), packed, lax.Precision.HIGHEST)
    await_all(later)


def prepare_kernel(chunk, taps_ref, value_hbm, value_ref, tap_ref, rows_ref, sems):
    half = rows_ref.shape[-1]
    tokens = value_ref.shape[1]
    copies = []
    for slot in range(2):
        for start in range(0, half, chunk):
            span = pl.ds(start, chunk)
            copy = pltpu.make_async_copy(
                value_hbm.at[slot, :, span], rows_ref.at[slot, :, span], sems.at[len(copies)]
            )
            copy.start()
            copies.append(copy)
    for slot in range(2):
        for start in range(0, half, LANES):
            size = min(LANES, half - start)
            span = slice(start, start + size)
            there = slice(slot * half + start, slot * half + start + size)
            if start % chunk == 0:
                copies[(slot * half + start) // chunk].wait()
            value_ref[slot, :, span] = rows_ref[slot, RIM:, span]
            for tap in range(1, KERNEL):
                lag = DILATION * tap
                rows = rows_ref[slot, RIM - lag : RIM - lag + tokens, span]
                tap_ref[tap - 1, slot, :, span] = taps_ref[tap : tap + 1, there] * rows


def finish_kernel(count, step, keep_ref, *refs):
    stats = refs[:count]
    value_ref, tap_ref, hidden_ref, taps_ref, out_hbm = refs[count : count + 5]
    columns, gates, factors, out_ref, sems = refs[count + 5 :]
    half = value_ref.shape[-1]
    tokens, width = out_ref.shape
    total = stats[0][...]
    for other in stats[1:]:
        total = total + other[...]
    inverse_states = lax.rsqrt(total[0:1] / D + EPSILON)
    inverse_keys = lax.rsqrt(total[1:2] / D + EPSILON)
    gate = jax.nn.sigmoid(total[2:3] * inverse_states * inverse_keys / D**0.5)
    factor = gate * lax.rsqrt(gate * gate * total[3:4] / D + EPSILON)
    factor = jnp.where((iota(factor.shape, 1) < RIM) & (keep_ref[0] == 0), 0.0, factor)
    line = iota(total.shape, 0)
    both = jnp.where(line == 0, gate, jnp.where(line == 1, factor, 0.0))
    columns[...] = dot_nt(unit(total.shape[1], F32), both, lax.Precision.HIGHEST)
    gates[...] = jnp.broadcast_to(columns[RIM:, 0:1], gates.shape)
    for tap in range(KERNEL):
        lag = DILATION * tap
        factors[tap] = jnp.broadcast_to(
            columns[RIM - lag : RIM - lag + tokens, 1:2], factors.shape[1:]
        )
    copies = []
    for slot in range(2):
        for start in range(0, half, LANES):
            size = min(LANES, half - start)
            span = slice(start, start + size)
            there = slice(slot * half + start, slot * half + start + size)
            values = value_ref[slot, :, span]
            conv = taps_ref[0:1, there] * values * factors[0, :, :size]
            for tap in range(1, KERNEL):
                conv = conv + tap_ref[tap - 1, slot, :, span] * factors[tap, :, :size]
            gated = values * gates[:, :size]
            out_ref[:, there] = (
                hidden_ref[:, there].astype(F32) + jax.nn.silu(conv) + gated
            ).astype(BF16)
            if there.stop % step == 0:
                ready = pl.ds(there.stop - step, step)
                copy = pltpu.make_async_copy(
                    out_ref.at[:, ready], out_hbm.at[:, ready], sems.at[len(copies)]
                )
                copy.start()
                copies.append(copy)
    for copy in copies:
        copy.wait()


def whole(array):
    return pl.BlockSpec(array.shape, lambda *_: (0,) * array.ndim)


def in_hbm(array):
    return pltpu.with_memory_space_constraint(array, pltpu.HBM)


def after(array, *others):
    return lax.optimization_barrier((array, *others))[0]


def limit(mib):
    return pltpu.CompilerParams(vmem_limit_bytes=mib << 20)


def scattered_sum(raw, place, stored, decoded, here, meanwhile, settled):
    mems = lax.axis_size("mem")
    heads, width, rows = decoded.shape
    tokens = stored.shape[1]
    asked = lax.all_gather(stored, "mem", axis=0)
    partial = pl.pallas_call(
        pick_kernel,
        grid=(mems,),
        in_specs=[
            pl.BlockSpec(memory_space=pltpu.SMEM),
            pl.BlockSpec((None, heads, tokens), lambda m: (m, 0, 0)),
            whole(decoded),
        ],
        out_specs=pl.BlockSpec((None, heads * width, tokens), lambda m: (m, 0, 0)),
        out_shape=jax.ShapeDtypeStruct((mems, heads * width, tokens), BF16),
        compiler_params=limit(16),
        name="pick_all",
    )((here * rows).astype(I32).reshape(1), asked, decoded)
    total = lax.psum_scatter(partial, "mem", scatter_dimension=0, tiled=False)
    return total, meanwhile(partial), settled


def line_sum(raw, place, stored, decoded, here, meanwhile, settled):
    heads, width, rows = decoded.shape
    tokens = stored.shape[1]
    base = (here * rows).astype(I32).reshape(1)
    block = jax.ShapeDtypeStruct((heads * width, tokens), BF16)

    def ask(ids, x):
        return lax.ppermute(ids, "mem", [(i, i ^ x) for i in range(4)])

    def crossing(x, pairs):
        return lax.ppermute(x, ("mem", "rep"), [(2 * a + b, 2 * c + d) for a, b, c, d in pairs])

    def pick(ids):
        return pl.pallas_call(
            pick_kernel,
            in_specs=[pl.BlockSpec(memory_space=pltpu.SMEM)]
            + [pl.BlockSpec(memory_space=pltpu.VMEM)] * 2,
            out_shape=block,
            compiler_params=limit(8),
            name="pick_rows",
        )(base, ids, decoded)

    def send(x, *pairs):
        return lax.ppermute(x, "mem", pairs)

    first = ask(raw, 3)
    second = crossing(
        raw,
        [(m, r, m ^ 2, r ^ int(m in (1, 2))) for m in range(4) for r in range(2)],
    )
    third = ask(raw, 1)
    rows_3 = pick(place(first))
    rows_3, second, third = lax.optimization_barrier((rows_3, second, third))
    inward = send(rows_3, (0, 1), (3, 2))
    across = send(rows_3, (1, 2), (2, 1))
    rows_1 = pick(place(after(third, rows_3)))
    beside = send(rows_1, (0, 1), (1, 0), (2, 3), (3, 2))
    second, settled = lax.optimization_barrier((after(second, rows_1), settled))
    rows_2 = pick(place(second))
    past = crossing(rows_2, [(m, r, m ^ 2, r ^ 1) for m in (0, 3) for r in range(2)])
    own = pick(after(stored, rows_2))
    onward = after(rows_2, rows_1, own) + inward
    onward = send(onward, (1, 3), (2, 0))
    other = meanwhile(across)
    own, other = lax.optimization_barrier((own + past + beside, other))
    memory = pl.pallas_call(
        merge_kernel,
        in_specs=[pl.BlockSpec(memory_space=pltpu.VMEM)] * 3,
        out_shape=block,
        compiler_params=limit(4),
        name="merge",
    )(own, across, onward)
    return memory, other, settled


def shards(
    hidden, row_ids, row_place, table_codes, table_scales, key_weight, value_weight, conv_weight
):
    mems = lax.axis_size("mem")
    tps = lax.axis_size("tp")
    reps = lax.axis_size("rep")
    blocks = mems * reps
    tokens, heads = row_ids.shape
    rows, width = table_codes.shape[1:]
    depth = heads * width
    half = key_weight.shape[1]
    seq_length = tokens * blocks // SEQS
    assert reps == 2 and seq_length % tokens == 0 and row_place.shape[0] % LANES == 0
    block = lax.axis_index(("mem", "rep"))
    smem = pl.BlockSpec(memory_space=pltpu.SMEM)

    anywhere = pl.BlockSpec(memory_space=pl.ANY)
    resident = pl.BlockSpec(memory_space=pltpu.VMEM)
    places = row_place.reshape(-1, LANES)
    codes = table_codes.transpose(0, 2, 1)
    scales = table_scales.transpose(2, 0, 1)
    raw = row_ids.T
    placed = jax.ShapeDtypeStruct(raw.shape, I32)
    places, codes, scales, stored = pl.pallas_call(
        fetch_kernel,
        in_specs=[anywhere] * 4,
        out_specs=(resident,) * 4,
        out_shape=(
            jax.ShapeDtypeStruct(places.shape, I32),
            jax.ShapeDtypeStruct(codes.shape, BF16),
            jax.ShapeDtypeStruct(scales.shape, BF16),
            placed,
        ),
        scratch_shapes=[
            pltpu.VMEM(raw.shape, I32),
            pltpu.SemaphoreType.DMA((heads + 3,)),
        ],
        compiler_params=limit(4),
        name="fetch_tables",
    )(*[in_hbm(x) for x in (places, raw, codes, scales)])

    def place(ids):
        return pl.pallas_call(
            place_kernel,
            in_specs=[resident] * 2,
            out_specs=resident,
            out_shape=placed,
            compiler_params=limit(4),
            name="place_rows",
        )(ids, places)

    decoded = pl.pallas_call(
        decode_kernel,
        in_specs=[resident] * 2,
        out_specs=resident,
        out_shape=jax.ShapeDtypeStruct(codes.shape, BF16),
        compiler_params=limit(6),
        name="decode_tables",
    )(codes, scales)
    here = lax.axis_index("mem")
    other_key = lax.ppermute(key_weight, "rep", [(0, 1), (1, 0)])
    other_value = lax.ppermute(value_weight, "rep", [(0, 1), (1, 0)])
    needed = [(i, i + 1) for i in range(blocks - 1) if (i + 1) * tokens % seq_length]

    def meanwhile(token):
        tail = after(hidden[tokens - RIM :], token)
        return lax.ppermute(tail, ("mem", "rep"), needed)

    summed = line_sum if mems == 4 else scattered_sum
    memory, hidden_halo, others = summed(
        raw, place, stored, decoded, here, meanwhile, (other_key, other_value)
    )
    weights = [in_hbm(w) for w in (key_weight, value_weight, *others)]

    where = jnp.stack([lax.axis_index("rep"), lax.axis_index("tp")]).astype(I32)
    extended = tokens + RIM
    bodies = [memory] + [
        lax.ppermute(memory, "tp", [(i, (i + s) % tps) for i in range(tps)])
        for s in range(1, tps)
    ]

    def next_rim(rim, s):
        pairs = [
            (
                (a // reps * tps + i) * reps + a % reps,
                (b // reps * tps + (i + s) % tps) * reps + b % reps,
            )
            for a, b in needed
            for i in range(tps)
        ]
        return lax.ppermute(rim, ("mem", "tp", "rep"), pairs)

    rim = memory[:, tokens - LANES :]
    rims = [next_rim(rim, s) for s in range(tps)]
    others = tps - 1
    field = jax.ShapeDtypeStruct((2, extended, half), F32)
    *begun, following, states, power = pl.pallas_call(
        functools.partial(project_own_kernel, tps),
        in_specs=[smem] + [resident] * 2 + [anywhere] * 4 + [resident] * 2,
        out_specs=(resident,) * 5,
        out_shape=(
            field,
            field,
            pltpu.VMEM((2, 2, others * depth, half), BF16),
            jax.ShapeDtypeStruct((2, extended, half), BF16),
            jax.ShapeDtypeStruct((extended, 8), F32),
        ),
        scratch_shapes=[
            pltpu.VMEM((2, 2, depth, half), BF16),
            pltpu.SemaphoreType.DMA((4, 1)),
            pltpu.SemaphoreType.DMA((4, others)),
        ],
        compiler_params=limit(12),
        name="project_own",
    )(where, rims[0], memory, *weights, hidden_halo, hidden)
    values, stats = pl.pallas_call(
        functools.partial(project_others_kernel, tps),
        in_specs=[smem] + [resident] * (2 * others + 5),
        out_specs=(pl.BlockSpec(memory_space=pltpu.HBM), resident),
        out_shape=(pltpu.HBM(field.shape, F32), jax.ShapeDtypeStruct((8, extended), F32)),
        scratch_shapes=[
            pltpu.VMEM((2, extended, half), F32),
            pltpu.SemaphoreType.DMA((2,)),
        ],
        compiler_params=limit(14),
        name="project_others",
    )(where, *rims[1:], *bodies[1:], following, *begun, states, power)

    all_stats = [stats] + [
        lax.ppermute(stats, "tp", [(i, (i + s) % tps) for i in range(tps)]) for s in range(1, tps)
    ]
    keep = (block * tokens % seq_length != 0).astype(I32).reshape(1)
    step = 2 * half
    if half % LANES == 0:
        step = next(c for c in (384, 256, 128) if half % c == 0)
    chunk = min(step, half)
    body = (2, tokens, half)
    values, products = pl.pallas_call(
        functools.partial(prepare_kernel, chunk),
        in_specs=[resident, anywhere],
        out_specs=(resident,) * 2,
        out_shape=(
            jax.ShapeDtypeStruct(body, F32),
            jax.ShapeDtypeStruct((KERNEL - 1, *body), F32),
        ),
        scratch_shapes=[
            pltpu.VMEM((2, extended, half), F32),
            pltpu.SemaphoreType.DMA((2 * half // chunk,)),
        ],
        compiler_params=limit(6),
        name="prepare",
    )(conv_weight, in_hbm(values))
    return pl.pallas_call(
        functools.partial(finish_kernel, tps, step),
        in_specs=[smem] + [resident] * (tps + 4),
        out_specs=anywhere,
        out_shape=jax.ShapeDtypeStruct((tokens, 2 * half), BF16),
        scratch_shapes=[
            pltpu.VMEM((extended, 8), F32),
            pltpu.VMEM((tokens, LANES), F32),
            pltpu.VMEM((KERNEL, tokens, LANES), F32),
            pltpu.VMEM((tokens, 2 * half), BF16),
            pltpu.SemaphoreType.DMA((2 * half // step,)),
        ],
        compiler_params=limit(6),
        name="finish",
    )(keep, *all_stats, values, products, hidden, conv_weight)


def solution(mesh):
    in_specs = (
        P(("parts", "mem", "rep"), "tp"),
        P(("parts", "mem", "rep"), "tp"),
        P("parts"),
        P(("parts", "tp"), "mem", None),
        P(("parts", "tp"), "mem", None),
        P(None, ("tp", "rep")),
        P(None, ("tp", "rep")),
        P(None, "tp"),
    )
    out_specs = P(("parts", "mem", "rep"), "tp")
    return jax.shard_map(shards, mesh=mesh, in_specs=in_specs, out_specs=out_specs, check_vma=False)
```

```python
import functools

import jax
import jax.numpy as jnp
from jax import lax
from jax.experimental import pallas as pl
from jax.experimental.pallas import tpu as pltpu
from jax.sharding import PartitionSpec as P

D = 4608
KERNEL = 4
DILATION = 3
SEQS = 4
EPSILON = 1e-06
RIM = 16
LANES = 128

F32 = jnp.float32
BF16 = jnp.bfloat16
I32 = jnp.int32


def iota(shape, axis):
    return lax.broadcasted_iota(I32, shape, axis)


def dot(a, b):
    return jnp.dot(a, b, preferred_element_type=F32)


def dot_nt(a, b, precision=None):
    return lax.dot_general(
        a, b, (((1,), (1,)), ((), ())), precision=precision, preferred_element_type=F32
    )


def unit(n, dtype):
    return (iota((n, n), 0) == iota((n, n), 1)).astype(F32).astype(dtype)


def to_bf16(x):
    return x.astype(F32).astype(BF16)


def place_kernel(
    ids_hbm, place_hbm, codes_hbm, scales_hbm, out_ref, codes_ref, scales_ref, ids_ref, place_ref, sems
):
    copies = [
        pltpu.make_async_copy(place_hbm, place_ref, sems.at[0]),
        pltpu.make_async_copy(ids_hbm, ids_ref, sems.at[1]),
        pltpu.make_async_copy(scales_hbm, scales_ref, sems.at[2]),
    ]
    for n in range(codes_ref.shape[0]):
        copies.append(
            pltpu.make_async_copy(codes_hbm.at[n], codes_ref.at[n], sems.at[3 + n])
        )
    for copy in copies:
        copy.start()
    copies[0].wait()
    place = place_ref[...]
    rows = place.shape[0]
    heads, tokens = ids_ref.shape
    eye = unit(LANES, BF16)
    table = jnp.concatenate(
        [dot_nt(eye, to_bf16(place >> 8)), dot_nt(eye, to_bf16(place & 255))], axis=0
    ).astype(BF16)
    copies[1].wait()
    for head in range(heads):
        row = ids_ref[head : head + 1, :]
        hot = to_bf16(iota((rows, tokens), 0) == (row >> 7))
        both = dot(table, hot)
        value = both[:LANES] * 256.0 + both[LANES:]
        chosen = jnp.where(iota(value.shape, 0) == (row & 127), value, 0.0)
        out_ref[head : head + 1, :] = jnp.sum(chosen, axis=0, keepdims=True).astype(I32)
    for copy in copies[2:]:
        copy.wait()


def decode_kernel(codes_ref, scales_ref, out_ref):
    heads, width, rows = codes_ref.shape
    blocks = scales_ref.shape[0]
    entry = iota((width, 2 * width), 0)
    column = iota((width, 2 * width), 1)
    column = jnp.where(column < width, column, column - width)
    parity = entry & column & 15
    parity = parity ^ (parity >> 2)
    parity = (parity ^ (parity >> 1)) & 1
    same = (entry >> 4) == (column >> 4)
    rotation = jnp.where(same, 0.25 - 0.5 * parity.astype(F32), 0.0).astype(BF16)
    for head in range(heads):
        factors = jnp.concatenate(
            [
                jnp.broadcast_to(scales_ref[b, head : head + 1, :].astype(F32), (16, rows))
                for b in range(blocks)
            ],
            axis=0,
        )
        scaled = codes_ref[head].astype(F32) * factors
        upper = scaled.astype(BF16)
        lower = (scaled - upper.astype(F32)).astype(BF16)
        out_ref[head] = dot(rotation, jnp.concatenate([upper, lower], axis=0)).astype(BF16)


def picked(local, table_ref, head):
    rows = table_ref.shape[2]
    hot = to_bf16(iota((rows, local.shape[1]), 0) == local[head : head + 1, :])
    return dot(table_ref[head], hot).astype(BF16)


def pick_kernel(base_ref, ids_ref, table_ref, out_ref):
    heads, width, _ = table_ref.shape
    local = ids_ref[...] - base_ref[0]
    for head in range(heads):
        out_ref[head * width : (head + 1) * width, :] = picked(local, table_ref, head)


def merge_kernel(*refs):
    total = refs[0][...].astype(F32)
    for other in refs[1:-1]:
        total = total + other[...].astype(F32)
    refs[-1][...] = total.astype(BF16)


def fetch(count, tp, depth, source, target, shifts, sems):
    copies = []
    for n, s in enumerate(shifts):
        owner = lax.rem(tp + count - s, count)
        rows = pl.ds(pl.multiple_of(owner * depth, depth), depth)
        copy = pltpu.make_async_copy(
            source.at[rows, :], target.at[pl.ds(n * depth, depth), :], sems.at[n]
        )
        copy.start()
        copies.append(copy)
    return copies


def await_all(copies):
    for copy in copies:
        copy.wait()


def with_rim(rims, bodies):
    body = jnp.concatenate([b[...].astype(F32) for b in bodies], axis=0).T.astype(BF16)
    rim = jnp.concatenate([r[...].astype(F32) for r in rims], axis=0).T.astype(BF16)
    return jnp.concatenate([rim[LANES - RIM :], body], axis=0)


def project_own_kernel(count, where_ref, rim_ref, body_ref, *refs):
    weights, hidden_halo, hidden = refs[:4], refs[4], refs[5]
    key_ref, value_ref, next_ref, states_ref, power_ref, held, sems, next_sems = refs[6:]
    half = value_ref.shape[-1]
    depth = body_ref.shape[0]
    rep = where_ref[0]
    tp = where_ref[1]
    order = [(far, which) for far in range(2) for which in (1, 0)]
    copies = {
        (far, which): fetch(
            count, tp, depth, weights[2 * far + which], held.at[far, which], (0,),
            sems.at[2 * far + which],
        )
        for far, which in order
    }
    memory = with_rim([rim_ref], [body_ref])
    later = []
    for far, which in order:
        slot = rep if far == 0 else 1 - rep
        await_all(copies[far, which])
        if not later:
            for f, w in order:
                later += fetch(
                    count, tp, depth, weights[2 * f + w], next_ref.at[f, w], range(1, count),
                    next_sems.at[2 * f + w],
                )
        target = value_ref if which == 1 else key_ref
        target[slot] = dot(memory, held[far, which])
        if (far, which) == (0, 1):
            power = 0.0
            for side in range(2):
                span = slice(side * half, (side + 1) * half)
                states_ref[side, :RIM] = hidden_halo[:, span]
                states_ref[side, RIM:] = hidden[:, span]
                here = states_ref[side].astype(F32)
                power = power + jnp.sum(here * here, axis=1, keepdims=True)
            power_ref[...] = jnp.broadcast_to(power, power_ref.shape)
    await_all(later)


def project_others_kernel(count, where_ref, *refs):
    pieces = count - 1
    rims, bodies = refs[:pieces], refs[pieces : 2 * pieces]
    held, begun_keys, begun_values, states_ref, power_ref = refs[2 * pieces :][:5]
    value_hbm, stats_ref, done, done_sems = refs[2 * pieces + 5 :]
    rep = where_ref[0]
    memory = with_rim(rims, bodies)
    sums = [0.0] * 3
    later = []
    for far in range(2):
        slot = rep if far == 0 else 1 - rep
        fields = [None, None]
        for which in (1, 0):
            fields[which] = dot(memory, held[far, which])
            if which == 1:
                done[far] = fields[1] + begun_values[slot]
                copy = pltpu.make_async_copy(done.at[far], value_hbm.at[slot], done_sems.at[far])
                copy.start()
                later.append(copy)
        keys = fields[0] + begun_keys[slot]
        values = done[far]
        terms = (keys * keys, states_ref[slot].astype(F32) * keys, values * values)
        sums = [a + jnp.sum(t, axis=1, keepdims=True) for a, t in zip(sums, terms)]
    packed = power_ref[...]
    lane = iota(packed.shape, 1)
    for k in range(3):
        packed = jnp.where(lane == k + 1, sums[k], packed)
    stats_ref[...] = dot_nt(unit(8, F32), packed, lax.Precision.HIGHEST)
    await_all(later)


def prepare_kernel(chunk, taps_ref, value_hbm, value_ref, tap_ref, rows_ref, sems):
    half = rows_ref.shape[-1]
    tokens = value_ref.shape[1]
    copies = []
    for slot in range(2):
        for start in range(0, half, chunk):
            span = pl.ds(start, chunk)
            copy = pltpu.make_async_copy(
                value_hbm.at[slot, :, span], rows_ref.at[slot, :, span], sems.at[len(copies)]
            )
            copy.start()
            copies.append(copy)
    for slot in range(2):
        for start in range(0, half, LANES):
            size = min(LANES, half - start)
            span = slice(start, start + size)
            there = slice(slot * half + start, slot * half + start + size)
            if start % chunk == 0:
                copies[(slot * half + start) // chunk].wait()
            value_ref[slot, :, span] = rows_ref[slot, RIM:, span]
            for tap in range(1, KERNEL):
                lag = DILATION * tap
                rows = rows_ref[slot, RIM - lag : RIM - lag + tokens, span]
                tap_ref[tap - 1, slot, :, span] = taps_ref[tap : tap + 1, there] * rows


def finish_kernel(count, step, keep_ref, *refs):
    stats = refs[:count]
    value_ref, tap_ref, hidden_ref, taps_ref, out_hbm = refs[count : count + 5]
    columns, gates, factors, out_ref, sems = refs[count + 5 :]
    half = value_ref.shape[-1]
    tokens, width = out_ref.shape
    total = stats[0][...]
    for other in stats[1:]:
        total = total + other[...]
    inverse_states = lax.rsqrt(total[0:1] / D + EPSILON)
    inverse_keys = lax.rsqrt(total[1:2] / D + EPSILON)
    gate = jax.nn.sigmoid(total[2:3] * inverse_states * inverse_keys / D**0.5)
    factor = gate * lax.rsqrt(gate * gate * total[3:4] / D + EPSILON)
    factor = jnp.where((iota(factor.shape, 1) < RIM) & (keep_ref[0] == 0), 0.0, factor)
    line = iota(total.shape, 0)
    both = jnp.where(line == 0, gate, jnp.where(line == 1, factor, 0.0))
    columns[...] = dot_nt(unit(total.shape[1], F32), both, lax.Precision.HIGHEST)
    gates[...] = jnp.broadcast_to(columns[RIM:, 0:1], gates.shape)
    for tap in range(KERNEL):
        lag = DILATION * tap
        factors[tap] = jnp.broadcast_to(
            columns[RIM - lag : RIM - lag + tokens, 1:2], factors.shape[1:]
        )
    copies = []
    for slot in range(2):
        for start in range(0, half, LANES):
            size = min(LANES, half - start)
            span = slice(start, start + size)
            there = slice(slot * half + start, slot * half + start + size)
            values = value_ref[slot, :, span]
            conv = taps_ref[0:1, there] * values * factors[0, :, :size]
            for tap in range(1, KERNEL):
                conv = conv + tap_ref[tap - 1, slot, :, span] * factors[tap, :, :size]
            gated = values * gates[:, :size]
            out_ref[:, there] = (
                hidden_ref[:, there].astype(F32) + jax.nn.silu(conv) + gated
            ).astype(BF16)
            if there.stop % step == 0:
                ready = pl.ds(there.stop - step, step)
                copy = pltpu.make_async_copy(
                    out_ref.at[:, ready], out_hbm.at[:, ready], sems.at[len(copies)]
                )
                copy.start()
                copies.append(copy)
    for copy in copies:
        copy.wait()


def whole(array):
    return pl.BlockSpec(array.shape, lambda *_: (0,) * array.ndim)


def in_hbm(array):
    return pltpu.with_memory_space_constraint(array, pltpu.HBM)


def after(array, *others):
    return lax.optimization_barrier((array, *others))[0]


def limit(mib):
    return pltpu.CompilerParams(vmem_limit_bytes=mib << 20)


def scattered_sum(stored, decoded, here, meanwhile, settled):
    mems = lax.axis_size("mem")
    heads, width, rows = decoded.shape
    tokens = stored.shape[1]
    asked = lax.all_gather(stored, "mem", axis=0)
    partial = pl.pallas_call(
        pick_kernel,
        grid=(mems,),
        in_specs=[
            pl.BlockSpec(memory_space=pltpu.SMEM),
            pl.BlockSpec((None, heads, tokens), lambda m: (m, 0, 0)),
            whole(decoded),
        ],
        out_specs=pl.BlockSpec((None, heads * width, tokens), lambda m: (m, 0, 0)),
        out_shape=jax.ShapeDtypeStruct((mems, heads * width, tokens), BF16),
        compiler_params=limit(16),
        name="pick_all",
    )((here * rows).astype(I32).reshape(1), asked, decoded)
    total = lax.psum_scatter(partial, "mem", scatter_dimension=0, tiled=False)
    return total, meanwhile(partial), settled


def line_sum(stored, decoded, here, meanwhile, settled):
    heads, width, rows = decoded.shape
    tokens = stored.shape[1]
    base = (here * rows).astype(I32).reshape(1)
    block = jax.ShapeDtypeStruct((heads * width, tokens), BF16)

    def ask(ids, x):
        return lax.ppermute(ids, "mem", [(i, i ^ x) for i in range(4)])

    def crossing(x, pairs):
        return lax.ppermute(x, ("mem", "rep"), [(2 * a + b, 2 * c + d) for a, b, c, d in pairs])

    def pick(ids):
        return pl.pallas_call(
            pick_kernel,
            in_specs=[pl.BlockSpec(memory_space=pltpu.SMEM)]
            + [pl.BlockSpec(memory_space=pltpu.VMEM)] * 2,
            out_shape=block,
            compiler_params=limit(8),
            name="pick_rows",
        )(base, ids, decoded)

    def send(x, *pairs):
        return lax.ppermute(x, "mem", pairs)

    first = ask(stored, 3)
    second = crossing(
        stored,
        [(m, r, m ^ 2, r ^ int(m in (1, 2))) for m in range(4) for r in range(2)],
    )
    third = ask(stored, 1)
    rows_3 = pick(first)
    rows_3, second, third = lax.optimization_barrier((rows_3, second, third))
    inward = send(rows_3, (0, 1), (3, 2))
    across = send(rows_3, (1, 2), (2, 1))
    rows_2 = pick(after(second, rows_3))
    third, settled = lax.optimization_barrier((after(third, rows_2), settled))
    past = crossing(rows_2, [(m, r, m ^ 2, r ^ 1) for m in (0, 3) for r in range(2)])
    rows_1 = pick(third)
    own = pick(after(stored, rows_1))
    beside = send(rows_1, (0, 1), (1, 0), (2, 3), (3, 2))
    onward = after(rows_2, rows_1, own) + inward
    onward = send(onward, (1, 3), (2, 0))
    other = meanwhile(across)
    own, other = lax.optimization_barrier((own + past + beside, other))
    memory = pl.pallas_call(
        merge_kernel,
        in_specs=[pl.BlockSpec(memory_space=pltpu.VMEM)] * 3,
        out_shape=block,
        compiler_params=limit(4),
        name="merge",
    )(own, across, onward)
    return memory, other, settled


def shards(
    hidden, row_ids, row_place, table_codes, table_scales, key_weight, value_weight, conv_weight
):
    mems = lax.axis_size("mem")
    tps = lax.axis_size("tp")
    reps = lax.axis_size("rep")
    blocks = mems * reps
    tokens, heads = row_ids.shape
    rows, width = table_codes.shape[1:]
    depth = heads * width
    half = key_weight.shape[1]
    seq_length = tokens * blocks // SEQS
    assert reps == 2 and seq_length % tokens == 0 and row_place.shape[0] % LANES == 0
    block = lax.axis_index(("mem", "rep"))
    smem = pl.BlockSpec(memory_space=pltpu.SMEM)

    anywhere = pl.BlockSpec(memory_space=pl.ANY)
    resident = pl.BlockSpec(memory_space=pltpu.VMEM)
    places = row_place.reshape(-1, LANES)
    codes = table_codes.transpose(0, 2, 1)
    scales = table_scales.transpose(2, 0, 1)
    stored, codes, scales = pl.pallas_call(
        place_kernel,
        in_specs=[anywhere] * 4,
        out_specs=(resident,) * 3,
        out_shape=(
            jax.ShapeDtypeStruct((heads, tokens), I32),
            jax.ShapeDtypeStruct(codes.shape, BF16),
            jax.ShapeDtypeStruct(scales.shape, BF16),
        ),
        scratch_shapes=[
            pltpu.VMEM((heads, tokens), I32),
            pltpu.VMEM(places.shape, I32),
            pltpu.SemaphoreType.DMA((heads + 3,)),
        ],
        compiler_params=limit(4),
        name="place_rows",
    )(*[in_hbm(x) for x in (row_ids.T, places, codes, scales)])
    decoded = pl.pallas_call(
        decode_kernel,
        in_specs=[resident] * 2,
        out_specs=resident,
        out_shape=jax.ShapeDtypeStruct(codes.shape, BF16),
        compiler_params=limit(6),
        name="decode_tables",
    )(codes, scales)
    here = lax.axis_index("mem")
    other_key = lax.ppermute(key_weight, "rep", [(0, 1), (1, 0)])
    other_value = lax.ppermute(value_weight, "rep", [(0, 1), (1, 0)])
    needed = [(i, i + 1) for i in range(blocks - 1) if (i + 1) * tokens % seq_length]

    def meanwhile(token):
        tail = after(hidden[tokens - RIM :], token)
        return lax.ppermute(tail, ("mem", "rep"), needed)

    summed = line_sum if mems == 4 else scattered_sum
    memory, hidden_halo, others = summed(
        stored, decoded, here, meanwhile, (other_key, other_value)
    )
    weights = [in_hbm(w) for w in (key_weight, value_weight, *others)]

    where = jnp.stack([lax.axis_index("rep"), lax.axis_index("tp")]).astype(I32)
    extended = tokens + RIM
    bodies = [memory] + [
        lax.ppermute(memory, "tp", [(i, (i + s) % tps) for i in range(tps)])
        for s in range(1, tps)
    ]

    def next_rim(rim, s):
        pairs = [
            (
                (a // reps * tps + i) * reps + a % reps,
                (b // reps * tps + (i + s) % tps) * reps + b % reps,
            )
            for a, b in needed
            for i in range(tps)
        ]
        return lax.ppermute(rim, ("mem", "tp", "rep"), pairs)

    rim = memory[:, tokens - LANES :]
    rims = [next_rim(rim, s) for s in range(tps)]
    others = tps - 1
    field = jax.ShapeDtypeStruct((2, extended, half), F32)
    *begun, following, states, power = pl.pallas_call(
        functools.partial(project_own_kernel, tps),
        in_specs=[smem] + [resident] * 2 + [anywhere] * 4 + [resident] * 2,
        out_specs=(resident,) * 5,
        out_shape=(
            field,
            field,
            pltpu.VMEM((2, 2, others * depth, half), BF16),
            jax.ShapeDtypeStruct((2, extended, half), BF16),
            jax.ShapeDtypeStruct((extended, 8), F32),
        ),
        scratch_shapes=[
            pltpu.VMEM((2, 2, depth, half), BF16),
            pltpu.SemaphoreType.DMA((4, 1)),
            pltpu.SemaphoreType.DMA((4, others)),
        ],
        compiler_params=limit(12),
        name="project_own",
    )(where, rims[0], memory, *weights, hidden_halo, hidden)
    values, stats = pl.pallas_call(
        functools.partial(project_others_kernel, tps),
        in_specs=[smem] + [resident] * (2 * others + 5),
        out_specs=(pl.BlockSpec(memory_space=pltpu.HBM), resident),
        out_shape=(pltpu.HBM(field.shape, F32), jax.ShapeDtypeStruct((8, extended), F32)),
        scratch_shapes=[
            pltpu.VMEM((2, extended, half), F32),
            pltpu.SemaphoreType.DMA((2,)),
        ],
        compiler_params=limit(14),
        name="project_others",
    )(where, *rims[1:], *bodies[1:], following, *begun, states, power)

    all_stats = [stats] + [
        lax.ppermute(stats, "tp", [(i, (i + s) % tps) for i in range(tps)]) for s in range(1, tps)
    ]
    keep = (block * tokens % seq_length != 0).astype(I32).reshape(1)
    step = 2 * half
    if half % LANES == 0:
        step = next(c for c in (384, 256, 128) if half % c == 0)
    chunk = min(step, half)
    body = (2, tokens, half)
    values, products = pl.pallas_call(
        functools.partial(prepare_kernel, chunk),
        in_specs=[resident, anywhere],
        out_specs=(resident,) * 2,
        out_shape=(
            jax.ShapeDtypeStruct(body, F32),
            jax.ShapeDtypeStruct((KERNEL - 1, *body), F32),
        ),
        scratch_shapes=[
            pltpu.VMEM((2, extended, half), F32),
            pltpu.SemaphoreType.DMA((2 * half // chunk,)),
        ],
        compiler_params=limit(6),
        name="prepare",
    )(conv_weight, in_hbm(values))
    return pl.pallas_call(
        functools.partial(finish_kernel, tps, step),
        in_specs=[smem] + [resident] * (tps + 4),
        out_specs=anywhere,
        out_shape=jax.ShapeDtypeStruct((tokens, 2 * half), BF16),
        scratch_shapes=[
            pltpu.VMEM((extended, 8), F32),
            pltpu.VMEM((tokens, LANES), F32),
            pltpu.VMEM((KERNEL, tokens, LANES), F32),
            pltpu.VMEM((tokens, 2 * half), BF16),
            pltpu.SemaphoreType.DMA((2 * half // step,)),
        ],
        compiler_params=limit(6),
        name="finish",
    )(keep, *all_stats, values, products, hidden, conv_weight)


def solution(mesh):
    in_specs = (
        P(("parts", "mem", "rep"), "tp"),
        P(("parts", "mem", "rep"), "tp"),
        P("parts"),
        P(("parts", "tp"), "mem", None),
        P(("parts", "tp"), "mem", None),
        P(None, ("tp", "rep")),
        P(None, ("tp", "rep")),
        P(None, "tp"),
    )
    out_specs = P(("parts", "mem", "rep"), "tp")
    return jax.shard_map(shards, mesh=mesh, in_specs=in_specs, out_specs=out_specs, check_vma=False)
```

```python
import functools

import jax
import jax.numpy as jnp
from jax import lax
from jax.experimental import pallas as pl
from jax.experimental.pallas import tpu as pltpu
from jax.sharding import PartitionSpec as P

D = 4608
KERNEL = 4
DILATION = 3
SEQS = 4
EPSILON = 1e-06
RIM = 16
LANES = 128

F32 = jnp.float32
BF16 = jnp.bfloat16
I32 = jnp.int32


def iota(shape, axis):
    return lax.broadcasted_iota(I32, shape, axis)


def dot(a, b):
    return jnp.dot(a, b, preferred_element_type=F32)


def dot_nt(a, b, precision=None):
    return lax.dot_general(
        a, b, (((1,), (1,)), ((), ())), precision=precision, preferred_element_type=F32
    )


def unit(n, dtype):
    return (iota((n, n), 0) == iota((n, n), 1)).astype(F32).astype(dtype)


def to_bf16(x):
    return x.astype(F32).astype(BF16)


def place_kernel(
    ids_hbm, place_hbm, codes_hbm, out_ref, codes_ref, ids_ref, place_ref, sems
):
    copies = [
        pltpu.make_async_copy(place_hbm, place_ref, sems.at[0]),
        pltpu.make_async_copy(ids_hbm, ids_ref, sems.at[1]),
    ]
    for n in range(codes_ref.shape[0]):
        copies.append(
            pltpu.make_async_copy(codes_hbm.at[n], codes_ref.at[n], sems.at[2 + n])
        )
    for copy in copies:
        copy.start()
    copies[0].wait()
    place = place_ref[...]
    rows = place.shape[0]
    heads, tokens = ids_ref.shape
    eye = unit(LANES, BF16)
    table = jnp.concatenate(
        [dot_nt(eye, to_bf16(place >> 8)), dot_nt(eye, to_bf16(place & 255))], axis=0
    ).astype(BF16)
    copies[1].wait()
    for head in range(heads):
        row = ids_ref[head : head + 1, :]
        hot = to_bf16(iota((rows, tokens), 0) == (row >> 7))
        both = dot(table, hot)
        value = both[:LANES] * 256.0 + both[LANES:]
        chosen = jnp.where(iota(value.shape, 0) == (row & 127), value, 0.0)
        out_ref[head : head + 1, :] = jnp.sum(chosen, axis=0, keepdims=True).astype(I32)
    for copy in copies[2:]:
        copy.wait()


def decode_kernel(codes_ref, scales_ref, out_ref):
    heads, width, rows = codes_ref.shape
    blocks = scales_ref.shape[0]
    entry = iota((width, 2 * width), 0)
    column = iota((width, 2 * width), 1)
    column = jnp.where(column < width, column, column - width)
    parity = entry & column & 15
    parity = parity ^ (parity >> 2)
    parity = (parity ^ (parity >> 1)) & 1
    same = (entry >> 4) == (column >> 4)
    rotation = jnp.where(same, 0.25 - 0.5 * parity.astype(F32), 0.0).astype(BF16)
    scales = scales_ref[...].astype(F32)
    for head in range(heads):
        factors = jnp.concatenate(
            [
                jnp.broadcast_to(scales[b, head : head + 1, :], (16, rows))
                for b in range(blocks)
            ],
            axis=0,
        )
        scaled = codes_ref[head].astype(F32) * factors
        upper = scaled.astype(BF16)
        lower = (scaled - upper.astype(F32)).astype(BF16)
        out_ref[head] = dot(rotation, jnp.concatenate([upper, lower], axis=0)).astype(BF16)


def picked(local, table_ref, head):
    rows = table_ref.shape[2]
    hot = to_bf16(iota((rows, local.shape[1]), 0) == local[head : head + 1, :])
    return dot(table_ref[head], hot).astype(BF16)


def pick_kernel(base_ref, ids_ref, table_ref, out_ref):
    heads, width, _ = table_ref.shape
    local = ids_ref[...] - base_ref[0]
    for head in range(heads):
        out_ref[head * width : (head + 1) * width, :] = picked(local, table_ref, head)


def merge_kernel(*refs):
    total = refs[0][...].astype(F32)
    for other in refs[1:-1]:
        total = total + other[...].astype(F32)
    refs[-1][...] = total.astype(BF16)


def fetch(count, tp, depth, source, target, shifts, sems):
    copies = []
    for n, s in enumerate(shifts):
        owner = lax.rem(tp + count - s, count)
        rows = pl.ds(pl.multiple_of(owner * depth, depth), depth)
        copy = pltpu.make_async_copy(
            source.at[rows, :], target.at[pl.ds(n * depth, depth), :], sems.at[n]
        )
        copy.start()
        copies.append(copy)
    return copies


def await_all(copies):
    for copy in copies:
        copy.wait()


def with_rim(rims, bodies):
    body = jnp.concatenate([b[...].astype(F32) for b in bodies], axis=0).T.astype(BF16)
    rim = jnp.concatenate([r[...].astype(F32) for r in rims], axis=0).T.astype(BF16)
    return jnp.concatenate([rim[LANES - RIM :], body], axis=0)


def project_own_kernel(count, where_ref, rim_ref, body_ref, *refs):
    weights, hidden_halo, hidden = refs[:4], refs[4], refs[5]
    key_ref, value_ref, next_ref, states_ref, power_ref, held, sems, next_sems = refs[6:]
    half = value_ref.shape[-1]
    depth = body_ref.shape[0]
    rep = where_ref[0]
    tp = where_ref[1]
    order = [(far, which) for far in range(2) for which in (1, 0)]
    copies = {
        (far, which): fetch(
            count, tp, depth, weights[2 * far + which], held.at[far, which], (0,),
            sems.at[2 * far + which],
        )
        for far, which in order
    }
    memory = with_rim([rim_ref], [body_ref])
    later = []
    for far, which in order:
        slot = rep if far == 0 else 1 - rep
        await_all(copies[far, which])
        if not later:
            for f, w in order:
                later += fetch(
                    count, tp, depth, weights[2 * f + w], next_ref.at[f, w], range(1, count),
                    next_sems.at[2 * f + w],
                )
        target = value_ref if which == 1 else key_ref
        target[slot] = dot(memory, held[far, which])
        if (far, which) == (0, 1):
            power = 0.0
            for side in range(2):
                span = slice(side * half, (side + 1) * half)
                states_ref[side, :RIM] = hidden_halo[:, span]
                states_ref[side, RIM:] = hidden[:, span]
                here = states_ref[side].astype(F32)
                power = power + jnp.sum(here * here, axis=1, keepdims=True)
            power_ref[...] = jnp.broadcast_to(power, power_ref.shape)
    await_all(later)


def project_others_kernel(count, where_ref, *refs):
    pieces = count - 1
    rims, bodies = refs[:pieces], refs[pieces : 2 * pieces]
    held, begun_keys, begun_values, states_ref, power_ref = refs[2 * pieces :][:5]
    value_hbm, stats_ref, done, done_sems = refs[2 * pieces + 5 :]
    rep = where_ref[0]
    memory = with_rim(rims, bodies)
    sums = [0.0] * 3
    later = []
    for far in range(2):
        slot = rep if far == 0 else 1 - rep
        fields = [None, None]
        for which in (1, 0):
            fields[which] = dot(memory, held[far, which])
            if which == 1:
                done[far] = fields[1] + begun_values[slot]
                copy = pltpu.make_async_copy(done.at[far], value_hbm.at[slot], done_sems.at[far])
                copy.start()
                later.append(copy)
        keys = fields[0] + begun_keys[slot]
        values = done[far]
        terms = (keys * keys, states_ref[slot].astype(F32) * keys, values * values)
        sums = [a + jnp.sum(t, axis=1, keepdims=True) for a, t in zip(sums, terms)]
    packed = power_ref[...]
    lane = iota(packed.shape, 1)
    for k in range(3):
        packed = jnp.where(lane == k + 1, sums[k], packed)
    stats_ref[...] = dot_nt(unit(8, F32), packed, lax.Precision.HIGHEST)
    await_all(later)


def prepare_kernel(chunk, taps_ref, value_hbm, value_ref, tap_ref, rows_ref, sems):
    half = rows_ref.shape[-1]
    tokens = value_ref.shape[1]
    copies = []
    for slot in range(2):
        for start in range(0, half, chunk):
            span = pl.ds(start, chunk)
            copy = pltpu.make_async_copy(
                value_hbm.at[slot, :, span], rows_ref.at[slot, :, span], sems.at[len(copies)]
            )
            copy.start()
            copies.append(copy)
    for slot in range(2):
        for start in range(0, half, LANES):
            size = min(LANES, half - start)
            span = slice(start, start + size)
            there = slice(slot * half + start, slot * half + start + size)
            if start % chunk == 0:
                copies[(slot * half + start) // chunk].wait()
            value_ref[slot, :, span] = rows_ref[slot, RIM:, span]
            for tap in range(1, KERNEL):
                lag = DILATION * tap
                rows = rows_ref[slot, RIM - lag : RIM - lag + tokens, span]
                tap_ref[tap - 1, slot, :, span] = taps_ref[tap : tap + 1, there] * rows


def finish_kernel(count, step, keep_ref, *refs):
    stats = refs[:count]
    value_ref, tap_ref, hidden_ref, taps_ref, out_hbm = refs[count : count + 5]
    columns, gates, factors, out_ref, sems = refs[count + 5 :]
    half = value_ref.shape[-1]
    tokens, width = out_ref.shape
    total = stats[0][...]
    for other in stats[1:]:
        total = total + other[...]
    inverse_states = lax.rsqrt(total[0:1] / D + EPSILON)
    inverse_keys = lax.rsqrt(total[1:2] / D + EPSILON)
    gate = jax.nn.sigmoid(total[2:3] * inverse_states * inverse_keys / D**0.5)
    factor = gate * lax.rsqrt(gate * gate * total[3:4] / D + EPSILON)
    factor = jnp.where((iota(factor.shape, 1) < RIM) & (keep_ref[0] == 0), 0.0, factor)
    line = iota(total.shape, 0)
    both = jnp.where(line == 0, gate, jnp.where(line == 1, factor, 0.0))
    columns[...] = dot_nt(unit(total.shape[1], F32), both, lax.Precision.HIGHEST)
    gates[...] = jnp.broadcast_to(columns[RIM:, 0:1], gates.shape)
    for tap in range(KERNEL):
        lag = DILATION * tap
        factors[tap] = jnp.broadcast_to(
            columns[RIM - lag : RIM - lag + tokens, 1:2], factors.shape[1:]
        )
    copies = []
    for slot in range(2):
        for start in range(0, half, LANES):
            size = min(LANES, half - start)
            span = slice(start, start + size)
            there = slice(slot * half + start, slot * half + start + size)
            values = value_ref[slot, :, span]
            conv = taps_ref[0:1, there] * values * factors[0, :, :size]
            for tap in range(1, KERNEL):
                conv = conv + tap_ref[tap - 1, slot, :, span] * factors[tap, :, :size]
            gated = values * gates[:, :size]
            out_ref[:, there] = (
                hidden_ref[:, there].astype(F32) + jax.nn.silu(conv) + gated
            ).astype(BF16)
            if there.stop % step == 0:
                ready = pl.ds(there.stop - step, step)
                copy = pltpu.make_async_copy(
                    out_ref.at[:, ready], out_hbm.at[:, ready], sems.at[len(copies)]
                )
                copy.start()
                copies.append(copy)
    for copy in copies:
        copy.wait()


def whole(array):
    return pl.BlockSpec(array.shape, lambda *_: (0,) * array.ndim)


def in_hbm(array):
    return pltpu.with_memory_space_constraint(array, pltpu.HBM)


def after(array, *others):
    return lax.optimization_barrier((array, *others))[0]


def limit(mib):
    return pltpu.CompilerParams(vmem_limit_bytes=mib << 20)


def scattered_sum(stored, decoded, here, meanwhile, settled):
    mems = lax.axis_size("mem")
    heads, width, rows = decoded.shape
    tokens = stored.shape[1]
    asked = lax.all_gather(stored, "mem", axis=0)
    partial = pl.pallas_call(
        pick_kernel,
        grid=(mems,),
        in_specs=[
            pl.BlockSpec(memory_space=pltpu.SMEM),
            pl.BlockSpec((None, heads, tokens), lambda m: (m, 0, 0)),
            whole(decoded),
        ],
        out_specs=pl.BlockSpec((None, heads * width, tokens), lambda m: (m, 0, 0)),
        out_shape=jax.ShapeDtypeStruct((mems, heads * width, tokens), BF16),
        compiler_params=limit(16),
        name="pick_all",
    )((here * rows).astype(I32).reshape(1), asked, decoded)
    total = lax.psum_scatter(partial, "mem", scatter_dimension=0, tiled=False)
    return total, meanwhile(partial), settled


def line_sum(stored, decoded, here, meanwhile, settled):
    heads, width, rows = decoded.shape
    tokens = stored.shape[1]
    base = (here * rows).astype(I32).reshape(1)
    block = jax.ShapeDtypeStruct((heads * width, tokens), BF16)

    def ask(ids, x):
        return lax.ppermute(ids, "mem", [(i, i ^ x) for i in range(4)])

    def crossing(x, pairs):
        return lax.ppermute(x, ("mem", "rep"), [(2 * a + b, 2 * c + d) for a, b, c, d in pairs])

    def pick(ids):
        return pl.pallas_call(
            pick_kernel,
            in_specs=[pl.BlockSpec(memory_space=pltpu.SMEM)]
            + [pl.BlockSpec(memory_space=pltpu.VMEM)] * 2,
            out_shape=block,
            compiler_params=limit(8),
            name="pick_rows",
        )(base, ids, decoded)

    def send(x, *pairs):
        return lax.ppermute(x, "mem", pairs)

    first = ask(stored, 3)
    second = crossing(
        stored,
        [(m, r, m ^ 2, r ^ int(m in (1, 2))) for m in range(4) for r in range(2)],
    )
    third = ask(stored, 1)
    rows_3 = pick(first)
    rows_3, second, third = lax.optimization_barrier((rows_3, second, third))
    inward = send(rows_3, (0, 1), (3, 2))
    across = send(rows_3, (1, 2), (2, 1))
    rows_2 = pick(after(second, rows_3))
    third, settled = lax.optimization_barrier((after(third, rows_2), settled))
    past = crossing(rows_2, [(m, r, m ^ 2, r ^ 1) for m in (0, 3) for r in range(2)])
    rows_1 = pick(third)
    own = pick(after(stored, rows_1))
    beside = send(rows_1, (0, 1), (1, 0), (2, 3), (3, 2))
    onward = after(rows_2, rows_1, own) + inward
    onward = send(onward, (1, 3), (2, 0))
    other = meanwhile(across)
    own, other = lax.optimization_barrier((own + past + beside, other))
    memory = pl.pallas_call(
        merge_kernel,
        in_specs=[pl.BlockSpec(memory_space=pltpu.VMEM)] * 3,
        out_shape=block,
        compiler_params=limit(4),
        name="merge",
    )(own, across, onward)
    return memory, other, settled


def shards(
    hidden, row_ids, row_place, table_codes, table_scales, key_weight, value_weight, conv_weight
):
    mems = lax.axis_size("mem")
    tps = lax.axis_size("tp")
    reps = lax.axis_size("rep")
    blocks = mems * reps
    tokens, heads = row_ids.shape
    rows, width = table_codes.shape[1:]
    depth = heads * width
    half = key_weight.shape[1]
    seq_length = tokens * blocks // SEQS
    assert reps == 2 and seq_length % tokens == 0 and row_place.shape[0] % LANES == 0
    block = lax.axis_index(("mem", "rep"))
    smem = pl.BlockSpec(memory_space=pltpu.SMEM)

    anywhere = pl.BlockSpec(memory_space=pl.ANY)
    resident = pl.BlockSpec(memory_space=pltpu.VMEM)
    places = row_place.reshape(-1, LANES)
    codes = table_codes.transpose(0, 2, 1)
    scales = table_scales.transpose(2, 0, 1)
    stored, codes = pl.pallas_call(
        place_kernel,
        in_specs=[anywhere] * 3,
        out_specs=(resident,) * 2,
        out_shape=(
            jax.ShapeDtypeStruct((heads, tokens), I32),
            jax.ShapeDtypeStruct(codes.shape, BF16),
        ),
        scratch_shapes=[
            pltpu.VMEM((heads, tokens), I32),
            pltpu.VMEM(places.shape, I32),
            pltpu.SemaphoreType.DMA((heads + 2,)),
        ],
        compiler_params=limit(4),
        name="place_rows",
    )(*[in_hbm(x) for x in (row_ids.T, places, codes)])
    decoded = pl.pallas_call(
        decode_kernel,
        in_specs=[resident] * 2,
        out_specs=resident,
        out_shape=jax.ShapeDtypeStruct(codes.shape, BF16),
        compiler_params=limit(6),
        name="decode_tables",
    )(codes, scales)
    here = lax.axis_index("mem")
    other_key = lax.ppermute(key_weight, "rep", [(0, 1), (1, 0)])
    other_value = lax.ppermute(value_weight, "rep", [(0, 1), (1, 0)])
    needed = [(i, i + 1) for i in range(blocks - 1) if (i + 1) * tokens % seq_length]

    def meanwhile(token):
        tail = after(hidden[tokens - RIM :], token)
        return lax.ppermute(tail, ("mem", "rep"), needed)

    summed = line_sum if mems == 4 else scattered_sum
    memory, hidden_halo, others = summed(
        stored, decoded, here, meanwhile, (other_key, other_value)
    )
    weights = [in_hbm(w) for w in (key_weight, value_weight, *others)]

    where = jnp.stack([lax.axis_index("rep"), lax.axis_index("tp")]).astype(I32)
    extended = tokens + RIM
    bodies = [memory] + [
        lax.ppermute(memory, "tp", [(i, (i + s) % tps) for i in range(tps)])
        for s in range(1, tps)
    ]

    def next_rim(rim, s):
        pairs = [
            (
                (a // reps * tps + i) * reps + a % reps,
                (b // reps * tps + (i + s) % tps) * reps + b % reps,
            )
            for a, b in needed
            for i in range(tps)
        ]
        return lax.ppermute(rim, ("mem", "tp", "rep"), pairs)

    rim = memory[:, tokens - LANES :]
    rims = [next_rim(rim, s) for s in range(tps)]
    others = tps - 1
    field = jax.ShapeDtypeStruct((2, extended, half), F32)
    *begun, following, states, power = pl.pallas_call(
        functools.partial(project_own_kernel, tps),
        in_specs=[smem] + [resident] * 2 + [anywhere] * 4 + [resident] * 2,
        out_specs=(resident,) * 5,
        out_shape=(
            field,
            field,
            pltpu.VMEM((2, 2, others * depth, half), BF16),
            jax.ShapeDtypeStruct((2, extended, half), BF16),
            jax.ShapeDtypeStruct((extended, 8), F32),
        ),
        scratch_shapes=[
            pltpu.VMEM((2, 2, depth, half), BF16),
            pltpu.SemaphoreType.DMA((4, 1)),
            pltpu.SemaphoreType.DMA((4, others)),
        ],
        compiler_params=limit(12),
        name="project_own",
    )(where, rims[0], memory, *weights, hidden_halo, hidden)
    values, stats = pl.pallas_call(
        functools.partial(project_others_kernel, tps),
        in_specs=[smem] + [resident] * (2 * others + 5),
        out_specs=(pl.BlockSpec(memory_space=pltpu.HBM), resident),
        out_shape=(pltpu.HBM(field.shape, F32), jax.ShapeDtypeStruct((8, extended), F32)),
        scratch_shapes=[
            pltpu.VMEM((2, extended, half), F32),
            pltpu.SemaphoreType.DMA((2,)),
        ],
        compiler_params=limit(14),
        name="project_others",
    )(where, *rims[1:], *bodies[1:], following, *begun, states, power)

    all_stats = [stats] + [
        lax.ppermute(stats, "tp", [(i, (i + s) % tps) for i in range(tps)]) for s in range(1, tps)
    ]
    keep = (block * tokens % seq_length != 0).astype(I32).reshape(1)
    step = 2 * half
    if half % LANES == 0:
        step = next(c for c in (384, 256, 128) if half % c == 0)
    chunk = min(step, half)
    body = (2, tokens, half)
    values, products = pl.pallas_call(
        functools.partial(prepare_kernel, chunk),
        in_specs=[resident, anywhere],
        out_specs=(resident,) * 2,
        out_shape=(
            jax.ShapeDtypeStruct(body, F32),
            jax.ShapeDtypeStruct((KERNEL - 1, *body), F32),
        ),
        scratch_shapes=[
            pltpu.VMEM((2, extended, half), F32),
            pltpu.SemaphoreType.DMA((2 * half // chunk,)),
        ],
        compiler_params=limit(6),
        name="prepare",
    )(conv_weight, in_hbm(values))
    return pl.pallas_call(
        functools.partial(finish_kernel, tps, step),
        in_specs=[smem] + [resident] * (tps + 4),
        out_specs=anywhere,
        out_shape=jax.ShapeDtypeStruct((tokens, 2 * half), BF16),
        scratch_shapes=[
            pltpu.VMEM((extended, 8), F32),
            pltpu.VMEM((tokens, LANES), F32),
            pltpu.VMEM((KERNEL, tokens, LANES), F32),
            pltpu.VMEM((tokens, 2 * half), BF16),
            pltpu.SemaphoreType.DMA((2 * half // step,)),
        ],
        compiler_params=limit(6),
        name="finish",
    )(keep, *all_stats, values, products, hidden, conv_weight)


def solution(mesh):
    in_specs = (
        P(("parts", "mem", "rep"), "tp"),
        P(("parts", "mem", "rep"), "tp"),
        P("parts"),
        P(("parts", "tp"), "mem", None),
        P(("parts", "tp"), "mem", None),
        P(None, ("tp", "rep")),
        P(None, ("tp", "rep")),
        P(None, "tp"),
    )
    out_specs = P(("parts", "mem", "rep"), "tp")
    return jax.shard_map(shards, mesh=mesh, in_specs=in_specs, out_specs=out_specs, check_vma=False)
```

```python
import functools

import jax
import jax.numpy as jnp
from jax import lax
from jax.experimental import pallas as pl
from jax.experimental.pallas import tpu as pltpu
from jax.sharding import PartitionSpec as P

D = 4608
KERNEL = 4
DILATION = 3
SEQS = 4
EPSILON = 1e-06
RIM = 16
LANES = 128

F32 = jnp.float32
BF16 = jnp.bfloat16
I32 = jnp.int32


def iota(shape, axis):
    return lax.broadcasted_iota(I32, shape, axis)


def dot(a, b):
    return jnp.dot(a, b, preferred_element_type=F32)


def dot_nt(a, b, precision=None):
    return lax.dot_general(
        a, b, (((1,), (1,)), ((), ())), precision=precision, preferred_element_type=F32
    )


def unit(n, dtype):
    return (iota((n, n), 0) == iota((n, n), 1)).astype(F32).astype(dtype)


def to_bf16(x):
    return x.astype(F32).astype(BF16)


def place_kernel(
    ids_hbm, place_hbm, codes_hbm, out_ref, codes_ref, ids_ref, place_ref, sems
):
    copies = [
        pltpu.make_async_copy(place_hbm, place_ref, sems.at[0]),
        pltpu.make_async_copy(ids_hbm, ids_ref, sems.at[1]),
    ]
    for n in range(codes_ref.shape[0]):
        copies.append(
            pltpu.make_async_copy(codes_hbm.at[n], codes_ref.at[n], sems.at[2 + n])
        )
    for copy in copies:
        copy.start()
    copies[0].wait()
    place = place_ref[...]
    rows = place.shape[0]
    heads, tokens = ids_ref.shape
    eye = unit(LANES, BF16)
    table = jnp.concatenate(
        [dot_nt(eye, to_bf16(place >> 8)), dot_nt(eye, to_bf16(place & 255))], axis=0
    ).astype(BF16)
    copies[1].wait()
    for head in range(heads):
        row = ids_ref[head : head + 1, :]
        hot = to_bf16(iota((rows, tokens), 0) == (row >> 7))
        both = dot(table, hot)
        value = both[:LANES] * 256.0 + both[LANES:]
        chosen = jnp.where(iota(value.shape, 0) == (row & 127), value, 0.0)
        out_ref[head : head + 1, :] = jnp.sum(chosen, axis=0, keepdims=True).astype(I32)
    for copy in copies[2:]:
        copy.wait()


def decode_kernel(codes_ref, scales_ref, out_ref):
    heads, width, rows = codes_ref.shape
    blocks = scales_ref.shape[0]
    entry = iota((width, 2 * width), 0)
    column = iota((width, 2 * width), 1)
    column = jnp.where(column < width, column, column - width)
    parity = entry & column & 15
    parity = parity ^ (parity >> 2)
    parity = (parity ^ (parity >> 1)) & 1
    same = (entry >> 4) == (column >> 4)
    rotation = jnp.where(same, 0.25 - 0.5 * parity.astype(F32), 0.0).astype(BF16)
    scales = scales_ref[...].astype(F32)
    for head in range(heads):
        factors = jnp.concatenate(
            [
                jnp.broadcast_to(scales[b, head : head + 1, :], (16, rows))
                for b in range(blocks)
            ],
            axis=0,
        )
        scaled = codes_ref[head].astype(F32) * factors
        upper = scaled.astype(BF16)
        lower = (scaled - upper.astype(F32)).astype(BF16)
        out_ref[head] = dot(rotation, jnp.concatenate([upper, lower], axis=0)).astype(BF16)


def picked(local, table_ref, head):
    rows = table_ref.shape[2]
    hot = to_bf16(iota((rows, local.shape[1]), 0) == local[head : head + 1, :])
    return dot(table_ref[head], hot).astype(BF16)


def pick_kernel(base_ref, ids_ref, table_ref, out_ref):
    heads, width, _ = table_ref.shape
    local = ids_ref[...] - base_ref[0]
    for head in range(heads):
        out_ref[head * width : (head + 1) * width, :] = picked(local, table_ref, head)


def merge_kernel(*refs):
    total = refs[0][...].astype(F32)
    for other in refs[1:-1]:
        total = total + other[...].astype(F32)
    refs[-1][...] = total.astype(BF16)


def fetch(count, tp, depth, source, target, shifts, sems):
    copies = []
    for n, s in enumerate(shifts):
        owner = lax.rem(tp + count - s, count)
        rows = pl.ds(pl.multiple_of(owner * depth, depth), depth)
        copy = pltpu.make_async_copy(
            source.at[rows, :], target.at[pl.ds(n * depth, depth), :], sems.at[n]
        )
        copy.start()
        copies.append(copy)
    return copies


def await_all(copies):
    for copy in copies:
        copy.wait()


def with_rim(rims, bodies):
    body = jnp.concatenate([b[...].astype(F32) for b in bodies], axis=0).T.astype(BF16)
    rim = jnp.concatenate([r[...].astype(F32) for r in rims], axis=0).T.astype(BF16)
    return jnp.concatenate([rim[LANES - RIM :], body], axis=0)


def project_own_kernel(count, where_ref, rim_ref, body_ref, *refs):
    weights, hidden_halo, hidden = refs[:4], refs[4], refs[5]
    key_ref, value_ref, next_ref, states_ref, power_ref, held, sems, next_sems = refs[6:]
    half = value_ref.shape[-1]
    depth = body_ref.shape[0]
    rep = where_ref[0]
    tp = where_ref[1]
    order = [(far, which) for far in range(2) for which in (1, 0)]
    copies = {
        (far, which): fetch(
            count, tp, depth, weights[2 * far + which], held.at[far, which], (0,),
            sems.at[2 * far + which],
        )
        for far, which in order
    }
    memory = with_rim([rim_ref], [body_ref])
    later = []
    for far, which in order:
        slot = rep if far == 0 else 1 - rep
        await_all(copies[far, which])
        if not later:
            for f, w in order:
                later += fetch(
                    count, tp, depth, weights[2 * f + w], next_ref.at[f, w], range(1, count),
                    next_sems.at[2 * f + w],
                )
        target = value_ref if which == 1 else key_ref
        target[slot] = dot(memory, held[far, which])
        if (far, which) == (0, 1):
            power = 0.0
            for side in range(2):
                span = slice(side * half, (side + 1) * half)
                states_ref[side, :RIM] = hidden_halo[:, span]
                states_ref[side, RIM:] = hidden[:, span]
                here = states_ref[side].astype(F32)
                power = power + jnp.sum(here * here, axis=1, keepdims=True)
            power_ref[...] = jnp.broadcast_to(power, power_ref.shape)
    await_all(later)


def project_others_kernel(count, where_ref, *refs):
    pieces = count - 1
    rims, bodies = refs[:pieces], refs[pieces : 2 * pieces]
    held, begun_keys, begun_values, states_ref, power_ref = refs[2 * pieces :][:5]
    value_hbm, stats_ref, done, done_sems = refs[2 * pieces + 5 :]
    rep = where_ref[0]
    memory = with_rim(rims, bodies)
    sums = [0.0] * 3
    later = []
    for far in range(2):
        slot = rep if far == 0 else 1 - rep
        fields = [None, None]
        for which in (1, 0):
            fields[which] = dot(memory, held[far, which])
            if which == 1:
                done[far] = fields[1] + begun_values[slot]
                copy = pltpu.make_async_copy(done.at[far], value_hbm.at[slot], done_sems.at[far])
                copy.start()
                later.append(copy)
        keys = fields[0] + begun_keys[slot]
        values = done[far]
        terms = (keys * keys, states_ref[slot].astype(F32) * keys, values * values)
        sums = [a + jnp.sum(t, axis=1, keepdims=True) for a, t in zip(sums, terms)]
    packed = power_ref[...]
    lane = iota(packed.shape, 1)
    for k in range(3):
        packed = jnp.where(lane == k + 1, sums[k], packed)
    stats_ref[...] = dot_nt(unit(8, F32), packed, lax.Precision.HIGHEST)
    await_all(later)


def prepare_kernel(chunk, taps_ref, value_hbm, value_ref, tap_ref, rows_ref, sems):
    half = rows_ref.shape[-1]
    tokens = value_ref.shape[1]
    copies = []
    for slot in range(2):
        for start in range(0, half, chunk):
            span = pl.ds(start, chunk)
            copy = pltpu.make_async_copy(
                value_hbm.at[slot, :, span], rows_ref.at[slot, :, span], sems.at[len(copies)]
            )
            copy.start()
            copies.append(copy)
    for slot in range(2):
        for start in range(0, half, LANES):
            size = min(LANES, half - start)
            span = slice(start, start + size)
            there = slice(slot * half + start, slot * half + start + size)
            if start % chunk == 0:
                copies[(slot * half + start) // chunk].wait()
            value_ref[slot, :, span] = rows_ref[slot, RIM:, span]
            for tap in range(1, KERNEL):
                lag = DILATION * tap
                rows = rows_ref[slot, RIM - lag : RIM - lag + tokens, span]
                tap_ref[tap - 1, slot, :, span] = taps_ref[tap : tap + 1, there] * rows


def finish_kernel(count, step, keep_ref, *refs):
    stats = refs[:count]
    value_ref, tap_ref, hidden_ref, taps_ref, out_hbm = refs[count : count + 5]
    columns, gates, factors, out_ref, sems = refs[count + 5 :]
    half = value_ref.shape[-1]
    tokens, width = out_ref.shape
    total = stats[0][...]
    for other in stats[1:]:
        total = total + other[...]
    inverse_states = lax.rsqrt(total[0:1] / D + EPSILON)
    inverse_keys = lax.rsqrt(total[1:2] / D + EPSILON)
    gate = jax.nn.sigmoid(total[2:3] * inverse_states * inverse_keys / D**0.5)
    factor = gate * lax.rsqrt(gate * gate * total[3:4] / D + EPSILON)
    factor = jnp.where((iota(factor.shape, 1) < RIM) & (keep_ref[0] == 0), 0.0, factor)
    line = iota(total.shape, 0)
    both = jnp.where(line == 0, gate, jnp.where(line == 1, factor, 0.0))
    columns[...] = dot_nt(unit(total.shape[1], F32), both, lax.Precision.HIGHEST)
    gates[...] = jnp.broadcast_to(columns[RIM:, 0:1], gates.shape)
    for tap in range(KERNEL):
        lag = DILATION * tap
        factors[tap] = jnp.broadcast_to(
            columns[RIM - lag : RIM - lag + tokens, 1:2], factors.shape[1:]
        )
    copies = []
    for slot in range(2):
        for start in range(0, half, LANES):
            size = min(LANES, half - start)
            span = slice(start, start + size)
            there = slice(slot * half + start, slot * half + start + size)
            values = value_ref[slot, :, span]
            conv = taps_ref[0:1, there] * values * factors[0, :, :size]
            for tap in range(1, KERNEL):
                conv = conv + tap_ref[tap - 1, slot, :, span] * factors[tap, :, :size]
            gated = values * gates[:, :size]
            out_ref[:, there] = (
                hidden_ref[:, there].astype(F32) + jax.nn.silu(conv) + gated
            ).astype(BF16)
            if there.stop % step == 0:
                ready = pl.ds(there.stop - step, step)
                copy = pltpu.make_async_copy(
                    out_ref.at[:, ready], out_hbm.at[:, ready], sems.at[len(copies)]
                )
                copy.start()
                copies.append(copy)
    for copy in copies:
        copy.wait()


def whole(array):
    return pl.BlockSpec(array.shape, lambda *_: (0,) * array.ndim)


def in_hbm(array):
    return pltpu.with_memory_space_constraint(array, pltpu.HBM)


def after(array, *others):
    return lax.optimization_barrier((array, *others))[0]


def limit(mib):
    return pltpu.CompilerParams(vmem_limit_bytes=mib << 20)


def scattered_sum(stored, decoded, here, meanwhile, settled):
    mems = lax.axis_size("mem")
    heads, width, rows = decoded.shape
    tokens = stored.shape[1]
    asked = lax.all_gather(stored, "mem", axis=0)
    partial = pl.pallas_call(
        pick_kernel,
        grid=(mems,),
        in_specs=[
            pl.BlockSpec(memory_space=pltpu.SMEM),
            pl.BlockSpec((None, heads, tokens), lambda m: (m, 0, 0)),
            whole(decoded),
        ],
        out_specs=pl.BlockSpec((None, heads * width, tokens), lambda m: (m, 0, 0)),
        out_shape=jax.ShapeDtypeStruct((mems, heads * width, tokens), BF16),
        compiler_params=limit(16),
        name="pick_all",
    )((here * rows).astype(I32).reshape(1), asked, decoded)
    total = lax.psum_scatter(partial, "mem", scatter_dimension=0, tiled=False)
    return total, meanwhile(partial), settled


def line_sum(stored, decoded, here, meanwhile, settled):
    heads, width, rows = decoded.shape
    tokens = stored.shape[1]
    base = (here * rows).astype(I32).reshape(1)
    block = jax.ShapeDtypeStruct((heads * width, tokens), BF16)

    def ask(ids, x):
        return lax.ppermute(ids, "mem", [(i, i ^ x) for i in range(4)])

    def crossing(x, pairs):
        return lax.ppermute(x, ("mem", "rep"), [(2 * a + b, 2 * c + d) for a, b, c, d in pairs])

    def pick(ids):
        return pl.pallas_call(
            pick_kernel,
            in_specs=[pl.BlockSpec(memory_space=pltpu.SMEM)]
            + [pl.BlockSpec(memory_space=pltpu.VMEM)] * 2,
            out_shape=block,
            compiler_params=limit(8),
            name="pick_rows",
        )(base, ids, decoded)

    def send(x, *pairs):
        return lax.ppermute(x, "mem", pairs)

    first = ask(stored, 3)
    second = crossing(
        stored,
        [(m, r, m ^ 2, r ^ int(m in (1, 2))) for m in range(4) for r in range(2)],
    )
    third = ask(stored, 1)
    rows_3 = pick(first)
    rows_3, second, third = lax.optimization_barrier((rows_3, second, third))
    inward = send(rows_3, (0, 1), (3, 2))
    across = send(rows_3, (1, 2), (2, 1))
    rows_2 = pick(after(second, rows_3))
    third, settled = lax.optimization_barrier((after(third, rows_2), settled))
    past = crossing(rows_2, [(m, r, m ^ 2, r ^ 1) for m in (0, 3) for r in range(2)])
    rows_1 = pick(third)
    own = pick(after(stored, rows_1))
    beside = send(rows_1, (0, 1), (1, 0), (2, 3), (3, 2))
    onward = after(rows_2, rows_1, own) + inward
    onward = send(onward, (1, 3), (2, 0))
    other = meanwhile(across)
    own, other = lax.optimization_barrier((own + past + beside, other))
    memory = pl.pallas_call(
        merge_kernel,
        in_specs=[pl.BlockSpec(memory_space=pltpu.VMEM)] * 3,
        out_shape=block,
        compiler_params=limit(4),
        name="merge",
    )(own, across, onward)
    return memory, other, settled


def shards(
    hidden, row_ids, row_place, table_codes, table_scales, key_weight, value_weight, conv_weight
):
    mems = lax.axis_size("mem")
    tps = lax.axis_size("tp")
    reps = lax.axis_size("rep")
    blocks = mems * reps
    tokens, heads = row_ids.shape
    rows, width = table_codes.shape[1:]
    depth = heads * width
    half = key_weight.shape[1]
    seq_length = tokens * blocks // SEQS
    assert reps == 2 and seq_length % tokens == 0 and row_place.shape[0] % LANES == 0
    block = lax.axis_index(("mem", "rep"))
    smem = pl.BlockSpec(memory_space=pltpu.SMEM)

    anywhere = pl.BlockSpec(memory_space=pl.ANY)
    resident = pl.BlockSpec(memory_space=pltpu.VMEM)
    places = row_place.reshape(-1, LANES)
    codes = table_codes.transpose(0, 2, 1)
    scales = table_scales.transpose(2, 0, 1)
    stored, codes = pl.pallas_call(
        place_kernel,
        in_specs=[anywhere] * 3,
        out_specs=(resident,) * 2,
        out_shape=(
            jax.ShapeDtypeStruct((heads, tokens), I32),
            jax.ShapeDtypeStruct(codes.shape, BF16),
        ),
        scratch_shapes=[
            pltpu.VMEM((heads, tokens), I32),
            pltpu.VMEM(places.shape, I32),
            pltpu.SemaphoreType.DMA((heads + 2,)),
        ],
        compiler_params=limit(4),
        name="place_rows",
    )(*[in_hbm(x) for x in (row_ids.T, places, codes)])
    decoded = pl.pallas_call(
        decode_kernel,
        in_specs=[resident] * 2,
        out_specs=resident,
        out_shape=jax.ShapeDtypeStruct(codes.shape, BF16),
        compiler_params=limit(6),
        name="decode_tables",
    )(codes, scales)
    here = lax.axis_index("mem")
    other_key = lax.ppermute(after(key_weight, decoded), "rep", [(0, 1), (1, 0)])
    other_value = lax.ppermute(after(value_weight, decoded), "rep", [(0, 1), (1, 0)])
    needed = [(i, i + 1) for i in range(blocks - 1) if (i + 1) * tokens % seq_length]

    def meanwhile(token):
        tail = after(hidden[tokens - RIM :], token)
        return lax.ppermute(tail, ("mem", "rep"), needed)

    summed = line_sum if mems == 4 else scattered_sum
    memory, hidden_halo, others = summed(
        stored, decoded, here, meanwhile, (other_key, other_value)
    )
    weights = [in_hbm(w) for w in (key_weight, value_weight, *others)]

    where = jnp.stack([lax.axis_index("rep"), lax.axis_index("tp")]).astype(I32)
    extended = tokens + RIM
    bodies = [memory] + [
        lax.ppermute(memory, "tp", [(i, (i + s) % tps) for i in range(tps)])
        for s in range(1, tps)
    ]

    def next_rim(rim, s):
        pairs = [
            (
                (a // reps * tps + i) * reps + a % reps,
                (b // reps * tps + (i + s) % tps) * reps + b % reps,
            )
            for a, b in needed
            for i in range(tps)
        ]
        return lax.ppermute(rim, ("mem", "tp", "rep"), pairs)

    rim = memory[:, tokens - LANES :]
    rims = [next_rim(rim, s) for s in range(tps)]
    others = tps - 1
    field = jax.ShapeDtypeStruct((2, extended, half), F32)
    *begun, following, states, power = pl.pallas_call(
        functools.partial(project_own_kernel, tps),
        in_specs=[smem] + [resident] * 2 + [anywhere] * 4 + [resident] * 2,
        out_specs=(resident,) * 5,
        out_shape=(
            field,
            field,
            pltpu.VMEM((2, 2, others * depth, half), BF16),
            jax.ShapeDtypeStruct((2, extended, half), BF16),
            jax.ShapeDtypeStruct((extended, 8), F32),
        ),
        scratch_shapes=[
            pltpu.VMEM((2, 2, depth, half), BF16),
            pltpu.SemaphoreType.DMA((4, 1)),
            pltpu.SemaphoreType.DMA((4, others)),
        ],
        compiler_params=limit(12),
        name="project_own",
    )(where, rims[0], memory, *weights, hidden_halo, hidden)
    values, stats = pl.pallas_call(
        functools.partial(project_others_kernel, tps),
        in_specs=[smem] + [resident] * (2 * others + 5),
        out_specs=(pl.BlockSpec(memory_space=pltpu.HBM), resident),
        out_shape=(pltpu.HBM(field.shape, F32), jax.ShapeDtypeStruct((8, extended), F32)),
        scratch_shapes=[
            pltpu.VMEM((2, extended, half), F32),
            pltpu.SemaphoreType.DMA((2,)),
        ],
        compiler_params=limit(14),
        name="project_others",
    )(where, *rims[1:], *bodies[1:], following, *begun, states, power)

    all_stats = [stats] + [
        lax.ppermute(stats, "tp", [(i, (i + s) % tps) for i in range(tps)]) for s in range(1, tps)
    ]
    keep = (block * tokens % seq_length != 0).astype(I32).reshape(1)
    step = 2 * half
    if half % LANES == 0:
        step = next(c for c in (384, 256, 128) if half % c == 0)
    chunk = min(step, half)
    body = (2, tokens, half)
    values, products = pl.pallas_call(
        functools.partial(prepare_kernel, chunk),
        in_specs=[resident, anywhere],
        out_specs=(resident,) * 2,
        out_shape=(
            jax.ShapeDtypeStruct(body, F32),
            jax.ShapeDtypeStruct((KERNEL - 1, *body), F32),
        ),
        scratch_shapes=[
            pltpu.VMEM((2, extended, half), F32),
            pltpu.SemaphoreType.DMA((2 * half // chunk,)),
        ],
        compiler_params=limit(6),
        name="prepare",
    )(conv_weight, in_hbm(values))
    return pl.pallas_call(
        functools.partial(finish_kernel, tps, step),
        in_specs=[smem] + [resident] * (tps + 4),
        out_specs=anywhere,
        out_shape=jax.ShapeDtypeStruct((tokens, 2 * half), BF16),
        scratch_shapes=[
            pltpu.VMEM((extended, 8), F32),
            pltpu.VMEM((tokens, LANES), F32),
            pltpu.VMEM((KERNEL, tokens, LANES), F32),
            pltpu.VMEM((tokens, 2 * half), BF16),
            pltpu.SemaphoreType.DMA((2 * half // step,)),
        ],
        compiler_params=limit(6),
        name="finish",
    )(keep, *all_stats, values, products, hidden, conv_weight)


def solution(mesh):
    in_specs = (
        P(("parts", "mem", "rep"), "tp"),
        P(("parts", "mem", "rep"), "tp"),
        P("parts"),
        P(("parts", "tp"), "mem", None),
        P(("parts", "tp"), "mem", None),
        P(None, ("tp", "rep")),
        P(None, ("tp", "rep")),
        P(None, "tp"),
    )
    out_specs = P(("parts", "mem", "rep"), "tp")
    return jax.shard_map(shards, mesh=mesh, in_specs=in_specs, out_specs=out_specs, check_vma=False)
```
